512 devices in a mesh: dates: 8 (over x, core), cols: 64 (over y, z).
Axes of the slice: x: 4, y: 8, z: 8, core: 2. Of those that a mesh axis runs over, the one named last changes fastest.
Arguments:
- slc: bfloat16 [2, 32, 128, 16384], P(None, 'dates', None, 'cols')
- pairs: int32 [64, 2], replicated, may hold values from 0 to 31, as said below
- owner: int32 [64], replicated, may hold values from 0 to 7, as said below
Outputs:
- interferogram: float32 [2, 96, 32, 1024], P(None, 'dates', None, 'cols')
- coherence: float32 [96, 32, 1024], P('dates', None, 'cols')
The draws below stay inside these ranges and needn't reach their ends.
Inputs may be any that keep to these rules, and one draw needn't show every extreme that they name: `pairs`: reference < secondary <= reference + 5 for every pair. Each owner holds at most 12 pairs, and some owner holds exactly 12.
All inputs are finite; a program needn't handle non-finite values.
Results may differ from the reference program's by a relative error of at most 0.0003.
Values may be sent and summed in bfloat16 or wider, within the bound.
A program may use at most 64 MiB of HBM per device.

```python
import math
import jax
import jax.numpy as jnp
from jax import lax

ROWS = 128
DATES = 32
COLS = 16384
PAIRS = 64
PAIR_CAP = 12
SLOTS = 96
N_DATES = 8


def draw_slc(key, part):
    key = jax.random.fold_in(key, 5)
    keys = jax.random.split(key, 4)
    common = jax.random.normal(keys[0], (2, 1, ROWS, COLS), jnp.float32)
    noise = jax.random.normal(keys[1], (2, DATES, ROWS, COLS), jnp.float32)
    columns = jnp.arange(COLS, dtype=jnp.float32)
    envelope = 1.0 + 2.0 * columns / max(COLS - 1, 1)
    texture = jnp.exp(jax.random.uniform(keys[2], (1, DATES, 1, COLS), jnp.float32) * math.log(3.3))
    shared = jax.random.uniform(keys[3], (1, DATES, 1, 1), jnp.float32, 0.5, 0.9)
    field = (shared * common + jnp.sqrt(1.0 - shared * shared) * noise) * envelope * texture
    return field.astype(jnp.bfloat16)


def draw_pairs(key, part):
    key = jax.random.fold_in(key, 7)
    first_key, gap_key = jax.random.split(key)
    first = jax.random.randint(first_key, (PAIRS,), 0, DATES - 1)
    gap = jax.random.randint(gap_key, (PAIRS,), 1, 6)
    second = jnp.minimum(first + gap, DATES - 1)
    return jnp.stack([first, second], axis=1).astype(jnp.int32)


def shuffled(key, count):
    scores = jax.random.randint(key, (count,), 0, 1 << 20) * 1024 + jnp.arange(count, dtype=jnp.int32)
    return jnp.argsort(scores, stable=True).astype(jnp.int32)


def draw_owner(key, part):
    key = jax.random.fold_in(key, 11)
    keys = jax.random.split(key, 3)
    busiest = jax.random.randint(keys[0], (1,), 0, N_DATES)[0]
    spare = shuffled(keys[1], (N_DATES - 1) * PAIR_CAP)[0:PAIRS - PAIR_CAP]
    others = (spare // PAIR_CAP + 1 + busiest) % N_DATES
    owners = jnp.concatenate([jnp.full((PAIR_CAP,), busiest, jnp.int32), others.astype(jnp.int32)])
    return owners[shuffled(keys[2], PAIRS)].astype(jnp.int32)


def setup_inputs(seed: int = 0) -> dict:
    seeds = jax.random.split(jax.random.key(seed), 4)
    slc = draw_slc(jax.random.fold_in(seeds[3], 71), 0)
    pairs = draw_pairs(jax.random.fold_in(seeds[3], 71), 0)
    owner = draw_owner(jax.random.fold_in(seeds[3], 71), 0)
    return {"slc": slc, "pairs": pairs, "owner": owner}


TAPS = [math.exp(-k * k / 8.0) for k in range(-4, 5)]
WEIGHTS = [t / sum(TAPS) for t in TAPS]

def smooth(plane):
    count = plane.shape[0]
    inner = plane.shape[1] - 8
    padded = jnp.pad(plane, ((4, 4), (0, 0)))
    along = WEIGHTS[0] * padded[0:count]
    for k in range(1, 9):
        along = along + WEIGHTS[k] * padded[k:k + count]
    result = WEIGHTS[0] * along[:, 0:inner]
    for k in range(1, 9):
        result = result + WEIGHTS[k] * along[:, k:k + inner]
    return result

def looks(plane):
    count, inner = plane.shape
    return lax.optimization_barrier(jnp.mean(plane.reshape(count // 4, 4, inner // 16, 16), axis=(1, 3)))

def one_pair(tile, first_scale, second_scale):
    values = tile.astype(jnp.float32)
    real_a = values[0, 0]
    imag_a = values[0, 1]
    real_b = values[1, 0]
    imag_b = values[1, 1]
    real_part = real_a * real_b + imag_a * imag_b
    imag_part = imag_a * real_b - real_a * imag_b
    power_first = real_a * real_a + imag_a * imag_a
    power_second = real_b * real_b + imag_b * imag_b
    smooth_real = smooth(real_part)
    smooth_imag = smooth(imag_part)
    smooth_first = smooth(power_first)
    smooth_second = smooth(power_second)
    cell_coherence = jnp.sqrt(smooth_real * smooth_real + smooth_imag * smooth_imag) / (jnp.sqrt(smooth_first * smooth_second) + 1e-06)
    inner = real_part.shape[1] - 8
    product_scale = first_scale * second_scale
    look_real = looks(real_part[:, 4:4 + inner]) / product_scale
    look_imag = looks(imag_part[:, 4:4 + inner]) / product_scale
    return jnp.stack([look_real, look_imag, looks(cell_coherence)])

def reference(slc, pairs, owner):

    def date_power(index):
        image = lax.dynamic_index_in_dim(slc, index, 1, keepdims=False).astype(jnp.float32)
        return jnp.sum(image * image)
    squares = lax.map(date_power, jnp.arange(DATES, dtype=jnp.int32))
    scales = jnp.sqrt(squares / (ROWS * COLS) + 1e-06)

    def one(pair):
        first = lax.dynamic_index_in_dim(slc, pair[0], 1, keepdims=False)
        second = lax.dynamic_index_in_dim(slc, pair[1], 1, keepdims=False)
        tile = jnp.pad(jnp.stack([first, second]), ((0, 0), (0, 0), (0, 0), (4, 4)))
        return one_pair(tile, scales[pair[0]], scales[pair[1]])
    results = lax.map(one, pairs)
    order = jnp.arange(PAIRS, dtype=jnp.int32)
    same = owner[:, None] == owner[None, :]
    rank = lax.optimization_barrier(jnp.sum(same & (order[None, :] < order[:, None]), axis=1)).astype(jnp.int32)
    slot = (owner * PAIR_CAP + rank).astype(jnp.int32)
    placed = jnp.zeros((SLOTS, 3, ROWS // 4, COLS // 16), jnp.float32).at[slot].set(results)
    return (jnp.moveaxis(placed[:, 0:2], 1, 0), placed[:, 2])
```

```python
import math

import jax
import jax.numpy as jnp
import ml_dtypes
import numpy as np
from jax import lax
from jax.experimental import pallas as pl
from jax.experimental.pallas import tpu as pltpu
from jax.sharding import PartitionSpec as P

MESH = pl.DeviceIdType.MESH
F32 = jnp.float32
BF16 = jnp.bfloat16

TAPS = [math.exp(-k * k / 8.0) for k in range(-4, 5)]
WEIGHTS = [float(np.float32(t / sum(TAPS))) for t in TAPS]
HIGH = [float(np.float32(w).astype(ml_dtypes.bfloat16)) for w in WEIGHTS]
LOW = [float(np.float32(w - h).astype(ml_dtypes.bfloat16)) for w, h in zip(WEIGHTS, HIGH)]

GROUP = 8
EACH = 4
DATES = GROUP * EACH
PAIRS = 64
CAP = 12
ROWS = 128
PART = 32
TILE = PART + 8
WIDTH = GROUP * PART
BLOCK = EACH * 2 * TILE
EDGE = EACH * 2 * 8
CHUNK = 8


def split(x):
    high = x.astype(BF16)
    return high, (x - high.astype(F32)).astype(BF16)


def split3(x):
    high = x.astype(BF16)
    rest = x - high.astype(F32)
    mid = rest.astype(BF16)
    return high, mid, (rest - mid.astype(F32)).astype(BF16)


def dot(a, b):
    return jnp.dot(a, b, preferred_element_type=F32)


def iota(shape, axis):
    return lax.broadcasted_iota(jnp.int32, shape, axis)


def cutter():
    lane = iota((TILE, WIDTH), 1)
    row = iota((TILE, WIDTH), 0)
    pieces = [jnp.where(lane == row + (PART * e - 4), 1.0, 0.0) for e in range(GROUP)]
    lane = iota((8, WIDTH), 1)
    row = iota((8, WIDTH), 0)
    pieces.append(jnp.where(lane == row + (WIDTH - 4), 1.0, 0.0))
    pieces.append(jnp.where(lane == row - 4, 1.0, 0.0))
    return jnp.concatenate(pieces, axis=0).astype(BF16)


def band(weights):
    gap = jnp.abs(iota((ROWS, ROWS), 0) - iota((ROWS, ROWS), 1))
    result = jnp.zeros((ROWS, ROWS), F32)
    for k in range(5):
        result = jnp.where(gap == k, weights[4 + k], result)
    return result.astype(BF16)


def along_columns(ref, index):
    result = WEIGHTS[4] * ref[index, 4 : 4 + PART, :]
    for k in range(4):
        both = ref[index, k : k + PART, :] + ref[index, 8 - k : 8 - k + PART, :]
        result = result + WEIGHTS[k] * both
    return result


def kernel(
    ny, nz, slc, pairs_s, pairs_v, owner_v, landed,
    smoother, sent, got, edge_out, edge_in, images, roots, fields, lhs, sums,
    power_y, power_z, power_d, power_y_in, power_z_in, totals, results,
    main_send, main_recv, edge_send, edge_recv, y_send, y_recv, z_send, z_recv,
    d_send, d_recv, out_send, out_recv,
):
    d = lax.axis_index("dates")
    c = lax.axis_index("cols")
    count = ny * nz
    y = c // nz
    z = c % nz

    def date_peer(k):
        return {"dates": (d + k) % GROUP, "cols": c}

    def y_peer(k):
        return {"dates": d, "cols": ((y + k) % ny) * nz + z}

    def z_peer(k):
        return {"dates": d, "cols": y * nz + (z + k) % nz}

    after = (c + 1) % count
    before = (c + count - 1) % count

    barrier = pltpu.get_barrier_semaphore()

    def greet(device):
        pl.semaphore_signal(barrier, inc=1, device_id=device, device_id_type=MESH)

    for k in range(1, GROUP):
        greet(date_peer(k))
    for k in range(1, ny):
        greet(y_peer(k))
    for k in range(1, nz):
        greet(z_peer(k))

    @pl.when(d == 0)
    def _():
        for e in range(GROUP):
            greet({"dates": e, "cols": before})

    @pl.when(d == GROUP - 1)
    def _():
        for e in range(GROUP):
            greet({"dates": e, "cols": after})

    cut = cutter()
    power_rows = []
    for t in range(EACH):
        both = jnp.concatenate([slc[0, t], slc[1, t]], axis=0)
        turned = lax.dot_general(cut, both, (((1,), (1,)), ((), ())), preferred_element_type=F32)
        real = turned[:, :ROWS]
        imag = turned[:, ROWS:]
        for e in range(GROUP):
            part = slice(TILE * e, TILE * e + TILE)
            sent[e, 2 * TILE * t : 2 * TILE * (t + 1), :] = jnp.concatenate(
                [real[part], imag[part]], axis=0
            ).astype(BF16)
        for side in range(2):
            part = slice(TILE * GROUP + 8 * side, TILE * GROUP + 8 * side + 8)
            edge_out[side, 16 * t : 16 * (t + 1), :] = jnp.concatenate(
                [real[part], imag[part]], axis=0
            ).astype(BF16)
        wide = both.astype(F32)
        square = jnp.sum(wide * wide, axis=0, keepdims=True)
        power_rows.append(square[:, :ROWS] + square[:, ROWS:])
    power_y[...] = jnp.concatenate(power_rows + [jnp.zeros((8 - EACH, ROWS), F32)], axis=0)

    pl.semaphore_wait(barrier, (GROUP - 1) + (ny - 1) + (nz - 1) + 2)

    def spread(src, dst, send, recv, peer, number):
        copies = []
        for k in range(1, number):
            copy = pltpu.make_async_remote_copy(
                src_ref=src(k), dst_ref=dst(k), send_sem=send.at[k - 1], recv_sem=recv.at[k - 1],
                device_id=peer(k), device_id_type=MESH,
            )
            copy.start()
            copies.append(copy)
        return copies

    y_copies = spread(lambda k: power_y, lambda k: power_y_in.at[k - 1], y_send, y_recv, y_peer, ny)
    main_copies = spread(
        lambda k: sent.at[(d + k) % GROUP], lambda k: got.at[d], main_send, main_recv, date_peer, GROUP
    )
    edge_copies = []
    for side, device in enumerate(
        ({"dates": 0, "cols": after}, {"dates": GROUP - 1, "cols": before})
    ):
        copy = pltpu.make_async_remote_copy(
            src_ref=edge_out.at[side], dst_ref=edge_in.at[d], send_sem=edge_send.at[side],
            recv_sem=edge_recv.at[d], device_id=device, device_id_type=MESH,
        )
        copy.start()
        edge_copies.append(copy)

    high = band(HIGH)
    low = band(LOW)
    smoother[:, :ROWS] = jnp.concatenate([high, high], axis=0)
    smoother[:, ROWS:] = jnp.concatenate([low, low], axis=0)

    owner_row = owner_v[...]
    owner_down = jnp.transpose(jnp.broadcast_to(owner_row.astype(F32), (ROWS, PAIRS)))[:, :PAIRS]
    earlier = iota((PAIRS, PAIRS), 0) < iota((PAIRS, PAIRS), 1)
    same = owner_down == owner_row.astype(F32)
    rank = jnp.sum(jnp.where(same & earlier, 1.0, 0.0), axis=0, keepdims=True).astype(jnp.int32)
    place = (rank & 3) * 32 + owner_row * 4 + (rank >> 2)
    select = jnp.where(iota((128, PAIRS), 0) == place, 1.0, 0.0).astype(BF16)

    def date_rows(which):
        date = pairs_v[which : which + 1, :]
        row = ((date >> 2) * 8 + (date & 3)).astype(F32)
        down = jnp.transpose(jnp.broadcast_to(row, (ROWS, PAIRS)))[:, : 8 * GROUP]
        lane = iota((PAIRS, 8 * GROUP), 1).astype(F32)
        return jnp.where(down == lane, 1.0, 0.0).astype(BF16)

    def take(source, block):
        for t in range(EACH):
            piece = block[2 * TILE * t : 2 * TILE * (t + 1), :].astype(F32)
            images[source * EACH + t, 0] = piece[:TILE]
            images[source * EACH + t, 1] = piece[TILE:]

        @pl.when((d == 0) & (c > 0))
        def _():
            for t in range(EACH):
                piece = edge_in[source, 16 * t : 16 * (t + 1), :].astype(F32)
                images[source * EACH + t, 0, 0:8] += piece[:8]
                images[source * EACH + t, 1, 0:8] += piece[8:]

        @pl.when((d == GROUP - 1) & (c < count - 1))
        def _():
            for t in range(EACH):
                piece = edge_in[source, 16 * t : 16 * (t + 1), :].astype(F32)
                images[source * EACH + t, 0, TILE - 8 : TILE] += piece[:8]
                images[source * EACH + t, 1, TILE - 8 : TILE] += piece[8:]

        for t in range(EACH):
            real = images[source * EACH + t, 0]
            imag = images[source * EACH + t, 1]
            fields[t] = real * real + imag * imag
        for t in range(EACH):
            big, small = split(along_columns(fields, t))
            lhs[PART * t : PART * (t + 1), :ROWS] = big
            lhs[PART * t : PART * (t + 1), ROWS:] = small
        smooth = dot(lhs[: EACH * PART, :], smoother[...])
        smooth = jnp.sqrt(smooth[:, :ROWS] + smooth[:, ROWS:])
        for t in range(EACH):
            roots[source * EACH + t] = smooth[PART * t : PART * (t + 1)]

    @pl.when((d == 0) | (d == GROUP - 1))
    def _():
        for e in range(GROUP):
            pltpu.make_async_remote_copy(
                src_ref=edge_out.at[0], dst_ref=edge_in.at[e], send_sem=edge_send.at[0],
                recv_sem=edge_recv.at[e], device_id=date_peer(1), device_id_type=MESH,
            ).wait_recv()

    take(d, sent.at[d])

    def arrive(k):
        main_copies[k - 1].wait_recv()
        source = (d + GROUP - k) % GROUP
        take(source, got.at[source])

    for copy in y_copies:
        copy.wait_recv()
    power = power_y[...]
    for k in range(1, ny):
        power = power + power_y_in[k - 1]
    power_z[...] = power
    z_copies = spread(lambda k: power_z, lambda k: power_z_in.at[k - 1], z_send, z_recv, z_peer, nz)
    arrive(1)
    arrive(7)
    for copy in z_copies:
        copy.wait_recv()
    power = power_z[...]
    for k in range(1, nz):
        power = power + power_z_in[k - 1]
    power_d[...] = power
    totals[d] = power
    d_copies = spread(lambda k: power_d, lambda k: totals.at[d], d_send, d_recv, date_peer, GROUP)
    arrive(2)
    arrive(6)
    arrive(3)
    arrive(5)
    arrive(4)
    for copy in d_copies:
        copy.wait_recv()

    def chunk(index, carry):
        dates = []
        for i in range(CHUNK):
            p = index * CHUNK + i
            first = pairs_s[0, p]
            second = pairs_s[1, p]
            dates.append((first, second))
            real_a = images[first, 0]
            imag_a = images[first, 1]
            real_b = images[second, 0]
            imag_b = images[second, 1]
            fields[2 * i] = real_a * real_b + imag_a * imag_b
            fields[2 * i + 1] = imag_a * real_b - real_a * imag_b
        for i in range(CHUNK):
            p = index * CHUNK + i
            for f in range(2):
                n = 2 * i + f
                big, small = split(along_columns(fields, n))
                lhs[PART * n : PART * (n + 1), :ROWS] = big
                lhs[PART * n : PART * (n + 1), ROWS:] = small
                sums[f, p] = fields[n, 4:12, :] + fields[n, 12:20, :]
                sums[3 + f, p] = fields[n, 20:28, :] + fields[n, 28:36, :]
        smooth = dot(lhs[...], smoother[...])
        smooth = smooth[:, :ROWS] + smooth[:, ROWS:]
        for i in range(CHUNK):
            p = index * CHUNK + i
            first, second = dates[i]
            real = smooth[2 * PART * i : 2 * PART * i + PART]
            imag = smooth[2 * PART * i + PART : 2 * PART * (i + 1)]
            value = jnp.sqrt(real * real + imag * imag) / (roots[first] * roots[second] + 1e-06)
            sums[2, p] = value[0:8] + value[8:16]
            sums[5, p] = value[16:24] + value[24:32]
        return carry

    lax.fori_loop(0, PAIRS // CHUNK, chunk, 0)

    flat = totals[...].reshape(8 * GROUP, ROWS)
    parts = split3(flat)

    def scale(which):
        hot = date_rows(which)
        taken = dot(hot, parts[0]) + dot(hot, parts[1]) + dot(hot, parts[2])
        total = jnp.sum(taken, axis=1, keepdims=True)
        return jnp.sqrt(total / (ROWS * WIDTH * count) + 1e-06)

    factor = (1.0 / 64.0) / (scale(0) * scale(1))

    look = jnp.where((iota((ROWS, 128), 0) >> 2) == (iota((ROWS, 128), 1) & 31), 1.0, 0.0).astype(BF16)
    lane = iota((32, 128), 1)
    for q in range(6):
        rows = sums[q, :, 0, :]
        for s in range(1, 8):
            rows = rows + sums[q, :, s, :]
        a, b, e = split3(rows)
        looked = dot(a, look) + dot(b, look) + dot(e, look)
        looked = looked * (factor if q % 3 < 2 else 1.0 / 64.0)
        a, b, e = split3(looked)
        placed = dot(select, a) + dot(select, b) + dot(select, e)
        value = jnp.where(
            lane < 64,
            jnp.where(lane < 32, placed[0:32], placed[32:64]),
            jnp.where(lane < 96, placed[64:96], placed[96:128]),
        )
        for e in range(GROUP):
            results[e, 4 * q : 4 * q + 4, :] = value[4 * e : 4 * e + 4]

    out_copies = spread(
        lambda k: results.at[(d + k) % GROUP], lambda k: landed.at[d], out_send, out_recv, date_peer, GROUP
    )
    landed[d] = results[d]
    for copy in out_copies:
        copy.wait()
    for copy in y_copies + z_copies + d_copies + main_copies + edge_copies:
        copy.wait_send()


def place_kernel(landed, interferogram, coherence):
    for f in range(3):
        for g in range(3):
            block = landed[pl.ds(f * 4 + g, 16, stride=12), :]
            for j in range(4):
                piece = block[:, 32 * j : 32 * j + 32]
                if f < 2:
                    interferogram[f, 4 * g + j] = piece
                else:
                    coherence[4 * g + j] = piece


def solution(mesh):
    columns = mesh.shape["cols"]
    nz = 8 if columns % 8 == 0 else columns
    ny = columns // nz
    sem = pltpu.SemaphoreType.DMA
    vmem = pl.BlockSpec(memory_space=pltpu.VMEM)

    def local(slc, pairs, owner):
        pairs = pairs.T
        owner = owner.reshape(1, PAIRS)
        landed = pl.pallas_call(
            lambda *refs: kernel(ny, nz, *refs),
            out_shape=jax.ShapeDtypeStruct((GROUP, 24, 128), F32),
            in_specs=[vmem, pl.BlockSpec(memory_space=pltpu.SMEM), vmem, vmem],
            out_specs=vmem,
            scratch_shapes=[
                pltpu.VMEM((2 * ROWS, 2 * ROWS), BF16),
                pltpu.VMEM((GROUP, BLOCK, ROWS), BF16),
                pltpu.VMEM((GROUP, BLOCK, ROWS), BF16),
                pltpu.VMEM((2, EDGE, ROWS), BF16),
                pltpu.VMEM((GROUP, EDGE, ROWS), BF16),
                pltpu.VMEM((DATES, 2, TILE, ROWS), F32),
                pltpu.VMEM((DATES, PART, ROWS), F32),
                pltpu.VMEM((2 * CHUNK, TILE, ROWS), F32),
                pltpu.VMEM((2 * CHUNK * PART, 2 * ROWS), BF16),
                pltpu.VMEM((6, PAIRS, 8, ROWS), F32),
                pltpu.VMEM((8, ROWS), F32),
                pltpu.VMEM((8, ROWS), F32),
                pltpu.VMEM((8, ROWS), F32),
                pltpu.VMEM((max(ny - 1, 1), 8, ROWS), F32),
                pltpu.VMEM((max(nz - 1, 1), 8, ROWS), F32),
                pltpu.VMEM((GROUP, 8, ROWS), F32),
                pltpu.VMEM((GROUP, 24, 128), F32),
                sem((GROUP - 1,)), sem((GROUP - 1,)),
                sem((2,)), sem((GROUP,)),
                sem((max(ny - 1, 1),)), sem((max(ny - 1, 1),)),
                sem((max(nz - 1, 1),)), sem((max(nz - 1, 1),)),
                sem((GROUP - 1,)), sem((GROUP - 1,)),
                sem((GROUP - 1,)), sem((GROUP - 1,)),
            ],
            compiler_params=pltpu.CompilerParams(
                collective_id=0, has_side_effects=True, vmem_limit_bytes=40 * 1024 * 1024
            ),
        )(slc, pairs, pairs, owner)
        interferogram, coherence = pl.pallas_call(
            place_kernel,
            out_shape=(
                jax.ShapeDtypeStruct((2, CAP, 16, 32), F32),
                jax.ShapeDtypeStruct((CAP, 16, 32), F32),
            ),
            in_specs=[vmem],
            out_specs=(vmem, vmem),
        )(landed.reshape(GROUP * 24, 128))
        return jnp.swapaxes(interferogram, 2, 3), jnp.swapaxes(coherence, 1, 2)

    return jax.shard_map(
        local,
        mesh=mesh,
        in_specs=(P(None, "dates", None, "cols"), P(), P()),
        out_specs=(P(None, "dates", None, "cols"), P("dates", None, "cols")),
        check_vma=False,
    )
```

```python
import math

import jax
import jax.numpy as jnp
import ml_dtypes
import numpy as np
from jax import lax
from jax.experimental import pallas as pl
from jax.experimental.pallas import tpu as pltpu
from jax.sharding import PartitionSpec as P

MESH = pl.DeviceIdType.MESH
F32 = jnp.float32
BF16 = jnp.bfloat16

TAPS = [math.exp(-k * k / 8.0) for k in range(-4, 5)]
WEIGHTS = [float(np.float32(t / sum(TAPS))) for t in TAPS]
HIGH = [float(np.float32(w).astype(ml_dtypes.bfloat16)) for w in WEIGHTS]
LOW = [float(np.float32(w - h).astype(ml_dtypes.bfloat16)) for w, h in zip(WEIGHTS, HIGH)]

GROUP = 8
EACH = 4
DATES = GROUP * EACH
PAIRS = 64
CAP = 12
ROWS = 128
PART = 32
TILE = PART + 8
WIDTH = GROUP * PART
BLOCK = EACH * 2 * TILE
EDGE = EACH * 2 * 8
CHUNK = 8


def split(x):
    high = x.astype(BF16)
    return high, (x - high.astype(F32)).astype(BF16)


def split3(x):
    high = x.astype(BF16)
    rest = x - high.astype(F32)
    mid = rest.astype(BF16)
    return high, mid, (rest - mid.astype(F32)).astype(BF16)


def dot(a, b):
    return jnp.dot(a, b, preferred_element_type=F32)


def iota(shape, axis):
    return lax.broadcasted_iota(jnp.int32, shape, axis)


def cutter():
    lane = iota((TILE, WIDTH), 1)
    row = iota((TILE, WIDTH), 0)
    pieces = [jnp.where(lane == row + (PART * e - 4), 1.0, 0.0) for e in range(GROUP)]
    lane = iota((8, WIDTH), 1)
    row = iota((8, WIDTH), 0)
    pieces.append(jnp.where(lane == row + (WIDTH - 4), 1.0, 0.0))
    pieces.append(jnp.where(lane == row - 4, 1.0, 0.0))
    return jnp.concatenate(pieces, axis=0).astype(BF16)


def band(weights):
    gap = jnp.abs(iota((ROWS, ROWS), 0) - iota((ROWS, ROWS), 1))
    result = jnp.zeros((ROWS, ROWS), F32)
    for k in range(5):
        result = jnp.where(gap == k, weights[4 + k], result)
    return result.astype(BF16)


def along_columns(ref, index):
    result = WEIGHTS[4] * ref[index, 4 : 4 + PART, :]
    for k in range(4):
        both = ref[index, k : k + PART, :] + ref[index, 8 - k : 8 - k + PART, :]
        result = result + WEIGHTS[k] * both
    return result


def kernel(
    ny, nz, slc_hbm, pairs_hbm, owner_hbm, landed,
    slc, pairs_s, pairs_v, owner_v, select, look, hot, smoother, sent, got, edge_out, edge_in, images, roots, fields, lhs, sums,
    power_y, power_z, power_d, power_y_in, power_z_in, totals, results,
    main_send, main_recv, edge_send, edge_recv, y_send, y_recv, z_send, z_recv,
    d_send, d_recv, out_send, out_recv, in_sem, table_sem,
):
    d = lax.axis_index("dates")
    c = lax.axis_index("cols")
    count = ny * nz
    y = c // nz
    z = c % nz

    def date_peer(k):
        return {"dates": (d + k) % GROUP, "cols": c}

    def y_peer(k):
        return {"dates": d, "cols": ((y + k) % ny) * nz + z}

    def z_peer(k):
        return {"dates": d, "cols": y * nz + (z + k) % nz}

    after = (c + 1) % count
    before = (c + count - 1) % count

    loads = [
        pltpu.make_async_copy(slc_hbm.at[:, t], slc.at[:, t], in_sem.at[t]) for t in range(EACH)
    ]
    for load in loads:
        load.start()

    barrier = pltpu.get_barrier_semaphore()

    def greet(device):
        pl.semaphore_signal(barrier, inc=1, device_id=device, device_id_type=MESH)

    for k in range(1, GROUP):
        greet(date_peer(k))
    for k in range(1, ny):
        greet(y_peer(k))
    for k in range(1, nz):
        greet(z_peer(k))

    @pl.when(d == 0)
    def _():
        for e in range(GROUP):
            greet({"dates": e, "cols": before})

    @pl.when(d == GROUP - 1)
    def _():
        for e in range(GROUP):
            greet({"dates": e, "cols": after})

    tables = [
        pltpu.make_async_copy(pairs_hbm, pairs_s, table_sem.at[0]),
        pltpu.make_async_copy(pairs_hbm, pairs_v, table_sem.at[1]),
        pltpu.make_async_copy(owner_hbm, owner_v, table_sem.at[2]),
    ]
    for table in tables:
        table.start()

    cut = cutter()
    power_rows = []
    for t in range(EACH):
        loads[t].wait()
        both = jnp.concatenate([slc[0, t], slc[1, t]], axis=0)
        turned = lax.dot_general(cut, both, (((1,), (1,)), ((), ())), preferred_element_type=F32)
        real = turned[:, :ROWS]
        imag = turned[:, ROWS:]
        for e in range(GROUP):
            part = slice(TILE * e, TILE * e + TILE)
            sent[e, 2 * TILE * t : 2 * TILE * (t + 1), :] = jnp.concatenate(
                [real[part], imag[part]], axis=0
            ).astype(BF16)
        for side in range(2):
            part = slice(TILE * GROUP + 8 * side, TILE * GROUP + 8 * side + 8)
            edge_out[side, 16 * t : 16 * (t + 1), :] = jnp.concatenate(
                [real[part], imag[part]], axis=0
            ).astype(BF16)
        wide = both.astype(F32)
        square = jnp.sum(wide * wide, axis=0, keepdims=True)
        power_rows.append(square[:, :ROWS] + square[:, ROWS:])
    power_y[...] = jnp.concatenate(power_rows + [jnp.zeros((8 - EACH, ROWS), F32)], axis=0)

    pl.semaphore_wait(barrier, (GROUP - 1) + (ny - 1) + (nz - 1) + 2)

    def spread(src, dst, send, recv, peer, number):
        copies = {}
        for k in sorted(range(1, number), key=lambda k: -min(k, number - k)):
            copy = pltpu.make_async_remote_copy(
                src_ref=src(k), dst_ref=dst(k), send_sem=send.at[k - 1], recv_sem=recv.at[k - 1],
                device_id=peer(k), device_id_type=MESH,
            )
            copy.start()
            copies[k] = copy
        return copies

    y_copies = spread(lambda k: power_y, lambda k: power_y_in.at[k - 1], y_send, y_recv, y_peer, ny)
    edge_copies = []
    for side, device in enumerate(
        ({"dates": 0, "cols": after}, {"dates": GROUP - 1, "cols": before})
    ):
        copy = pltpu.make_async_remote_copy(
            src_ref=edge_out.at[side], dst_ref=edge_in.at[d], send_sem=edge_send.at[side],
            recv_sem=edge_recv.at[d], device_id=device, device_id_type=MESH,
        )
        copy.start()
        edge_copies.append(copy)
    main_copies = spread(
        lambda k: sent.at[(d + k) % GROUP], lambda k: got.at[d], main_send, main_recv, date_peer, GROUP
    )

    high = band(HIGH)
    low = band(LOW)
    smoother[:, :ROWS] = jnp.concatenate([high, high], axis=0)
    smoother[:, ROWS:] = jnp.concatenate([low, low], axis=0)

    for table in tables:
        table.wait()
    owner_row = owner_v[...]
    owner_down = jnp.transpose(jnp.broadcast_to(owner_row.astype(F32), (ROWS, PAIRS)))[:, :PAIRS]
    earlier = iota((PAIRS, PAIRS), 0) < iota((PAIRS, PAIRS), 1)
    same = owner_down == owner_row.astype(F32)
    rank = jnp.sum(jnp.where(same & earlier, 1.0, 0.0), axis=0, keepdims=True).astype(jnp.int32)
    place = (rank & 3) * 32 + owner_row * 4 + (rank >> 2)
    one = jnp.where(iota((128, PAIRS), 0) == place, 1.0, 0.0)
    select[...] = jnp.concatenate([one, one, one], axis=1).astype(BF16)

    def date_rows(which):
        date = pairs_v[which : which + 1, :]
        row = ((date >> 2) * 8 + (date & 3)).astype(F32)
        down = jnp.transpose(jnp.broadcast_to(row, (ROWS, PAIRS)))[:, : 8 * GROUP]
        lane = iota((PAIRS, 8 * GROUP), 1).astype(F32)
        one = jnp.where(down == lane, 1.0, 0.0)
        return jnp.concatenate([one, one, one], axis=1).astype(BF16)

    hot[...] = jnp.concatenate([date_rows(0), date_rows(1)], axis=0)
    one = jnp.where((iota((ROWS, 128), 0) >> 2) == (iota((ROWS, 128), 1) & 31), 1.0, 0.0)
    look[...] = jnp.concatenate([one, one, one], axis=0).astype(BF16)

    def take(source, block):
        for t in range(EACH):
            piece = block[2 * TILE * t : 2 * TILE * (t + 1), :].astype(F32)
            images[source * EACH + t, 0] = piece[:TILE]
            images[source * EACH + t, 1] = piece[TILE:]

        @pl.when((d == 0) & (c > 0))
        def _():
            for t in range(EACH):
                piece = edge_in[source, 16 * t : 16 * (t + 1), :].astype(F32)
                images[source * EACH + t, 0, 0:8] += piece[:8]
                images[source * EACH + t, 1, 0:8] += piece[8:]

        @pl.when((d == GROUP - 1) & (c < count - 1))
        def _():
            for t in range(EACH):
                piece = edge_in[source, 16 * t : 16 * (t + 1), :].astype(F32)
                images[source * EACH + t, 0, TILE - 8 : TILE] += piece[:8]
                images[source * EACH + t, 1, TILE - 8 : TILE] += piece[8:]

        for t in range(EACH):
            real = images[source * EACH + t, 0]
            imag = images[source * EACH + t, 1]
            fields[t] = real * real + imag * imag
        for t in range(EACH):
            big, small = split(along_columns(fields, t))
            lhs[PART * t : PART * (t + 1), :ROWS] = big
            lhs[PART * t : PART * (t + 1), ROWS:] = small
        smooth = dot(lhs[: EACH * PART, :], smoother[...])
        smooth = jnp.sqrt(smooth[:, :ROWS] + smooth[:, ROWS:])
        for t in range(EACH):
            roots[source * EACH + t] = smooth[PART * t : PART * (t + 1)]

    def arrive(k):
        main_copies[k].wait_recv()
        source = (d + GROUP - k) % GROUP
        take(source, got.at[source])

    for copy in y_copies.values():
        copy.wait_recv()
    power = power_y[...]
    for k in range(1, ny):
        power = power + power_y_in[k - 1]
    power_z[...] = power
    z_copies = spread(lambda k: power_z, lambda k: power_z_in.at[k - 1], z_send, z_recv, z_peer, nz)

    @pl.when((d == 0) | (d == GROUP - 1))
    def _():
        for e in range(GROUP):
            pltpu.make_async_remote_copy(
                src_ref=edge_out.at[0], dst_ref=edge_in.at[e], send_sem=edge_send.at[0],
                recv_sem=edge_recv.at[e], device_id=date_peer(1), device_id_type=MESH,
            ).wait_recv()

    take(d, sent.at[d])
    arrive(1)
    arrive(7)
    arrive(2)
    arrive(6)
    for copy in z_copies.values():
        copy.wait_recv()
    power = power_z[...]
    for k in range(1, nz):
        power = power + power_z_in[k - 1]
    power_d[...] = power
    totals[d] = power
    d_copies = spread(lambda k: power_d, lambda k: totals.at[d], d_send, d_recv, date_peer, GROUP)
    arrive(3)
    arrive(5)
    arrive(4)

    def chunk(index, carry):
        dates = []
        for i in range(CHUNK):
            p = index * CHUNK + i
            first = pairs_s[0, p]
            second = pairs_s[1, p]
            dates.append((first, second))
            real_a = images[first, 0]
            imag_a = images[first, 1]
            real_b = images[second, 0]
            imag_b = images[second, 1]
            fields[2 * i] = real_a * real_b + imag_a * imag_b
            fields[2 * i + 1] = imag_a * real_b - real_a * imag_b
        for i in range(CHUNK):
            p = index * CHUNK + i
            for f in range(2):
                n = 2 * i + f
                big, small = split(along_columns(fields, n))
                lhs[PART * n : PART * (n + 1), :ROWS] = big
                lhs[PART * n : PART * (n + 1), ROWS:] = small
                sums[pl.ds((f * PAIRS + p) * 8, 8), :] = fields[n, 4:12, :] + fields[n, 12:20, :]
                sums[pl.ds(((3 + f) * PAIRS + p) * 8, 8), :] = fields[n, 20:28, :] + fields[n, 28:36, :]
        smooth = dot(lhs[...], smoother[...])
        smooth = smooth[:, :ROWS] + smooth[:, ROWS:]
        for i in range(CHUNK):
            p = index * CHUNK + i
            first, second = dates[i]
            real = smooth[2 * PART * i : 2 * PART * i + PART]
            imag = smooth[2 * PART * i + PART : 2 * PART * (i + 1)]
            value = jnp.sqrt(real * real + imag * imag) / (roots[first] * roots[second] + 1e-06)
            sums[pl.ds((2 * PAIRS + p) * 8, 8), :] = value[0:8] + value[8:16]
            sums[pl.ds((5 * PAIRS + p) * 8, 8), :] = value[16:24] + value[24:32]
        return carry

    lax.fori_loop(0, PAIRS // CHUNK, chunk, 0)

    for copy in d_copies.values():
        copy.wait_recv()
    parts = jnp.concatenate(split3(totals[...].reshape(8 * GROUP, ROWS)), axis=0)
    total = jnp.sum(dot(hot[...], parts), axis=1, keepdims=True)
    scale = jnp.sqrt(total / (ROWS * WIDTH * count) + 1e-06)
    factor = (1.0 / 64.0) / (scale[:PAIRS] * scale[PAIRS:])

    rows = sums[pl.ds(0, 6 * PAIRS, stride=8), :]
    for i in range(1, 8):
        rows = rows + sums[pl.ds(i, 6 * PAIRS, stride=8), :]
    looked = dot(jnp.concatenate(split3(rows), axis=1), look[...])
    wide = []
    for q in range(6):
        piece = looked[PAIRS * q : PAIRS * (q + 1)]
        wide.append(piece * (factor if q % 3 < 2 else 1.0 / 64.0))
    stacked = jnp.concatenate(split3(jnp.concatenate(wide, axis=1)), axis=0)
    placed = dot(select[...], stacked)
    lane = iota((32, 128), 1)
    for q in range(6):
        part = placed[:, 128 * q : 128 * (q + 1)]
        value = jnp.where(
            lane < 64,
            jnp.where(lane < 32, part[0:32], part[32:64]),
            jnp.where(lane < 96, part[64:96], part[96:128]),
        )
        for e in range(GROUP):
            results[e, 4 * q : 4 * q + 4, :] = value[4 * e : 4 * e + 4]

    out_copies = spread(
        lambda k: results.at[(d + k) % GROUP], lambda k: landed.at[d], out_send, out_recv, date_peer, GROUP
    )
    landed[d] = results[d]
    for copies in (y_copies, z_copies, d_copies, main_copies):
        for copy in copies.values():
            copy.wait_send()
    for copy in edge_copies:
        copy.wait_send()
    for copy in out_copies.values():
        copy.wait()


def place_kernel(landed, interferogram, coherence):
    for f in range(3):
        for g in range(3):
            block = landed[pl.ds(f * 4 + g, 16, stride=12), :]
            for j in range(4):
                piece = block[:, 32 * j : 32 * j + 32]
                if f < 2:
                    interferogram[f, 4 * g + j] = piece
                else:
                    coherence[4 * g + j] = piece


def solution(mesh):
    columns = mesh.shape["cols"]
    nz = 8 if columns % 8 == 0 else columns
    ny = columns // nz
    sem = pltpu.SemaphoreType.DMA
    vmem = pl.BlockSpec(memory_space=pltpu.VMEM)

    def local(slc, pairs, owner):
        pairs = pairs.T
        owner = owner.reshape(1, PAIRS)
        landed = pl.pallas_call(
            lambda *refs: kernel(ny, nz, *refs),
            out_shape=jax.ShapeDtypeStruct((GROUP, 24, 128), F32),
            in_specs=[pl.BlockSpec(memory_space=pl.ANY)] * 3,
            out_specs=vmem,
            scratch_shapes=[
                pltpu.VMEM((2, EACH, ROWS, WIDTH), BF16),
                pltpu.SMEM((2, PAIRS), jnp.int32),
                pltpu.VMEM((2, PAIRS), jnp.int32),
                pltpu.VMEM((1, PAIRS), jnp.int32),
                pltpu.VMEM((128, 3 * PAIRS), BF16),
                pltpu.VMEM((3 * ROWS, 128), BF16),
                pltpu.VMEM((2 * PAIRS, 24 * GROUP), BF16),
                pltpu.VMEM((2 * ROWS, 2 * ROWS), BF16),
                pltpu.VMEM((GROUP, BLOCK, ROWS), BF16),
                pltpu.VMEM((GROUP, BLOCK, ROWS), BF16),
                pltpu.VMEM((2, EDGE, ROWS), BF16),
                pltpu.VMEM((GROUP, EDGE, ROWS), BF16),
                pltpu.VMEM((DATES, 2, TILE, ROWS), F32),
                pltpu.VMEM((DATES, PART, ROWS), F32),
                pltpu.VMEM((2 * CHUNK, TILE, ROWS), F32),
                pltpu.VMEM((2 * CHUNK * PART, 2 * ROWS), BF16),
                pltpu.VMEM((6 * PAIRS * 8, ROWS), F32),
                pltpu.VMEM((8, ROWS), F32),
                pltpu.VMEM((8, ROWS), F32),
                pltpu.VMEM((8, ROWS), F32),
                pltpu.VMEM((max(ny - 1, 1), 8, ROWS), F32),
                pltpu.VMEM((max(nz - 1, 1), 8, ROWS), F32),
                pltpu.VMEM((GROUP, 8, ROWS), F32),
                pltpu.VMEM((GROUP, 24, 128), F32),
                sem((GROUP - 1,)), sem((GROUP - 1,)),
                sem((2,)), sem((GROUP,)),
                sem((max(ny - 1, 1),)), sem((max(ny - 1, 1),)),
                sem((max(nz - 1, 1),)), sem((max(nz - 1, 1),)),
                sem((GROUP - 1,)), sem((GROUP - 1,)),
                sem((GROUP - 1,)), sem((GROUP - 1,)),
                sem((EACH,)), sem((3,)),
            ],
            compiler_params=pltpu.CompilerParams(
                collective_id=0, has_side_effects=True, vmem_limit_bytes=62 * 1024 * 1024
            ),
        )(slc, pairs, owner)
        interferogram, coherence = pl.pallas_call(
            place_kernel,
            out_shape=(
                jax.ShapeDtypeStruct((2, CAP, 16, 32), F32),
                jax.ShapeDtypeStruct((CAP, 16, 32), F32),
            ),
            in_specs=[vmem],
            out_specs=(vmem, vmem),
        )(landed.reshape(GROUP * 24, 128))
        return jnp.swapaxes(interferogram, 2, 3), jnp.swapaxes(coherence, 1, 2)

    return jax.shard_map(
        local,
        mesh=mesh,
        in_specs=(P(None, "dates", None, "cols"), P(), P()),
        out_specs=(P(None, "dates", None, "cols"), P("dates", None, "cols")),
        check_vma=False,
    )
```

```python
import math

import jax
import jax.numpy as jnp
import ml_dtypes
import numpy as np
from jax import lax
from jax.experimental import pallas as pl
from jax.experimental.pallas import tpu as pltpu
from jax.sharding import PartitionSpec as P

MESH = pl.DeviceIdType.MESH
F32 = jnp.float32
BF16 = jnp.bfloat16

TAPS = [math.exp(-k * k / 8.0) for k in range(-4, 5)]
WEIGHTS = [float(np.float32(t / sum(TAPS))) for t in TAPS]
HIGH = [float(np.float32(w).astype(ml_dtypes.bfloat16)) for w in WEIGHTS]
LOW = [float(np.float32(w - h).astype(ml_dtypes.bfloat16)) for w, h in zip(WEIGHTS, HIGH)]

GROUP = 8
EACH = 4
DATES = GROUP * EACH
PAIRS = 64
CAP = 12
ROWS = 128
PART = 32
TILE = PART + 8
WIDTH = GROUP * PART
PIECES = (24, 16)
HALF = PART // 2
WINDOW = HALF + 8
EDGE = EACH * 2 * 8
CHUNK = 16


def split(x):
    high = x.astype(BF16)
    return high, (x - high.astype(F32)).astype(BF16)


def split3(x):
    high = x.astype(BF16)
    rest = x - high.astype(F32)
    mid = rest.astype(BF16)
    return high, mid, (rest - mid.astype(F32)).astype(BF16)


def dot(a, b):
    return jnp.dot(a, b, preferred_element_type=F32)


def iota(shape, axis):
    return lax.broadcasted_iota(jnp.int32, shape, axis)


def cutter(half):
    start, size = (-4, PIECES[0]) if half == 0 else (PIECES[0] - 4, PIECES[1])
    lane = iota((size, WIDTH), 1)
    row = iota((size, WIDTH), 0)
    pieces = [jnp.where(lane == row + (PART * e + start), 1.0, 0.0) for e in range(GROUP)]
    lane = iota((8, WIDTH), 1)
    row = iota((8, WIDTH), 0)
    pieces.append(jnp.where(lane == row + (WIDTH - 4 if half == 0 else -4), 1.0, 0.0))
    return jnp.concatenate(pieces, axis=0).astype(BF16)


def band(weights):
    gap = jnp.abs(iota((ROWS, ROWS), 0) - iota((ROWS, ROWS), 1))
    result = jnp.zeros((ROWS, ROWS), F32)
    for k in range(5):
        result = jnp.where(gap == k, weights[4 + k], result)
    return result.astype(BF16)


def along_columns(ref, index):
    result = WEIGHTS[4] * ref[index, 4 : 4 + HALF, :]
    for k in range(4):
        both = ref[index, k : k + HALF, :] + ref[index, 8 - k : 8 - k + HALF, :]
        result = result + WEIGHTS[k] * both
    return result


def kernel(
    ny, nz, slc_hbm, pairs_hbm, owner_hbm, interferogram, coherence,
    landed,    slc, pairs_s, pairs_v, owner_v, select, look, hot, smoother, sent_0, sent_1, got_0, got_1, edge_out, edge_left, edge_right, images, roots, fields, lhs, sums,
    looked, power_y, power_z, power_d, power_y_in, power_z_in, totals, results,
    main_send_0, main_recv_0, main_send_1, main_recv_1, edge_send, edge_recv, y_send, y_recv, z_send, z_recv,
    d_send, d_recv, out_send, out_recv, in_sem, table_sem,
):
    d = lax.axis_index("dates")
    c = lax.axis_index("cols")
    count = ny * nz
    y = c // nz
    z = c % nz

    def date_peer(k):
        return {"dates": (d + k) % GROUP, "cols": c}

    def y_peer(k):
        return {"dates": d, "cols": ((y + k) % ny) * nz + z}

    def z_peer(k):
        return {"dates": d, "cols": y * nz + (z + k) % nz}

    after = (c + 1) % count
    before = (c + count - 1) % count

    loads = [
        pltpu.make_async_copy(slc_hbm.at[:, t], slc.at[:, t], in_sem.at[t]) for t in range(EACH)
    ]
    for load in loads:
        load.start()

    barrier = pltpu.get_barrier_semaphore()

    def greet(device):
        pl.semaphore_signal(barrier, inc=1, device_id=device, device_id_type=MESH)

    for k in range(1, GROUP):
        greet(date_peer(k))
    for k in range(1, ny):
        greet(y_peer(k))
    for k in range(1, nz):
        greet(z_peer(k))

    @pl.when(d == 0)
    def _():
        for e in range(GROUP):
            greet({"dates": e, "cols": before})

    @pl.when(d == GROUP - 1)
    def _():
        for e in range(GROUP):
            greet({"dates": e, "cols": after})

    tables = [
        pltpu.make_async_copy(pairs_hbm, pairs_s, table_sem.at[0]),
        pltpu.make_async_copy(pairs_hbm, pairs_v, table_sem.at[1]),
        pltpu.make_async_copy(owner_hbm, owner_v, table_sem.at[2]),
    ]
    for table in tables:
        table.start()

    sent = (sent_0, sent_1)
    edge_in = (edge_left, edge_right)
    got = (got_0, got_1)

    def cut(half):
        size = PIECES[half]
        matrix = cutter(half)
        for t in range(EACH):
            if half == 0:
                loads[t].wait()
            both = jnp.concatenate([slc[0, t], slc[1, t]], axis=0)
            turned = lax.dot_general(
                matrix, both, (((1,), (1,)), ((), ())), preferred_element_type=F32
            )
            for e in range(GROUP + 1):
                rows = turned[size * e : size * (e + 1)] if e < GROUP else turned[size * GROUP :]
                value = jnp.concatenate([rows[:, :ROWS], rows[:, ROWS:]], axis=0).astype(BF16)
                if e < GROUP:
                    sent[half][e, 2 * size * t : 2 * size * (t + 1), :] = value
                else:
                    edge_out[half, 16 * t : 16 * (t + 1), :] = value

    cut(0)

    pl.semaphore_wait(barrier, (GROUP - 1) + (ny - 1) + (nz - 1) + 2)

    def spread(src, dst, send, recv, peer, number):
        copies = {}
        for k in sorted(range(1, number), key=lambda k: -min(k, number - k)):
            copy = pltpu.make_async_remote_copy(
                src_ref=src(k), dst_ref=dst(k), send_sem=send.at[k - 1], recv_sem=recv.at[k - 1],
                device_id=peer(k), device_id_type=MESH,
            )
            copy.start()
            copies[k] = copy
        return copies

    edge_copies = []

    def send_edge(side, device):
        copy = pltpu.make_async_remote_copy(
            src_ref=edge_out.at[side], dst_ref=edge_in[side].at[d], send_sem=edge_send.at[side],
            recv_sem=edge_recv.at[d], device_id=device, device_id_type=MESH,
        )
        copy.start()
        edge_copies.append(copy)

    def send_half(half, send, recv):
        return spread(
            lambda k: sent[half].at[(d + k) % GROUP], lambda k: got[half].at[d], send, recv,
            date_peer, GROUP,
        )

    send_edge(0, {"dates": 0, "cols": after})
    main_0 = send_half(0, main_send_0, main_recv_0)
    power_rows = []
    for t in range(EACH):
        wide = jnp.concatenate([slc[0, t], slc[1, t]], axis=0).astype(F32)
        square = jnp.sum(wide * wide, axis=0, keepdims=True)
        power_rows.append(square[:, :ROWS] + square[:, ROWS:])
    power_y[...] = jnp.concatenate(power_rows + [jnp.zeros((8 - EACH, ROWS), F32)], axis=0)
    y_copies = spread(lambda k: power_y, lambda k: power_y_in.at[k - 1], y_send, y_recv, y_peer, ny)
    cut(1)
    send_edge(1, {"dates": GROUP - 1, "cols": before})
    main_1 = send_half(1, main_send_1, main_recv_1)
    got_1[d] = sent_1[d]

    @pl.when(d != 0)
    def _():
        edge_left[...] = jnp.zeros_like(edge_left)

    @pl.when(d != GROUP - 1)
    def _():
        edge_right[...] = jnp.zeros_like(edge_right)


    high = band(HIGH)
    low = band(LOW)
    smoother[:, :ROWS] = jnp.concatenate([high, high], axis=0)
    smoother[:, ROWS:] = jnp.concatenate([low, low], axis=0)

    for table in tables:
        table.wait()
    owner_row = owner_v[...]
    owner_down = jnp.transpose(jnp.broadcast_to(owner_row.astype(F32), (ROWS, PAIRS)))[:, :PAIRS]
    earlier = iota((PAIRS, PAIRS), 0) < iota((PAIRS, PAIRS), 1)
    same = owner_down == owner_row.astype(F32)
    rank = jnp.sum(jnp.where(same & earlier, 1.0, 0.0), axis=0, keepdims=True).astype(jnp.int32)
    place = (rank & 3) * 32 + owner_row * 4 + (rank >> 2)
    one = jnp.where(iota((128, PAIRS), 0) == place, 1.0, 0.0)
    select[...] = jnp.concatenate([one, one, one], axis=1).astype(BF16)

    def date_rows(which):
        date = pairs_v[which : which + 1, :]
        row = ((date >> 2) * 8 + (date & 3)).astype(F32)
        down = jnp.transpose(jnp.broadcast_to(row, (ROWS, PAIRS)))[:, : 8 * GROUP]
        lane = iota((PAIRS, 8 * GROUP), 1).astype(F32)
        one = jnp.where(down == lane, 1.0, 0.0)
        return jnp.concatenate([one, one, one], axis=1).astype(BF16)

    hot[...] = jnp.concatenate([date_rows(0), date_rows(1)], axis=0)
    one = jnp.where((iota((ROWS, 128), 0) >> 2) == (iota((ROWS, 128), 1) & 31), 1.0, 0.0)
    look[...] = jnp.concatenate([one, one, one], axis=0).astype(BF16)

    def edges(side):
        for e in range(GROUP):
            pltpu.make_async_remote_copy(
                src_ref=edge_out.at[side], dst_ref=edge_in[side].at[e], send_sem=edge_send.at[side],
                recv_sem=edge_recv.at[e], device_id=date_peer(1), device_id_type=MESH,
            ).wait_recv()

    left_gate = jnp.where(c > 0, 1.0, 0.0).astype(F32)
    right_gate = jnp.where(c < count - 1, 1.0, 0.0).astype(F32)

    def smooth_powers(number):
        for t in range(number):
            big, small = split(along_columns(fields, t))
            lhs[HALF * t : HALF * (t + 1), :ROWS] = big
            lhs[HALF * t : HALF * (t + 1), ROWS:] = small
        smooth = dot(lhs[: number * HALF, :], smoother[...])
        return jnp.sqrt(smooth[:, :ROWS] + smooth[:, ROWS:])

    def take_first(source, block):
        size = PIECES[0]
        for t in range(EACH):
            piece = block[2 * size * t : 2 * size * (t + 1), :].astype(F32)
            edge = edge_left[source, 16 * t : 16 * (t + 1), :].astype(F32) * left_gate
            real = jnp.concatenate([piece[:8] + edge[:8], piece[8:size]], axis=0)
            imag = jnp.concatenate([piece[size : size + 8] + edge[8:], piece[size + 8 :]], axis=0)
            images[source * EACH + t, 0, :size] = real
            images[source * EACH + t, 1, :size] = imag
            fields[t] = real * real + imag * imag
        smooth = smooth_powers(EACH)
        for t in range(EACH):
            roots[source * EACH + t, :HALF] = smooth[HALF * t : HALF * (t + 1)]

    def arrive(k):
        main_0[k].wait_recv()
        source = (d + GROUP - k) % GROUP
        take_first(source, got_0.at[source])

    def take_second():
        size = PIECES[1]
        for date in range(DATES):
            source, t = date // EACH, date % EACH
            piece = got_1[source, 2 * size * t : 2 * size * (t + 1), :].astype(F32)
            edge = edge_right[source, 16 * t : 16 * (t + 1), :].astype(F32) * right_gate
            real = jnp.concatenate([piece[:8], piece[8:size] + edge[:8]], axis=0)
            imag = jnp.concatenate([piece[size : size + 8], piece[size + 8 :] + edge[8:]], axis=0)
            images[date, 0, PIECES[0] :] = real
            images[date, 1, PIECES[0] :] = imag
            real = jnp.concatenate([images[date, 0, HALF : PIECES[0]], real], axis=0)
            imag = jnp.concatenate([images[date, 1, HALF : PIECES[0]], imag], axis=0)
            fields[date] = real * real + imag * imag
        smooth = smooth_powers(DATES)
        for date in range(DATES):
            roots[date, HALF:] = smooth[HALF * date : HALF * (date + 1)]

    def pairs_of(half):
        window = slice(HALF * half, HALF * half + WINDOW)

        def place(field, p):
            return pl.ds(((3 * half + field) * PAIRS + p) * 8, 8)

        def chunk(index, carry):
            dates = []
            for i in range(CHUNK):
                p = index * CHUNK + i
                first = pairs_s[0, p]
                second = pairs_s[1, p]
                dates.append((first, second))
                real_a = images[first, 0, window]
                imag_a = images[first, 1, window]
                real_b = images[second, 0, window]
                imag_b = images[second, 1, window]
                fields[2 * i] = real_a * real_b + imag_a * imag_b
                fields[2 * i + 1] = imag_a * real_b - real_a * imag_b
            for i in range(CHUNK):
                p = index * CHUNK + i
                for f in range(2):
                    n = 2 * i + f
                    big, small = split(along_columns(fields, n))
                    lhs[HALF * n : HALF * (n + 1), :ROWS] = big
                    lhs[HALF * n : HALF * (n + 1), ROWS:] = small
                    sums[place(f, p), :] = fields[n, 4:12, :] + fields[n, 12:20, :]
            smooth = dot(lhs[...], smoother[...])
            smooth = smooth[:, :ROWS] + smooth[:, ROWS:]
            for i in range(CHUNK):
                p = index * CHUNK + i
                first, second = dates[i]
                real = smooth[2 * HALF * i : 2 * HALF * i + HALF]
                imag = smooth[2 * HALF * i + HALF : 2 * HALF * (i + 1)]
                below = (
                    roots[first, HALF * half : HALF * (half + 1)]
                    * roots[second, HALF * half : HALF * (half + 1)]
                )
                value = jnp.sqrt(real * real + imag * imag) / (below + 1e-06)
                sums[place(2, p), :] = value[0:8] + value[8:16]
            return carry

        lax.fori_loop(0, PAIRS // CHUNK, chunk, 0)
        rows = sums[pl.ds(3 * half * PAIRS * 8, 3 * PAIRS, stride=8), :]
        for i in range(1, 8):
            rows = rows + sums[pl.ds(3 * half * PAIRS * 8 + i, 3 * PAIRS, stride=8), :]
        looked[half] = dot(jnp.concatenate(split3(rows), axis=1), look[...])

    for copy in y_copies.values():
        copy.wait_recv()
    power = power_y[...]
    for k in range(1, ny):
        power = power + power_y_in[k - 1]
    power_z[...] = power
    z_copies = spread(lambda k: power_z, lambda k: power_z_in.at[k - 1], z_send, z_recv, z_peer, nz)

    @pl.when(d == 0)
    def _():
        edges(0)

    take_first(d, sent_0.at[d])
    for k in (4, 3, 5, 2, 6, 1, 7):
        arrive(k)
    for copy in z_copies.values():
        copy.wait_recv()
    power = power_z[...]
    for k in range(1, nz):
        power = power + power_z_in[k - 1]
    power_d[...] = power
    totals[d] = power
    d_copies = spread(lambda k: power_d, lambda k: totals.at[d], d_send, d_recv, date_peer, GROUP)
    pairs_of(0)

    @pl.when(d == GROUP - 1)
    def _():
        edges(1)

    for k in (4, 3, 5, 2, 6, 1, 7):
        main_1[k].wait_recv()
    take_second()
    pairs_of(1)

    for copy in d_copies.values():
        copy.wait_recv()
    parts = jnp.concatenate(split3(totals[...].reshape(8 * GROUP, ROWS)), axis=0)
    total = jnp.sum(dot(hot[...], parts), axis=1, keepdims=True)
    scale = jnp.sqrt(total / (ROWS * WIDTH * count) + 1e-06)
    factor = (1.0 / 64.0) / (scale[:PAIRS] * scale[PAIRS:])

    wide = []
    for q in range(6):
        piece = looked[q // 3, PAIRS * (q % 3) : PAIRS * (q % 3 + 1)]
        wide.append(piece * (factor if q % 3 < 2 else 1.0 / 64.0))
    stacked = jnp.concatenate(split3(jnp.concatenate(wide, axis=1)), axis=0)
    placed = dot(select[...], stacked)
    lane = iota((32, 128), 1)
    for q in range(6):
        part = placed[:, 128 * q : 128 * (q + 1)]
        value = jnp.where(
            lane < 64,
            jnp.where(lane < 32, part[0:32], part[32:64]),
            jnp.where(lane < 96, part[64:96], part[96:128]),
        )
        for e in range(GROUP):
            results[e, 4 * q : 4 * q + 4, :] = value[4 * e : 4 * e + 4]

    out_copies = spread(
        lambda k: results.at[(d + k) % GROUP], lambda k: landed.at[d], out_send, out_recv, date_peer, GROUP
    )
    landed[d] = results[d]
    for copy in out_copies.values():
        copy.wait_recv()
    flat = landed.reshape(GROUP * 24, 128)
    for f in range(3):
        for g in range(3):
            block = flat[pl.ds(f * 4 + g, 16, stride=12), :]
            for j in range(4):
                piece = block[:, 32 * j : 32 * j + 32]
                if f < 2:
                    interferogram[f, 4 * g + j] = piece
                else:
                    coherence[4 * g + j] = piece
    for copies in (y_copies, z_copies, d_copies, main_0, main_1, out_copies):
        for copy in copies.values():
            copy.wait_send()
    for copy in edge_copies:
        copy.wait_send()


def solution(mesh):
    columns = mesh.shape["cols"]
    nz = 8 if columns % 8 == 0 else columns
    ny = columns // nz
    sem = pltpu.SemaphoreType.DMA
    vmem = pl.BlockSpec(memory_space=pltpu.VMEM)

    def local(slc, pairs, owner):
        pairs = pairs.T
        owner = owner.reshape(1, PAIRS)
        interferogram, coherence = pl.pallas_call(
            lambda *refs: kernel(ny, nz, *refs),
            out_shape=(jax.ShapeDtypeStruct((2, CAP, 16, 32), F32), jax.ShapeDtypeStruct((CAP, 16, 32), F32)),
            in_specs=[pl.BlockSpec(memory_space=pl.ANY)] * 3,
            out_specs=(vmem, vmem),
            scratch_shapes=[
                pltpu.VMEM((GROUP, 24, 128), F32),
                pltpu.VMEM((2, EACH, ROWS, WIDTH), BF16),
                pltpu.SMEM((2, PAIRS), jnp.int32),
                pltpu.VMEM((2, PAIRS), jnp.int32),
                pltpu.VMEM((1, PAIRS), jnp.int32),
                pltpu.VMEM((128, 3 * PAIRS), BF16),
                pltpu.VMEM((3 * ROWS, 128), BF16),
                pltpu.VMEM((2 * PAIRS, 24 * GROUP), BF16),
                pltpu.VMEM((2 * ROWS, 2 * ROWS), BF16),
                pltpu.VMEM((GROUP, EACH * 2 * PIECES[0], ROWS), BF16),
                pltpu.VMEM((GROUP, EACH * 2 * PIECES[1], ROWS), BF16),
                pltpu.VMEM((GROUP, EACH * 2 * PIECES[0], ROWS), BF16),
                pltpu.VMEM((GROUP, EACH * 2 * PIECES[1], ROWS), BF16),
                pltpu.VMEM((2, EDGE, ROWS), BF16),
                pltpu.VMEM((GROUP, EDGE, ROWS), BF16),
                pltpu.VMEM((GROUP, EDGE, ROWS), BF16),
                pltpu.VMEM((DATES, 2, TILE, ROWS), F32),
                pltpu.VMEM((DATES, PART, ROWS), F32),
                pltpu.VMEM((2 * CHUNK, WINDOW, ROWS), F32),
                pltpu.VMEM((2 * CHUNK * HALF, 2 * ROWS), BF16),
                pltpu.VMEM((6 * PAIRS * 8, ROWS), F32),
                pltpu.VMEM((2, 3 * PAIRS, ROWS), F32),
                pltpu.VMEM((8, ROWS), F32),
                pltpu.VMEM((8, ROWS), F32),
                pltpu.VMEM((8, ROWS), F32),
                pltpu.VMEM((max(ny - 1, 1), 8, ROWS), F32),
                pltpu.VMEM((max(nz - 1, 1), 8, ROWS), F32),
                pltpu.VMEM((GROUP, 8, ROWS), F32),
                pltpu.VMEM((GROUP, 24, 128), F32),
                sem((GROUP - 1,)), sem((GROUP - 1,)),
                sem((GROUP - 1,)), sem((GROUP - 1,)),
                sem((2,)), sem((GROUP,)),
                sem((max(ny - 1, 1),)), sem((max(ny - 1, 1),)),
                sem((max(nz - 1, 1),)), sem((max(nz - 1, 1),)),
                sem((GROUP - 1,)), sem((GROUP - 1,)),
                sem((GROUP - 1,)), sem((GROUP - 1,)),
                sem((EACH,)), sem((3,)),
            ],
            compiler_params=pltpu.CompilerParams(
                collective_id=0, has_side_effects=True, vmem_limit_bytes=54682 * 1024
            ),
        )(slc, pairs, owner)
        return jnp.swapaxes(interferogram, 2, 3), jnp.swapaxes(coherence, 1, 2)

    return jax.shard_map(
        local,
        mesh=mesh,
        in_specs=(P(None, "dates", None, "cols"), P(), P()),
        out_specs=(P(None, "dates", None, "cols"), P("dates", None, "cols")),
        check_vma=False,
    )
```

```python
import math

import jax
import jax.numpy as jnp
import ml_dtypes
import numpy as np
from jax import lax
from jax.experimental import pallas as pl
from jax.experimental.pallas import tpu as pltpu
from jax.sharding import PartitionSpec as P

MESH = pl.DeviceIdType.MESH
F32 = jnp.float32
BF16 = jnp.bfloat16

TAPS = [math.exp(-k * k / 8.0) for k in range(-4, 5)]
WEIGHTS = [float(np.float32(t / sum(TAPS))) for t in TAPS]
HIGH = [float(np.float32(w).astype(ml_dtypes.bfloat16)) for w in WEIGHTS]
LOW = [float(np.float32(w - h).astype(ml_dtypes.bfloat16)) for w, h in zip(WEIGHTS, HIGH)]

GROUP = 8
EACH = 4
DATES = GROUP * EACH
PAIRS = 64
CAP = 12
ROWS = 128
PART = 32
TILE = PART + 8
WIDTH = GROUP * PART
PIECES = (24, 16)
HALF = PART // 2
WINDOW = HALF + 8
EDGE = EACH * 2 * 8
CHUNK = 16


def split(x):
    high = x.astype(BF16)
    return high, (x - high.astype(F32)).astype(BF16)


def split3(x):
    high = x.astype(BF16)
    rest = x - high.astype(F32)
    mid = rest.astype(BF16)
    return high, mid, (rest - mid.astype(F32)).astype(BF16)


def dot(a, b):
    return jnp.dot(a, b, preferred_element_type=F32)


def iota(shape, axis):
    return lax.broadcasted_iota(jnp.int32, shape, axis)


def cutter(half):
    start, size = (-4, PIECES[0]) if half == 0 else (PIECES[0] - 4, PIECES[1])
    lane = iota((size, WIDTH), 1)
    row = iota((size, WIDTH), 0)
    pieces = [jnp.where(lane == row + (PART * e + start), 1.0, 0.0) for e in range(GROUP)]
    lane = iota((8, WIDTH), 1)
    row = iota((8, WIDTH), 0)
    pieces.append(jnp.where(lane == row + (WIDTH - 4 if half == 0 else -4), 1.0, 0.0))
    return jnp.concatenate(pieces, axis=0).astype(BF16)


def band(weights):
    gap = jnp.abs(iota((ROWS, ROWS), 0) - iota((ROWS, ROWS), 1))
    result = jnp.zeros((ROWS, ROWS), F32)
    for k in range(5):
        result = jnp.where(gap == k, weights[4 + k], result)
    return result.astype(BF16)


def along_columns(ref, index):
    result = WEIGHTS[4] * ref[index, 4 : 4 + HALF, :]
    for k in range(4):
        both = ref[index, k : k + HALF, :] + ref[index, 8 - k : 8 - k + HALF, :]
        result = result + WEIGHTS[k] * both
    return result


def kernel(
    ny, nz, slc_hbm, pairs_hbm, owner_hbm, landed, scaling,
       slc, pairs_s, pairs_v, owner_v, select, own, look, hot, smoother, sent_0, sent_1, got_0, got_1, edge_out, edge_left, edge_right, images, roots, fields, lhs, sums,
    looked, power_y, power_z, power_d, power_y_in, power_z_in, totals, results,
    main_send_0, main_recv_0, main_send_1, main_recv_1, edge_send, edge_recv, y_send, y_recv, z_send, z_recv,
    d_send, d_recv, out_send, out_recv, in_sem, table_sem,
):
    d = lax.axis_index("dates")
    c = lax.axis_index("cols")
    count = ny * nz
    y = c // nz
    z = c % nz

    def date_peer(k):
        return {"dates": (d + k) % GROUP, "cols": c}

    def y_peer(k):
        return {"dates": d, "cols": ((y + k) % ny) * nz + z}

    def z_peer(k):
        return {"dates": d, "cols": y * nz + (z + k) % nz}

    after = (c + 1) % count
    before = (c + count - 1) % count

    loads = [
        pltpu.make_async_copy(slc_hbm.at[:, t], slc.at[:, t], in_sem.at[t]) for t in range(EACH)
    ]
    for load in loads:
        load.start()

    barrier = pltpu.get_barrier_semaphore()

    def greet(device):
        pl.semaphore_signal(barrier, inc=1, device_id=device, device_id_type=MESH)

    for k in range(1, ny):
        greet(y_peer(k))
    for k in range(1, nz):
        greet(z_peer(k))
    for k in range(1, GROUP):
        greet(date_peer(k))

    @pl.when(d == 0)
    def _():
        for e in range(GROUP):
            greet({"dates": e, "cols": before})

    @pl.when(d == GROUP - 1)
    def _():
        for e in range(GROUP):
            greet({"dates": e, "cols": after})

    tables = [
        pltpu.make_async_copy(pairs_hbm, pairs_s, table_sem.at[0]),
        pltpu.make_async_copy(pairs_hbm, pairs_v, table_sem.at[1]),
        pltpu.make_async_copy(owner_hbm, owner_v, table_sem.at[2]),
    ]
    for table in tables:
        table.start()

    sent = (sent_0, sent_1)
    edge_in = (edge_left, edge_right)
    got = (got_0, got_1)

    def cut(half):
        size = PIECES[half]
        matrix = cutter(half)
        for t in range(EACH):
            if half == 0:
                loads[t].wait()
            both = jnp.concatenate([slc[0, t], slc[1, t]], axis=0)
            turned = lax.dot_general(
                matrix, both, (((1,), (1,)), ((), ())), preferred_element_type=F32
            )
            for e in range(GROUP + 1):
                rows = turned[size * e : size * (e + 1)] if e < GROUP else turned[size * GROUP :]
                value = jnp.concatenate([rows[:, :ROWS], rows[:, ROWS:]], axis=0).astype(BF16)
                if e < GROUP:
                    sent[half][e, 2 * size * t : 2 * size * (t + 1), :] = value
                else:
                    edge_out[half, 16 * t : 16 * (t + 1), :] = value

    cut(0)

    pl.semaphore_wait(barrier, (GROUP - 1) + (ny - 1) + (nz - 1) + 2)

    def spread(src, dst, send, recv, peer, number):
        copies = {}
        for k in sorted(range(1, number), key=lambda k: -min(k, number - k)):
            copy = pltpu.make_async_remote_copy(
                src_ref=src(k), dst_ref=dst(k), send_sem=send.at[k - 1], recv_sem=recv.at[k - 1],
                device_id=peer(k), device_id_type=MESH,
            )
            copy.start()
            copies[k] = copy
        return copies

    edge_copies = []

    def send_edge(side, device):
        copy = pltpu.make_async_remote_copy(
            src_ref=edge_out.at[side], dst_ref=edge_in[side].at[d], send_sem=edge_send.at[side],
            recv_sem=edge_recv.at[d], device_id=device, device_id_type=MESH,
        )
        copy.start()
        edge_copies.append(copy)

    def send_half(half, send, recv):
        return spread(
            lambda k: sent[half].at[(d + k) % GROUP], lambda k: got[half].at[d], send, recv,
            date_peer, GROUP,
        )

    send_edge(0, {"dates": 0, "cols": after})
    main_0 = send_half(0, main_send_0, main_recv_0)
    power_rows = []
    for t in range(EACH):
        wide = jnp.concatenate([slc[0, t], slc[1, t]], axis=0).astype(F32)
        square = jnp.sum(wide * wide, axis=0, keepdims=True)
        power_rows.append(square[:, :ROWS] + square[:, ROWS:])
    power_y[...] = jnp.concatenate(power_rows + [jnp.zeros((8 - EACH, ROWS), F32)], axis=0)
    y_copies = spread(lambda k: power_y, lambda k: power_y_in.at[k - 1], y_send, y_recv, y_peer, ny)
    cut(1)
    send_edge(1, {"dates": GROUP - 1, "cols": before})
    main_1 = send_half(1, main_send_1, main_recv_1)
    got_1[d] = sent_1[d]

    @pl.when(d != 0)
    def _():
        edge_left[...] = jnp.zeros_like(edge_left)

    @pl.when(d != GROUP - 1)
    def _():
        edge_right[...] = jnp.zeros_like(edge_right)


    high = band(HIGH)
    low = band(LOW)
    smoother[:, :ROWS] = jnp.concatenate([high, high], axis=0)
    smoother[:, ROWS:] = jnp.concatenate([low, low], axis=0)

    for table in tables:
        table.wait()
    owner_row = owner_v[...]
    owner_down = jnp.transpose(jnp.broadcast_to(owner_row.astype(F32), (ROWS, PAIRS)))[:, :PAIRS]
    earlier = iota((PAIRS, PAIRS), 0) < iota((PAIRS, PAIRS), 1)
    same = owner_down == owner_row.astype(F32)
    rank = jnp.sum(jnp.where(same & earlier, 1.0, 0.0), axis=0, keepdims=True).astype(jnp.int32)
    place = (rank & 3) * 32 + owner_row * 4 + (rank >> 2)
    one = jnp.where(iota((128, PAIRS), 0) == place, 1.0, 0.0)
    select[...] = jnp.concatenate([one, one, one], axis=1).astype(BF16)
    later = iota((PAIRS, PAIRS), 0) > iota((PAIRS, PAIRS), 1)
    rank_down = jnp.sum(jnp.where(same & later, 1.0, 0.0), axis=1, keepdims=True)
    quarter = (iota((PAIRS, 128), 1) >> 5).astype(F32)
    here = jnp.where(owner_down[:, :1] == d.astype(F32), rank_down, -1.0)
    for g in range(3):
        own[g] = jnp.where(here == quarter + 4.0 * g, 1.0, 0.0)

    def date_rows(which):
        date = pairs_v[which : which + 1, :]
        row = ((date >> 2) * 8 + (date & 3)).astype(F32)
        down = jnp.transpose(jnp.broadcast_to(row, (ROWS, PAIRS)))[:, : 8 * GROUP]
        lane = iota((PAIRS, 8 * GROUP), 1).astype(F32)
        one = jnp.where(down == lane, 1.0, 0.0)
        return jnp.concatenate([one, one, one], axis=1).astype(BF16)

    hot[...] = jnp.concatenate([date_rows(0), date_rows(1)], axis=0)
    one = jnp.where((iota((ROWS, 128), 0) >> 2) == (iota((ROWS, 128), 1) & 31), 1.0, 0.0)
    look[...] = jnp.concatenate([one, one, one], axis=0).astype(BF16)

    def edges(side):
        for e in range(GROUP):
            pltpu.make_async_remote_copy(
                src_ref=edge_out.at[side], dst_ref=edge_in[side].at[e], send_sem=edge_send.at[side],
                recv_sem=edge_recv.at[e], device_id=date_peer(1), device_id_type=MESH,
            ).wait_recv()

    left_gate = jnp.where(c > 0, 1.0, 0.0).astype(F32)
    right_gate = jnp.where(c < count - 1, 1.0, 0.0).astype(F32)

    def smooth_powers(number):
        for t in range(number):
            big, small = split(along_columns(fields, t))
            lhs[HALF * t : HALF * (t + 1), :ROWS] = big
            lhs[HALF * t : HALF * (t + 1), ROWS:] = small
        smooth = dot(lhs[: number * HALF, :], smoother[...])
        return jnp.sqrt(smooth[:, :ROWS] + smooth[:, ROWS:])

    def take_first(source, block):
        size = PIECES[0]
        for t in range(EACH):
            piece = block[2 * size * t : 2 * size * (t + 1), :].astype(F32)
            edge = edge_left[source, 16 * t : 16 * (t + 1), :].astype(F32) * left_gate
            real = jnp.concatenate([piece[:8] + edge[:8], piece[8:size]], axis=0)
            imag = jnp.concatenate([piece[size : size + 8] + edge[8:], piece[size + 8 :]], axis=0)
            images[source * EACH + t, 0, :size] = real
            images[source * EACH + t, 1, :size] = imag
            fields[t] = real * real + imag * imag
        smooth = smooth_powers(EACH)
        for t in range(EACH):
            roots[source * EACH + t, :HALF] = smooth[HALF * t : HALF * (t + 1)]

    def arrive(k):
        main_0[k].wait_recv()
        source = (d + GROUP - k) % GROUP
        take_first(source, got_0.at[source])

    def take_second():
        size = PIECES[1]
        for date in range(DATES):
            source, t = date // EACH, date % EACH
            piece = got_1[source, 2 * size * t : 2 * size * (t + 1), :].astype(F32)
            edge = edge_right[source, 16 * t : 16 * (t + 1), :].astype(F32) * right_gate
            real = jnp.concatenate([piece[:8], piece[8:size] + edge[:8]], axis=0)
            imag = jnp.concatenate([piece[size : size + 8], piece[size + 8 :] + edge[8:]], axis=0)
            images[date, 0, PIECES[0] :] = real
            images[date, 1, PIECES[0] :] = imag
            real = jnp.concatenate([images[date, 0, HALF : PIECES[0]], real], axis=0)
            imag = jnp.concatenate([images[date, 1, HALF : PIECES[0]], imag], axis=0)
            fields[date] = real * real + imag * imag
        smooth = smooth_powers(DATES)
        for date in range(DATES):
            roots[date, HALF:] = smooth[HALF * date : HALF * (date + 1)]

    def pairs_of(half):
        window = slice(HALF * half, HALF * half + WINDOW)

        def place(field, p):
            return pl.ds(((3 * half + field) * PAIRS + p) * 8, 8)

        def chunk(index, carry):
            dates = []
            for i in range(CHUNK):
                p = index * CHUNK + i
                first = pairs_s[0, p]
                second = pairs_s[1, p]
                dates.append((first, second))
                real_a = images[first, 0, window]
                imag_a = images[first, 1, window]
                real_b = images[second, 0, window]
                imag_b = images[second, 1, window]
                fields[2 * i] = real_a * real_b + imag_a * imag_b
                fields[2 * i + 1] = imag_a * real_b - real_a * imag_b
            for i in range(CHUNK):
                p = index * CHUNK + i
                for f in range(2):
                    n = 2 * i + f
                    big, small = split(along_columns(fields, n))
                    lhs[HALF * n : HALF * (n + 1), :ROWS] = big
                    lhs[HALF * n : HALF * (n + 1), ROWS:] = small
                    sums[place(f, p), :] = fields[n, 4:12, :] + fields[n, 12:20, :]
            smooth = dot(lhs[...], smoother[...])
            smooth = smooth[:, :ROWS] + smooth[:, ROWS:]
            for i in range(CHUNK):
                p = index * CHUNK + i
                first, second = dates[i]
                real = smooth[2 * HALF * i : 2 * HALF * i + HALF]
                imag = smooth[2 * HALF * i + HALF : 2 * HALF * (i + 1)]
                below = (
                    roots[first, HALF * half : HALF * (half + 1)]
                    * roots[second, HALF * half : HALF * (half + 1)]
                )
                value = jnp.sqrt(real * real + imag * imag) / (below + 1e-06)
                sums[place(2, p), :] = value[0:8] + value[8:16]
            return carry

        lax.fori_loop(0, PAIRS // CHUNK, chunk, 0)
        rows = sums[pl.ds(3 * half * PAIRS * 8, 3 * PAIRS, stride=8), :]
        for i in range(1, 8):
            rows = rows + sums[pl.ds(3 * half * PAIRS * 8 + i, 3 * PAIRS, stride=8), :]
        looked[half] = dot(jnp.concatenate(split3(rows), axis=1), look[...])

    for copy in y_copies.values():
        copy.wait_recv()
    power = power_y[...]
    for k in range(1, ny):
        power = power + power_y_in[k - 1]
    power_z[...] = power
    z_copies = spread(lambda k: power_z, lambda k: power_z_in.at[k - 1], z_send, z_recv, z_peer, nz)

    @pl.when(d == 0)
    def _():
        edges(0)

    take_first(d, sent_0.at[d])
    for k in (4, 3, 5, 2, 6, 1, 7):
        arrive(k)
    pairs_of(0)
    for copy in z_copies.values():
        copy.wait_recv()
    power = power_z[...]
    for k in range(1, nz):
        power = power + power_z_in[k - 1]
    power_d[...] = power
    totals[d] = power
    d_copies = spread(lambda k: power_d, lambda k: totals.at[d], d_send, d_recv, date_peer, GROUP)

    @pl.when(d == GROUP - 1)
    def _():
        edges(1)

    for k in (4, 3, 5, 2, 6, 1, 7):
        main_1[k].wait_recv()
    take_second()
    pairs_of(1)

    wide = []
    for q in range(6):
        piece = looked[q // 3, PAIRS * (q % 3) : PAIRS * (q % 3 + 1)]
        wide.append(piece if q % 3 < 2 else piece * (1.0 / 64.0))
    stacked = jnp.concatenate(split3(jnp.concatenate(wide, axis=1)), axis=0)
    placed = dot(select[...], stacked)
    lane = iota((32, 128), 1)
    for q in range(6):
        part = placed[:, 128 * q : 128 * (q + 1)]
        value = jnp.where(
            lane < 64,
            jnp.where(lane < 32, part[0:32], part[32:64]),
            jnp.where(lane < 96, part[64:96], part[96:128]),
        )
        for e in range(GROUP):
            results[e, 4 * q : 4 * q + 4, :] = value[4 * e : 4 * e + 4]

    out_copies = spread(
        lambda k: results.at[(d + k) % GROUP], lambda k: landed.at[d], out_send, out_recv, date_peer, GROUP
    )
    landed[d] = results[d]

    for copy in d_copies.values():
        copy.wait_recv()
    parts = jnp.concatenate(split3(totals[...].reshape(8 * GROUP, ROWS)), axis=0)
    total = jnp.sum(dot(hot[...], parts), axis=1, keepdims=True)
    scale = jnp.sqrt(total / (ROWS * WIDTH * count) + 1e-06)
    factor = (1.0 / 64.0) / (scale[:PAIRS] * scale[PAIRS:])
    factors = [jnp.sum(own[g] * factor, axis=0, keepdims=True) for g in range(3)]

    for copy in out_copies.values():
        copy.wait_recv()
    scaling[...] = jnp.concatenate(factors + [jnp.zeros((5, 128), F32)], axis=0)
    for copies in (y_copies, z_copies, d_copies, main_0, main_1, out_copies):
        for copy in copies.values():
            copy.wait_send()
    for copy in edge_copies:
        copy.wait_send()


def place_kernel(landed, scaling, interferogram, coherence):
    for f in range(3):
        for g in range(3):
            block = landed[pl.ds(f * 4 + g, 16, stride=12), :]
            if f < 2:
                block = block * scaling[g : g + 1, :]
            for j in range(4):
                piece = block[:, 32 * j : 32 * j + 32]
                if f < 2:
                    interferogram[f, 4 * g + j] = piece
                else:
                    coherence[4 * g + j] = piece


def solution(mesh):
    columns = mesh.shape["cols"]
    nz = 8 if columns % 8 == 0 else columns
    ny = columns // nz
    sem = pltpu.SemaphoreType.DMA
    vmem = pl.BlockSpec(memory_space=pltpu.VMEM)

    def local(slc, pairs, owner):
        pairs = pairs.T
        owner = owner.reshape(1, PAIRS)
        landed, scaling = pl.pallas_call(
            lambda *refs: kernel(ny, nz, *refs),
            out_shape=(jax.ShapeDtypeStruct((GROUP, 24, 128), F32), jax.ShapeDtypeStruct((8, 128), F32)),
            in_specs=[pl.BlockSpec(memory_space=pl.ANY)] * 3,
            out_specs=(vmem, vmem),
            scratch_shapes=[
                pltpu.VMEM((2, EACH, ROWS, WIDTH), BF16),
                pltpu.SMEM((2, PAIRS), jnp.int32),
                pltpu.VMEM((2, PAIRS), jnp.int32),
                pltpu.VMEM((1, PAIRS), jnp.int32),
                pltpu.VMEM((128, 3 * PAIRS), BF16),
                pltpu.VMEM((3, PAIRS, 128), F32),
                pltpu.VMEM((3 * ROWS, 128), BF16),
                pltpu.VMEM((2 * PAIRS, 24 * GROUP), BF16),
                pltpu.VMEM((2 * ROWS, 2 * ROWS), BF16),
                pltpu.VMEM((GROUP, EACH * 2 * PIECES[0], ROWS), BF16),
                pltpu.VMEM((GROUP, EACH * 2 * PIECES[1], ROWS), BF16),
                pltpu.VMEM((GROUP, EACH * 2 * PIECES[0], ROWS), BF16),
                pltpu.VMEM((GROUP, EACH * 2 * PIECES[1], ROWS), BF16),
                pltpu.VMEM((2, EDGE, ROWS), BF16),
                pltpu.VMEM((GROUP, EDGE, ROWS), BF16),
                pltpu.VMEM((GROUP, EDGE, ROWS), BF16),
                pltpu.VMEM((DATES, 2, TILE, ROWS), F32),
                pltpu.VMEM((DATES, PART, ROWS), F32),
                pltpu.VMEM((2 * CHUNK, WINDOW, ROWS), F32),
                pltpu.VMEM((2 * CHUNK * HALF, 2 * ROWS), BF16),
                pltpu.VMEM((6 * PAIRS * 8, ROWS), F32),
                pltpu.VMEM((2, 3 * PAIRS, ROWS), F32),
                pltpu.VMEM((8, ROWS), F32),
                pltpu.VMEM((8, ROWS), F32),
                pltpu.VMEM((8, ROWS), F32),
                pltpu.VMEM((max(ny - 1, 1), 8, ROWS), F32),
                pltpu.VMEM((max(nz - 1, 1), 8, ROWS), F32),
                pltpu.VMEM((GROUP, 8, ROWS), F32),
                pltpu.VMEM((GROUP, 24, 128), F32),
                sem((GROUP - 1,)), sem((GROUP - 1,)),
                sem((GROUP - 1,)), sem((GROUP - 1,)),
                sem((2,)), sem((GROUP,)),
                sem((max(ny - 1, 1),)), sem((max(ny - 1, 1),)),
                sem((max(nz - 1, 1),)), sem((max(nz - 1, 1),)),
                sem((GROUP - 1,)), sem((GROUP - 1,)),
                sem((GROUP - 1,)), sem((GROUP - 1,)),
                sem((EACH,)), sem((3,)),
            ],
            compiler_params=pltpu.CompilerParams(
                collective_id=0, has_side_effects=True, vmem_limit_bytes=54682 * 1024
            ),
        )(slc, pairs, owner)
        interferogram, coherence = pl.pallas_call(
            place_kernel,
            out_shape=(
                jax.ShapeDtypeStruct((2, CAP, 16, 32), F32),
                jax.ShapeDtypeStruct((CAP, 16, 32), F32),
            ),
            in_specs=[vmem, vmem],
            out_specs=(vmem, vmem),
            compiler_params=pltpu.CompilerParams(vmem_limit_bytes=2 * 1024 * 1024),
        )(landed.reshape(GROUP * 24, 128), scaling)
        return jnp.swapaxes(interferogram, 2, 3), jnp.swapaxes(coherence, 1, 2)

    return jax.shard_map(
        local,
        mesh=mesh,
        in_specs=(P(None, "dates", None, "cols"), P(), P()),
        out_specs=(P(None, "dates", None, "cols"), P("dates", None, "cols")),
        check_vma=False,
    )
```

```python
import math

import jax
import jax.numpy as jnp
import ml_dtypes
import numpy as np
from jax import lax
from jax.experimental import pallas as pl
from jax.experimental.pallas import tpu as pltpu
from jax.sharding import PartitionSpec as P

MESH = pl.DeviceIdType.MESH
F32 = jnp.float32
BF16 = jnp.bfloat16

TAPS = [math.exp(-k * k / 8.0) for k in range(-4, 5)]
WEIGHTS = [float(np.float32(t / sum(TAPS))) for t in TAPS]
HIGH = [float(np.float32(w).astype(ml_dtypes.bfloat16)) for w in WEIGHTS]
LOW = [float(np.float32(w - h).astype(ml_dtypes.bfloat16)) for w, h in zip(WEIGHTS, HIGH)]

GROUP = 8
EACH = 4
DATES = GROUP * EACH
PAIRS = 64
CAP = 12
ROWS = 128
PART = 32
TILE = PART + 8
WIDTH = GROUP * PART
PIECES = (24, 16)
HALF = PART // 2
WINDOW = HALF + 8
EDGE = EACH * 2 * 8
CHUNK = 16


def split(x):
    high = x.astype(BF16)
    return high, (x - high.astype(F32)).astype(BF16)


def split3(x):
    high = x.astype(BF16)
    rest = x - high.astype(F32)
    mid = rest.astype(BF16)
    return high, mid, (rest - mid.astype(F32)).astype(BF16)


def dot(a, b):
    return jnp.dot(a, b, preferred_element_type=F32)


def iota(shape, axis):
    return lax.broadcasted_iota(jnp.int32, shape, axis)


def cutter(half):
    start, size = (-4, PIECES[0]) if half == 0 else (PIECES[0] - 4, PIECES[1])
    lane = iota((size, WIDTH), 1)
    row = iota((size, WIDTH), 0)
    pieces = [jnp.where(lane == row + (PART * e + start), 1.0, 0.0) for e in range(GROUP)]
    lane = iota((8, WIDTH), 1)
    row = iota((8, WIDTH), 0)
    pieces.append(jnp.where(lane == row + (WIDTH - 4 if half == 0 else -4), 1.0, 0.0))
    return jnp.concatenate(pieces, axis=0).astype(BF16)


def band(weights):
    gap = jnp.abs(iota((ROWS, ROWS), 0) - iota((ROWS, ROWS), 1))
    result = jnp.zeros((ROWS, ROWS), F32)
    for k in range(5):
        result = jnp.where(gap == k, weights[4 + k], result)
    return result.astype(BF16)


def along_columns(ref, index):
    result = WEIGHTS[4] * ref[index, 4 : 4 + HALF, :]
    for k in range(4):
        both = ref[index, k : k + HALF, :] + ref[index, 8 - k : 8 - k + HALF, :]
        result = result + WEIGHTS[k] * both
    return result


def kernel(
    nz, count, slc_hbm, pairs_hbm, owner_hbm, landed, scaling,
    slc, pairs_s, pairs_v, owner_v, select, own, look, hot, smoother, sent_0, sent_1, got_0, got_1,
    edge_out, edge_left, edge_right, images, roots, fields, lhs, sums, looked,
    power_up, power_in, power_d, totals, factor_out, factor_in, results,
    main_send_0, main_recv_0, main_send_1, main_recv_1, edge_send, edge_recv, ready,
    up_send, up_recv, down_send, down_recv, d_send, d_recv, out_send, out_recv, in_sem, table_sem,
):
    d = lax.axis_index("dates")
    c = lax.axis_index("cols")
    z = c % nz

    def date_peer(k):
        return {"dates": (d + k) % GROUP, "cols": c}

    right = (c + 1) % count
    left = (c + count - 1) % count
    right_later = (z < nz - 1) & (c < count - 1)
    right_earlier = (z == nz - 1) & (c < count - 1)
    left_later = (z == 0) & (c > 0)
    left_earlier = (z > 0) & (c > 0)

    loads = [
        pltpu.make_async_copy(slc_hbm.at[:, t], slc.at[:, t], in_sem.at[t]) for t in range(EACH)
    ]
    for load in loads:
        load.start()

    barrier = pltpu.get_barrier_semaphore()

    def greet(device):
        pl.semaphore_signal(barrier, inc=1, device_id=device, device_id_type=MESH)

    for k in range(1, GROUP):
        greet(date_peer(k))

    def greet_neighbour(later, receiver, other):
        @pl.when(later)
        def _():
            greet({"dates": receiver, "cols": other})

        @pl.when(later & (d == GROUP - 1 - receiver))
        def _():
            for e in range(GROUP):
                greet({"dates": e, "cols": other})

    greet_neighbour(right_later, 0, right)
    greet_neighbour(left_later, GROUP - 1, left)

    @pl.when(c == 0)
    def _():
        def one(i, carry):
            greet({"dates": d, "cols": i})
            return carry

        lax.fori_loop(1, count, one, 0)

    tables = [
        pltpu.make_async_copy(pairs_hbm, pairs_s, table_sem.at[0]),
        pltpu.make_async_copy(pairs_hbm, pairs_v, table_sem.at[1]),
        pltpu.make_async_copy(owner_hbm, owner_v, table_sem.at[2]),
    ]
    for table in tables:
        table.start()

    sent = (sent_0, sent_1)
    edge_in = (edge_left, edge_right)
    got = (got_0, got_1)

    def cut(half):
        size = PIECES[half]
        matrix = cutter(half)
        for t in range(EACH):
            both = jnp.concatenate([slc[0, t], slc[1, t]], axis=0)
            turned = lax.dot_general(
                matrix, both, (((1,), (1,)), ((), ())), preferred_element_type=F32
            )
            for e in range(GROUP + 1):
                rows = turned[size * e : size * (e + 1)] if e < GROUP else turned[size * GROUP :]
                value = jnp.concatenate([rows[:, :ROWS], rows[:, ROWS:]], axis=0).astype(BF16)
                if e < GROUP:
                    sent[half][e, 2 * size * t : 2 * size * (t + 1), :] = value
                else:
                    edge_out[half, 16 * t : 16 * (t + 1), :] = value

    for load in loads:
        load.wait()
    cut(0)

    first = (d == 0).astype(jnp.int32)
    last = (d == GROUP - 1).astype(jnp.int32)
    pl.semaphore_wait(
        barrier,
        (GROUP - 1)
        + (c > 0).astype(jnp.int32)
        + right_earlier.astype(jnp.int32) * (1 + GROUP * last)
        + left_earlier.astype(jnp.int32) * (1 + GROUP * first),
    )

    def tell_ready(side, condition, other):
        @pl.when(condition)
        def _():
            for e in range(GROUP):
                pl.semaphore_signal(
                    ready.at[side], inc=1, device_id={"dates": e, "cols": other}, device_id_type=MESH
                )

    tell_ready(0, left_earlier & (d == 0), left)
    tell_ready(1, right_earlier & (d == GROUP - 1), right)

    def spread(src, dst, send, recv, peer, number):
        copies = {}
        for k in sorted(range(1, number), key=lambda k: -min(k, number - k)):
            copy = pltpu.make_async_remote_copy(
                src_ref=src(k), dst_ref=dst(k), send_sem=send.at[k - 1], recv_sem=recv.at[k - 1],
                device_id=peer(k), device_id_type=MESH,
            )
            copy.start()
            copies[k] = copy
        return copies

    targets = ({"dates": 0, "cols": right}, {"dates": GROUP - 1, "cols": left})

    def edge_copy(side):
        return pltpu.make_async_remote_copy(
            src_ref=edge_out.at[side], dst_ref=edge_in[side].at[d], send_sem=edge_send.at[side],
            recv_sem=edge_recv.at[GROUP * side + d], device_id=targets[side], device_id_type=MESH,
        )

    def send_half(half, send, recv):
        return spread(
            lambda k: sent[half].at[(d + k) % GROUP], lambda k: got[half].at[d], send, recv,
            date_peer, GROUP,
        )

    main_0 = send_half(0, main_send_0, main_recv_0)

    @pl.when(right_earlier)
    def _():
        edge_copy(0).start()

    power_rows = []
    for t in range(EACH):
        wide = jnp.concatenate([slc[0, t], slc[1, t]], axis=0).astype(F32)
        square = jnp.sum(wide * wide, axis=0, keepdims=True)
        power_rows.append(square[:, :ROWS] + square[:, ROWS:])
    power_up[...] = jnp.concatenate(power_rows + [jnp.zeros((8 - EACH, ROWS), F32)], axis=0)

    def up_copy(i):
        return pltpu.make_async_remote_copy(
            src_ref=power_up, dst_ref=power_in.at[i], send_sem=up_send.at[0], recv_sem=up_recv.at[i],
            device_id={"dates": d, "cols": 0}, device_id_type=MESH,
        )

    def down_copy(i):
        return pltpu.make_async_remote_copy(
            src_ref=factor_out, dst_ref=factor_in, send_sem=down_send.at[i], recv_sem=down_recv.at[0],
            device_id={"dates": d, "cols": i}, device_id_type=MESH,
        )

    @pl.when(c > 0)
    def _():
        up_copy(c).start()

    cut(1)
    main_1 = send_half(1, main_send_1, main_recv_1)

    @pl.when(left_earlier)
    def _():
        edge_copy(1).start()

    got_1[d] = sent_1[d]

    @pl.when((d != 0) | (c == 0))
    def _():
        edge_left[...] = jnp.zeros_like(edge_left)

    @pl.when((d != GROUP - 1) | (c == count - 1))
    def _():
        edge_right[...] = jnp.zeros_like(edge_right)


    high = band(HIGH)
    low = band(LOW)
    smoother[:, :ROWS] = jnp.concatenate([high, high], axis=0)
    smoother[:, ROWS:] = jnp.concatenate([low, low], axis=0)

    for table in tables:
        table.wait()
    owner_row = owner_v[...]
    owner_down = jnp.transpose(jnp.broadcast_to(owner_row.astype(F32), (ROWS, PAIRS)))[:, :PAIRS]
    earlier = iota((PAIRS, PAIRS), 0) < iota((PAIRS, PAIRS), 1)
    same = owner_down == owner_row.astype(F32)
    rank = jnp.sum(jnp.where(same & earlier, 1.0, 0.0), axis=0, keepdims=True).astype(jnp.int32)
    place = (rank & 3) * 32 + owner_row * 4 + (rank >> 2)
    one = jnp.where(iota((128, PAIRS), 0) == place, 1.0, 0.0)
    select[...] = jnp.concatenate([one, one, one], axis=1).astype(BF16)
    later = iota((PAIRS, PAIRS), 0) > iota((PAIRS, PAIRS), 1)
    rank_down = jnp.sum(jnp.where(same & later, 1.0, 0.0), axis=1, keepdims=True)
    quarter = (iota((PAIRS, 128), 1) >> 5).astype(F32)
    here = jnp.where(owner_down[:, :1] == d.astype(F32), rank_down, -1.0)
    for g in range(3):
        own[g] = jnp.where(here == quarter + 4.0 * g, 1.0, 0.0)

    def date_rows(which):
        date = pairs_v[which : which + 1, :]
        row = ((date >> 2) * 8 + (date & 3)).astype(F32)
        down = jnp.transpose(jnp.broadcast_to(row, (ROWS, PAIRS)))[:, : 8 * GROUP]
        lane = iota((PAIRS, 8 * GROUP), 1).astype(F32)
        one = jnp.where(down == lane, 1.0, 0.0)
        return jnp.concatenate([one, one, one], axis=1).astype(BF16)

    hot[...] = jnp.concatenate([date_rows(0), date_rows(1)], axis=0)
    one = jnp.where((iota((ROWS, 128), 0) >> 2) == (iota((ROWS, 128), 1) & 31), 1.0, 0.0)
    look[...] = jnp.concatenate([one, one, one], axis=0).astype(BF16)

    def edges(side):
        for e in range(GROUP):
            pltpu.make_async_remote_copy(
                src_ref=edge_out.at[side], dst_ref=edge_in[side].at[e], send_sem=edge_send.at[side],
                recv_sem=edge_recv.at[GROUP * side + e], device_id=targets[side], device_id_type=MESH,
            ).wait_recv()

    def smooth_powers(number):
        for t in range(number):
            big, small = split(along_columns(fields, t))
            lhs[HALF * t : HALF * (t + 1), :ROWS] = big
            lhs[HALF * t : HALF * (t + 1), ROWS:] = small
        smooth = dot(lhs[: number * HALF, :], smoother[...])
        return jnp.sqrt(smooth[:, :ROWS] + smooth[:, ROWS:])

    def take_first(source, block):
        size = PIECES[0]
        for t in range(EACH):
            piece = block[2 * size * t : 2 * size * (t + 1), :].astype(F32)
            edge = edge_left[source, 16 * t : 16 * (t + 1), :].astype(F32)
            real = jnp.concatenate([piece[:8] + edge[:8], piece[8:size]], axis=0)
            imag = jnp.concatenate([piece[size : size + 8] + edge[8:], piece[size + 8 :]], axis=0)
            images[source * EACH + t, 0, :size] = real
            images[source * EACH + t, 1, :size] = imag
            fields[t] = real * real + imag * imag
        smooth = smooth_powers(EACH)
        for t in range(EACH):
            roots[source * EACH + t, :HALF] = smooth[HALF * t : HALF * (t + 1)]

    def arrive(k):
        main_0[k].wait_recv()
        source = (d + GROUP - k) % GROUP
        take_first(source, got_0.at[source])

    def take_second():
        size = PIECES[1]
        for date in range(DATES):
            source, t = date // EACH, date % EACH
            piece = got_1[source, 2 * size * t : 2 * size * (t + 1), :].astype(F32)
            edge = edge_right[source, 16 * t : 16 * (t + 1), :].astype(F32)
            real = jnp.concatenate([piece[:8], piece[8:size] + edge[:8]], axis=0)
            imag = jnp.concatenate([piece[size : size + 8], piece[size + 8 :] + edge[8:]], axis=0)
            images[date, 0, PIECES[0] :] = real
            images[date, 1, PIECES[0] :] = imag
            real = jnp.concatenate([images[date, 0, HALF : PIECES[0]], real], axis=0)
            imag = jnp.concatenate([images[date, 1, HALF : PIECES[0]], imag], axis=0)
            fields[date] = real * real + imag * imag
        smooth = smooth_powers(DATES)
        for date in range(DATES):
            roots[date, HALF:] = smooth[HALF * date : HALF * (date + 1)]

    def pairs_of(half):
        window = slice(HALF * half, HALF * half + WINDOW)

        def place(field, p):
            return pl.ds(((3 * half + field) * PAIRS + p) * 8, 8)

        def chunk(index, carry):
            dates = []
            for i in range(CHUNK):
                p = index * CHUNK + i
                first = pairs_s[0, p]
                second = pairs_s[1, p]
                dates.append((first, second))
                real_a = images[first, 0, window]
                imag_a = images[first, 1, window]
                real_b = images[second, 0, window]
                imag_b = images[second, 1, window]
                fields[2 * i] = real_a * real_b + imag_a * imag_b
                fields[2 * i + 1] = imag_a * real_b - real_a * imag_b
            for i in range(CHUNK):
                p = index * CHUNK + i
                for f in range(2):
                    n = 2 * i + f
                    big, small = split(along_columns(fields, n))
                    lhs[HALF * n : HALF * (n + 1), :ROWS] = big
                    lhs[HALF * n : HALF * (n + 1), ROWS:] = small
                    sums[place(f, p), :] = fields[n, 4:12, :] + fields[n, 12:20, :]
            smooth = dot(lhs[...], smoother[...])
            smooth = smooth[:, :ROWS] + smooth[:, ROWS:]
            for i in range(CHUNK):
                p = index * CHUNK + i
                first, second = dates[i]
                real = smooth[2 * HALF * i : 2 * HALF * i + HALF]
                imag = smooth[2 * HALF * i + HALF : 2 * HALF * (i + 1)]
                below = (
                    roots[first, HALF * half : HALF * (half + 1)]
                    * roots[second, HALF * half : HALF * (half + 1)]
                )
                value = jnp.sqrt(real * real + imag * imag) / (below + 1e-06)
                sums[place(2, p), :] = value[0:8] + value[8:16]
            return carry

        lax.fori_loop(0, PAIRS // CHUNK, chunk, 0)
        rows = sums[pl.ds(3 * half * PAIRS * 8, 3 * PAIRS, stride=8), :]
        for i in range(1, 8):
            rows = rows + sums[pl.ds(3 * half * PAIRS * 8 + i, 3 * PAIRS, stride=8), :]
        looked[half] = dot(jnp.concatenate(split3(rows), axis=1), look[...])

    @pl.when(right_later)
    def _():
        pl.semaphore_wait(ready.at[0], 1)
        edge_copy(0).start()

    @pl.when(left_later)
    def _():
        pl.semaphore_wait(ready.at[1], 1)
        edge_copy(1).start()

    @pl.when((d == 0) & (c > 0))
    def _():
        edges(0)

    take_first(d, sent_0.at[d])
    for k in (4, 3, 5, 2, 6, 1, 7):
        arrive(k)
    pairs_of(0)

    def d_copy(k):
        return pltpu.make_async_remote_copy(
            src_ref=power_d, dst_ref=totals.at[d], send_sem=d_send.at[k - 1], recv_sem=d_recv.at[k - 1],
            device_id=date_peer(k), device_id_type=MESH,
        )

    @pl.when(c == 0)
    def _():
        def one(i, carry):
            up_copy(i).wait_recv()
            return carry

        lax.fori_loop(1, count, one, 0)
        power = power_up[...] + jnp.sum(power_in[1:count], axis=0)
        power_d[...] = power
        totals[d] = power
        for k in range(1, GROUP):
            d_copy(k).start()

    @pl.when((d == GROUP - 1) & (c < count - 1))
    def _():
        edges(1)

    for k in (4, 3, 5, 2, 6, 1, 7):
        main_1[k].wait_recv()
    take_second()
    pairs_of(1)

    wide = []
    for q in range(6):
        piece = looked[q // 3, PAIRS * (q % 3) : PAIRS * (q % 3 + 1)]
        wide.append(piece if q % 3 < 2 else piece * (1.0 / 64.0))
    stacked = jnp.concatenate(split3(jnp.concatenate(wide, axis=1)), axis=0)
    placed = dot(select[...], stacked)
    lane = iota((32, 128), 1)
    for q in range(6):
        part = placed[:, 128 * q : 128 * (q + 1)]
        value = jnp.where(
            lane < 64,
            jnp.where(lane < 32, part[0:32], part[32:64]),
            jnp.where(lane < 96, part[64:96], part[96:128]),
        )
        for e in range(GROUP):
            results[e, 4 * q : 4 * q + 4, :] = value[4 * e : 4 * e + 4]

    out_copies = spread(
        lambda k: results.at[(d + k) % GROUP], lambda k: landed.at[d], out_send, out_recv, date_peer, GROUP
    )
    landed[d] = results[d]

    @pl.when(c == 0)
    def _():
        for k in range(1, GROUP):
            d_copy(k).wait_recv()
        parts = jnp.concatenate(split3(totals[...].reshape(8 * GROUP, ROWS)), axis=0)
        total = jnp.sum(dot(hot[...], parts), axis=1, keepdims=True)
        scale = jnp.sqrt(total / (ROWS * WIDTH * count) + 1e-06)
        factor = (1.0 / 64.0) / (scale[:PAIRS] * scale[PAIRS:])
        factor = jnp.broadcast_to(jnp.concatenate([factor, factor], axis=0), (ROWS, ROWS))
        factor = jnp.transpose(factor)[:8]
        factor_out[...] = factor
        factor_in[...] = factor

        def one(i, carry):
            down_copy((i % (count // nz)) * nz + i // (count // nz)).start()
            return carry

        lax.fori_loop(1, count, one, 0)

    @pl.when(c > 0)
    def _():
        down_copy(0).wait_recv()

    factor = jnp.transpose(jnp.broadcast_to(factor_in[0:1, :PAIRS], (ROWS, PAIRS)))
    factors = [jnp.sum(own[g] * factor, axis=0, keepdims=True) for g in range(3)]
    for copy in out_copies.values():
        copy.wait_recv()
    scaling[...] = jnp.concatenate(factors + [jnp.zeros((5, 128), F32)], axis=0)
    for copies in (main_0, main_1, out_copies):
        for copy in copies.values():
            copy.wait_send()

    @pl.when(right_later | right_earlier)
    def _():
        edge_copy(0).wait_send()

    @pl.when(left_later | left_earlier)
    def _():
        edge_copy(1).wait_send()

    @pl.when(c > 0)
    def _():
        up_copy(c).wait_send()

    @pl.when(c == 0)
    def _():
        for k in range(1, GROUP):
            d_copy(k).wait_send()

        def one(i, carry):
            down_copy(i).wait_send()
            return carry

        lax.fori_loop(1, count, one, 0)


def place_kernel(landed, scaling, interferogram, coherence):
    for f in range(3):
        for g in range(3):
            block = landed[pl.ds(f * 4 + g, 16, stride=12), :]
            if f < 2:
                block = block * scaling[g : g + 1, :]
            for j in range(4):
                piece = block[:, 32 * j : 32 * j + 32]
                if f < 2:
                    interferogram[f, 4 * g + j] = piece
                else:
                    coherence[4 * g + j] = piece


def solution(mesh):
    columns = mesh.shape["cols"]
    nz = 8 if columns % 8 == 0 else 2
    sem = pltpu.SemaphoreType.DMA
    vmem = pl.BlockSpec(memory_space=pltpu.VMEM)

    def local(slc, pairs, owner):
        pairs = pairs.T
        owner = owner.reshape(1, PAIRS)
        landed, scaling = pl.pallas_call(
            lambda *refs: kernel(nz, columns, *refs),
            out_shape=(jax.ShapeDtypeStruct((GROUP, 24, 128), F32), jax.ShapeDtypeStruct((8, 128), F32)),
            in_specs=[pl.BlockSpec(memory_space=pl.ANY)] * 3,
            out_specs=(vmem, vmem),
            scratch_shapes=[
                pltpu.VMEM((2, EACH, ROWS, WIDTH), BF16),
                pltpu.SMEM((2, PAIRS), jnp.int32),
                pltpu.VMEM((2, PAIRS), jnp.int32),
                pltpu.VMEM((1, PAIRS), jnp.int32),
                pltpu.VMEM((128, 3 * PAIRS), BF16),
                pltpu.VMEM((3, PAIRS, 128), F32),
                pltpu.VMEM((3 * ROWS, 128), BF16),
                pltpu.VMEM((2 * PAIRS, 24 * GROUP), BF16),
                pltpu.VMEM((2 * ROWS, 2 * ROWS), BF16),
                pltpu.VMEM((GROUP, EACH * 2 * PIECES[0], ROWS), BF16),
                pltpu.VMEM((GROUP, EACH * 2 * PIECES[1], ROWS), BF16),
                pltpu.VMEM((GROUP, EACH * 2 * PIECES[0], ROWS), BF16),
                pltpu.VMEM((GROUP, EACH * 2 * PIECES[1], ROWS), BF16),
                pltpu.VMEM((2, EDGE, ROWS), BF16),
                pltpu.VMEM((GROUP, EDGE, ROWS), BF16),
                pltpu.VMEM((GROUP, EDGE, ROWS), BF16),
                pltpu.VMEM((DATES, 2, TILE, ROWS), F32),
                pltpu.VMEM((DATES, PART, ROWS), F32),
                pltpu.VMEM((2 * CHUNK, WINDOW, ROWS), F32),
                pltpu.VMEM((2 * CHUNK * HALF, 2 * ROWS), BF16),
                pltpu.VMEM((6 * PAIRS * 8, ROWS), F32),
                pltpu.VMEM((2, 3 * PAIRS, ROWS), F32),
                pltpu.VMEM((8, ROWS), F32),
                pltpu.VMEM((columns, 8, ROWS), F32),
                pltpu.VMEM((8, ROWS), F32),
                pltpu.VMEM((GROUP, 8, ROWS), F32),
                pltpu.VMEM((8, ROWS), F32),
                pltpu.VMEM((8, ROWS), F32),
                pltpu.VMEM((GROUP, 24, 128), F32),
                sem((GROUP - 1,)), sem((GROUP - 1,)),
                sem((GROUP - 1,)), sem((GROUP - 1,)),
                sem((2,)), sem((2 * GROUP,)), pltpu.SemaphoreType.REGULAR((2,)),
                sem((1,)), sem((columns,)), sem((columns,)), sem((1,)),
                sem((GROUP - 1,)), sem((GROUP - 1,)),
                sem((GROUP - 1,)), sem((GROUP - 1,)),
                sem((EACH,)), sem((3,)),
            ],
            compiler_params=pltpu.CompilerParams(
                collective_id=0, has_side_effects=True, vmem_limit_bytes=54682 * 1024
            ),
        )(slc, pairs, owner)
        interferogram, coherence = pl.pallas_call(
            place_kernel,
            out_shape=(
                jax.ShapeDtypeStruct((2, CAP, 16, 32), F32),
                jax.ShapeDtypeStruct((CAP, 16, 32), F32),
            ),
            in_specs=[vmem, vmem],
            out_specs=(vmem, vmem),
            compiler_params=pltpu.CompilerParams(vmem_limit_bytes=2 * 1024 * 1024),
        )(landed.reshape(GROUP * 24, 128), scaling)
        return jnp.swapaxes(interferogram, 2, 3), jnp.swapaxes(coherence, 1, 2)

    return jax.shard_map(
        local,
        mesh=mesh,
        in_specs=(P(None, "dates", None, "cols"), P(), P()),
        out_specs=(P(None, "dates", None, "cols"), P("dates", None, "cols")),
        check_vma=False,
    )
```

```python
import math

import jax
import jax.numpy as jnp
import ml_dtypes
import numpy as np
from jax import lax
from jax.experimental import pallas as pl
from jax.experimental.pallas import tpu as pltpu
from jax.sharding import PartitionSpec as P

MESH = pl.DeviceIdType.MESH
F32 = jnp.float32
BF16 = jnp.bfloat16

TAPS = [math.exp(-k * k / 8.0) for k in range(-4, 5)]
WEIGHTS = [float(np.float32(t / sum(TAPS))) for t in TAPS]
HIGH = [float(np.float32(w).astype(ml_dtypes.bfloat16)) for w in WEIGHTS]
LOW = [float(np.float32(w - h).astype(ml_dtypes.bfloat16)) for w, h in zip(WEIGHTS, HIGH)]

GROUP = 8
EACH = 4
DATES = GROUP * EACH
PAIRS = 64
CAP = 12
ROWS = 128
PART = 32
TILE = PART + 8
WIDTH = GROUP * PART
PIECES = (24, 16)
HALF = PART // 2
WINDOW = HALF + 8
EDGE = EACH * 2 * 8
CHUNK = 16


def split(x):
    high = x.astype(BF16)
    return high, (x - high.astype(F32)).astype(BF16)


def split3(x):
    high = x.astype(BF16)
    rest = x - high.astype(F32)
    mid = rest.astype(BF16)
    return high, mid, (rest - mid.astype(F32)).astype(BF16)


def dot(a, b):
    return jnp.dot(a, b, preferred_element_type=F32)


def iota(shape, axis):
    return lax.broadcasted_iota(jnp.int32, shape, axis)


def cutter(half):
    start, size = (-4, PIECES[0]) if half == 0 else (PIECES[0] - 4, PIECES[1])
    lane = iota((size, WIDTH), 1)
    row = iota((size, WIDTH), 0)
    pieces = [jnp.where(lane == row + (PART * e + start), 1.0, 0.0) for e in range(GROUP)]
    lane = iota((8, WIDTH), 1)
    row = iota((8, WIDTH), 0)
    pieces.append(jnp.where(lane == row + (WIDTH - 4 if half == 0 else -4), 1.0, 0.0))
    return jnp.concatenate(pieces, axis=0).astype(BF16)


def band(weights):
    gap = jnp.abs(iota((ROWS, ROWS), 0) - iota((ROWS, ROWS), 1))
    result = jnp.zeros((ROWS, ROWS), F32)
    for k in range(5):
        result = jnp.where(gap == k, weights[4 + k], result)
    return result.astype(BF16)


def along_columns(ref, index):
    result = WEIGHTS[4] * ref[index, 4 : 4 + HALF, :]
    for k in range(4):
        both = ref[index, k : k + HALF, :] + ref[index, 8 - k : 8 - k + HALF, :]
        result = result + WEIGHTS[k] * both
    return result


def kernel(
    nz, count, slc_hbm, pairs_hbm, owner_hbm, landed, scaling,
    slc, pairs_s, pairs_v, owner_v, select, own, look, hot, smoother, sent_0, sent_1, got_0, got_1,
    edge_out, edge_left, edge_right, images, roots, fields, lhs, sums, looked,
    power_in, totals, factor_in, results,
    main_send_0, main_recv_0, main_send_1, main_recv_1, edge_send, edge_recv, ready,
    here, up_send, up_recv, down_send, down_recv, d_send, d_recv, out_send, out_recv, in_sem, table_sem,
):
    d = lax.axis_index("dates")
    c = lax.axis_index("cols")
    z = c % nz

    def date_peer(k):
        return {"dates": (d + k) % GROUP, "cols": c}

    right = (c + 1) % count
    left = (c + count - 1) % count
    near = min(2, nz)
    right_later = (z < nz - 1) & (c < count - 1)
    right_earlier = (z == nz - 1) & (c < count - 1)
    left_later = (z == 0) & (c > 0)
    left_earlier = (z > 0) & (c > 0)

    load = pltpu.make_async_copy(slc_hbm, slc, in_sem.at[0])
    load.start()

    barrier = pltpu.get_barrier_semaphore()

    def greet(device):
        pl.semaphore_signal(barrier, inc=1, device_id=device, device_id_type=MESH)

    for k in range(1, GROUP):
        greet(date_peer(k))

    def greet_neighbour(later, receiver, other):
        @pl.when(later)
        def _():
            greet({"dates": receiver, "cols": other})

        @pl.when(later & (d == GROUP - 1 - receiver))
        def _():
            for e in range(GROUP):
                greet({"dates": e, "cols": other})

    greet_neighbour(right_later, 0, right)
    greet_neighbour(left_later, GROUP - 1, left)

    @pl.when(c == 0)
    def _():
        def one(i, carry):
            greet({"dates": d, "cols": i})
            return carry

        lax.fori_loop(1, count, one, 0)

    hands_on = (z == 0) & (c > 0)
    handed = (z >= near) & (c >= nz)

    @pl.when(hands_on)
    def _():
        for i in range(near, nz):
            greet({"dates": d, "cols": c - z + i})

    tables = [
        pltpu.make_async_copy(pairs_hbm, pairs_s, table_sem.at[0]),
        pltpu.make_async_copy(pairs_hbm, pairs_v, table_sem.at[1]),
        pltpu.make_async_copy(owner_hbm, owner_v, table_sem.at[2]),
    ]
    for table in tables:
        table.start()

    sent = (sent_0, sent_1)
    edge_in = (edge_left, edge_right)
    got = (got_0, got_1)

    def cut(half, matrix):
        size = PIECES[half]
        for t in range(EACH):
            both = jnp.concatenate([slc[0, t], slc[1, t]], axis=0)
            turned = lax.dot_general(
                matrix, both, (((1,), (1,)), ((), ())), preferred_element_type=F32
            )
            for e in range(GROUP + 1):
                rows = turned[size * e : size * (e + 1)] if e < GROUP else turned[size * GROUP :]
                value = jnp.concatenate([rows[:, :ROWS], rows[:, ROWS:]], axis=0).astype(BF16)
                if e < GROUP:
                    sent[half][e, 2 * size * t : 2 * size * (t + 1), :] = value
                else:
                    edge_out[half, 16 * t : 16 * (t + 1), :] = value

    matrix = cutter(0)
    high = band(HIGH)
    low = band(LOW)
    smoother[:, :ROWS] = jnp.concatenate([high, high], axis=0)
    smoother[:, ROWS:] = jnp.concatenate([low, low], axis=0)
    load.wait()
    power_rows = []
    for t in range(EACH):
        wide = jnp.concatenate([slc[0, t], slc[1, t]], axis=0).astype(F32)
        square = jnp.sum(wide * wide, axis=0, keepdims=True)
        power_rows.append(square[:, :ROWS] + square[:, ROWS:])
    power_in[0] = jnp.concatenate(power_rows + [jnp.zeros((8 - EACH, ROWS), F32)], axis=0)
    cut(0, matrix)

    first = (d == 0).astype(jnp.int32)
    last = (d == GROUP - 1).astype(jnp.int32)
    pl.semaphore_wait(
        barrier,
        (GROUP - 1)
        + (c > 0).astype(jnp.int32)
        + handed.astype(jnp.int32)
        + right_earlier.astype(jnp.int32) * (1 + GROUP * last)
        + left_earlier.astype(jnp.int32) * (1 + GROUP * first),
    )

    def tell_ready(side, condition, other):
        @pl.when(condition)
        def _():
            for e in range(GROUP):
                pl.semaphore_signal(
                    ready.at[side], inc=1, device_id={"dates": e, "cols": other}, device_id_type=MESH
                )

    @pl.when(handed)
    def _():
        pl.semaphore_signal(
            here, inc=1, device_id={"dates": d, "cols": c - z}, device_id_type=MESH
        )

    tell_ready(0, left_earlier & (d == 0), left)
    tell_ready(1, right_earlier & (d == GROUP - 1), right)

    def stage(src, dst, send, recv, peer):
        return pltpu.make_async_remote_copy(
            src_ref=src, dst_ref=dst, send_sem=send, recv_sem=recv, device_id=peer, device_id_type=MESH
        )

    def up_copy(i, size=1):
        return stage(
            power_in.at[pl.ds(0, size)], power_in.at[pl.ds(i, size)], up_send.at[0], up_recv.at[0],
            {"dates": d, "cols": 0},
        )

    def down_copy(i):
        return stage(factor_in, factor_in, down_send.at[0], down_recv.at[0], {"dates": d, "cols": i})

    @pl.when(c > 0)
    def _():
        up_copy(c).start()

    targets = ({"dates": 0, "cols": right}, {"dates": GROUP - 1, "cols": left})

    def edge_copy(side):
        return pltpu.make_async_remote_copy(
            src_ref=edge_out.at[side], dst_ref=edge_in[side].at[d], send_sem=edge_send.at[side],
            recv_sem=edge_recv.at[0], device_id=targets[side], device_id_type=MESH,
        )

    order = (4, 3, 5, 2, 6, 1, 7)
    slots = {4: 0, 3: 1, 5: 2}

    def first_copy(k, size=1):
        return stage(
            sent_0.at[pl.ds((d + k) % GROUP if size == 1 else 0, size)],
            got_0.at[pl.ds(d if size == 1 else 0, size)],
            main_send_0.at[0], main_recv_0.at[slots.get(k, 3)], date_peer(k),
        )

    def second_copy(k, size=1):
        return stage(
            sent_1.at[pl.ds((d + k) % GROUP if size == 1 else 0, size)],
            got_1.at[pl.ds(d if size == 1 else 0, size)],
            main_send_1.at[0], main_recv_1.at[0], date_peer(k),
        )

    for k in order:
        first_copy(k).start()

    @pl.when(right_earlier)
    def _():
        edge_copy(0).start()

    cut(1, cutter(1))
    for k in order:
        second_copy(k).start()

    @pl.when(left_earlier)
    def _():
        edge_copy(1).start()

    got_1[d] = sent_1[d]

    @pl.when((d != 0) | (c == 0))
    def _():
        edge_left[...] = jnp.zeros_like(edge_left)

    @pl.when((d != GROUP - 1) | (c == count - 1))
    def _():
        edge_right[...] = jnp.zeros_like(edge_right)


    for table in tables:
        table.wait()
    owner_row = owner_v[...]
    owner_down = jnp.transpose(jnp.broadcast_to(owner_row.astype(F32), (ROWS, PAIRS)))[:, :PAIRS]
    earlier = iota((PAIRS, PAIRS), 0) < iota((PAIRS, PAIRS), 1)
    same = owner_down == owner_row.astype(F32)
    rank = jnp.sum(jnp.where(same & earlier, 1.0, 0.0), axis=0, keepdims=True).astype(jnp.int32)
    place = (rank & 3) * 32 + owner_row * 4 + (rank >> 2)
    one = jnp.where(iota((128, PAIRS), 0) == place, 1.0, 0.0)
    select[...] = jnp.concatenate([one, one, one], axis=1).astype(BF16)
    later = iota((PAIRS, PAIRS), 0) > iota((PAIRS, PAIRS), 1)
    rank_down = jnp.sum(jnp.where(same & later, 1.0, 0.0), axis=1, keepdims=True)
    quarter = (iota((PAIRS, 128), 1) >> 5).astype(F32)
    mine = jnp.where(owner_down[:, :1] == d.astype(F32), rank_down, -1.0)
    for g in range(3):
        own[g] = jnp.where(mine == quarter + 4.0 * g, 1.0, 0.0)

    def date_rows(which):
        date = pairs_v[which : which + 1, :]
        row = ((date >> 2) * 8 + (date & 3)).astype(F32)
        down = jnp.transpose(jnp.broadcast_to(row, (ROWS, PAIRS)))[:, : 8 * GROUP]
        lane = iota((PAIRS, 8 * GROUP), 1).astype(F32)
        one = jnp.where(down == lane, 1.0, 0.0)
        return jnp.concatenate([one, one, one], axis=1).astype(BF16)

    hot[...] = jnp.concatenate([date_rows(0), date_rows(1)], axis=0)
    one = jnp.where((iota((ROWS, 128), 0) >> 2) == (iota((ROWS, 128), 1) & 31), 1.0, 0.0)
    look[...] = jnp.concatenate([one, one, one], axis=0).astype(BF16)

    def edges(side):
        stage(
            edge_in[side], edge_in[side], edge_send.at[side], edge_recv.at[0], targets[side]
        ).wait_recv()

    def smooth_powers(number):
        for t in range(number):
            big, small = split(along_columns(fields, t))
            lhs[HALF * t : HALF * (t + 1), :ROWS] = big
            lhs[HALF * t : HALF * (t + 1), ROWS:] = small
        smooth = dot(lhs[: number * HALF, :], smoother[...])
        return jnp.sqrt(smooth[:, :ROWS] + smooth[:, ROWS:])

    def take_first(sources, ref):
        size = PIECES[0]
        for i, source in enumerate(sources):
            for t in range(EACH):
                piece = ref[source, 2 * size * t : 2 * size * (t + 1), :].astype(F32)
                edge = edge_left[source, 16 * t : 16 * (t + 1), :].astype(F32)
                real = jnp.concatenate([piece[:8] + edge[:8], piece[8:size]], axis=0)
                imag = jnp.concatenate([piece[size : size + 8] + edge[8:], piece[size + 8 :]], axis=0)
                images[source * EACH + t, 0, :size] = real
                images[source * EACH + t, 1, :size] = imag
                fields[EACH * i + t] = real * real + imag * imag
        smooth = smooth_powers(EACH * len(sources))
        for i, source in enumerate(sources):
            for t in range(EACH):
                at = HALF * (EACH * i + t)
                roots[source * EACH + t, :HALF] = smooth[at : at + HALF]

    def arrive(*ks):
        first_copy(ks[0], len(ks)).wait_recv()
        take_first([(d + GROUP - k) % GROUP for k in ks], got_0)

    def take_second():
        size = PIECES[1]
        for date in range(DATES):
            source, t = date // EACH, date % EACH
            piece = got_1[source, 2 * size * t : 2 * size * (t + 1), :].astype(F32)
            edge = edge_right[source, 16 * t : 16 * (t + 1), :].astype(F32)
            real = jnp.concatenate([piece[:8], piece[8:size] + edge[:8]], axis=0)
            imag = jnp.concatenate([piece[size : size + 8], piece[size + 8 :] + edge[8:]], axis=0)
            images[date, 0, PIECES[0] :] = real
            images[date, 1, PIECES[0] :] = imag
            real = jnp.concatenate([images[date, 0, HALF : PIECES[0]], real], axis=0)
            imag = jnp.concatenate([images[date, 1, HALF : PIECES[0]], imag], axis=0)
            fields[date] = real * real + imag * imag
        smooth = smooth_powers(DATES)
        for date in range(DATES):
            roots[date, HALF:] = smooth[HALF * date : HALF * (date + 1)]

    def pairs_of(half):
        window = slice(HALF * half, HALF * half + WINDOW)

        def place(field, p):
            return pl.ds(((3 * half + field) * PAIRS + p) * 8, 8)

        def chunk(index, carry):
            dates = []
            for i in range(CHUNK):
                p = index * CHUNK + i
                first = pairs_s[0, p]
                second = pairs_s[1, p]
                dates.append((first, second))
                real_a = images[first, 0, window]
                imag_a = images[first, 1, window]
                real_b = images[second, 0, window]
                imag_b = images[second, 1, window]
                fields[2 * i] = real_a * real_b + imag_a * imag_b
                fields[2 * i + 1] = imag_a * real_b - real_a * imag_b
            for i in range(CHUNK):
                p = index * CHUNK + i
                for f in range(2):
                    n = 2 * i + f
                    big, small = split(along_columns(fields, n))
                    lhs[HALF * n : HALF * (n + 1), :ROWS] = big
                    lhs[HALF * n : HALF * (n + 1), ROWS:] = small
                    sums[place(f, p), :] = fields[n, 4:12, :] + fields[n, 12:20, :]
            smooth = dot(lhs[...], smoother[...])
            smooth = smooth[:, :ROWS] + smooth[:, ROWS:]
            for i in range(CHUNK):
                p = index * CHUNK + i
                first, second = dates[i]
                real = smooth[2 * HALF * i : 2 * HALF * i + HALF]
                imag = smooth[2 * HALF * i + HALF : 2 * HALF * (i + 1)]
                below = (
                    roots[first, HALF * half : HALF * (half + 1)]
                    * roots[second, HALF * half : HALF * (half + 1)]
                )
                value = jnp.sqrt(real * real + imag * imag) / (below + 1e-06)
                sums[place(2, p), :] = value[0:8] + value[8:16]
            return carry

        lax.fori_loop(0, PAIRS // CHUNK, chunk, 0)
        rows = sums[pl.ds(3 * half * PAIRS * 8, 3 * PAIRS, stride=8), :]
        for i in range(1, 8):
            rows = rows + sums[pl.ds(3 * half * PAIRS * 8 + i, 3 * PAIRS, stride=8), :]
        looked[half] = dot(jnp.concatenate(split3(rows), axis=1), look[...])

    @pl.when(right_later)
    def _():
        pl.semaphore_wait(ready.at[0], 1)
        edge_copy(0).start()

    @pl.when(left_later)
    def _():
        pl.semaphore_wait(ready.at[1], 1)
        edge_copy(1).start()

    @pl.when((d == 0) & (c > 0))
    def _():
        edges(0)

    take_first([d], sent_0)
    arrive(4)
    arrive(3)
    arrive(5)
    arrive(2, 6, 1, 7)
    pairs_of(0)

    def d_copy(k, size=1):
        return stage(
            totals.at[pl.ds(d if size == 1 else 0, size)], totals.at[pl.ds(d if size == 1 else 0, size)],
            d_send.at[0], d_recv.at[0], date_peer(k),
        )

    @pl.when(c == 0)
    def _():
        up_copy(1, count - 1).wait_recv()
        totals[d] = jnp.sum(power_in[...], axis=0)
        for k in order:
            d_copy(k).start()

    @pl.when((d == GROUP - 1) & (c < count - 1))
    def _():
        edges(1)

    second_copy(1, GROUP - 1).wait_recv()
    take_second()
    pairs_of(1)

    wide = []
    for q in range(6):
        piece = looked[q // 3, PAIRS * (q % 3) : PAIRS * (q % 3 + 1)]
        wide.append(piece if q % 3 < 2 else piece * (1.0 / 64.0))
    stacked = jnp.concatenate(split3(jnp.concatenate(wide, axis=1)), axis=0)
    placed = dot(select[...], stacked)
    lane = iota((32, 128), 1)
    for q in range(6):
        part = placed[:, 128 * q : 128 * (q + 1)]
        value = jnp.where(
            lane < 64,
            jnp.where(lane < 32, part[0:32], part[32:64]),
            jnp.where(lane < 96, part[64:96], part[96:128]),
        )
        for e in range(GROUP):
            results[e, 4 * q : 4 * q + 4, :] = value[4 * e : 4 * e + 4]

    def out_copy(k, size=1):
        return stage(
            results.at[pl.ds((d + k) % GROUP if size == 1 else 0, size)],
            landed.at[pl.ds(d if size == 1 else 0, size)],
            out_send.at[0], out_recv.at[0], date_peer(k),
        )

    for k in order:
        out_copy(k).start()
    landed[d] = results[d]

    @pl.when(c == 0)
    def _():
        d_copy(1, GROUP - 1).wait_recv()
        parts = jnp.concatenate(split3(totals[...].reshape(8 * GROUP, ROWS)), axis=0)
        total = jnp.sum(dot(hot[...], parts), axis=1, keepdims=True)
        scale = jnp.sqrt(total / (ROWS * WIDTH * count) + 1e-06)
        factor = (1.0 / 64.0) / (scale[:PAIRS] * scale[PAIRS:])
        factor = jnp.broadcast_to(jnp.concatenate([factor, factor], axis=0), (ROWS, ROWS))
        factor = jnp.transpose(factor)[:8]
        factor_in[...] = factor
        for i in range(near):
            for j in range(count // nz):
                if i + j > 0:
                    down_copy(j * nz + i).start()
        for i in range(near, nz):
            down_copy(i).start()

    @pl.when(c > 0)
    def _():
        down_copy(0).wait_recv()

    @pl.when(hands_on)
    def _():
        if nz > near:
            pl.semaphore_wait(here, nz - near)
        for i in range(near, nz):
            down_copy(c - z + i).start()

    factor = jnp.transpose(jnp.broadcast_to(factor_in[0:1, :PAIRS], (ROWS, PAIRS)))
    factors = [jnp.sum(own[g] * factor, axis=0, keepdims=True) for g in range(3)]
    out_copy(1, GROUP - 1).wait_recv()
    scaling[...] = jnp.concatenate(factors + [jnp.zeros((5, 128), F32)], axis=0)
    first_copy(1, GROUP - 1).wait_send()
    second_copy(1, GROUP - 1).wait_send()
    out_copy(1, GROUP - 1).wait_send()

    @pl.when(right_later | right_earlier)
    def _():
        edge_copy(0).wait_send()

    @pl.when(left_later | left_earlier)
    def _():
        edge_copy(1).wait_send()

    def sent_down(number):
        stage(
            power_in.at[pl.ds(0, number)], power_in.at[pl.ds(0, number)], down_send.at[0],
            down_recv.at[0], {"dates": d, "cols": c},
        ).wait_send()

    @pl.when(c > 0)
    def _():
        up_copy(c).wait_send()

    @pl.when(c == 0)
    def _():
        d_copy(1, GROUP - 1).wait_send()
        sent_down(near * (count // nz) - 1 + nz - near)

    if nz > near:

        @pl.when(hands_on)
        def _():
            sent_down(nz - near)


def place_kernel(landed, scaling, interferogram, coherence):
    for f in range(3):
        for g in range(3):
            block = landed[pl.ds(f * 4 + g, 16, stride=12), :]
            if f < 2:
                block = block * scaling[g : g + 1, :]
            for j in range(4):
                piece = block[:, 32 * j : 32 * j + 32]
                if f < 2:
                    interferogram[f, 4 * g + j] = piece
                else:
                    coherence[4 * g + j] = piece


def solution(mesh):
    columns = mesh.shape["cols"]
    nz = 8 if columns % 8 == 0 else 2
    sem = pltpu.SemaphoreType.DMA
    vmem = pl.BlockSpec(memory_space=pltpu.VMEM)

    def local(slc, pairs, owner):
        pairs = pairs.T
        owner = owner.reshape(1, PAIRS)
        landed, scaling = pl.pallas_call(
            lambda *refs: kernel(nz, columns, *refs),
            out_shape=(jax.ShapeDtypeStruct((GROUP, 24, 128), F32), jax.ShapeDtypeStruct((8, 128), F32)),
            in_specs=[pl.BlockSpec(memory_space=pl.ANY)] * 3,
            out_specs=(vmem, vmem),
            scratch_shapes=[
                pltpu.VMEM((2, EACH, ROWS, WIDTH), BF16),
                pltpu.SMEM((2, PAIRS), jnp.int32),
                pltpu.VMEM((2, PAIRS), jnp.int32),
                pltpu.VMEM((1, PAIRS), jnp.int32),
                pltpu.VMEM((128, 3 * PAIRS), BF16),
                pltpu.VMEM((3, PAIRS, 128), F32),
                pltpu.VMEM((3 * ROWS, 128), BF16),
                pltpu.VMEM((2 * PAIRS, 24 * GROUP), BF16),
                pltpu.VMEM((2 * ROWS, 2 * ROWS), BF16),
                pltpu.VMEM((GROUP, EACH * 2 * PIECES[0], ROWS), BF16),
                pltpu.VMEM((GROUP, EACH * 2 * PIECES[1], ROWS), BF16),
                pltpu.VMEM((GROUP, EACH * 2 * PIECES[0], ROWS), BF16),
                pltpu.VMEM((GROUP, EACH * 2 * PIECES[1], ROWS), BF16),
                pltpu.VMEM((2, EDGE, ROWS), BF16),
                pltpu.VMEM((GROUP, EDGE, ROWS), BF16),
                pltpu.VMEM((GROUP, EDGE, ROWS), BF16),
                pltpu.VMEM((DATES, 2, TILE, ROWS), F32),
                pltpu.VMEM((DATES, PART, ROWS), F32),
                pltpu.VMEM((2 * CHUNK, WINDOW, ROWS), F32),
                pltpu.VMEM((2 * CHUNK * HALF, 2 * ROWS), BF16),
                pltpu.VMEM((6 * PAIRS * 8, ROWS), F32),
                pltpu.VMEM((2, 3 * PAIRS, ROWS), F32),
                pltpu.VMEM((columns, 8, ROWS), F32),
                pltpu.VMEM((GROUP, 8, ROWS), F32),
                pltpu.VMEM((8, ROWS), F32),
                pltpu.VMEM((GROUP, 24, 128), F32),
                sem((1,)), sem((4,)), sem((1,)), sem((1,)),
                sem((2,)), sem((1,)), pltpu.SemaphoreType.REGULAR((2,)), pltpu.SemaphoreType.REGULAR,
                sem((1,)), sem((1,)), sem((1,)), sem((1,)),
                sem((1,)), sem((1,)), sem((1,)), sem((1,)),
                sem((1,)), sem((3,)),
            ],
            compiler_params=pltpu.CompilerParams(
                collective_id=0, has_side_effects=True, vmem_limit_bytes=54682 * 1024
            ),
        )(slc, pairs, owner)
        interferogram, coherence = pl.pallas_call(
            place_kernel,
            out_shape=(
                jax.ShapeDtypeStruct((2, CAP, 16, 32), F32),
                jax.ShapeDtypeStruct((CAP, 16, 32), F32),
            ),
            in_specs=[vmem, vmem],
            out_specs=(vmem, vmem),
            compiler_params=pltpu.CompilerParams(vmem_limit_bytes=2 * 1024 * 1024),
        )(landed.reshape(GROUP * 24, 128), scaling)
        return jnp.swapaxes(interferogram, 2, 3), jnp.swapaxes(coherence, 1, 2)

    return jax.shard_map(
        local,
        mesh=mesh,
        in_specs=(P(None, "dates", None, "cols"), P(), P()),
        out_specs=(P(None, "dates", None, "cols"), P("dates", None, "cols")),
        check_vma=False,
    )
```

```python
import math

import jax
import jax.numpy as jnp
import ml_dtypes
import numpy as np
from jax import lax
from jax.experimental import pallas as pl
from jax.experimental.pallas import tpu as pltpu
from jax.sharding import PartitionSpec as P

MESH = pl.DeviceIdType.MESH
F32 = jnp.float32
BF16 = jnp.bfloat16

TAPS = [math.exp(-k * k / 8.0) for k in range(-4, 5)]
WEIGHTS = [float(np.float32(t / sum(TAPS))) for t in TAPS]
HIGH = [float(np.float32(w).astype(ml_dtypes.bfloat16)) for w in WEIGHTS]
LOW = [float(np.float32(w - h).astype(ml_dtypes.bfloat16)) for w, h in zip(WEIGHTS, HIGH)]

GROUP = 8
EACH = 4
DATES = GROUP * EACH
PAIRS = 64
CAP = 12
ROWS = 128
PART = 32
TILE = PART + 8
WIDTH = GROUP * PART
PIECES = (24, 16)
HALF = PART // 2
WINDOW = HALF + 8
EDGE = EACH * 2 * 8
CHUNK = 16


def split(x):
    high = x.astype(BF16)
    return high, (x - high.astype(F32)).astype(BF16)


def split3(x):
    high = x.astype(BF16)
    rest = x - high.astype(F32)
    mid = rest.astype(BF16)
    return high, mid, (rest - mid.astype(F32)).astype(BF16)


def dot(a, b):
    return jnp.dot(a, b, preferred_element_type=F32)


def iota(shape, axis):
    return lax.broadcasted_iota(jnp.int32, shape, axis)


def cutter(half):
    start, size = (-4, PIECES[0]) if half == 0 else (PIECES[0] - 4, PIECES[1])
    lane = iota((size, WIDTH), 1)
    row = iota((size, WIDTH), 0)
    pieces = [jnp.where(lane == row + (PART * e + start), 1.0, 0.0) for e in range(GROUP)]
    lane = iota((8, WIDTH), 1)
    row = iota((8, WIDTH), 0)
    pieces.append(jnp.where(lane == row + (WIDTH - 4 if half == 0 else -4), 1.0, 0.0))
    return jnp.concatenate(pieces, axis=0).astype(BF16)


def band(weights):
    gap = jnp.abs(iota((ROWS, ROWS), 0) - iota((ROWS, ROWS), 1))
    result = jnp.zeros((ROWS, ROWS), F32)
    for k in range(5):
        result = jnp.where(gap == k, weights[4 + k], result)
    return result.astype(BF16)


def along_columns(ref, index):
    result = WEIGHTS[4] * ref[index, 4 : 4 + HALF, :]
    for k in range(4):
        both = ref[index, k : k + HALF, :] + ref[index, 8 - k : 8 - k + HALF, :]
        result = result + WEIGHTS[k] * both
    return result


def kernel(
    nz, count, slc_hbm, pairs_hbm, owner_hbm, landed, scaling,
    slc, pairs_s, pairs_v, owner_v, select, own, look, hot, quarters, smoother, sent_0, sent_1, got_0, got_1,
    edge_out, edge_left, edge_right, images, roots, fields, lhs, sums, looked,
    power_row, power_in, factor_in, results,
    main_send_0, main_recv_0, main_send_1, main_recv_1, edge_send, edge_recv, ready,
    here, up_send, up_recv, down_send, down_recv, out_send, out_recv, in_sem, table_sem,
):
    d = lax.axis_index("dates")
    c = lax.axis_index("cols")
    z = c % nz

    def date_peer(k):
        return {"dates": (d + k) % GROUP, "cols": c}

    right = (c + 1) % count
    left = (c + count - 1) % count
    near = min(2, nz)
    right_later = (z < nz - 1) & (c < count - 1)
    right_earlier = (z == nz - 1) & (c < count - 1)
    left_later = (z == 0) & (c > 0)
    left_earlier = (z > 0) & (c > 0)

    load = pltpu.make_async_copy(slc_hbm, slc, in_sem.at[0])
    load.start()

    barrier = pltpu.get_barrier_semaphore()

    def greet(device):
        pl.semaphore_signal(barrier, inc=1, device_id=device, device_id_type=MESH)

    for k in range(1, GROUP):
        greet(date_peer(k))

    def greet_neighbour(later, receiver, other):
        @pl.when(later)
        def _():
            greet({"dates": receiver, "cols": other})

        @pl.when(later & (d == GROUP - 1 - receiver))
        def _():
            for e in range(GROUP):
                greet({"dates": e, "cols": other})

    greet_neighbour(right_later, 0, right)
    greet_neighbour(left_later, GROUP - 1, left)

    hands_on = (z == 0) & (c > 0)
    handed = (z >= near) & (c >= nz)

    @pl.when(hands_on)
    def _():
        for i in range(near, nz):
            greet({"dates": d, "cols": c - z + i})

    tables = [
        pltpu.make_async_copy(pairs_hbm, pairs_s, table_sem.at[0]),
        pltpu.make_async_copy(pairs_hbm, pairs_v, table_sem.at[1]),
        pltpu.make_async_copy(owner_hbm, owner_v, table_sem.at[2]),
    ]
    for table in tables:
        table.start()

    sent = (sent_0, sent_1)
    edge_in = (edge_left, edge_right)
    got = (got_0, got_1)

    def cut(half, matrix):
        size = PIECES[half]
        for t in range(EACH):
            both = jnp.concatenate([slc[0, t], slc[1, t]], axis=0)
            turned = lax.dot_general(
                matrix, both, (((1,), (1,)), ((), ())), preferred_element_type=F32
            )
            for e in range(GROUP + 1):
                rows = turned[size * e : size * (e + 1)] if e < GROUP else turned[size * GROUP :]
                value = jnp.concatenate([rows[:, :ROWS], rows[:, ROWS:]], axis=0).astype(BF16)
                if e < GROUP:
                    sent[half][e, 2 * size * t : 2 * size * (t + 1), :] = value
                else:
                    edge_out[half, 16 * t : 16 * (t + 1), :] = value

    matrix = cutter(0)
    high = band(HIGH)
    low = band(LOW)
    smoother[:, :ROWS] = jnp.concatenate([high, high], axis=0)
    smoother[:, ROWS:] = jnp.concatenate([low, low], axis=0)
    load.wait()
    power_rows = []
    for t in range(EACH):
        wide = jnp.concatenate([slc[0, t], slc[1, t]], axis=0).astype(F32)
        square = jnp.sum(wide * wide, axis=0, keepdims=True)
        power_rows.append(square[:, :ROWS] + square[:, ROWS:])
    folded = jnp.concatenate(power_rows + [jnp.zeros((8 - EACH, ROWS), F32)], axis=0)
    folded = folded + pltpu.roll(folded, 64, 1)
    folded = folded + pltpu.roll(folded, 32, 1)
    own_lane = (iota((8, ROWS), 1) >> 5) == iota((8, ROWS), 0)
    power_row[...] = jnp.sum(jnp.where(own_lane, folded, 0.0), axis=0, keepdims=True)
    cut(0, matrix)

    first = (d == 0).astype(jnp.int32)
    last = (d == GROUP - 1).astype(jnp.int32)
    pl.semaphore_wait(
        barrier,
        (GROUP - 1)
        + (c > 0).astype(jnp.int32)
        + handed.astype(jnp.int32)
        + right_earlier.astype(jnp.int32) * (1 + GROUP * last)
        + left_earlier.astype(jnp.int32) * (1 + GROUP * first),
    )

    def tell_ready(side, condition, other):
        @pl.when(condition)
        def _():
            for e in range(GROUP):
                pl.semaphore_signal(
                    ready.at[side], inc=1, device_id={"dates": e, "cols": other}, device_id_type=MESH
                )

    @pl.when(c == 0)
    def _():
        def one(i, carry):
            greet({"dates": d, "cols": i})
            return carry

        lax.fori_loop(1, count, one, 0)

    @pl.when(handed)
    def _():
        pl.semaphore_signal(
            here, inc=1, device_id={"dates": d, "cols": c - z}, device_id_type=MESH
        )

    tell_ready(0, left_earlier & (d == 0), left)
    tell_ready(1, right_earlier & (d == GROUP - 1), right)

    def stage(src, dst, send, recv, peer):
        return pltpu.make_async_remote_copy(
            src_ref=src, dst_ref=dst, send_sem=send, recv_sem=recv, device_id=peer, device_id_type=MESH
        )

    def up_copy(e, size=1):
        return stage(
            power_in.at[pl.ds(0, size)] if size > 1 else power_row,
            power_in.at[pl.ds(0 if size > 1 else d * count + c, size)],
            up_send.at[0], up_recv.at[0], {"dates": e, "cols": 0},
        )

    def down_copy(i):
        return stage(factor_in, factor_in, down_send.at[0], down_recv.at[0], {"dates": d, "cols": i})

    for k in range(1, GROUP):
        up_copy((d + k) % GROUP).start()

    @pl.when(c > 0)
    def _():
        up_copy(d).start()

    @pl.when(c == 0)
    def _():
        power_in[pl.ds(d * count, 1), :] = power_row[...]

    targets = ({"dates": 0, "cols": right}, {"dates": GROUP - 1, "cols": left})

    def edge_copy(side):
        return pltpu.make_async_remote_copy(
            src_ref=edge_out.at[side], dst_ref=edge_in[side].at[d], send_sem=edge_send.at[side],
            recv_sem=edge_recv.at[0], device_id=targets[side], device_id_type=MESH,
        )

    order = (4, 3, 5, 2, 6, 1, 7)
    slots = {4: 0, 3: 1, 5: 2}

    def first_copy(k, size=1):
        return stage(
            sent_0.at[pl.ds((d + k) % GROUP if size == 1 else 0, size)],
            got_0.at[pl.ds(d if size == 1 else 0, size)],
            main_send_0.at[0], main_recv_0.at[slots.get(k, 3)], date_peer(k),
        )

    def second_copy(k, size=1):
        return stage(
            sent_1.at[pl.ds((d + k) % GROUP if size == 1 else 0, size)],
            got_1.at[pl.ds(d if size == 1 else 0, size)],
            main_send_1.at[0], main_recv_1.at[0], date_peer(k),
        )

    for k in order:
        first_copy(k).start()

    @pl.when(right_earlier)
    def _():
        edge_copy(0).start()

    cut(1, cutter(1))
    for k in order:
        second_copy(k).start()

    @pl.when(left_earlier)
    def _():
        edge_copy(1).start()

    got_1[d] = sent_1[d]

    @pl.when((d != 0) | (c == 0))
    def _():
        edge_left[...] = jnp.zeros_like(edge_left)

    @pl.when((d != GROUP - 1) | (c == count - 1))
    def _():
        edge_right[...] = jnp.zeros_like(edge_right)


    for table in tables:
        table.wait()
    owner_row = owner_v[...]
    owner_down = jnp.transpose(jnp.broadcast_to(owner_row.astype(F32), (ROWS, PAIRS)))[:, :PAIRS]
    earlier = iota((PAIRS, PAIRS), 0) < iota((PAIRS, PAIRS), 1)
    same = owner_down == owner_row.astype(F32)
    rank = jnp.sum(jnp.where(same & earlier, 1.0, 0.0), axis=0, keepdims=True).astype(jnp.int32)
    place = (rank & 3) * 32 + owner_row * 4 + (rank >> 2)
    one = jnp.where(iota((128, PAIRS), 0) == place, 1.0, 0.0)
    select[...] = jnp.concatenate([one, one, one], axis=1).astype(BF16)
    later = iota((PAIRS, PAIRS), 0) > iota((PAIRS, PAIRS), 1)
    rank_down = jnp.sum(jnp.where(same & later, 1.0, 0.0), axis=1, keepdims=True)
    quarter = (iota((PAIRS, 128), 1) >> 5).astype(F32)
    mine = jnp.where(owner_down[:, :1] == d.astype(F32), rank_down, -1.0)
    for g in range(3):
        own[g] = jnp.where(mine == quarter + 4.0 * g, 1.0, 0.0)

    def date_rows(which):
        date = pairs_v[which : which + 1, :].astype(F32)
        return jnp.transpose(jnp.broadcast_to(date, (ROWS, PAIRS)))

    date = jnp.concatenate([date_rows(0), date_rows(1)], axis=0)
    lane = iota((2 * PAIRS, ROWS), 1)
    first_date = (EACH * (lane & 7)).astype(F32)
    one = jnp.where((date >= first_date) & (date < first_date + EACH) & (lane < 24), 1.0, 0.0)
    hot[...] = one[:, : 3 * GROUP].astype(BF16)
    phase = date - EACH * jnp.floor(date * (1.0 / EACH))
    quarters[...] = jnp.where(phase == (lane >> 5).astype(F32), 1.0, 0.0)
    one = jnp.where((iota((ROWS, 128), 0) >> 2) == (iota((ROWS, 128), 1) & 31), 1.0, 0.0)
    look[...] = jnp.concatenate([one, one, one], axis=0).astype(BF16)

    def edges(side):
        stage(
            edge_in[side], edge_in[side], edge_send.at[side], edge_recv.at[0], targets[side]
        ).wait_recv()

    def smooth_powers(number):
        for t in range(number):
            big, small = split(along_columns(fields, t))
            lhs[HALF * t : HALF * (t + 1), :ROWS] = big
            lhs[HALF * t : HALF * (t + 1), ROWS:] = small
        smooth = dot(lhs[: number * HALF, :], smoother[...])
        return jnp.sqrt(smooth[:, :ROWS] + smooth[:, ROWS:])

    def take_first(sources, ref):
        size = PIECES[0]
        for i, source in enumerate(sources):
            for t in range(EACH):
                piece = ref[source, 2 * size * t : 2 * size * (t + 1), :].astype(F32)
                edge = edge_left[source, 16 * t : 16 * (t + 1), :].astype(F32)
                real = jnp.concatenate([piece[:8] + edge[:8], piece[8:size]], axis=0)
                imag = jnp.concatenate([piece[size : size + 8] + edge[8:], piece[size + 8 :]], axis=0)
                images[source * EACH + t, 0, :size] = real
                images[source * EACH + t, 1, :size] = imag
                fields[EACH * i + t] = real * real + imag * imag
        smooth = smooth_powers(EACH * len(sources))
        for i, source in enumerate(sources):
            for t in range(EACH):
                at = HALF * (EACH * i + t)
                roots[source * EACH + t, :HALF] = smooth[at : at + HALF]

    def arrive(*ks):
        first_copy(ks[0], len(ks)).wait_recv()
        take_first([(d + GROUP - k) % GROUP for k in ks], got_0)

    def take_second():
        size = PIECES[1]
        for date in range(DATES):
            source, t = date // EACH, date % EACH
            piece = got_1[source, 2 * size * t : 2 * size * (t + 1), :].astype(F32)
            edge = edge_right[source, 16 * t : 16 * (t + 1), :].astype(F32)
            real = jnp.concatenate([piece[:8], piece[8:size] + edge[:8]], axis=0)
            imag = jnp.concatenate([piece[size : size + 8], piece[size + 8 :] + edge[8:]], axis=0)
            images[date, 0, PIECES[0] :] = real
            images[date, 1, PIECES[0] :] = imag
            real = jnp.concatenate([images[date, 0, HALF : PIECES[0]], real], axis=0)
            imag = jnp.concatenate([images[date, 1, HALF : PIECES[0]], imag], axis=0)
            fields[date] = real * real + imag * imag
        smooth = smooth_powers(DATES)
        for date in range(DATES):
            roots[date, HALF:] = smooth[HALF * date : HALF * (date + 1)]

    def pairs_of(half):
        window = slice(HALF * half, HALF * half + WINDOW)

        def place(field, p):
            return pl.ds(((3 * half + field) * PAIRS + p) * 8, 8)

        def chunk(index, carry):
            dates = []
            for i in range(CHUNK):
                p = index * CHUNK + i
                first = pairs_s[0, p]
                second = pairs_s[1, p]
                dates.append((first, second))
                real_a = images[first, 0, window]
                imag_a = images[first, 1, window]
                real_b = images[second, 0, window]
                imag_b = images[second, 1, window]
                fields[2 * i] = real_a * real_b + imag_a * imag_b
                fields[2 * i + 1] = imag_a * real_b - real_a * imag_b
            for i in range(CHUNK):
                p = index * CHUNK + i
                for f in range(2):
                    n = 2 * i + f
                    big, small = split(along_columns(fields, n))
                    lhs[HALF * n : HALF * (n + 1), :ROWS] = big
                    lhs[HALF * n : HALF * (n + 1), ROWS:] = small
                    sums[place(f, p), :] = fields[n, 4:12, :] + fields[n, 12:20, :]
            smooth = dot(lhs[...], smoother[...])
            smooth = smooth[:, :ROWS] + smooth[:, ROWS:]
            for i in range(CHUNK):
                p = index * CHUNK + i
                first, second = dates[i]
                real = smooth[2 * HALF * i : 2 * HALF * i + HALF]
                imag = smooth[2 * HALF * i + HALF : 2 * HALF * (i + 1)]
                below = (
                    roots[first, HALF * half : HALF * (half + 1)]
                    * roots[second, HALF * half : HALF * (half + 1)]
                )
                value = jnp.sqrt(real * real + imag * imag) / (below + 1e-06)
                sums[place(2, p), :] = value[0:8] + value[8:16]
            return carry

        lax.fori_loop(0, PAIRS // CHUNK, chunk, 0)
        rows = sums[pl.ds(3 * half * PAIRS * 8, 3 * PAIRS, stride=8), :]
        for i in range(1, 8):
            rows = rows + sums[pl.ds(3 * half * PAIRS * 8 + i, 3 * PAIRS, stride=8), :]
        looked[half] = dot(jnp.concatenate(split3(rows), axis=1), look[...])

    @pl.when(right_later)
    def _():
        pl.semaphore_wait(ready.at[0], 1)
        edge_copy(0).start()

    @pl.when(left_later)
    def _():
        pl.semaphore_wait(ready.at[1], 1)
        edge_copy(1).start()

    @pl.when((d == 0) & (c > 0))
    def _():
        edges(0)

    take_first([d], sent_0)
    arrive(4)
    arrive(3)
    arrive(5)
    arrive(2, 6, 1, 7)
    pairs_of(0)

    @pl.when((d == GROUP - 1) & (c < count - 1))
    def _():
        edges(1)

    second_copy(1, GROUP - 1).wait_recv()
    take_second()
    pairs_of(1)

    wide = []
    for q in range(6):
        piece = looked[q // 3, PAIRS * (q % 3) : PAIRS * (q % 3 + 1)]
        wide.append(piece if q % 3 < 2 else piece * (1.0 / 64.0))
    stacked = jnp.concatenate(split3(jnp.concatenate(wide, axis=1)), axis=0)
    placed = dot(select[...], stacked)
    lane = iota((32, 128), 1)
    for q in range(6):
        part = placed[:, 128 * q : 128 * (q + 1)]
        value = jnp.where(
            lane < 64,
            jnp.where(lane < 32, part[0:32], part[32:64]),
            jnp.where(lane < 96, part[64:96], part[96:128]),
        )
        for e in range(GROUP):
            results[e, 4 * q : 4 * q + 4, :] = value[4 * e : 4 * e + 4]

    def out_copy(k, size=1):
        return stage(
            results.at[pl.ds((d + k) % GROUP if size == 1 else 0, size)],
            landed.at[pl.ds(d if size == 1 else 0, size)],
            out_send.at[0], out_recv.at[0], date_peer(k),
        )

    for k in order:
        out_copy(k).start()
    landed[d] = results[d]

    @pl.when(c == 0)
    def _():
        up_copy(0, GROUP * count - 1).wait_recv()
        rows = [
            jnp.sum(power_in[count * e : count * (e + 1), :], axis=0, keepdims=True)
            for e in range(GROUP)
        ]
        parts = jnp.concatenate(split3(jnp.concatenate(rows, axis=0)), axis=0)
        total = jnp.sum(dot(hot[...], parts) * quarters[...], axis=1, keepdims=True)
        scale = jnp.sqrt(total / (ROWS * WIDTH * count) + 1e-06)
        factor = (1.0 / 64.0) / (scale[:PAIRS] * scale[PAIRS:])
        factor = jnp.broadcast_to(jnp.concatenate([factor, factor], axis=0), (ROWS, ROWS))
        factor = jnp.transpose(factor)[:8]
        factor_in[...] = factor
        for i in range(near):
            for j in range(count // nz):
                if i + j > 0:
                    down_copy(j * nz + i).start()
        for i in range(near, nz):
            down_copy(i).start()

    @pl.when(c > 0)
    def _():
        down_copy(0).wait_recv()

    @pl.when(hands_on)
    def _():
        if nz > near:
            pl.semaphore_wait(here, nz - near)
        for i in range(near, nz):
            down_copy(c - z + i).start()

    factor = jnp.transpose(jnp.broadcast_to(factor_in[0:1, :PAIRS], (ROWS, PAIRS)))
    factors = [jnp.sum(own[g] * factor, axis=0, keepdims=True) for g in range(3)]
    out_copy(1, GROUP - 1).wait_recv()
    scaling[...] = jnp.concatenate(factors + [jnp.zeros((5, 128), F32)], axis=0)
    first_copy(1, GROUP - 1).wait_send()
    second_copy(1, GROUP - 1).wait_send()
    out_copy(1, GROUP - 1).wait_send()

    @pl.when(right_later | right_earlier)
    def _():
        edge_copy(0).wait_send()

    @pl.when(left_later | left_earlier)
    def _():
        edge_copy(1).wait_send()

    def sent_down(number):
        stage(
            power_in.at[pl.ds(0, 8 * number)], power_in.at[pl.ds(0, 8 * number)], down_send.at[0],
            down_recv.at[0], {"dates": d, "cols": c},
        ).wait_send()

    @pl.when(c > 0)
    def _():
        up_copy(0, GROUP).wait_send()

    @pl.when(c == 0)
    def _():
        up_copy(0, GROUP - 1).wait_send()
        sent_down(near * (count // nz) - 1 + nz - near)

    if nz > near:

        @pl.when(hands_on)
        def _():
            sent_down(nz - near)


def place_kernel(landed, scaling, interferogram, coherence):
    for f in range(3):
        for g in range(3):
            block = landed[pl.ds(f * 4 + g, 16, stride=12), :]
            if f < 2:
                block = block * scaling[g : g + 1, :]
            for j in range(4):
                piece = block[:, 32 * j : 32 * j + 32]
                if f < 2:
                    interferogram[f, 4 * g + j] = piece
                else:
                    coherence[4 * g + j] = piece


def solution(mesh):
    columns = mesh.shape["cols"]
    nz = 8 if columns % 8 == 0 else 2
    sem = pltpu.SemaphoreType.DMA
    vmem = pl.BlockSpec(memory_space=pltpu.VMEM)

    def local(slc, pairs, owner):
        pairs = pairs.T
        owner = owner.reshape(1, PAIRS)
        landed, scaling = pl.pallas_call(
            lambda *refs: kernel(nz, columns, *refs),
            out_shape=(jax.ShapeDtypeStruct((GROUP, 24, 128), F32), jax.ShapeDtypeStruct((8, 128), F32)),
            in_specs=[pl.BlockSpec(memory_space=pl.ANY)] * 3,
            out_specs=(vmem, vmem),
            scratch_shapes=[
                pltpu.VMEM((2, EACH, ROWS, WIDTH), BF16),
                pltpu.SMEM((2, PAIRS), jnp.int32),
                pltpu.VMEM((2, PAIRS), jnp.int32),
                pltpu.VMEM((1, PAIRS), jnp.int32),
                pltpu.VMEM((128, 3 * PAIRS), BF16),
                pltpu.VMEM((3, PAIRS, 128), F32),
                pltpu.VMEM((3 * ROWS, 128), BF16),
                pltpu.VMEM((2 * PAIRS, 3 * GROUP), BF16),
                pltpu.VMEM((2 * PAIRS, ROWS), F32),
                pltpu.VMEM((2 * ROWS, 2 * ROWS), BF16),
                pltpu.VMEM((GROUP, EACH * 2 * PIECES[0], ROWS), BF16),
                pltpu.VMEM((GROUP, EACH * 2 * PIECES[1], ROWS), BF16),
                pltpu.VMEM((GROUP, EACH * 2 * PIECES[0], ROWS), BF16),
                pltpu.VMEM((GROUP, EACH * 2 * PIECES[1], ROWS), BF16),
                pltpu.VMEM((2, EDGE, ROWS), BF16),
                pltpu.VMEM((GROUP, EDGE, ROWS), BF16),
                pltpu.VMEM((GROUP, EDGE, ROWS), BF16),
                pltpu.VMEM((DATES, 2, TILE, ROWS), F32),
                pltpu.VMEM((DATES, PART, ROWS), F32),
                pltpu.VMEM((2 * CHUNK, WINDOW, ROWS), F32),
                pltpu.VMEM((2 * CHUNK * HALF, 2 * ROWS), BF16),
                pltpu.VMEM((6 * PAIRS * 8, ROWS), F32),
                pltpu.VMEM((2, 3 * PAIRS, ROWS), F32),
                pltpu.VMEM((1, ROWS), F32),
                pltpu.VMEM((GROUP * columns, ROWS), F32),
                pltpu.VMEM((8, ROWS), F32),
                pltpu.VMEM((GROUP, 24, 128), F32),
                sem((1,)), sem((4,)), sem((1,)), sem((1,)),
                sem((2,)), sem((1,)), pltpu.SemaphoreType.REGULAR((2,)), pltpu.SemaphoreType.REGULAR,
                sem((1,)), sem((1,)), sem((1,)), sem((1,)), sem((1,)), sem((1,)),
                sem((1,)), sem((3,)),
            ],
            compiler_params=pltpu.CompilerParams(
                collective_id=0, has_side_effects=True, vmem_limit_bytes=54682 * 1024
            ),
        )(slc, pairs, owner)
        interferogram, coherence = pl.pallas_call(
            place_kernel,
            out_shape=(
                jax.ShapeDtypeStruct((2, CAP, 16, 32), F32),
                jax.ShapeDtypeStruct((CAP, 16, 32), F32),
            ),
            in_specs=[vmem, vmem],
            out_specs=(vmem, vmem),
            compiler_params=pltpu.CompilerParams(vmem_limit_bytes=2 * 1024 * 1024),
        )(landed.reshape(GROUP * 24, 128), scaling)
        return jnp.swapaxes(interferogram, 2, 3), jnp.swapaxes(coherence, 1, 2)

    return jax.shard_map(
        local,
        mesh=mesh,
        in_specs=(P(None, "dates", None, "cols"), P(), P()),
        out_specs=(P(None, "dates", None, "cols"), P("dates", None, "cols")),
        check_vma=False,
    )
```

```python
import math

import jax
import jax.numpy as jnp
import ml_dtypes
import numpy as np
from jax import lax
from jax.experimental import pallas as pl
from jax.experimental.pallas import tpu as pltpu
from jax.sharding import PartitionSpec as P

MESH = pl.DeviceIdType.MESH
F32 = jnp.float32
BF16 = jnp.bfloat16

TAPS = [math.exp(-k * k / 8.0) for k in range(-4, 5)]
WEIGHTS = [float(np.float32(t / sum(TAPS))) for t in TAPS]
HIGH = [float(np.float32(w).astype(ml_dtypes.bfloat16)) for w in WEIGHTS]
LOW = [float(np.float32(w - h).astype(ml_dtypes.bfloat16)) for w, h in zip(WEIGHTS, HIGH)]

GROUP = 8
EACH = 4
DATES = GROUP * EACH
PAIRS = 64
CAP = 12
ROWS = 128
PART = 32
TILE = PART + 8
WIDTH = GROUP * PART
PIECES = (24, 16)
HALF = PART // 2
WINDOW = HALF + 8
EDGE = EACH * 2 * 8
CHUNK = 16


def split(x):
    high = x.astype(BF16)
    return high, (x - high.astype(F32)).astype(BF16)


def split3(x):
    high = x.astype(BF16)
    rest = x - high.astype(F32)
    mid = rest.astype(BF16)
    return high, mid, (rest - mid.astype(F32)).astype(BF16)


def dot(a, b):
    return jnp.dot(a, b, preferred_element_type=F32)


def iota(shape, axis):
    return lax.broadcasted_iota(jnp.int32, shape, axis)


def cutter(half):
    start, size = (-4, PIECES[0]) if half == 0 else (PIECES[0] - 4, PIECES[1])
    lane = iota((size, WIDTH), 1)
    row = iota((size, WIDTH), 0)
    pieces = [jnp.where(lane == row + (PART * e + start), 1.0, 0.0) for e in range(GROUP)]
    lane = iota((8, WIDTH), 1)
    row = iota((8, WIDTH), 0)
    pieces.append(jnp.where(lane == row + (WIDTH - 4 if half == 0 else -4), 1.0, 0.0))
    return jnp.concatenate(pieces, axis=0).astype(BF16)


def band(weights):
    gap = jnp.abs(iota((ROWS, ROWS), 0) - iota((ROWS, ROWS), 1))
    result = jnp.zeros((ROWS, ROWS), F32)
    for k in range(5):
        result = jnp.where(gap == k, weights[4 + k], result)
    return result.astype(BF16)


def along_columns(ref, index):
    result = WEIGHTS[4] * ref[index, 4 : 4 + HALF, :]
    for k in range(4):
        both = ref[index, k : k + HALF, :] + ref[index, 8 - k : 8 - k + HALF, :]
        result = result + WEIGHTS[k] * both
    return result


def kernel(
    nz, count, slc_hbm, pairs_hbm, owner_hbm, landed, scaling,
    slc, pairs_s, pairs_v, owner_v, select, own, look, hot, quarters, smoother, sent_0, sent_1, got_0, got_1,
    edge_out, edge_left, edge_right, images, roots, fields, lhs, sums, looked,
    power_row, power_in, totals, factor_in, results,
    main_send_0, main_recv_0, main_send_1, main_recv_1, edge_send, edge_recv, ready,
    here, up_send, up_recv, down_send, down_recv, d_send, d_recv, out_send, out_recv, in_sem, table_sem,
):
    d = lax.axis_index("dates")
    c = lax.axis_index("cols")
    z = c % nz

    def date_peer(k):
        return {"dates": (d + k) % GROUP, "cols": c}

    right = (c + 1) % count
    left = (c + count - 1) % count
    near = min(2, nz)
    right_later = (z < nz - 1) & (c < count - 1)
    right_earlier = (z == nz - 1) & (c < count - 1)
    left_later = (z == 0) & (c > 0)
    left_earlier = (z > 0) & (c > 0)

    load = pltpu.make_async_copy(slc_hbm, slc, in_sem.at[0])
    load.start()

    barrier = pltpu.get_barrier_semaphore()

    def greet(device):
        pl.semaphore_signal(barrier, inc=1, device_id=device, device_id_type=MESH)

    for k in range(1, GROUP):
        greet(date_peer(k))

    def greet_neighbour(later, receiver, other):
        @pl.when(later)
        def _():
            greet({"dates": receiver, "cols": other})

        @pl.when(later & (d == GROUP - 1 - receiver))
        def _():
            for e in range(GROUP):
                greet({"dates": e, "cols": other})

    greet_neighbour(right_later, 0, right)
    greet_neighbour(left_later, GROUP - 1, left)

    @pl.when(c == 0)
    def _():
        def one(i, carry):
            greet({"dates": d, "cols": i})
            return carry

        lax.fori_loop(1, count, one, 0)

    hands_on = (z == 0) & (c > 0)
    handed = (z >= near) & (c >= nz)

    @pl.when(hands_on)
    def _():
        for i in range(near, nz):
            greet({"dates": d, "cols": c - z + i})

    tables = [
        pltpu.make_async_copy(pairs_hbm, pairs_s, table_sem.at[0]),
        pltpu.make_async_copy(pairs_hbm, pairs_v, table_sem.at[1]),
        pltpu.make_async_copy(owner_hbm, owner_v, table_sem.at[2]),
    ]
    for table in tables:
        table.start()

    sent = (sent_0, sent_1)
    edge_in = (edge_left, edge_right)
    got = (got_0, got_1)

    def cut(half, matrix):
        size = PIECES[half]
        for t in range(EACH):
            both = jnp.concatenate([slc[0, t], slc[1, t]], axis=0)
            turned = lax.dot_general(
                matrix, both, (((1,), (1,)), ((), ())), preferred_element_type=F32
            )
            for e in range(GROUP + 1):
                rows = turned[size * e : size * (e + 1)] if e < GROUP else turned[size * GROUP :]
                value = jnp.concatenate([rows[:, :ROWS], rows[:, ROWS:]], axis=0).astype(BF16)
                if e < GROUP:
                    sent[half][e, 2 * size * t : 2 * size * (t + 1), :] = value
                else:
                    edge_out[half, 16 * t : 16 * (t + 1), :] = value

    matrix = cutter(0)
    high = band(HIGH)
    low = band(LOW)
    smoother[:, :ROWS] = jnp.concatenate([high, high], axis=0)
    smoother[:, ROWS:] = jnp.concatenate([low, low], axis=0)
    load.wait()
    power_rows = []
    for t in range(EACH):
        wide = jnp.concatenate([slc[0, t], slc[1, t]], axis=0).astype(F32)
        square = jnp.sum(wide * wide, axis=0, keepdims=True)
        power_rows.append(square[:, :ROWS] + square[:, ROWS:])
    folded = jnp.concatenate(power_rows + [jnp.zeros((8 - EACH, ROWS), F32)], axis=0)
    folded = folded + pltpu.roll(folded, 64, 1)
    folded = folded + pltpu.roll(folded, 32, 1)
    own_lane = (iota((8, ROWS), 1) >> 5) == iota((8, ROWS), 0)
    power_row[...] = jnp.sum(jnp.where(own_lane, folded, 0.0), axis=0, keepdims=True)
    cut(0, matrix)

    first = (d == 0).astype(jnp.int32)
    last = (d == GROUP - 1).astype(jnp.int32)
    pl.semaphore_wait(
        barrier,
        (GROUP - 1)
        + (c > 0).astype(jnp.int32)
        + handed.astype(jnp.int32)
        + right_earlier.astype(jnp.int32) * (1 + GROUP * last)
        + left_earlier.astype(jnp.int32) * (1 + GROUP * first),
    )

    def tell_ready(side, condition, other):
        @pl.when(condition)
        def _():
            for e in range(GROUP):
                pl.semaphore_signal(
                    ready.at[side], inc=1, device_id={"dates": e, "cols": other}, device_id_type=MESH
                )

    @pl.when(handed)
    def _():
        pl.semaphore_signal(
            here, inc=1, device_id={"dates": d, "cols": c - z}, device_id_type=MESH
        )

    tell_ready(0, left_earlier & (d == 0), left)
    tell_ready(1, right_earlier & (d == GROUP - 1), right)

    def stage(src, dst, send, recv, peer):
        return pltpu.make_async_remote_copy(
            src_ref=src, dst_ref=dst, send_sem=send, recv_sem=recv, device_id=peer, device_id_type=MESH
        )

    def up_copy(i, size=1):
        return stage(
            power_in.at[pl.ds(0, size)] if size > 1 else power_row, power_in.at[pl.ds(i, size)],
            up_send.at[0], up_recv.at[0], {"dates": d, "cols": 0},
        )

    def down_copy(i):
        return stage(factor_in, factor_in, down_send.at[0], down_recv.at[0], {"dates": d, "cols": i})

    @pl.when(c > 0)
    def _():
        up_copy(c).start()

    targets = ({"dates": 0, "cols": right}, {"dates": GROUP - 1, "cols": left})

    def edge_copy(side):
        return pltpu.make_async_remote_copy(
            src_ref=edge_out.at[side], dst_ref=edge_in[side].at[d], send_sem=edge_send.at[side],
            recv_sem=edge_recv.at[0], device_id=targets[side], device_id_type=MESH,
        )

    order = (4, 3, 5, 2, 6, 1, 7)
    slots = {4: 0, 3: 1, 5: 2}

    def first_copy(k, size=1):
        return stage(
            sent_0.at[pl.ds((d + k) % GROUP if size == 1 else 0, size)],
            got_0.at[pl.ds(d if size == 1 else 0, size)],
            main_send_0.at[0], main_recv_0.at[slots.get(k, 3)], date_peer(k),
        )

    def second_copy(k, size=1):
        return stage(
            sent_1.at[pl.ds((d + k) % GROUP if size == 1 else 0, size)],
            got_1.at[pl.ds(d if size == 1 else 0, size)],
            main_send_1.at[0], main_recv_1.at[0], date_peer(k),
        )

    for k in order:
        first_copy(k).start()

    @pl.when(right_earlier)
    def _():
        edge_copy(0).start()

    cut(1, cutter(1))
    for k in order:
        second_copy(k).start()

    @pl.when(left_earlier)
    def _():
        edge_copy(1).start()

    got_1[d] = sent_1[d]

    @pl.when((d != 0) | (c == 0))
    def _():
        edge_left[...] = jnp.zeros_like(edge_left)

    @pl.when((d != GROUP - 1) | (c == count - 1))
    def _():
        edge_right[...] = jnp.zeros_like(edge_right)


    for table in tables:
        table.wait()
    owner_row = owner_v[...]
    owner_down = jnp.transpose(jnp.broadcast_to(owner_row.astype(F32), (ROWS, PAIRS)))[:, :PAIRS]
    earlier = iota((PAIRS, PAIRS), 0) < iota((PAIRS, PAIRS), 1)
    same = owner_down == owner_row.astype(F32)
    rank = jnp.sum(jnp.where(same & earlier, 1.0, 0.0), axis=0, keepdims=True).astype(jnp.int32)
    place = (rank & 3) * 32 + owner_row * 4 + (rank >> 2)
    one = jnp.where(iota((128, PAIRS), 0) == place, 1.0, 0.0)
    select[...] = jnp.concatenate([one, one, one], axis=1).astype(BF16)
    later = iota((PAIRS, PAIRS), 0) > iota((PAIRS, PAIRS), 1)
    rank_down = jnp.sum(jnp.where(same & later, 1.0, 0.0), axis=1, keepdims=True)
    quarter = (iota((PAIRS, 128), 1) >> 5).astype(F32)
    mine = jnp.where(owner_down[:, :1] == d.astype(F32), rank_down, -1.0)
    for g in range(3):
        own[g] = jnp.where(mine == quarter + 4.0 * g, 1.0, 0.0)

    def date_rows(which):
        date = pairs_v[which : which + 1, :].astype(F32)
        return jnp.transpose(jnp.broadcast_to(date, (ROWS, PAIRS)))

    date = jnp.concatenate([date_rows(0), date_rows(1)], axis=0)
    lane = iota((2 * PAIRS, ROWS), 1)
    first_date = (EACH * (lane & 7)).astype(F32)
    one = jnp.where((date >= first_date) & (date < first_date + EACH) & (lane < 24), 1.0, 0.0)
    hot[...] = one[:, : 3 * GROUP].astype(BF16)
    phase = date - EACH * jnp.floor(date * (1.0 / EACH))
    quarters[...] = jnp.where(phase == (lane >> 5).astype(F32), 1.0, 0.0)
    one = jnp.where((iota((ROWS, 128), 0) >> 2) == (iota((ROWS, 128), 1) & 31), 1.0, 0.0)
    look[...] = jnp.concatenate([one, one, one], axis=0).astype(BF16)

    def edges(side):
        stage(
            edge_in[side], edge_in[side], edge_send.at[side], edge_recv.at[0], targets[side]
        ).wait_recv()

    def smooth_powers(number):
        for t in range(number):
            big, small = split(along_columns(fields, t))
            lhs[HALF * t : HALF * (t + 1), :ROWS] = big
            lhs[HALF * t : HALF * (t + 1), ROWS:] = small
        smooth = dot(lhs[: number * HALF, :], smoother[...])
        return jnp.sqrt(smooth[:, :ROWS] + smooth[:, ROWS:])

    def take_first(sources, ref):
        size = PIECES[0]
        for i, source in enumerate(sources):
            for t in range(EACH):
                piece = ref[source, 2 * size * t : 2 * size * (t + 1), :].astype(F32)
                edge = edge_left[source, 16 * t : 16 * (t + 1), :].astype(F32)
                real = jnp.concatenate([piece[:8] + edge[:8], piece[8:size]], axis=0)
                imag = jnp.concatenate([piece[size : size + 8] + edge[8:], piece[size + 8 :]], axis=0)
                images[source * EACH + t, 0, :size] = real
                images[source * EACH + t, 1, :size] = imag
                fields[EACH * i + t] = real * real + imag * imag
        smooth = smooth_powers(EACH * len(sources))
        for i, source in enumerate(sources):
            for t in range(EACH):
                at = HALF * (EACH * i + t)
                roots[source * EACH + t, :HALF] = smooth[at : at + HALF]

    def arrive(*ks):
        first_copy(ks[0], len(ks)).wait_recv()
        take_first([(d + GROUP - k) % GROUP for k in ks], got_0)

    def take_second():
        size = PIECES[1]
        for date in range(DATES):
            source, t = date // EACH, date % EACH
            piece = got_1[source, 2 * size * t : 2 * size * (t + 1), :].astype(F32)
            edge = edge_right[source, 16 * t : 16 * (t + 1), :].astype(F32)
            real = jnp.concatenate([piece[:8], piece[8:size] + edge[:8]], axis=0)
            imag = jnp.concatenate([piece[size : size + 8], piece[size + 8 :] + edge[8:]], axis=0)
            images[date, 0, PIECES[0] :] = real
            images[date, 1, PIECES[0] :] = imag
            real = jnp.concatenate([images[date, 0, HALF : PIECES[0]], real], axis=0)
            imag = jnp.concatenate([images[date, 1, HALF : PIECES[0]], imag], axis=0)
            fields[date] = real * real + imag * imag
        smooth = smooth_powers(DATES)
        for date in range(DATES):
            roots[date, HALF:] = smooth[HALF * date : HALF * (date + 1)]

    def pairs_of(half, between=None):
        window = slice(HALF * half, HALF * half + WINDOW)

        def place(field, p):
            return pl.ds(((3 * half + field) * PAIRS + p) * 8, 8)

        def chunk(index, carry):
            dates = []
            for i in range(CHUNK):
                p = index * CHUNK + i
                first = pairs_s[0, p]
                second = pairs_s[1, p]
                dates.append((first, second))
                real_a = images[first, 0, window]
                imag_a = images[first, 1, window]
                real_b = images[second, 0, window]
                imag_b = images[second, 1, window]
                fields[2 * i] = real_a * real_b + imag_a * imag_b
                fields[2 * i + 1] = imag_a * real_b - real_a * imag_b
            for i in range(CHUNK):
                p = index * CHUNK + i
                for f in range(2):
                    n = 2 * i + f
                    big, small = split(along_columns(fields, n))
                    lhs[HALF * n : HALF * (n + 1), :ROWS] = big
                    lhs[HALF * n : HALF * (n + 1), ROWS:] = small
                    sums[place(f, p), :] = fields[n, 4:12, :] + fields[n, 12:20, :]
            smooth = dot(lhs[...], smoother[...])
            smooth = smooth[:, :ROWS] + smooth[:, ROWS:]
            for i in range(CHUNK):
                p = index * CHUNK + i
                first, second = dates[i]
                real = smooth[2 * HALF * i : 2 * HALF * i + HALF]
                imag = smooth[2 * HALF * i + HALF : 2 * HALF * (i + 1)]
                below = (
                    roots[first, HALF * half : HALF * (half + 1)]
                    * roots[second, HALF * half : HALF * (half + 1)]
                )
                value = jnp.sqrt(real * real + imag * imag) / (below + 1e-06)
                sums[place(2, p), :] = value[0:8] + value[8:16]
            return carry

        if between is None:
            lax.fori_loop(0, PAIRS // CHUNK, chunk, 0)
        else:
            lax.fori_loop(0, PAIRS // CHUNK // 2, chunk, 0)
            between()
            lax.fori_loop(PAIRS // CHUNK // 2, PAIRS // CHUNK, chunk, 0)
        rows = sums[pl.ds(3 * half * PAIRS * 8, 3 * PAIRS, stride=8), :]
        for i in range(1, 8):
            rows = rows + sums[pl.ds(3 * half * PAIRS * 8 + i, 3 * PAIRS, stride=8), :]
        looked[half] = dot(jnp.concatenate(split3(rows), axis=1), look[...])

    @pl.when(right_later)
    def _():
        pl.semaphore_wait(ready.at[0], 1)
        edge_copy(0).start()

    @pl.when(left_later)
    def _():
        pl.semaphore_wait(ready.at[1], 1)
        edge_copy(1).start()

    @pl.when((d == 0) & (c > 0))
    def _():
        edges(0)

    take_first([d], sent_0)
    arrive(4)
    arrive(3)
    arrive(5)
    arrive(2, 6, 1, 7)
    pairs_of(0)

    def d_copy(k, size=1):
        return stage(
            totals.at[pl.ds(d if size == 1 else 0, size)], totals.at[pl.ds(d if size == 1 else 0, size)],
            d_send.at[0], d_recv.at[0], date_peer(k),
        )

    def add_up():
        @pl.when(c == 0)
        def _():
            up_copy(1, count - 1).wait_recv()
            total = power_row[...] + jnp.sum(power_in[1:count, :], axis=0, keepdims=True)
            totals[pl.ds(d, 1), :] = total
            for k in order:
                d_copy(k).start()

    @pl.when((d == GROUP - 1) & (c < count - 1))
    def _():
        edges(1)

    second_copy(1, GROUP - 1).wait_recv()
    take_second()
    pairs_of(1, add_up)

    wide = []
    for q in range(6):
        piece = looked[q // 3, PAIRS * (q % 3) : PAIRS * (q % 3 + 1)]
        wide.append(piece if q % 3 < 2 else piece * (1.0 / 64.0))
    stacked = jnp.concatenate(split3(jnp.concatenate(wide, axis=1)), axis=0)
    placed = dot(select[...], stacked)
    lane = iota((32, 128), 1)
    for q in range(6):
        part = placed[:, 128 * q : 128 * (q + 1)]
        value = jnp.where(
            lane < 64,
            jnp.where(lane < 32, part[0:32], part[32:64]),
            jnp.where(lane < 96, part[64:96], part[96:128]),
        )
        for e in range(GROUP):
            results[e, 4 * q : 4 * q + 4, :] = value[4 * e : 4 * e + 4]

    def out_copy(k, size=1):
        return stage(
            results.at[pl.ds((d + k) % GROUP if size == 1 else 0, size)],
            landed.at[pl.ds(d if size == 1 else 0, size)],
            out_send.at[0], out_recv.at[0], date_peer(k),
        )

    for k in order:
        out_copy(k).start()
    landed[d] = results[d]

    @pl.when(c == 0)
    def _():
        d_copy(1, GROUP - 1).wait_recv()
        parts = jnp.concatenate(split3(totals[...]), axis=0)
        total = jnp.sum(dot(hot[...], parts) * quarters[...], axis=1, keepdims=True)
        scale = jnp.sqrt(total / (ROWS * WIDTH * count) + 1e-06)
        factor = (1.0 / 64.0) / (scale[:PAIRS] * scale[PAIRS:])
        factor = jnp.broadcast_to(jnp.concatenate([factor, factor], axis=0), (ROWS, ROWS))
        factor = jnp.transpose(factor)[:8]
        factor_in[...] = factor
        for i in range(near):
            for j in range(count // nz):
                if i + j > 0:
                    down_copy(j * nz + i).start()
        for i in range(near, nz):
            down_copy(i).start()

    @pl.when(c > 0)
    def _():
        down_copy(0).wait_recv()

    @pl.when(hands_on)
    def _():
        if nz > near:
            pl.semaphore_wait(here, nz - near)
        for i in range(near, nz):
            down_copy(c - z + i).start()

    factor = jnp.transpose(jnp.broadcast_to(factor_in[0:1, :PAIRS], (ROWS, PAIRS)))
    factors = [jnp.sum(own[g] * factor, axis=0, keepdims=True) for g in range(3)]
    out_copy(1, GROUP - 1).wait_recv()
    scaling[...] = jnp.concatenate(factors + [jnp.zeros((5, 128), F32)], axis=0)
    first_copy(1, GROUP - 1).wait_send()
    second_copy(1, GROUP - 1).wait_send()
    out_copy(1, GROUP - 1).wait_send()

    @pl.when(right_later | right_earlier)
    def _():
        edge_copy(0).wait_send()

    @pl.when(left_later | left_earlier)
    def _():
        edge_copy(1).wait_send()

    def sent_down(number):
        stage(
            power_in.at[pl.ds(0, 8 * number)], power_in.at[pl.ds(0, 8 * number)], down_send.at[0],
            down_recv.at[0], {"dates": d, "cols": c},
        ).wait_send()

    @pl.when(c > 0)
    def _():
        up_copy(c).wait_send()

    @pl.when(c == 0)
    def _():
        d_copy(1, GROUP - 1).wait_send()
        sent_down(near * (count // nz) - 1 + nz - near)

    if nz > near:

        @pl.when(hands_on)
        def _():
            sent_down(nz - near)


def place_kernel(landed, scaling, interferogram, coherence):
    for f in range(3):
        for g in range(3):
            block = landed[pl.ds(f * 4 + g, 16, stride=12), :]
            if f < 2:
                block = block * scaling[g : g + 1, :]
            for j in range(4):
                piece = block[:, 32 * j : 32 * j + 32]
                if f < 2:
                    interferogram[f, 4 * g + j] = piece
                else:
                    coherence[4 * g + j] = piece


def solution(mesh):
    columns = mesh.shape["cols"]
    nz = 8 if columns % 8 == 0 else 2
    sem = pltpu.SemaphoreType.DMA
    vmem = pl.BlockSpec(memory_space=pltpu.VMEM)

    def local(slc, pairs, owner):
        pairs = pairs.T
        owner = owner.reshape(1, PAIRS)
        landed, scaling = pl.pallas_call(
            lambda *refs: kernel(nz, columns, *refs),
            out_shape=(jax.ShapeDtypeStruct((GROUP, 24, 128), F32), jax.ShapeDtypeStruct((8, 128), F32)),
            in_specs=[pl.BlockSpec(memory_space=pl.ANY)] * 3,
            out_specs=(vmem, vmem),
            scratch_shapes=[
                pltpu.VMEM((2, EACH, ROWS, WIDTH), BF16),
                pltpu.SMEM((2, PAIRS), jnp.int32),
                pltpu.VMEM((2, PAIRS), jnp.int32),
                pltpu.VMEM((1, PAIRS), jnp.int32),
                pltpu.VMEM((128, 3 * PAIRS), BF16),
                pltpu.VMEM((3, PAIRS, 128), F32),
                pltpu.VMEM((3 * ROWS, 128), BF16),
                pltpu.VMEM((2 * PAIRS, 3 * GROUP), BF16),
                pltpu.VMEM((2 * PAIRS, ROWS), F32),
                pltpu.VMEM((2 * ROWS, 2 * ROWS), BF16),
                pltpu.VMEM((GROUP, EACH * 2 * PIECES[0], ROWS), BF16),
                pltpu.VMEM((GROUP, EACH * 2 * PIECES[1], ROWS), BF16),
                pltpu.VMEM((GROUP, EACH * 2 * PIECES[0], ROWS), BF16),
                pltpu.VMEM((GROUP, EACH * 2 * PIECES[1], ROWS), BF16),
                pltpu.VMEM((2, EDGE, ROWS), BF16),
                pltpu.VMEM((GROUP, EDGE, ROWS), BF16),
                pltpu.VMEM((GROUP, EDGE, ROWS), BF16),
                pltpu.VMEM((DATES, 2, TILE, ROWS), F32),
                pltpu.VMEM((DATES, PART, ROWS), F32),
                pltpu.VMEM((2 * CHUNK, WINDOW, ROWS), F32),
                pltpu.VMEM((2 * CHUNK * HALF, 2 * ROWS), BF16),
                pltpu.VMEM((6 * PAIRS * 8, ROWS), F32),
                pltpu.VMEM((2, 3 * PAIRS, ROWS), F32),
                pltpu.VMEM((1, ROWS), F32),
                pltpu.VMEM((8 * columns, ROWS), F32),
                pltpu.VMEM((GROUP, ROWS), F32),
                pltpu.VMEM((8, ROWS), F32),
                pltpu.VMEM((GROUP, 24, 128), F32),
                sem((1,)), sem((4,)), sem((1,)), sem((1,)),
                sem((2,)), sem((1,)), pltpu.SemaphoreType.REGULAR((2,)), pltpu.SemaphoreType.REGULAR,
                sem((1,)), sem((1,)), sem((1,)), sem((1,)),
                sem((1,)), sem((1,)), sem((1,)), sem((1,)),
                sem((1,)), sem((3,)),
            ],
            compiler_params=pltpu.CompilerParams(
                collective_id=0, has_side_effects=True, vmem_limit_bytes=54682 * 1024
            ),
        )(slc, pairs, owner)
        interferogram, coherence = pl.pallas_call(
            place_kernel,
            out_shape=(
                jax.ShapeDtypeStruct((2, CAP, 16, 32), F32),
                jax.ShapeDtypeStruct((CAP, 16, 32), F32),
            ),
            in_specs=[vmem, vmem],
            out_specs=(vmem, vmem),
            compiler_params=pltpu.CompilerParams(vmem_limit_bytes=2 * 1024 * 1024),
        )(landed.reshape(GROUP * 24, 128), scaling)
        return jnp.swapaxes(interferogram, 2, 3), jnp.swapaxes(coherence, 1, 2)

    return jax.shard_map(
        local,
        mesh=mesh,
        in_specs=(P(None, "dates", None, "cols"), P(), P()),
        out_specs=(P(None, "dates", None, "cols"), P("dates", None, "cols")),
        check_vma=False,
    )
```

```python
import math

import jax
import jax.numpy as jnp
import ml_dtypes
import numpy as np
from jax import lax
from jax.experimental import pallas as pl
from jax.experimental.pallas import tpu as pltpu
from jax.sharding import PartitionSpec as P

MESH = pl.DeviceIdType.MESH
F32 = jnp.float32
BF16 = jnp.bfloat16

TAPS = [math.exp(-k * k / 8.0) for k in range(-4, 5)]
WEIGHTS = [float(np.float32(t / sum(TAPS))) for t in TAPS]
HIGH = [float(np.float32(w).astype(ml_dtypes.bfloat16)) for w in WEIGHTS]
LOW = [float(np.float32(w - h).astype(ml_dtypes.bfloat16)) for w, h in zip(WEIGHTS, HIGH)]

GROUP = 8
EACH = 4
DATES = GROUP * EACH
PAIRS = 64
CAP = 12
ROWS = 128
PART = 32
TILE = PART + 8
WIDTH = GROUP * PART
PIECES = (24, 16)
HALF = PART // 2
WINDOW = HALF + 8
EDGE = EACH * 2 * 8
CHUNK = 16


def split(x):
    high = x.astype(BF16)
    return high, (x - high.astype(F32)).astype(BF16)


def split3(x):
    high = x.astype(BF16)
    rest = x - high.astype(F32)
    mid = rest.astype(BF16)
    return high, mid, (rest - mid.astype(F32)).astype(BF16)


def dot(a, b):
    return jnp.dot(a, b, preferred_element_type=F32)


def iota(shape, axis):
    return lax.broadcasted_iota(jnp.int32, shape, axis)


def cutter(half):
    start, size = (-4, PIECES[0]) if half == 0 else (PIECES[0] - 4, PIECES[1])
    lane = iota((size, WIDTH), 1)
    row = iota((size, WIDTH), 0)
    pieces = [jnp.where(lane == row + (PART * e + start), 1.0, 0.0) for e in range(GROUP)]
    lane = iota((8, WIDTH), 1)
    row = iota((8, WIDTH), 0)
    pieces.append(jnp.where(lane == row + (WIDTH - 4 if half == 0 else -4), 1.0, 0.0))
    return jnp.concatenate(pieces, axis=0).astype(BF16)


def band(weights):
    gap = jnp.abs(iota((ROWS, ROWS), 0) - iota((ROWS, ROWS), 1))
    result = jnp.zeros((ROWS, ROWS), F32)
    for k in range(5):
        result = jnp.where(gap == k, weights[4 + k], result)
    return result.astype(BF16)


def along_columns(ref, index):
    result = WEIGHTS[4] * ref[index, 4 : 4 + HALF, :]
    for k in range(4):
        both = ref[index, k : k + HALF, :] + ref[index, 8 - k : 8 - k + HALF, :]
        result = result + WEIGHTS[k] * both
    return result


def kernel(
    nz, count, slc_hbm, pairs_hbm, owner_hbm, landed, scaling,
    slc, pairs_s, pairs_v, owner_v, select, own, look, hot, quarters, smoother, sent_0, sent_1, got_0, got_1,
    edge_out, edge_left, edge_right, images, roots, fields, lhs, sums, looked,
    power_row, power_in, totals, factor_in, results,
    main_send_0, main_recv_0, main_send_1, main_recv_1, edge_send, edge_recv, ready,
    here, up_send, up_recv, down_send, down_recv, d_send, d_recv, out_send, out_recv, in_sem, table_sem,
):
    d = lax.axis_index("dates")
    c = lax.axis_index("cols")
    z = c % nz

    def date_peer(k):
        return {"dates": (d + k) % GROUP, "cols": c}

    right = (c + 1) % count
    left = (c + count - 1) % count
    near = min(3, nz)
    right_later = (z < nz - 1) & (c < count - 1)
    right_earlier = (z == nz - 1) & (c < count - 1)
    left_later = (z == 0) & (c > 0)
    left_earlier = (z > 0) & (c > 0)

    load = pltpu.make_async_copy(slc_hbm, slc, in_sem.at[0])
    load.start()

    barrier = pltpu.get_barrier_semaphore()

    def greet(device):
        pl.semaphore_signal(barrier, inc=1, device_id=device, device_id_type=MESH)

    for k in range(1, GROUP):
        greet(date_peer(k))

    def greet_neighbour(later, receiver, other):
        @pl.when(later)
        def _():
            greet({"dates": receiver, "cols": other})

        @pl.when(later & (d == GROUP - 1 - receiver))
        def _():
            for e in range(GROUP):
                greet({"dates": e, "cols": other})

    greet_neighbour(right_later, 0, right)
    greet_neighbour(left_later, GROUP - 1, left)

    @pl.when(c == 0)
    def _():
        def one(i, carry):
            greet({"dates": d, "cols": i})
            return carry

        lax.fori_loop(1, count, one, 0)

    hands_on = z == near - 1
    handed = z >= near
    hand = c - z + near - 1

    @pl.when(hands_on)
    def _():
        for i in range(near, nz):
            greet({"dates": d, "cols": hand - (near - 1) + i})

    tables = [
        pltpu.make_async_copy(pairs_hbm, pairs_s, table_sem.at[0]),
        pltpu.make_async_copy(pairs_hbm, pairs_v, table_sem.at[1]),
        pltpu.make_async_copy(owner_hbm, owner_v, table_sem.at[2]),
    ]
    for table in tables:
        table.start()

    sent = (sent_0, sent_1)
    edge_in = (edge_left, edge_right)
    got = (got_0, got_1)

    def cut(half, matrix):
        size = PIECES[half]
        for t in range(EACH):
            both = jnp.concatenate([slc[0, t], slc[1, t]], axis=0)
            turned = lax.dot_general(
                matrix, both, (((1,), (1,)), ((), ())), preferred_element_type=F32
            )
            for e in range(GROUP + 1):
                rows = turned[size * e : size * (e + 1)] if e < GROUP else turned[size * GROUP :]
                value = jnp.concatenate([rows[:, :ROWS], rows[:, ROWS:]], axis=0).astype(BF16)
                if e < GROUP:
                    sent[half][e, 2 * size * t : 2 * size * (t + 1), :] = value
                else:
                    edge_out[half, 16 * t : 16 * (t + 1), :] = value

    matrix = cutter(0)
    high = band(HIGH)
    low = band(LOW)
    smoother[:, :ROWS] = jnp.concatenate([high, high], axis=0)
    smoother[:, ROWS:] = jnp.concatenate([low, low], axis=0)
    load.wait()
    power_rows = []
    for t in range(EACH):
        wide = jnp.concatenate([slc[0, t], slc[1, t]], axis=0).astype(F32)
        square = jnp.sum(wide * wide, axis=0, keepdims=True)
        power_rows.append(square[:, :ROWS] + square[:, ROWS:])
    folded = jnp.concatenate(power_rows + [jnp.zeros((8 - EACH, ROWS), F32)], axis=0)
    folded = folded + pltpu.roll(folded, 64, 1)
    folded = folded + pltpu.roll(folded, 32, 1)
    own_lane = (iota((8, ROWS), 1) >> 5) == iota((8, ROWS), 0)
    power_row[...] = jnp.sum(jnp.where(own_lane, folded, 0.0), axis=0, keepdims=True)

    def stage(src, dst, send, recv, peer):
        return pltpu.make_async_remote_copy(
            src_ref=src, dst_ref=dst, send_sem=send, recv_sem=recv, device_id=peer, device_id_type=MESH
        )

    def up_copy(i, size=1):
        return stage(
            power_in.at[pl.ds(0, size)] if size > 1 else power_row, power_in.at[pl.ds(i, size)],
            up_send.at[0], up_recv.at[0], {"dates": d, "cols": 0},
        )

    def down_copy(i):
        return stage(factor_in, factor_in, down_send.at[0], down_recv.at[0], {"dates": d, "cols": i})

    first = (d == 0).astype(jnp.int32)
    last = (d == GROUP - 1).astype(jnp.int32)

    def enter():
        pl.semaphore_wait(
            barrier,
            (GROUP - 1)
            + (c > 0).astype(jnp.int32)
            + handed.astype(jnp.int32)
            + right_earlier.astype(jnp.int32) * (1 + GROUP * last)
            + left_earlier.astype(jnp.int32) * (1 + GROUP * first),
        )

        def tell_ready(side, condition, other):
            @pl.when(condition)
            def _():
                for e in range(GROUP):
                    pl.semaphore_signal(
                        ready.at[side], inc=1, device_id={"dates": e, "cols": other}, device_id_type=MESH
                    )

        @pl.when(handed)
        def _():
            pl.semaphore_signal(
                here, inc=1, device_id={"dates": d, "cols": hand}, device_id_type=MESH
            )

        tell_ready(0, left_earlier & (d == 0), left)
        tell_ready(1, right_earlier & (d == GROUP - 1), right)

        @pl.when(c > 0)
        def _():
            up_copy(c).start()

    pl.when(z >= nz // 2)(enter)
    cut(0, matrix)
    pl.when(z < nz // 2)(enter)

    targets = ({"dates": 0, "cols": right}, {"dates": GROUP - 1, "cols": left})

    def edge_copy(side):
        return pltpu.make_async_remote_copy(
            src_ref=edge_out.at[side], dst_ref=edge_in[side].at[d], send_sem=edge_send.at[side],
            recv_sem=edge_recv.at[0], device_id=targets[side], device_id_type=MESH,
        )

    order = (4, 3, 5, 2, 6, 1, 7)
    slots = {4: 0, 3: 1, 5: 2}

    def first_copy(k, size=1):
        return stage(
            sent_0.at[pl.ds((d + k) % GROUP if size == 1 else 0, size)],
            got_0.at[pl.ds(d if size == 1 else 0, size)],
            main_send_0.at[0], main_recv_0.at[slots.get(k, 3)], date_peer(k),
        )

    def second_copy(k, size=1):
        return stage(
            sent_1.at[pl.ds((d + k) % GROUP if size == 1 else 0, size)],
            got_1.at[pl.ds(d if size == 1 else 0, size)],
            main_send_1.at[0], main_recv_1.at[0], date_peer(k),
        )

    for k in order:
        first_copy(k).start()

    @pl.when(right_earlier)
    def _():
        edge_copy(0).start()

    cut(1, cutter(1))
    for k in order:
        second_copy(k).start()

    @pl.when(left_earlier)
    def _():
        edge_copy(1).start()

    got_1[d] = sent_1[d]

    @pl.when((d != 0) | (c == 0))
    def _():
        edge_left[...] = jnp.zeros_like(edge_left)

    @pl.when((d != GROUP - 1) | (c == count - 1))
    def _():
        edge_right[...] = jnp.zeros_like(edge_right)


    for table in tables:
        table.wait()
    owner_row = owner_v[...]
    owner_down = jnp.transpose(jnp.broadcast_to(owner_row.astype(F32), (ROWS, PAIRS)))[:, :PAIRS]
    earlier = iota((PAIRS, PAIRS), 0) < iota((PAIRS, PAIRS), 1)
    same = owner_down == owner_row.astype(F32)
    rank = jnp.sum(jnp.where(same & earlier, 1.0, 0.0), axis=0, keepdims=True).astype(jnp.int32)
    place = (rank & 3) * 32 + owner_row * 4 + (rank >> 2)
    one = jnp.where(iota((128, PAIRS), 0) == place, 1.0, 0.0)
    select[...] = jnp.concatenate([one, one, one], axis=1).astype(BF16)
    later = iota((PAIRS, PAIRS), 0) > iota((PAIRS, PAIRS), 1)
    rank_down = jnp.sum(jnp.where(same & later, 1.0, 0.0), axis=1, keepdims=True)
    quarter = (iota((PAIRS, 128), 1) >> 5).astype(F32)
    mine = jnp.where(owner_down[:, :1] == d.astype(F32), rank_down, -1.0)
    for g in range(3):
        own[g] = jnp.where(mine == quarter + 4.0 * g, 1.0, 0.0)

    def date_rows(which):
        date = pairs_v[which : which + 1, :].astype(F32)
        return jnp.transpose(jnp.broadcast_to(date, (ROWS, PAIRS)))

    date = jnp.concatenate([date_rows(0), date_rows(1)], axis=0)
    lane = iota((2 * PAIRS, ROWS), 1)
    first_date = (EACH * (lane & 7)).astype(F32)
    one = jnp.where((date >= first_date) & (date < first_date + EACH) & (lane < 24), 1.0, 0.0)
    hot[...] = one[:, : 3 * GROUP].astype(BF16)
    phase = date - EACH * jnp.floor(date * (1.0 / EACH))
    quarters[...] = jnp.where(phase == (lane >> 5).astype(F32), 1.0, 0.0)
    one = jnp.where((iota((ROWS, 128), 0) >> 2) == (iota((ROWS, 128), 1) & 31), 1.0, 0.0)
    look[...] = jnp.concatenate([one, one, one], axis=0).astype(BF16)

    def edges(side):
        stage(
            edge_in[side], edge_in[side], edge_send.at[side], edge_recv.at[0], targets[side]
        ).wait_recv()

    def smooth_powers(number):
        for t in range(number):
            big, small = split(along_columns(fields, t))
            lhs[HALF * t : HALF * (t + 1), :ROWS] = big
            lhs[HALF * t : HALF * (t + 1), ROWS:] = small
        smooth = dot(lhs[: number * HALF, :], smoother[...])
        return jnp.sqrt(smooth[:, :ROWS] + smooth[:, ROWS:])

    def take_first(sources, ref):
        size = PIECES[0]
        for i, source in enumerate(sources):
            for t in range(EACH):
                piece = ref[source, 2 * size * t : 2 * size * (t + 1), :].astype(F32)
                edge = edge_left[source, 16 * t : 16 * (t + 1), :].astype(F32)
                real = jnp.concatenate([piece[:8] + edge[:8], piece[8:size]], axis=0)
                imag = jnp.concatenate([piece[size : size + 8] + edge[8:], piece[size + 8 :]], axis=0)
                images[source * EACH + t, 0, :size] = real
                images[source * EACH + t, 1, :size] = imag
                fields[EACH * i + t] = real * real + imag * imag
        smooth = smooth_powers(EACH * len(sources))
        for i, source in enumerate(sources):
            for t in range(EACH):
                at = HALF * (EACH * i + t)
                roots[source * EACH + t, :HALF] = smooth[at : at + HALF]

    def arrive(*ks):
        first_copy(ks[0], len(ks)).wait_recv()
        take_first([(d + GROUP - k) % GROUP for k in ks], got_0)

    def take_second():
        size = PIECES[1]
        for date in range(DATES):
            source, t = date // EACH, date % EACH
            piece = got_1[source, 2 * size * t : 2 * size * (t + 1), :].astype(F32)
            edge = edge_right[source, 16 * t : 16 * (t + 1), :].astype(F32)
            real = jnp.concatenate([piece[:8], piece[8:size] + edge[:8]], axis=0)
            imag = jnp.concatenate([piece[size : size + 8], piece[size + 8 :] + edge[8:]], axis=0)
            images[date, 0, PIECES[0] :] = real
            images[date, 1, PIECES[0] :] = imag
            real = jnp.concatenate([images[date, 0, HALF : PIECES[0]], real], axis=0)
            imag = jnp.concatenate([images[date, 1, HALF : PIECES[0]], imag], axis=0)
            fields[date] = real * real + imag * imag
        smooth = smooth_powers(DATES)
        for date in range(DATES):
            roots[date, HALF:] = smooth[HALF * date : HALF * (date + 1)]

    def pairs_of(half, then=None):
        window = slice(HALF * half, HALF * half + WINDOW)

        def place(field, p):
            return pl.ds(((3 * half + field) * PAIRS + p) * 8, 8)

        def chunk(index, carry):
            dates = []
            for i in range(CHUNK):
                p = index * CHUNK + i
                first = pairs_s[0, p]
                second = pairs_s[1, p]
                dates.append((first, second))
                real_a = images[first, 0, window]
                imag_a = images[first, 1, window]
                real_b = images[second, 0, window]
                imag_b = images[second, 1, window]
                fields[2 * i] = real_a * real_b + imag_a * imag_b
                fields[2 * i + 1] = imag_a * real_b - real_a * imag_b
            for i in range(CHUNK):
                p = index * CHUNK + i
                for f in range(2):
                    n = 2 * i + f
                    big, small = split(along_columns(fields, n))
                    lhs[HALF * n : HALF * (n + 1), :ROWS] = big
                    lhs[HALF * n : HALF * (n + 1), ROWS:] = small
                    sums[place(f, p), :] = fields[n, 4:12, :] + fields[n, 12:20, :]
            smooth = dot(lhs[...], smoother[...])
            smooth = smooth[:, :ROWS] + smooth[:, ROWS:]
            for i in range(CHUNK):
                p = index * CHUNK + i
                first, second = dates[i]
                real = smooth[2 * HALF * i : 2 * HALF * i + HALF]
                imag = smooth[2 * HALF * i + HALF : 2 * HALF * (i + 1)]
                below = (
                    roots[first, HALF * half : HALF * (half + 1)]
                    * roots[second, HALF * half : HALF * (half + 1)]
                )
                value = jnp.sqrt(real * real + imag * imag) / (below + 1e-06)
                sums[place(2, p), :] = value[0:8] + value[8:16]
            return carry

        lax.fori_loop(0, PAIRS // CHUNK, chunk, 0)
        if then is not None:
            then()
        rows = sums[pl.ds(3 * half * PAIRS * 8, 3 * PAIRS, stride=8), :]
        for i in range(1, 8):
            rows = rows + sums[pl.ds(3 * half * PAIRS * 8 + i, 3 * PAIRS, stride=8), :]
        looked[half] = dot(jnp.concatenate(split3(rows), axis=1), look[...])

    @pl.when(right_later)
    def _():
        pl.semaphore_wait(ready.at[0], 1)
        edge_copy(0).start()

    @pl.when(left_later)
    def _():
        pl.semaphore_wait(ready.at[1], 1)
        edge_copy(1).start()

    @pl.when((d == 0) & (c > 0))
    def _():
        edges(0)

    take_first([d], sent_0)
    arrive(4)
    arrive(3)
    arrive(5)
    arrive(2, 6, 1, 7)
    pairs_of(0)

    def d_copy(k, size=1):
        return stage(
            totals.at[pl.ds(d if size == 1 else 0, size)], totals.at[pl.ds(d if size == 1 else 0, size)],
            d_send.at[0], d_recv.at[0], date_peer(k),
        )

    def add_up():
        @pl.when(c == 0)
        def _():
            up_copy(1, count - 1).wait_recv()
            total = power_row[...] + jnp.sum(power_in[1:count, :], axis=0, keepdims=True)
            totals[pl.ds(d, 1), :] = total
            for k in order:
                d_copy(k).start()

    @pl.when((d == GROUP - 1) & (c < count - 1))
    def _():
        edges(1)

    second_copy(1, GROUP - 1).wait_recv()
    take_second()
    pairs_of(1, add_up)

    wide = []
    for q in range(6):
        piece = looked[q // 3, PAIRS * (q % 3) : PAIRS * (q % 3 + 1)]
        wide.append(piece if q % 3 < 2 else piece * (1.0 / 64.0))
    stacked = jnp.concatenate(split3(jnp.concatenate(wide, axis=1)), axis=0)
    placed = dot(select[...], stacked)
    lane = iota((32, 128), 1)
    for q in range(6):
        part = placed[:, 128 * q : 128 * (q + 1)]
        value = jnp.where(
            lane < 64,
            jnp.where(lane < 32, part[0:32], part[32:64]),
            jnp.where(lane < 96, part[64:96], part[96:128]),
        )
        for e in range(GROUP):
            results[e, 4 * q : 4 * q + 4, :] = value[4 * e : 4 * e + 4]

    def out_copy(k, size=1):
        return stage(
            results.at[pl.ds((d + k) % GROUP if size == 1 else 0, size)],
            landed.at[pl.ds(d if size == 1 else 0, size)],
            out_send.at[0], out_recv.at[0], date_peer(k),
        )

    for k in order:
        out_copy(k).start()
    landed[d] = results[d]

    @pl.when(c == 0)
    def _():
        d_copy(1, GROUP - 1).wait_recv()
        parts = jnp.concatenate(split3(totals[...]), axis=0)
        total = jnp.sum(dot(hot[...], parts) * quarters[...], axis=1, keepdims=True)
        scale = jnp.sqrt(total / (ROWS * WIDTH * count) + 1e-06)
        factor = (1.0 / 64.0) / (scale[:PAIRS] * scale[PAIRS:])
        factor = jnp.broadcast_to(jnp.concatenate([factor, factor], axis=0), (ROWS, ROWS))
        factor = jnp.transpose(factor)[:1]
        factor_in[...] = factor
        for i in range(near):
            for j in range(count // nz):
                if i + j > 0:
                    down_copy(j * nz + i).start()

    @pl.when(c > 0)
    def _():
        down_copy(0).wait_recv()

    @pl.when(hands_on)
    def _():
        if nz > near:
            pl.semaphore_wait(here, nz - near)
        for i in range(near, nz):
            down_copy(hand - (near - 1) + i).start()

    factor = jnp.transpose(jnp.broadcast_to(factor_in[0:1, :PAIRS], (ROWS, PAIRS)))
    factors = [jnp.sum(own[g] * factor, axis=0, keepdims=True) for g in range(3)]
    out_copy(1, GROUP - 1).wait_recv()
    scaling[...] = jnp.concatenate(factors + [jnp.zeros((5, 128), F32)], axis=0)
    first_copy(1, GROUP - 1).wait_send()
    second_copy(1, GROUP - 1).wait_send()
    out_copy(1, GROUP - 1).wait_send()

    @pl.when(right_later | right_earlier)
    def _():
        edge_copy(0).wait_send()

    @pl.when(left_later | left_earlier)
    def _():
        edge_copy(1).wait_send()

    def sent_down(number):
        stage(
            power_in.at[pl.ds(0, number)], power_in.at[pl.ds(0, number)], down_send.at[0],
            down_recv.at[0], {"dates": d, "cols": c},
        ).wait_send()

    @pl.when(c > 0)
    def _():
        up_copy(c).wait_send()

    @pl.when(c == 0)
    def _():
        d_copy(1, GROUP - 1).wait_send()
        sent_down(near * (count // nz) - 1)

    if nz > near:

        @pl.when(hands_on)
        def _():
            sent_down(nz - near)


def place_kernel(landed, scaling, interferogram, coherence):
    for f in range(3):
        for g in range(3):
            block = landed[pl.ds(f * 4 + g, 16, stride=12), :]
            if f < 2:
                block = block * scaling[g : g + 1, :]
            for j in range(4):
                piece = block[:, 32 * j : 32 * j + 32]
                if f < 2:
                    interferogram[f, 4 * g + j] = piece
                else:
                    coherence[4 * g + j] = piece


def solution(mesh):
    columns = mesh.shape["cols"]
    nz = 8 if columns % 8 == 0 else 2
    sem = pltpu.SemaphoreType.DMA
    vmem = pl.BlockSpec(memory_space=pltpu.VMEM)

    def local(slc, pairs, owner):
        pairs = pairs.T
        owner = owner.reshape(1, PAIRS)
        landed, scaling = pl.pallas_call(
            lambda *refs: kernel(nz, columns, *refs),
            out_shape=(jax.ShapeDtypeStruct((GROUP, 24, 128), F32), jax.ShapeDtypeStruct((8, 128), F32)),
            in_specs=[pl.BlockSpec(memory_space=pl.ANY)] * 3,
            out_specs=(vmem, vmem),
            scratch_shapes=[
                pltpu.VMEM((2, EACH, ROWS, WIDTH), BF16),
                pltpu.SMEM((2, PAIRS), jnp.int32),
                pltpu.VMEM((2, PAIRS), jnp.int32),
                pltpu.VMEM((1, PAIRS), jnp.int32),
                pltpu.VMEM((128, 3 * PAIRS), BF16),
                pltpu.VMEM((3, PAIRS, 128), F32),
                pltpu.VMEM((3 * ROWS, 128), BF16),
                pltpu.VMEM((2 * PAIRS, 3 * GROUP), BF16),
                pltpu.VMEM((2 * PAIRS, ROWS), F32),
                pltpu.VMEM((2 * ROWS, 2 * ROWS), BF16),
                pltpu.VMEM((GROUP, EACH * 2 * PIECES[0], ROWS), BF16),
                pltpu.VMEM((GROUP, EACH * 2 * PIECES[1], ROWS), BF16),
                pltpu.VMEM((GROUP, EACH * 2 * PIECES[0], ROWS), BF16),
                pltpu.VMEM((GROUP, EACH * 2 * PIECES[1], ROWS), BF16),
                pltpu.VMEM((2, EDGE, ROWS), BF16),
                pltpu.VMEM((GROUP, EDGE, ROWS), BF16),
                pltpu.VMEM((GROUP, EDGE, ROWS), BF16),
                pltpu.VMEM((DATES, 2, TILE, ROWS), F32),
                pltpu.VMEM((DATES, PART, ROWS), F32),
                pltpu.VMEM((2 * CHUNK, WINDOW, ROWS), F32),
                pltpu.VMEM((2 * CHUNK * HALF, 2 * ROWS), BF16),
                pltpu.VMEM((6 * PAIRS * 8, ROWS), F32),
                pltpu.VMEM((2, 3 * PAIRS, ROWS), F32),
                pltpu.VMEM((1, ROWS), F32),
                pltpu.VMEM((columns, ROWS), F32),
                pltpu.VMEM((GROUP, ROWS), F32),
                pltpu.VMEM((1, ROWS), F32),
                pltpu.VMEM((GROUP, 24, 128), F32),
                sem((1,)), sem((4,)), sem((1,)), sem((1,)),
                sem((2,)), sem((1,)), pltpu.SemaphoreType.REGULAR((2,)), pltpu.SemaphoreType.REGULAR,
                sem((1,)), sem((1,)), sem((1,)), sem((1,)),
                sem((1,)), sem((1,)), sem((1,)), sem((1,)),
                sem((1,)), sem((3,)),
            ],
            compiler_params=pltpu.CompilerParams(
                collective_id=0, has_side_effects=True, vmem_limit_bytes=54682 * 1024
            ),
        )(slc, pairs, owner)
        interferogram, coherence = pl.pallas_call(
            place_kernel,
            out_shape=(
                jax.ShapeDtypeStruct((2, CAP, 16, 32), F32),
                jax.ShapeDtypeStruct((CAP, 16, 32), F32),
            ),
            in_specs=[vmem, vmem],
            out_specs=(vmem, vmem),
            compiler_params=pltpu.CompilerParams(vmem_limit_bytes=2 * 1024 * 1024),
        )(landed.reshape(GROUP * 24, 128), scaling)
        return jnp.swapaxes(interferogram, 2, 3), jnp.swapaxes(coherence, 1, 2)

    return jax.shard_map(
        local,
        mesh=mesh,
        in_specs=(P(None, "dates", None, "cols"), P(), P()),
        out_specs=(P(None, "dates", None, "cols"), P("dates", None, "cols")),
        check_vma=False,
    )
```

```python
import math

import jax
import jax.numpy as jnp
import ml_dtypes
import numpy as np
from jax import lax
from jax.experimental import pallas as pl
from jax.experimental.pallas import tpu as pltpu
from jax.sharding import PartitionSpec as P

MESH = pl.DeviceIdType.MESH
F32 = jnp.float32
BF16 = jnp.bfloat16

TAPS = [math.exp(-k * k / 8.0) for k in range(-4, 5)]
WEIGHTS = [float(np.float32(t / sum(TAPS))) for t in TAPS]
HIGH = [float(np.float32(w).astype(ml_dtypes.bfloat16)) for w in WEIGHTS]
LOW = [float(np.float32(w - h).astype(ml_dtypes.bfloat16)) for w, h in zip(WEIGHTS, HIGH)]

GROUP = 8
EACH = 4
DATES = GROUP * EACH
PAIRS = 64
CAP = 12
ROWS = 128
PART = 32
TILE = PART + 8
WIDTH = GROUP * PART
PIECES = (24, 16)
HALF = PART // 2
WINDOW = HALF + 8
EDGE = EACH * 2 * 8
CHUNK = 16


def split(x):
    high = x.astype(BF16)
    return high, (x - high.astype(F32)).astype(BF16)


def split3(x):
    high = x.astype(BF16)
    rest = x - high.astype(F32)
    mid = rest.astype(BF16)
    return high, mid, (rest - mid.astype(F32)).astype(BF16)


def dot(a, b):
    return jnp.dot(a, b, preferred_element_type=F32)


def iota(shape, axis):
    return lax.broadcasted_iota(jnp.int32, shape, axis)


def cutter(half):
    start, size = (-4, PIECES[0]) if half == 0 else (PIECES[0] - 4, PIECES[1])
    lane = iota((size, WIDTH), 1)
    row = iota((size, WIDTH), 0)
    pieces = [jnp.where(lane == row + (PART * e + start), 1.0, 0.0) for e in range(GROUP)]
    lane = iota((8, WIDTH), 1)
    row = iota((8, WIDTH), 0)
    pieces.append(jnp.where(lane == row + (WIDTH - 4 if half == 0 else -4), 1.0, 0.0))
    return jnp.concatenate(pieces, axis=0).astype(BF16)


def band(weights):
    gap = jnp.abs(iota((ROWS, ROWS), 0) - iota((ROWS, ROWS), 1))
    result = jnp.zeros((ROWS, ROWS), F32)
    for k in range(5):
        result = jnp.where(gap == k, weights[4 + k], result)
    return result.astype(BF16)


def along_columns(ref, index):
    result = WEIGHTS[4] * ref[index, 4 : 4 + HALF, :]
    for k in range(4):
        both = ref[index, k : k + HALF, :] + ref[index, 8 - k : 8 - k + HALF, :]
        result = result + WEIGHTS[k] * both
    return result


def kernel(
    nz, count, slc_hbm, pairs_hbm, owner_hbm, landed, scaling,
    slc, pairs_s, pairs_v, owner_v, select, own, look, hot, source_of, smoother, sent_0, sent_1, got_0, got_1,
    edge_out, edge_left, edge_right, images, roots, fields, lhs, sums, looked,
    power_row, power_in, totals, factor_in, results,
    main_send_0, main_recv_0, main_send_1, main_recv_1, edge_send, edge_recv, ready,
    here, up_send, up_recv, down_send, down_recv, d_send, d_recv, out_send, out_recv, in_sem, table_sem,
):
    load = pltpu.make_async_copy(slc_hbm, slc, in_sem.at[0])
    load.start()

    d = lax.axis_index("dates")
    c = lax.axis_index("cols")
    z = c % nz

    def date_peer(k):
        return {"dates": (d + k) % GROUP, "cols": c}

    right = (c + 1) % count
    left = (c + count - 1) % count
    near = min(3, nz)
    right_later = (z < nz - 1) & (c < count - 1)
    right_earlier = (z == nz - 1) & (c < count - 1)
    left_later = (z == 0) & (c > 0)
    left_earlier = (z > 0) & (c > 0)

    barrier = pltpu.get_barrier_semaphore()

    def greet(device):
        pl.semaphore_signal(barrier, inc=1, device_id=device, device_id_type=MESH)

    for k in range(1, GROUP):
        greet(date_peer(k))

    def greet_neighbour(later, receiver, other):
        @pl.when(later)
        def _():
            greet({"dates": receiver, "cols": other})

        @pl.when(later & (d == GROUP - 1 - receiver))
        def _():
            for e in range(GROUP):
                greet({"dates": e, "cols": other})

    greet_neighbour(right_later, 0, right)
    greet_neighbour(left_later, GROUP - 1, left)

    @pl.when(c == 0)
    def _():
        def one(i, carry):
            greet({"dates": d, "cols": i})
            return carry

        lax.fori_loop(1, count, one, 0)

    hands_on = z == near - 1
    handed = z >= near
    hand = c - z + near - 1

    @pl.when(hands_on)
    def _():
        for i in range(near, nz):
            greet({"dates": d, "cols": hand - (near - 1) + i})

    tables = [
        pltpu.make_async_copy(pairs_hbm, pairs_s, table_sem.at[0]),
        pltpu.make_async_copy(pairs_hbm, pairs_v, table_sem.at[1]),
        pltpu.make_async_copy(owner_hbm, owner_v, table_sem.at[2]),
    ]
    for table in tables:
        table.start()

    sent = (sent_0, sent_1)
    edge_in = (edge_left, edge_right)
    got = (got_0, got_1)

    def cut(half, matrix):
        size = PIECES[half]
        for t in range(EACH):
            both = jnp.concatenate([slc[0, t], slc[1, t]], axis=0)
            turned = lax.dot_general(
                matrix, both, (((1,), (1,)), ((), ())), preferred_element_type=F32
            )
            for e in range(GROUP + 1):
                rows = turned[size * e : size * (e + 1)] if e < GROUP else turned[size * GROUP :]
                value = jnp.concatenate([rows[:, :ROWS], rows[:, ROWS:]], axis=0).astype(BF16)
                if e < GROUP:
                    sent[half][e, 2 * size * t : 2 * size * (t + 1), :] = value
                else:
                    edge_out[half, 16 * t : 16 * (t + 1), :] = value

    matrix = cutter(0)
    high = band(HIGH)
    low = band(LOW)
    smoother[:, :ROWS] = jnp.concatenate([high, high], axis=0)
    smoother[:, ROWS:] = jnp.concatenate([low, low], axis=0)
    load.wait()
    power_rows = []
    for t in range(EACH):
        wide = jnp.concatenate([slc[0, t], slc[1, t]], axis=0).astype(F32)
        square = jnp.sum(wide * wide, axis=0, keepdims=True)
        power_rows.append(square[:, :ROWS] + square[:, ROWS:])
    folded = jnp.concatenate(power_rows + [jnp.zeros((8 - EACH, ROWS), F32)], axis=0)
    folded = folded + pltpu.roll(folded, 64, 1)
    folded = folded + pltpu.roll(folded, 32, 1)
    own_lane = (iota((8, ROWS), 1) >> 5) == iota((8, ROWS), 0)
    power_row[...] = jnp.sum(jnp.where(own_lane, folded, 0.0), axis=0, keepdims=True)

    def stage(src, dst, send, recv, peer):
        return pltpu.make_async_remote_copy(
            src_ref=src, dst_ref=dst, send_sem=send, recv_sem=recv, device_id=peer, device_id_type=MESH
        )

    def up_copy(i, size=1):
        return stage(
            power_in.at[pl.ds(0, size)] if size > 1 else power_row, power_in.at[pl.ds(i, size)],
            up_send.at[0], up_recv.at[0], {"dates": d, "cols": 0},
        )

    def down_copy(i):
        return stage(factor_in, factor_in, down_send.at[0], down_recv.at[0], {"dates": d, "cols": i})

    first = (d == 0).astype(jnp.int32)
    last = (d == GROUP - 1).astype(jnp.int32)

    def enter():
        pl.semaphore_wait(
            barrier,
            (GROUP - 1)
            + (c > 0).astype(jnp.int32)
            + handed.astype(jnp.int32)
            + right_earlier.astype(jnp.int32) * (1 + GROUP * last)
            + left_earlier.astype(jnp.int32) * (1 + GROUP * first),
        )

        def tell_ready(side, condition, other):
            @pl.when(condition)
            def _():
                for e in range(GROUP):
                    pl.semaphore_signal(
                        ready.at[side], inc=1, device_id={"dates": e, "cols": other}, device_id_type=MESH
                    )

        @pl.when(handed)
        def _():
            pl.semaphore_signal(
                here, inc=1, device_id={"dates": d, "cols": hand}, device_id_type=MESH
            )

        tell_ready(0, left_earlier & (d == 0), left)
        tell_ready(1, right_earlier & (d == GROUP - 1), right)

        @pl.when(c > 0)
        def _():
            up_copy(c).start()

    pl.when(z >= nz // 2)(enter)
    cut(0, matrix)
    pl.when(z < nz // 2)(enter)

    targets = ({"dates": 0, "cols": right}, {"dates": GROUP - 1, "cols": left})

    def edge_copy(side):
        return pltpu.make_async_remote_copy(
            src_ref=edge_out.at[side], dst_ref=edge_in[side].at[d], send_sem=edge_send.at[side],
            recv_sem=edge_recv.at[0], device_id=targets[side], device_id_type=MESH,
        )

    order = (4, 3, 5, 2, 6, 1, 7)
    slots = {4: 0, 3: 1, 5: 2}

    def first_copy(k, size=1):
        return stage(
            sent_0.at[pl.ds((d + k) % GROUP if size == 1 else 0, size)],
            got_0.at[pl.ds(d if size == 1 else 0, size)],
            main_send_0.at[0], main_recv_0.at[slots.get(k, 3)], date_peer(k),
        )

    def second_copy(k, size=1):
        return stage(
            sent_1.at[pl.ds((d + k) % GROUP if size == 1 else 0, size)],
            got_1.at[pl.ds(d if size == 1 else 0, size)],
            main_send_1.at[0], main_recv_1.at[0], date_peer(k),
        )

    for k in order:
        first_copy(k).start()

    @pl.when(right_earlier)
    def _():
        edge_copy(0).start()

    cut(1, cutter(1))
    for k in order:
        second_copy(k).start()

    @pl.when(left_earlier)
    def _():
        edge_copy(1).start()

    got_1[d] = sent_1[d]

    @pl.when((d != 0) | (c == 0))
    def _():
        edge_left[...] = jnp.zeros_like(edge_left)

    @pl.when((d != GROUP - 1) | (c == count - 1))
    def _():
        edge_right[...] = jnp.zeros_like(edge_right)


    for table in tables:
        table.wait()
    owner_row = owner_v[...]
    owner_down = jnp.transpose(jnp.broadcast_to(owner_row.astype(F32), (ROWS, PAIRS)))[:, :PAIRS]
    earlier = iota((PAIRS, PAIRS), 0) < iota((PAIRS, PAIRS), 1)
    same = owner_down == owner_row.astype(F32)
    rank = jnp.sum(jnp.where(same & earlier, 1.0, 0.0), axis=0, keepdims=True).astype(jnp.int32)
    place = (rank & 3) * 32 + owner_row * 4 + (rank >> 2)
    one = jnp.where(iota((128, PAIRS), 0) == place, 1.0, 0.0)
    select[...] = jnp.concatenate([one, one, one], axis=1).astype(BF16)
    later = iota((PAIRS, PAIRS), 0) > iota((PAIRS, PAIRS), 1)
    rank_down = jnp.sum(jnp.where(same & later, 1.0, 0.0), axis=1, keepdims=True)
    quarter = (iota((PAIRS, 128), 1) >> 5).astype(F32)
    mine = jnp.where(owner_down[:, :1] == d.astype(F32), rank_down, -1.0)
    masks = [jnp.where(mine == quarter + 4.0 * g, 1.0, 0.0) for g in range(3)]
    masks = jnp.concatenate(masks, axis=1)
    own[...] = jnp.concatenate([masks, jnp.zeros_like(masks)], axis=0).astype(BF16)

    date = jnp.concatenate([pairs_v[0:1, :], pairs_v[1:2, :]], axis=1)
    one = jnp.where((iota((ROWS, 2 * PAIRS), 0) >> 5) == (date & (EACH - 1)), 1.0, 0.0)
    hot[...] = jnp.concatenate([one, one, one], axis=0).astype(BF16)
    source_of[...] = jnp.where(iota((GROUP, 2 * PAIRS), 0) == (date >> 2), 1.0, 0.0)
    one = jnp.where((iota((ROWS, 128), 0) >> 2) == (iota((ROWS, 128), 1) & 31), 1.0, 0.0)
    look[...] = jnp.concatenate([one, one, one], axis=0).astype(BF16)

    def edges(side):
        stage(
            edge_in[side], edge_in[side], edge_send.at[side], edge_recv.at[0], targets[side]
        ).wait_recv()

    def smooth_powers(number):
        for t in range(number):
            big, small = split(along_columns(fields, t))
            lhs[HALF * t : HALF * (t + 1), :ROWS] = big
            lhs[HALF * t : HALF * (t + 1), ROWS:] = small
        smooth = dot(lhs[: number * HALF, :], smoother[...])
        return jnp.sqrt(smooth[:, :ROWS] + smooth[:, ROWS:])

    def take_first(sources, ref):
        size = PIECES[0]
        for i, source in enumerate(sources):
            for t in range(EACH):
                piece = ref[source, 2 * size * t : 2 * size * (t + 1), :].astype(F32)
                edge = edge_left[source, 16 * t : 16 * (t + 1), :].astype(F32)
                real = jnp.concatenate([piece[:8] + edge[:8], piece[8:size]], axis=0)
                imag = jnp.concatenate([piece[size : size + 8] + edge[8:], piece[size + 8 :]], axis=0)
                images[source * EACH + t, 0, :size] = real
                images[source * EACH + t, 1, :size] = imag
                fields[EACH * i + t] = real * real + imag * imag
        smooth = smooth_powers(EACH * len(sources))
        for i, source in enumerate(sources):
            for t in range(EACH):
                at = HALF * (EACH * i + t)
                roots[source * EACH + t, :HALF] = smooth[at : at + HALF]

    def arrive(*ks):
        first_copy(ks[0], len(ks)).wait_recv()
        take_first([(d + GROUP - k) % GROUP for k in ks], got_0)

    def take_second():
        size = PIECES[1]
        for date in range(DATES):
            source, t = date // EACH, date % EACH
            piece = got_1[source, 2 * size * t : 2 * size * (t + 1), :].astype(F32)
            edge = edge_right[source, 16 * t : 16 * (t + 1), :].astype(F32)
            real = jnp.concatenate([piece[:8], piece[8:size] + edge[:8]], axis=0)
            imag = jnp.concatenate([piece[size : size + 8], piece[size + 8 :] + edge[8:]], axis=0)
            images[date, 0, PIECES[0] :] = real
            images[date, 1, PIECES[0] :] = imag
            real = jnp.concatenate([images[date, 0, HALF : PIECES[0]], real], axis=0)
            imag = jnp.concatenate([images[date, 1, HALF : PIECES[0]], imag], axis=0)
            fields[date] = real * real + imag * imag
        smooth = smooth_powers(DATES)
        for date in range(DATES):
            roots[date, HALF:] = smooth[HALF * date : HALF * (date + 1)]

    def pairs_of(half, then=None):
        window = slice(HALF * half, HALF * half + WINDOW)

        def place(field, p):
            return pl.ds(((3 * half + field) * PAIRS + p) * 8, 8)

        def chunk(index, carry):
            dates = []
            for i in range(CHUNK):
                p = index * CHUNK + i
                first = pairs_s[0, p]
                second = pairs_s[1, p]
                dates.append((first, second))
                real_a = images[first, 0, window]
                imag_a = images[first, 1, window]
                real_b = images[second, 0, window]
                imag_b = images[second, 1, window]
                fields[2 * i] = real_a * real_b + imag_a * imag_b
                fields[2 * i + 1] = imag_a * real_b - real_a * imag_b
            for i in range(CHUNK):
                p = index * CHUNK + i
                for f in range(2):
                    n = 2 * i + f
                    big, small = split(along_columns(fields, n))
                    lhs[HALF * n : HALF * (n + 1), :ROWS] = big
                    lhs[HALF * n : HALF * (n + 1), ROWS:] = small
                    sums[place(f, p), :] = fields[n, 4:12, :] + fields[n, 12:20, :]
            smooth = dot(lhs[...], smoother[...])
            smooth = smooth[:, :ROWS] + smooth[:, ROWS:]
            for i in range(CHUNK):
                p = index * CHUNK + i
                first, second = dates[i]
                real = smooth[2 * HALF * i : 2 * HALF * i + HALF]
                imag = smooth[2 * HALF * i + HALF : 2 * HALF * (i + 1)]
                below = (
                    roots[first, HALF * half : HALF * (half + 1)]
                    * roots[second, HALF * half : HALF * (half + 1)]
                )
                value = jnp.sqrt(real * real + imag * imag) / (below + 1e-06)
                sums[place(2, p), :] = value[0:8] + value[8:16]
            return carry

        lax.fori_loop(0, PAIRS // CHUNK, chunk, 0)
        if then is not None:
            then()
        rows = sums[pl.ds(3 * half * PAIRS * 8, 3 * PAIRS, stride=8), :]
        for i in range(1, 8):
            rows = rows + sums[pl.ds(3 * half * PAIRS * 8 + i, 3 * PAIRS, stride=8), :]
        looked[half] = dot(jnp.concatenate(split3(rows), axis=1), look[...])

    @pl.when(right_later)
    def _():
        pl.semaphore_wait(ready.at[0], 1)
        edge_copy(0).start()

    @pl.when(left_later)
    def _():
        pl.semaphore_wait(ready.at[1], 1)
        edge_copy(1).start()

    @pl.when((d == 0) & (c > 0))
    def _():
        edges(0)

    take_first([d], sent_0)
    arrive(4)
    arrive(3)
    arrive(5)
    arrive(2, 6, 1, 7)
    pairs_of(0)

    def d_copy(k, size=1):
        return stage(
            totals.at[pl.ds(d if size == 1 else 0, size)], totals.at[pl.ds(d if size == 1 else 0, size)],
            d_send.at[0], d_recv.at[0], date_peer(k),
        )

    def add_up():
        @pl.when(c == 0)
        def _():
            up_copy(1, count - 1).wait_recv()
            total = power_row[...] + jnp.sum(power_in[1:count, :], axis=0, keepdims=True)
            totals[pl.ds(d, 1), :] = total
            for k in order:
                d_copy(k).start()

    @pl.when((d == GROUP - 1) & (c < count - 1))
    def _():
        edges(1)

    second_copy(1, GROUP - 1).wait_recv()
    take_second()
    pairs_of(1, add_up)

    wide = []
    for q in range(6):
        piece = looked[q // 3, PAIRS * (q % 3) : PAIRS * (q % 3 + 1)]
        wide.append(piece if q % 3 < 2 else piece * (1.0 / 64.0))
    stacked = jnp.concatenate(split3(jnp.concatenate(wide, axis=1)), axis=0)
    placed = dot(select[...], stacked)
    lane = iota((32, 128), 1)
    for q in range(6):
        part = placed[:, 128 * q : 128 * (q + 1)]
        value = jnp.where(
            lane < 64,
            jnp.where(lane < 32, part[0:32], part[32:64]),
            jnp.where(lane < 96, part[64:96], part[96:128]),
        )
        for e in range(GROUP):
            results[e, 4 * q : 4 * q + 4, :] = value[4 * e : 4 * e + 4]

    def out_copy(k, size=1):
        return stage(
            results.at[pl.ds((d + k) % GROUP if size == 1 else 0, size)],
            landed.at[pl.ds(d if size == 1 else 0, size)],
            out_send.at[0], out_recv.at[0], date_peer(k),
        )

    for k in order:
        out_copy(k).start()
    landed[d] = results[d]

    @pl.when(c == 0)
    def _():
        d_copy(1, GROUP - 1).wait_recv()
        parts = jnp.concatenate(split3(totals[...]), axis=1)
        total = jnp.sum(dot(parts, hot[...]) * source_of[...], axis=0, keepdims=True)
        scale = jnp.sqrt(total / (ROWS * WIDTH * count) + 1e-06)
        factor = (1.0 / 64.0) / (scale * pltpu.roll(scale, PAIRS, 1))
        factor_in[...] = factor
        for i in range(near):
            for j in range(count // nz):
                if i + j > 0:
                    down_copy(j * nz + i).start()

    @pl.when(c > 0)
    def _():
        down_copy(0).wait_recv()

    @pl.when(hands_on)
    def _():
        if nz > near:
            pl.semaphore_wait(here, nz - near)
        for i in range(near, nz):
            down_copy(hand - (near - 1) + i).start()

    factors = dot(jnp.concatenate(split3(factor_in[...]), axis=0), own[...])
    factors = jnp.sum(factors, axis=0, keepdims=True)
    for g in range(3):
        scaling[g : g + 1, :] = factors[:, 128 * g : 128 * (g + 1)]
    out_copy(1, GROUP - 1).wait_recv()
    first_copy(1, GROUP - 1).wait_send()
    second_copy(1, GROUP - 1).wait_send()
    out_copy(1, GROUP - 1).wait_send()

    @pl.when(right_later | right_earlier)
    def _():
        edge_copy(0).wait_send()

    @pl.when(left_later | left_earlier)
    def _():
        edge_copy(1).wait_send()

    def sent_down(number):
        stage(
            power_in.at[pl.ds(0, number)], power_in.at[pl.ds(0, number)], down_send.at[0],
            down_recv.at[0], {"dates": d, "cols": c},
        ).wait_send()

    @pl.when(c > 0)
    def _():
        up_copy(c).wait_send()

    @pl.when(c == 0)
    def _():
        d_copy(1, GROUP - 1).wait_send()
        sent_down(near * (count // nz) - 1)

    if nz > near:

        @pl.when(hands_on)
        def _():
            sent_down(nz - near)


def place_kernel(landed, scaling, interferogram, coherence):
    for f in range(3):
        for g in range(3):
            block = landed[pl.ds(f * 4 + g, 16, stride=12), :]
            if f < 2:
                block = block * scaling[g : g + 1, :]
            for j in range(4):
                piece = block[:, 32 * j : 32 * j + 32]
                if f < 2:
                    interferogram[f, 4 * g + j] = piece
                else:
                    coherence[4 * g + j] = piece


def solution(mesh):
    columns = mesh.shape["cols"]
    nz = 8 if columns % 8 == 0 else 2
    sem = pltpu.SemaphoreType.DMA
    vmem = pl.BlockSpec(memory_space=pltpu.VMEM)

    def local(slc, pairs, owner):
        pairs = pairs.T
        owner = owner.reshape(1, PAIRS)
        landed, scaling = pl.pallas_call(
            lambda *refs: kernel(nz, columns, *refs),
            out_shape=(jax.ShapeDtypeStruct((GROUP, 24, 128), F32), jax.ShapeDtypeStruct((8, 128), F32)),
            in_specs=[pl.BlockSpec(memory_space=pl.ANY)] * 3,
            out_specs=(vmem, vmem),
            scratch_shapes=[
                pltpu.VMEM((2, EACH, ROWS, WIDTH), BF16),
                pltpu.SMEM((2, PAIRS), jnp.int32),
                pltpu.VMEM((2, PAIRS), jnp.int32),
                pltpu.VMEM((1, PAIRS), jnp.int32),
                pltpu.VMEM((128, 3 * PAIRS), BF16),
                pltpu.VMEM((128, 3 * 128), BF16),
                pltpu.VMEM((3 * ROWS, 128), BF16),
                pltpu.VMEM((3 * ROWS, 2 * PAIRS), BF16),
                pltpu.VMEM((GROUP, 2 * PAIRS), F32),
                pltpu.VMEM((2 * ROWS, 2 * ROWS), BF16),
                pltpu.VMEM((GROUP, EACH * 2 * PIECES[0], ROWS), BF16),
                pltpu.VMEM((GROUP, EACH * 2 * PIECES[1], ROWS), BF16),
                pltpu.VMEM((GROUP, EACH * 2 * PIECES[0], ROWS), BF16),
                pltpu.VMEM((GROUP, EACH * 2 * PIECES[1], ROWS), BF16),
                pltpu.VMEM((2, EDGE, ROWS), BF16),
                pltpu.VMEM((GROUP, EDGE, ROWS), BF16),
                pltpu.VMEM((GROUP, EDGE, ROWS), BF16),
                pltpu.VMEM((DATES, 2, TILE, ROWS), F32),
                pltpu.VMEM((DATES, PART, ROWS), F32),
                pltpu.VMEM((2 * CHUNK, WINDOW, ROWS), F32),
                pltpu.VMEM((2 * CHUNK * HALF, 2 * ROWS), BF16),
                pltpu.VMEM((6 * PAIRS * 8, ROWS), F32),
                pltpu.VMEM((2, 3 * PAIRS, ROWS), F32),
                pltpu.VMEM((1, ROWS), F32),
                pltpu.VMEM((columns, ROWS), F32),
                pltpu.VMEM((GROUP, ROWS), F32),
                pltpu.VMEM((1, ROWS), F32),
                pltpu.VMEM((GROUP, 24, 128), F32),
                sem((1,)), sem((4,)), sem((1,)), sem((1,)),
                sem((2,)), sem((1,)), pltpu.SemaphoreType.REGULAR((2,)), pltpu.SemaphoreType.REGULAR,
                sem((1,)), sem((1,)), sem((1,)), sem((1,)),
                sem((1,)), sem((1,)), sem((1,)), sem((1,)),
                sem((1,)), sem((3,)),
            ],
            compiler_params=pltpu.CompilerParams(
                collective_id=0, has_side_effects=True, vmem_limit_bytes=54682 * 1024
            ),
        )(slc, pairs, owner)
        interferogram, coherence = pl.pallas_call(
            place_kernel,
            out_shape=(
                jax.ShapeDtypeStruct((2, CAP, 16, 32), F32),
                jax.ShapeDtypeStruct((CAP, 16, 32), F32),
            ),
            in_specs=[vmem, vmem],
            out_specs=(vmem, vmem),
            compiler_params=pltpu.CompilerParams(vmem_limit_bytes=2 * 1024 * 1024),
        )(landed.reshape(GROUP * 24, 128), scaling)
        return jnp.swapaxes(interferogram, 2, 3), jnp.swapaxes(coherence, 1, 2)

    return jax.shard_map(
        local,
        mesh=mesh,
        in_specs=(P(None, "dates", None, "cols"), P(), P()),
        out_specs=(P(None, "dates", None, "cols"), P("dates", None, "cols")),
        check_vma=False,
    )
```

```python
import math

import jax
import jax.numpy as jnp
import ml_dtypes
import numpy as np
from jax import lax
from jax.experimental import pallas as pl
from jax.experimental.pallas import tpu as pltpu
from jax.sharding import PartitionSpec as P

MESH = pl.DeviceIdType.MESH
F32 = jnp.float32
BF16 = jnp.bfloat16

TAPS = [math.exp(-k * k / 8.0) for k in range(-4, 5)]
WEIGHTS = [float(np.float32(t / sum(TAPS))) for t in TAPS]
HIGH = [float(np.float32(w).astype(ml_dtypes.bfloat16)) for w in WEIGHTS]
LOW = [float(np.float32(w - h).astype(ml_dtypes.bfloat16)) for w, h in zip(WEIGHTS, HIGH)]

GROUP = 8
EACH = 4
DATES = GROUP * EACH
PAIRS = 64
CAP = 12
ROWS = 128
PART = 32
TILE = PART + 8
WIDTH = GROUP * PART
PIECES = (24, 16)
HALF = PART // 2
WINDOW = HALF + 8
EDGE = EACH * 2 * 8
CHUNK = 32


def split(x):
    high = x.astype(BF16)
    return high, (x - high.astype(F32)).astype(BF16)


def split3(x):
    high = x.astype(BF16)
    rest = x - high.astype(F32)
    mid = rest.astype(BF16)
    return high, mid, (rest - mid.astype(F32)).astype(BF16)


def dot(a, b):
    return jnp.dot(a, b, preferred_element_type=F32)


def iota(shape, axis):
    return lax.broadcasted_iota(jnp.int32, shape, axis)


def cutter(half):
    start, size = (-4, PIECES[0]) if half == 0 else (PIECES[0] - 4, PIECES[1])
    lane = iota((size, WIDTH), 1)
    row = iota((size, WIDTH), 0)
    pieces = [jnp.where(lane == row + (PART * e + start), 1.0, 0.0) for e in range(GROUP)]
    lane = iota((8, WIDTH), 1)
    row = iota((8, WIDTH), 0)
    pieces.append(jnp.where(lane == row + (WIDTH - 4 if half == 0 else -4), 1.0, 0.0))
    return jnp.concatenate(pieces, axis=0).astype(BF16)


def band(weights):
    gap = jnp.abs(iota((ROWS, ROWS), 0) - iota((ROWS, ROWS), 1))
    result = jnp.zeros((ROWS, ROWS), F32)
    for k in range(5):
        result = jnp.where(gap == k, weights[4 + k], result)
    return result.astype(BF16)


def along_columns(ref, index):
    result = WEIGHTS[4] * ref[index, 4 : 4 + HALF, :]
    for k in range(4):
        both = ref[index, k : k + HALF, :] + ref[index, 8 - k : 8 - k + HALF, :]
        result = result + WEIGHTS[k] * both
    return result


def kernel(
    nz, count, slc_hbm, pairs_hbm, owner_hbm, landed, scaling,
    slc, pairs_s, pairs_v, owner_v, select, own, look, hot, source_of, smoother, sent_0, sent_1, got_0, got_1,
    edge_out, edge_left, edge_right, images, roots, fields, lhs, sums, looked,
    power_row, power_in, totals, results,
    main_send_0, main_recv_0, main_send_1, main_recv_1, edge_send, edge_recv, ready,
    here, up_send, up_recv, down_send, down_recv, d_send, d_recv, out_send, out_recv, in_sem, table_sem,
):
    load = pltpu.make_async_copy(slc_hbm, slc, in_sem.at[0])
    load.start()

    d = lax.axis_index("dates")
    c = lax.axis_index("cols")
    z = c % nz

    def date_peer(k):
        return {"dates": (d + k) % GROUP, "cols": c}

    right = (c + 1) % count
    left = (c + count - 1) % count
    near = min(3, nz)
    right_later = (z < nz - 1) & (c < count - 1)
    right_earlier = (z == nz - 1) & (c < count - 1)
    left_later = (z == 0) & (c > 0)
    left_earlier = (z > 0) & (c > 0)

    barrier = pltpu.get_barrier_semaphore()

    def greet(device):
        pl.semaphore_signal(barrier, inc=1, device_id=device, device_id_type=MESH)

    for k in range(1, GROUP):
        greet(date_peer(k))

    def greet_neighbour(later, receiver, other):
        @pl.when(later)
        def _():
            greet({"dates": receiver, "cols": other})

        @pl.when(later & (d == GROUP - 1 - receiver))
        def _():
            for e in range(GROUP):
                greet({"dates": e, "cols": other})

    greet_neighbour(right_later, 0, right)
    greet_neighbour(left_later, GROUP - 1, left)

    @pl.when(c == 0)
    def _():
        def one(i, carry):
            greet({"dates": d, "cols": i})
            return carry

        lax.fori_loop(1, count, one, 0)

    hands_on = z == near - 1
    handed = z >= near
    hand = c - z + near - 1

    @pl.when(hands_on)
    def _():
        for i in range(near, nz):
            greet({"dates": d, "cols": hand - (near - 1) + i})

    tables = [
        pltpu.make_async_copy(pairs_hbm, pairs_s, table_sem.at[0]),
        pltpu.make_async_copy(pairs_hbm, pairs_v, table_sem.at[1]),
        pltpu.make_async_copy(owner_hbm, owner_v, table_sem.at[2]),
    ]
    for table in tables:
        table.start()

    sent = (sent_0, sent_1)
    edge_in = (edge_left, edge_right)
    got = (got_0, got_1)

    def cut(half, matrix):
        size = PIECES[half]
        for t in range(EACH):
            both = jnp.concatenate([slc[0, t], slc[1, t]], axis=0)
            turned = lax.dot_general(
                matrix, both, (((1,), (1,)), ((), ())), preferred_element_type=F32
            )
            for e in range(GROUP + 1):
                rows = turned[size * e : size * (e + 1)] if e < GROUP else turned[size * GROUP :]
                value = jnp.concatenate([rows[:, :ROWS], rows[:, ROWS:]], axis=0).astype(BF16)
                if e < GROUP:
                    sent[half][e, 2 * size * t : 2 * size * (t + 1), :] = value
                else:
                    edge_out[half, 16 * t : 16 * (t + 1), :] = value

    matrix = cutter(0)
    high = band(HIGH)
    low = band(LOW)
    smoother[:, :ROWS] = jnp.concatenate([high, high], axis=0)
    smoother[:, ROWS:] = jnp.concatenate([low, low], axis=0)
    load.wait()
    power_rows = []
    for t in range(EACH):
        wide = jnp.concatenate([slc[0, t], slc[1, t]], axis=0).astype(F32)
        square = jnp.sum(wide * wide, axis=0, keepdims=True)
        power_rows.append(square[:, :ROWS] + square[:, ROWS:])
    folded = jnp.concatenate(power_rows + [jnp.zeros((8 - EACH, ROWS), F32)], axis=0)
    folded = folded + pltpu.roll(folded, 64, 1)
    folded = folded + pltpu.roll(folded, 32, 1)
    own_lane = (iota((8, ROWS), 1) >> 5) == iota((8, ROWS), 0)
    power_row[...] = jnp.sum(jnp.where(own_lane, folded, 0.0), axis=0, keepdims=True)

    def stage(src, dst, send, recv, peer):
        return pltpu.make_async_remote_copy(
            src_ref=src, dst_ref=dst, send_sem=send, recv_sem=recv, device_id=peer, device_id_type=MESH
        )

    def up_copy(i, size=1):
        return stage(
            power_in.at[pl.ds(0, size)] if size > 1 else power_row, power_in.at[pl.ds(i, size)],
            up_send.at[0], up_recv.at[0], {"dates": d, "cols": 0},
        )

    def down_copy(i):
        return stage(scaling, scaling, down_send.at[0], down_recv.at[0], {"dates": d, "cols": i})

    first = (d == 0).astype(jnp.int32)
    last = (d == GROUP - 1).astype(jnp.int32)

    def enter():
        pl.semaphore_wait(
            barrier,
            (GROUP - 1)
            + (c > 0).astype(jnp.int32)
            + handed.astype(jnp.int32)
            + right_earlier.astype(jnp.int32) * (1 + GROUP * last)
            + left_earlier.astype(jnp.int32) * (1 + GROUP * first),
        )

        def tell_ready(side, condition, other):
            @pl.when(condition)
            def _():
                for e in range(GROUP):
                    pl.semaphore_signal(
                        ready.at[side], inc=1, device_id={"dates": e, "cols": other}, device_id_type=MESH
                    )

        @pl.when(handed)
        def _():
            pl.semaphore_signal(
                here, inc=1, device_id={"dates": d, "cols": hand}, device_id_type=MESH
            )

        tell_ready(0, left_earlier & (d == 0), left)
        tell_ready(1, right_earlier & (d == GROUP - 1), right)

        @pl.when(c > 0)
        def _():
            up_copy(c).start()

    pl.when(z >= nz // 2)(enter)
    cut(0, matrix)
    pl.when(z < nz // 2)(enter)

    targets = ({"dates": 0, "cols": right}, {"dates": GROUP - 1, "cols": left})

    def edge_copy(side):
        return pltpu.make_async_remote_copy(
            src_ref=edge_out.at[side], dst_ref=edge_in[side].at[d], send_sem=edge_send.at[side],
            recv_sem=edge_recv.at[0], device_id=targets[side], device_id_type=MESH,
        )

    order = (4, 3, 5, 2, 6, 1, 7)
    slots = {4: 0, 3: 1, 5: 2}

    def first_copy(k, size=1):
        return stage(
            sent_0.at[pl.ds((d + k) % GROUP if size == 1 else 0, size)],
            got_0.at[pl.ds(d if size == 1 else 0, size)],
            main_send_0.at[0], main_recv_0.at[slots.get(k, 3)], date_peer(k),
        )

    def second_copy(k, size=1):
        return stage(
            sent_1.at[pl.ds((d + k) % GROUP if size == 1 else 0, size)],
            got_1.at[pl.ds(d if size == 1 else 0, size)],
            main_send_1.at[0], main_recv_1.at[0], date_peer(k),
        )

    for k in order:
        first_copy(k).start()

    @pl.when(right_earlier)
    def _():
        edge_copy(0).start()

    cut(1, cutter(1))
    for k in order:
        second_copy(k).start()

    @pl.when(left_earlier)
    def _():
        edge_copy(1).start()

    got_1[d] = sent_1[d]

    @pl.when((d != 0) | (c == 0))
    def _():
        edge_left[...] = jnp.zeros_like(edge_left)

    @pl.when((d != GROUP - 1) | (c == count - 1))
    def _():
        edge_right[...] = jnp.zeros_like(edge_right)


    for table in tables:
        table.wait()
    owner_row = owner_v[...]
    owner_down = jnp.transpose(jnp.broadcast_to(owner_row.astype(F32), (ROWS, PAIRS)))[:, :PAIRS]
    earlier = iota((PAIRS, PAIRS), 0) < iota((PAIRS, PAIRS), 1)
    same = owner_down == owner_row.astype(F32)
    rank = jnp.sum(jnp.where(same & earlier, 1.0, 0.0), axis=0, keepdims=True).astype(jnp.int32)
    place = (rank & 3) * 32 + owner_row * 4 + (rank >> 2)
    one = jnp.where(iota((128, PAIRS), 0) == place, 1.0, 0.0)
    select[...] = jnp.concatenate([one, one, one], axis=1).astype(BF16)
    later = iota((PAIRS, PAIRS), 0) > iota((PAIRS, PAIRS), 1)
    rank_down = jnp.sum(jnp.where(same & later, 1.0, 0.0), axis=1, keepdims=True)
    quarter = (iota((PAIRS, 128), 1) >> 5).astype(F32)
    mine = jnp.where(owner_down[:, :1] == d.astype(F32), rank_down, -1.0)
    masks = [jnp.where(mine == quarter + 4.0 * g, 1.0, 0.0) for g in range(3)]
    masks = jnp.concatenate(masks, axis=1)
    own[...] = jnp.concatenate([masks, jnp.zeros_like(masks)], axis=0).astype(BF16)

    date = jnp.concatenate([pairs_v[0:1, :], pairs_v[1:2, :]], axis=1)
    one = jnp.where((iota((ROWS, 2 * PAIRS), 0) >> 5) == (date & (EACH - 1)), 1.0, 0.0)
    hot[...] = jnp.concatenate([one, one, one], axis=0).astype(BF16)
    source_of[...] = jnp.where(iota((GROUP, 2 * PAIRS), 0) == (date >> 2), 1.0, 0.0)
    one = jnp.where((iota((ROWS, 128), 0) >> 2) == (iota((ROWS, 128), 1) & 31), 1.0, 0.0)
    look[...] = jnp.concatenate([one, one, one], axis=0).astype(BF16)

    def edges(side):
        stage(
            edge_in[side], edge_in[side], edge_send.at[side], edge_recv.at[0], targets[side]
        ).wait_recv()

    def smooth_powers(number):
        for t in range(number):
            big, small = split(along_columns(fields, t))
            lhs[HALF * t : HALF * (t + 1), :ROWS] = big
            lhs[HALF * t : HALF * (t + 1), ROWS:] = small
        smooth = dot(lhs[: number * HALF, :], smoother[...])
        return jnp.sqrt(smooth[:, :ROWS] + smooth[:, ROWS:])

    def take_first(sources, ref):
        size = PIECES[0]
        for i, source in enumerate(sources):
            for t in range(EACH):
                piece = ref[source, 2 * size * t : 2 * size * (t + 1), :].astype(F32)
                edge = edge_left[source, 16 * t : 16 * (t + 1), :].astype(F32)
                real = jnp.concatenate([piece[:8] + edge[:8], piece[8:size]], axis=0)
                imag = jnp.concatenate([piece[size : size + 8] + edge[8:], piece[size + 8 :]], axis=0)
                images[source * EACH + t, 0, :size] = real
                images[source * EACH + t, 1, :size] = imag
                fields[EACH * i + t] = real * real + imag * imag
        smooth = smooth_powers(EACH * len(sources))
        for i, source in enumerate(sources):
            for t in range(EACH):
                at = HALF * (EACH * i + t)
                roots[source * EACH + t, :HALF] = smooth[at : at + HALF]

    def arrive(*ks):
        first_copy(ks[0], len(ks)).wait_recv()
        take_first([(d + GROUP - k) % GROUP for k in ks], got_0)

    def take_second():
        size = PIECES[1]
        for date in range(DATES):
            source, t = date // EACH, date % EACH
            piece = got_1[source, 2 * size * t : 2 * size * (t + 1), :].astype(F32)
            edge = edge_right[source, 16 * t : 16 * (t + 1), :].astype(F32)
            real = jnp.concatenate([piece[:8], piece[8:size] + edge[:8]], axis=0)
            imag = jnp.concatenate([piece[size : size + 8], piece[size + 8 :] + edge[8:]], axis=0)
            images[date, 0, PIECES[0] :] = real
            images[date, 1, PIECES[0] :] = imag
            real = jnp.concatenate([images[date, 0, HALF : PIECES[0]], real], axis=0)
            imag = jnp.concatenate([images[date, 1, HALF : PIECES[0]], imag], axis=0)
            fields[date] = real * real + imag * imag
        smooth = smooth_powers(DATES)
        for date in range(DATES):
            roots[date, HALF:] = smooth[HALF * date : HALF * (date + 1)]

    def pairs_of(half, then=None):
        window = slice(HALF * half, HALF * half + WINDOW)

        def place(field, p):
            return pl.ds(((3 * half + field) * PAIRS + p) * 8, 8)

        def chunk(index, carry):
            dates = []
            for i in range(CHUNK):
                p = index * CHUNK + i
                first = pairs_s[0, p]
                second = pairs_s[1, p]
                dates.append((first, second))
                real_a = images[first, 0, window]
                imag_a = images[first, 1, window]
                real_b = images[second, 0, window]
                imag_b = images[second, 1, window]
                fields[2 * i] = real_a * real_b + imag_a * imag_b
                fields[2 * i + 1] = imag_a * real_b - real_a * imag_b
            for i in range(CHUNK):
                p = index * CHUNK + i
                for f in range(2):
                    n = 2 * i + f
                    big, small = split(along_columns(fields, n))
                    lhs[HALF * n : HALF * (n + 1), :ROWS] = big
                    lhs[HALF * n : HALF * (n + 1), ROWS:] = small
                    sums[place(f, p), :] = fields[n, 4:12, :] + fields[n, 12:20, :]
            smooth = dot(lhs[...], smoother[...])
            smooth = smooth[:, :ROWS] + smooth[:, ROWS:]
            for i in range(CHUNK):
                p = index * CHUNK + i
                first, second = dates[i]
                real = smooth[2 * HALF * i : 2 * HALF * i + HALF]
                imag = smooth[2 * HALF * i + HALF : 2 * HALF * (i + 1)]
                below = (
                    roots[first, HALF * half : HALF * (half + 1)]
                    * roots[second, HALF * half : HALF * (half + 1)]
                )
                value = jnp.sqrt(real * real + imag * imag) / (below + 1e-06)
                sums[place(2, p), :] = value[0:8] + value[8:16]
            return carry

        lax.fori_loop(0, PAIRS // CHUNK, chunk, 0)
        if then is not None:
            then()
        rows = sums[pl.ds(3 * half * PAIRS * 8, 3 * PAIRS, stride=8), :]
        for i in range(1, 8):
            rows = rows + sums[pl.ds(3 * half * PAIRS * 8 + i, 3 * PAIRS, stride=8), :]
        looked[half] = dot(jnp.concatenate(split3(rows), axis=1), look[...])

    @pl.when(right_later)
    def _():
        pl.semaphore_wait(ready.at[0], 1)
        edge_copy(0).start()

    @pl.when(left_later)
    def _():
        pl.semaphore_wait(ready.at[1], 1)
        edge_copy(1).start()

    @pl.when((d == 0) & (c > 0))
    def _():
        edges(0)

    take_first([d], sent_0)
    arrive(4)
    arrive(3)
    arrive(5)
    arrive(2, 6, 1, 7)
    pairs_of(0)

    def d_copy(k, size=1):
        return stage(
            totals.at[pl.ds(d if size == 1 else 0, size)], totals.at[pl.ds(d if size == 1 else 0, size)],
            d_send.at[0], d_recv.at[0], date_peer(k),
        )

    def add_up():
        @pl.when(c == 0)
        def _():
            up_copy(1, count - 1).wait_recv()
            total = power_row[...] + jnp.sum(power_in[1:count, :], axis=0, keepdims=True)
            totals[pl.ds(d, 1), :] = total
            for k in order:
                d_copy(k).start()

    @pl.when((d == GROUP - 1) & (c < count - 1))
    def _():
        edges(1)

    second_copy(1, GROUP - 1).wait_recv()
    take_second()
    pairs_of(1, add_up)

    wide = []
    for q in range(6):
        piece = looked[q // 3, PAIRS * (q % 3) : PAIRS * (q % 3 + 1)]
        wide.append(piece if q % 3 < 2 else piece * (1.0 / 64.0))
    stacked = jnp.concatenate(split3(jnp.concatenate(wide, axis=1)), axis=0)
    placed = dot(select[...], stacked)
    lane = iota((32, 128), 1)
    for q in range(6):
        part = placed[:, 128 * q : 128 * (q + 1)]
        value = jnp.where(
            lane < 64,
            jnp.where(lane < 32, part[0:32], part[32:64]),
            jnp.where(lane < 96, part[64:96], part[96:128]),
        )
        for e in range(GROUP):
            results[e, 4 * q : 4 * q + 4, :] = value[4 * e : 4 * e + 4]

    def out_copy(k, size=1):
        return stage(
            results.at[pl.ds((d + k) % GROUP if size == 1 else 0, size)],
            landed.at[pl.ds(d if size == 1 else 0, size)],
            out_send.at[0], out_recv.at[0], date_peer(k),
        )

    for k in order:
        out_copy(k).start()
    landed[d] = results[d]

    @pl.when(c == 0)
    def _():
        d_copy(1, GROUP - 1).wait_recv()
        parts = jnp.concatenate(split3(totals[...]), axis=1)
        total = jnp.sum(dot(parts, hot[...]) * source_of[...], axis=0, keepdims=True)
        scale = jnp.sqrt(total / (ROWS * WIDTH * count) + 1e-06)
        factor = (1.0 / 64.0) / (scale * pltpu.roll(scale, PAIRS, 1))
        rows = dot(jnp.concatenate(split3(factor), axis=0), own[...])
        scaling[...] = jnp.sum(rows, axis=0, keepdims=True)
        for i in range(near):
            for j in range(count // nz):
                if i + j > 0:
                    down_copy(j * nz + i).start()

    @pl.when(c > 0)
    def _():
        down_copy(0).wait_recv()

    @pl.when(hands_on)
    def _():
        if nz > near:
            pl.semaphore_wait(here, nz - near)
        for i in range(near, nz):
            down_copy(hand - (near - 1) + i).start()

    out_copy(1, GROUP - 1).wait_recv()
    first_copy(1, GROUP - 1).wait_send()
    second_copy(1, GROUP - 1).wait_send()
    out_copy(1, GROUP - 1).wait_send()

    @pl.when(right_later | right_earlier)
    def _():
        edge_copy(0).wait_send()

    @pl.when(left_later | left_earlier)
    def _():
        edge_copy(1).wait_send()

    def sent_down(number):
        stage(
            power_in.at[pl.ds(0, 3 * number)], power_in.at[pl.ds(0, 3 * number)], down_send.at[0],
            down_recv.at[0], {"dates": d, "cols": c},
        ).wait_send()

    @pl.when(c > 0)
    def _():
        up_copy(c).wait_send()

    @pl.when(c == 0)
    def _():
        d_copy(1, GROUP - 1).wait_send()
        sent_down(near * (count // nz) - 1)

    if nz > near:

        @pl.when(hands_on)
        def _():
            sent_down(nz - near)


def place_kernel(landed, scaling, interferogram, coherence):
    for f in range(3):
        for g in range(3):
            block = landed[pl.ds(f * 4 + g, 16, stride=12), :]
            if f < 2:
                block = block * scaling[:, 128 * g : 128 * (g + 1)]
            for j in range(4):
                piece = block[:, 32 * j : 32 * j + 32]
                if f < 2:
                    interferogram[f, 4 * g + j] = piece
                else:
                    coherence[4 * g + j] = piece


def solution(mesh):
    columns = mesh.shape["cols"]
    nz = 8 if columns % 8 == 0 else 2
    sem = pltpu.SemaphoreType.DMA
    vmem = pl.BlockSpec(memory_space=pltpu.VMEM)

    def local(slc, pairs, owner):
        pairs = pairs.T
        owner = owner.reshape(1, PAIRS)
        landed, scaling = pl.pallas_call(
            lambda *refs: kernel(nz, columns, *refs),
            out_shape=(jax.ShapeDtypeStruct((GROUP, 24, 128), F32), jax.ShapeDtypeStruct((1, 384), F32)),
            in_specs=[pl.BlockSpec(memory_space=pl.ANY)] * 3,
            out_specs=(vmem, vmem),
            scratch_shapes=[
                pltpu.VMEM((2, EACH, ROWS, WIDTH), BF16),
                pltpu.SMEM((2, PAIRS), jnp.int32),
                pltpu.VMEM((2, PAIRS), jnp.int32),
                pltpu.VMEM((1, PAIRS), jnp.int32),
                pltpu.VMEM((128, 3 * PAIRS), BF16),
                pltpu.VMEM((128, 3 * 128), BF16),
                pltpu.VMEM((3 * ROWS, 128), BF16),
                pltpu.VMEM((3 * ROWS, 2 * PAIRS), BF16),
                pltpu.VMEM((GROUP, 2 * PAIRS), F32),
                pltpu.VMEM((2 * ROWS, 2 * ROWS), BF16),
                pltpu.VMEM((GROUP, EACH * 2 * PIECES[0], ROWS), BF16),
                pltpu.VMEM((GROUP, EACH * 2 * PIECES[1], ROWS), BF16),
                pltpu.VMEM((GROUP, EACH * 2 * PIECES[0], ROWS), BF16),
                pltpu.VMEM((GROUP, EACH * 2 * PIECES[1], ROWS), BF16),
                pltpu.VMEM((2, EDGE, ROWS), BF16),
                pltpu.VMEM((GROUP, EDGE, ROWS), BF16),
                pltpu.VMEM((GROUP, EDGE, ROWS), BF16),
                pltpu.VMEM((DATES, 2, TILE, ROWS), F32),
                pltpu.VMEM((DATES, PART, ROWS), F32),
                pltpu.VMEM((2 * CHUNK, WINDOW, ROWS), F32),
                pltpu.VMEM((2 * CHUNK * HALF, 2 * ROWS), BF16),
                pltpu.VMEM((6 * PAIRS * 8, ROWS), F32),
                pltpu.VMEM((2, 3 * PAIRS, ROWS), F32),
                pltpu.VMEM((1, ROWS), F32),
                pltpu.VMEM((2 * columns, ROWS), F32),
                pltpu.VMEM((GROUP, ROWS), F32),
                pltpu.VMEM((GROUP, 24, 128), F32),
                sem((1,)), sem((4,)), sem((1,)), sem((1,)),
                sem((2,)), sem((1,)), pltpu.SemaphoreType.REGULAR((2,)), pltpu.SemaphoreType.REGULAR,
                sem((1,)), sem((1,)), sem((1,)), sem((1,)),
                sem((1,)), sem((1,)), sem((1,)), sem((1,)),
                sem((1,)), sem((3,)),
            ],
            compiler_params=pltpu.CompilerParams(
                collective_id=0, has_side_effects=True, vmem_limit_bytes=54682 * 1024
            ),
        )(slc, pairs, owner)
        interferogram, coherence = pl.pallas_call(
            place_kernel,
            out_shape=(
                jax.ShapeDtypeStruct((2, CAP, 16, 32), F32),
                jax.ShapeDtypeStruct((CAP, 16, 32), F32),
            ),
            in_specs=[vmem, vmem],
            out_specs=(vmem, vmem),
            compiler_params=pltpu.CompilerParams(vmem_limit_bytes=2 * 1024 * 1024),
        )(landed.reshape(GROUP * 24, 128), scaling)
        return jnp.swapaxes(interferogram, 2, 3), jnp.swapaxes(coherence, 1, 2)

    return jax.shard_map(
        local,
        mesh=mesh,
        in_specs=(P(None, "dates", None, "cols"), P(), P()),
        out_specs=(P(None, "dates", None, "cols"), P("dates", None, "cols")),
        check_vma=False,
    )
```

```python
import math

import jax
import jax.numpy as jnp
import ml_dtypes
import numpy as np
from jax import lax
from jax.experimental import pallas as pl
from jax.experimental.pallas import tpu as pltpu
from jax.sharding import PartitionSpec as P

MESH = pl.DeviceIdType.MESH
F32 = jnp.float32
BF16 = jnp.bfloat16

TAPS = [math.exp(-k * k / 8.0) for k in range(-4, 5)]
WEIGHTS = [float(np.float32(t / sum(TAPS))) for t in TAPS]
HIGH = [float(np.float32(w).astype(ml_dtypes.bfloat16)) for w in WEIGHTS]
LOW = [float(np.float32(w - h).astype(ml_dtypes.bfloat16)) for w, h in zip(WEIGHTS, HIGH)]

GROUP = 8
EACH = 4
DATES = GROUP * EACH
PAIRS = 64
CAP = 12
ROWS = 128
PART = 32
TILE = PART + 8
WIDTH = GROUP * PART
PIECES = (24, 16)
HALF = PART // 2
WINDOW = HALF + 8
EDGE = EACH * 2 * 8
CHUNK = 32


def split(x):
    high = x.astype(BF16)
    return high, (x - high.astype(F32)).astype(BF16)


def split3(x):
    high = x.astype(BF16)
    rest = x - high.astype(F32)
    mid = rest.astype(BF16)
    return high, mid, (rest - mid.astype(F32)).astype(BF16)


def dot(a, b):
    return jnp.dot(a, b, preferred_element_type=F32)


def iota(shape, axis):
    return lax.broadcasted_iota(jnp.int32, shape, axis)


def cutter(half):
    start, size = (-4, PIECES[0]) if half == 0 else (PIECES[0] - 4, PIECES[1])
    lane = iota((size, WIDTH), 1)
    row = iota((size, WIDTH), 0)
    pieces = [jnp.where(lane == row + (PART * e + start), 1.0, 0.0) for e in range(GROUP)]
    lane = iota((8, WIDTH), 1)
    row = iota((8, WIDTH), 0)
    pieces.append(jnp.where(lane == row + (WIDTH - 4 if half == 0 else -4), 1.0, 0.0))
    return jnp.concatenate(pieces, axis=0).astype(BF16)


def band(weights):
    gap = jnp.abs(iota((ROWS, ROWS), 0) - iota((ROWS, ROWS), 1))
    result = jnp.zeros((ROWS, ROWS), F32)
    for k in range(5):
        result = jnp.where(gap == k, weights[4 + k], result)
    return result.astype(BF16)


def along_columns(ref, index):
    result = WEIGHTS[4] * ref[index, 4 : 4 + HALF, :]
    for k in range(4):
        both = ref[index, k : k + HALF, :] + ref[index, 8 - k : 8 - k + HALF, :]
        result = result + WEIGHTS[k] * both
    return result


def kernel(
    nz, count, slc_hbm, pairs_hbm, owner_hbm, landed, scaling,
    slc, pairs_s, pairs_v, owner_v, select, own, look, hot, source_of, smoother, sent_0, sent_1, got_0, got_1,
    edge_out, edge_left, edge_right, images, roots, fields, lhs, sums, looked,
    power_row, power_in, totals, results,
    main_send_0, main_recv_0, main_send_1, main_recv_1, edge_send, edge_recv, ready,
    here, up_send, up_recv, down_send, down_recv, d_send, d_recv, out_send, out_recv, in_sem, table_sem,
):
    load = pltpu.make_async_copy(slc_hbm, slc, in_sem.at[0])
    load.start()

    d = lax.axis_index("dates")
    c = lax.axis_index("cols")
    z = c % nz

    def date_peer(k):
        return {"dates": (d + k) % GROUP, "cols": c}

    right = (c + 1) % count
    left = (c + count - 1) % count
    near = min(3, nz)
    right_later = (z < nz - 1) & (c < count - 1)
    right_earlier = (z == nz - 1) & (c < count - 1)
    left_later = (z == 0) & (c > 0)
    left_earlier = (z > 0) & (c > 0)

    barrier = pltpu.get_barrier_semaphore()

    def greet(device):
        pl.semaphore_signal(barrier, inc=1, device_id=device, device_id_type=MESH)

    for k in range(1, GROUP):
        greet(date_peer(k))

    @pl.when(right_later & (d == GROUP - 1))
    def _():
        for e in range(GROUP):
            greet({"dates": e, "cols": right})

    @pl.when(left_later)
    def _():
        greet({"dates": GROUP - 1, "cols": left})

    @pl.when(left_later & (d == 0))
    def _():
        for e in range(GROUP):
            greet({"dates": e, "cols": left})

    @pl.when(c == 0)
    def _():
        def one(i, carry):
            greet({"dates": d, "cols": i})
            return carry

        lax.fori_loop(1, count, one, 0)

    hands_on = z == near - 1
    handed = z >= near
    hand = c - z + near - 1

    @pl.when(hands_on)
    def _():
        for i in range(near, nz):
            greet({"dates": d, "cols": hand - (near - 1) + i})

    tables = [
        pltpu.make_async_copy(pairs_hbm, pairs_s, table_sem.at[0]),
        pltpu.make_async_copy(pairs_hbm, pairs_v, table_sem.at[1]),
        pltpu.make_async_copy(owner_hbm, owner_v, table_sem.at[2]),
    ]
    for table in tables:
        table.start()

    sent = (sent_0, sent_1)
    edge_in = (edge_left, edge_right)
    got = (got_0, got_1)

    def cut(half, matrix):
        size = PIECES[half]
        for t in range(EACH):
            both = jnp.concatenate([slc[0, t], slc[1, t]], axis=0)
            turned = lax.dot_general(
                matrix, both, (((1,), (1,)), ((), ())), preferred_element_type=F32
            )
            for e in range(GROUP + 1):
                rows = turned[size * e : size * (e + 1)] if e < GROUP else turned[size * GROUP :]
                value = jnp.concatenate([rows[:, :ROWS], rows[:, ROWS:]], axis=0).astype(BF16)
                if e < GROUP:
                    sent[half][e, 2 * size * t : 2 * size * (t + 1), :] = value
                else:
                    edge_out[half, 16 * t : 16 * (t + 1), :] = value

    matrix = cutter(0)
    high = band(HIGH)
    low = band(LOW)
    smoother[:, :ROWS] = jnp.concatenate([high, high], axis=0)
    smoother[:, ROWS:] = jnp.concatenate([low, low], axis=0)
    load.wait()
    power_rows = []
    for t in range(EACH):
        wide = jnp.concatenate([slc[0, t], slc[1, t]], axis=0).astype(F32)
        square = jnp.sum(wide * wide, axis=0, keepdims=True)
        power_rows.append(square[:, :ROWS] + square[:, ROWS:])
    folded = jnp.concatenate(power_rows + [jnp.zeros((8 - EACH, ROWS), F32)], axis=0)
    folded = folded + pltpu.roll(folded, 64, 1)
    folded = folded + pltpu.roll(folded, 32, 1)
    own_lane = (iota((8, ROWS), 1) >> 5) == iota((8, ROWS), 0)
    power_row[...] = jnp.sum(jnp.where(own_lane, folded, 0.0), axis=0, keepdims=True)

    def stage(src, dst, send, recv, peer):
        return pltpu.make_async_remote_copy(
            src_ref=src, dst_ref=dst, send_sem=send, recv_sem=recv, device_id=peer, device_id_type=MESH
        )

    def up_copy(i, size=1):
        return stage(
            power_in.at[pl.ds(0, size)] if size > 1 else power_row, power_in.at[pl.ds(i, size)],
            up_send.at[0], up_recv.at[0], {"dates": d, "cols": 0},
        )

    def down_copy(i):
        return stage(scaling, scaling, down_send.at[0], down_recv.at[0], {"dates": d, "cols": i})

    last = (d == GROUP - 1).astype(jnp.int32)

    def tell_ready(side, e, other):
        pl.semaphore_signal(
            ready.at[side], inc=1, device_id={"dates": e, "cols": other}, device_id_type=MESH
        )

    def enter():
        pl.semaphore_wait(
            barrier,
            (GROUP - 1)
            + (c > 0).astype(jnp.int32)
            + handed.astype(jnp.int32)
            + right_earlier.astype(jnp.int32) * (1 + GROUP * last)
            + left_earlier.astype(jnp.int32),
        )

        @pl.when(handed)
        def _():
            pl.semaphore_signal(
                here, inc=1, device_id={"dates": d, "cols": hand}, device_id_type=MESH
            )

        @pl.when(c > 0)
        def _():
            up_copy(c).start()

        @pl.when(left_earlier & (d == 0))
        def _():
            tell_ready(0, GROUP - 1, left)

        @pl.when(right_earlier & (d == GROUP - 1))
        def _():
            for e in range(GROUP):
                tell_ready(1, e, right)

    pl.when(z >= nz // 2)(enter)
    cut(0, matrix)
    pl.when(z < nz // 2)(enter)

    targets = ({"dates": 0, "cols": right}, {"dates": GROUP - 1, "cols": left})

    def edge_copy(side):
        return pltpu.make_async_remote_copy(
            src_ref=edge_out.at[side], dst_ref=edge_in[side].at[d], send_sem=edge_send.at[side],
            recv_sem=edge_recv.at[0], device_id=targets[side], device_id_type=MESH,
        )

    order = (4, 3, 5, 2, 6, 1, 7)
    slots = {4: 0, 3: 1, 5: 2}

    def first_copy(k, size=1):
        return stage(
            sent_0.at[pl.ds((d + k) % GROUP if size == 1 else 0, size)],
            got_0.at[pl.ds(d if size == 1 else 0, size)],
            main_send_0.at[0], main_recv_0.at[slots.get(k, 3)], date_peer(k),
        )

    def second_copy(k, size=1):
        return stage(
            sent_1.at[pl.ds((d + k) % GROUP if size == 1 else 0, size)],
            got_1.at[pl.ds(d if size == 1 else 0, size)],
            main_send_1.at[0], main_recv_1.at[0], date_peer(k),
        )

    for k in order:
        first_copy(k).start()

    @pl.when(right_earlier)
    def _():
        edge_copy(0).start()

    cut(1, cutter(1))
    for k in order:
        second_copy(k).start()

    @pl.when(left_earlier)
    def _():
        edge_copy(1).start()

    got_1[d] = sent_1[d]

    @pl.when((d != 0) | (c == 0))
    def _():
        edge_left[...] = jnp.zeros_like(edge_left)

    @pl.when((d != GROUP - 1) | (c == count - 1))
    def _():
        edge_right[...] = jnp.zeros_like(edge_right)


    for table in tables:
        table.wait()
    owner_row = owner_v[...]
    owner_down = jnp.transpose(jnp.broadcast_to(owner_row.astype(F32), (ROWS, PAIRS)))[:, :PAIRS]
    earlier = iota((PAIRS, PAIRS), 0) < iota((PAIRS, PAIRS), 1)
    same = owner_down == owner_row.astype(F32)
    rank = jnp.sum(jnp.where(same & earlier, 1.0, 0.0), axis=0, keepdims=True).astype(jnp.int32)
    place = (rank & 3) * 32 + owner_row * 4 + (rank >> 2)
    one = jnp.where(iota((128, PAIRS), 0) == place, 1.0, 0.0)
    select[...] = jnp.concatenate([one, one, one], axis=1).astype(BF16)
    later = iota((PAIRS, PAIRS), 0) > iota((PAIRS, PAIRS), 1)
    rank_down = jnp.sum(jnp.where(same & later, 1.0, 0.0), axis=1, keepdims=True)
    quarter = (iota((PAIRS, 128), 1) >> 5).astype(F32)
    mine = jnp.where(owner_down[:, :1] == d.astype(F32), rank_down, -1.0)
    masks = [jnp.where(mine == quarter + 4.0 * g, 1.0, 0.0) for g in range(3)]
    masks = jnp.concatenate(masks, axis=1)
    own[...] = jnp.concatenate([masks, jnp.zeros_like(masks)], axis=0).astype(BF16)

    date = jnp.concatenate([pairs_v[0:1, :], pairs_v[1:2, :]], axis=1)
    one = jnp.where((iota((ROWS, 2 * PAIRS), 0) >> 5) == (date & (EACH - 1)), 1.0, 0.0)
    hot[...] = jnp.concatenate([one, one, one], axis=0).astype(BF16)
    source_of[...] = jnp.where(iota((GROUP, 2 * PAIRS), 0) == (date >> 2), 1.0, 0.0)
    one = jnp.where((iota((ROWS, 128), 0) >> 2) == (iota((ROWS, 128), 1) & 31), 1.0, 0.0)
    look[...] = jnp.concatenate([one, one, one], axis=0).astype(BF16)

    def edges(side):
        stage(
            edge_in[side], edge_in[side], edge_send.at[side], edge_recv.at[0], targets[side]
        ).wait_recv()

    def smooth_powers(number):
        for t in range(number):
            big, small = split(along_columns(fields, t))
            lhs[HALF * t : HALF * (t + 1), :ROWS] = big
            lhs[HALF * t : HALF * (t + 1), ROWS:] = small
        smooth = dot(lhs[: number * HALF, :], smoother[...])
        return jnp.sqrt(smooth[:, :ROWS] + smooth[:, ROWS:])

    def take_first(sources, ref):
        size = PIECES[0]
        for i, source in enumerate(sources):
            for t in range(EACH):
                piece = ref[source, 2 * size * t : 2 * size * (t + 1), :].astype(F32)
                edge = edge_left[source, 16 * t : 16 * (t + 1), :].astype(F32)
                real = jnp.concatenate([piece[:8] + edge[:8], piece[8:size]], axis=0)
                imag = jnp.concatenate([piece[size : size + 8] + edge[8:], piece[size + 8 :]], axis=0)
                images[source * EACH + t, 0, :size] = real
                images[source * EACH + t, 1, :size] = imag
                fields[EACH * i + t] = real * real + imag * imag
        smooth = smooth_powers(EACH * len(sources))
        for i, source in enumerate(sources):
            for t in range(EACH):
                at = HALF * (EACH * i + t)
                roots[source * EACH + t, :HALF] = smooth[at : at + HALF]

    def arrive(*ks):
        first_copy(ks[0], len(ks)).wait_recv()
        take_first([(d + GROUP - k) % GROUP for k in ks], got_0)

    def take_second():
        size = PIECES[1]
        for date in range(DATES):
            source, t = date // EACH, date % EACH
            piece = got_1[source, 2 * size * t : 2 * size * (t + 1), :].astype(F32)
            edge = edge_right[source, 16 * t : 16 * (t + 1), :].astype(F32)
            real = jnp.concatenate([piece[:8], piece[8:size] + edge[:8]], axis=0)
            imag = jnp.concatenate([piece[size : size + 8], piece[size + 8 :] + edge[8:]], axis=0)
            images[date, 0, PIECES[0] :] = real
            images[date, 1, PIECES[0] :] = imag
            real = jnp.concatenate([images[date, 0, HALF : PIECES[0]], real], axis=0)
            imag = jnp.concatenate([images[date, 1, HALF : PIECES[0]], imag], axis=0)
            fields[date] = real * real + imag * imag
        smooth = smooth_powers(DATES)
        for date in range(DATES):
            roots[date, HALF:] = smooth[HALF * date : HALF * (date + 1)]

    def pairs_of(half, between=None):
        window = slice(HALF * half, HALF * half + WINDOW)

        def place(field, p):
            return pl.ds(((3 * half + field) * PAIRS + p) * 8, 8)

        def chunk(index, carry):
            dates = []
            for i in range(CHUNK):
                p = index * CHUNK + i
                first = pairs_s[0, p]
                second = pairs_s[1, p]
                dates.append((first, second))
                real_a = images[first, 0, window]
                imag_a = images[first, 1, window]
                real_b = images[second, 0, window]
                imag_b = images[second, 1, window]
                fields[2 * i] = real_a * real_b + imag_a * imag_b
                fields[2 * i + 1] = imag_a * real_b - real_a * imag_b
            for i in range(CHUNK):
                p = index * CHUNK + i
                for f in range(2):
                    n = 2 * i + f
                    big, small = split(along_columns(fields, n))
                    lhs[HALF * n : HALF * (n + 1), :ROWS] = big
                    lhs[HALF * n : HALF * (n + 1), ROWS:] = small
                    sums[place(f, p), :] = fields[n, 4:12, :] + fields[n, 12:20, :]
            smooth = dot(lhs[...], smoother[...])
            smooth = smooth[:, :ROWS] + smooth[:, ROWS:]
            for i in range(CHUNK):
                p = index * CHUNK + i
                first, second = dates[i]
                real = smooth[2 * HALF * i : 2 * HALF * i + HALF]
                imag = smooth[2 * HALF * i + HALF : 2 * HALF * (i + 1)]
                below = (
                    roots[first, HALF * half : HALF * (half + 1)]
                    * roots[second, HALF * half : HALF * (half + 1)]
                )
                value = jnp.sqrt(real * real + imag * imag) / (below + 1e-06)
                sums[place(2, p), :] = value[0:8] + value[8:16]
            return carry

        if between is None:
            lax.fori_loop(0, PAIRS // CHUNK, chunk, 0)
        else:
            lax.fori_loop(0, PAIRS // CHUNK // 2, chunk, 0)
            between()
            lax.fori_loop(PAIRS // CHUNK // 2, PAIRS // CHUNK, chunk, 0)
        rows = sums[pl.ds(3 * half * PAIRS * 8, 3 * PAIRS, stride=8), :]
        for i in range(1, 8):
            rows = rows + sums[pl.ds(3 * half * PAIRS * 8 + i, 3 * PAIRS, stride=8), :]
        looked[half] = dot(jnp.concatenate(split3(rows), axis=1), look[...])

    @pl.when(right_later)
    def _():
        pl.semaphore_wait(ready.at[0], 1)

        @pl.when(d == GROUP - 1)
        def _():
            for e in range(GROUP - 1):
                tell_ready(0, e, c)

        edge_copy(0).start()

    @pl.when(left_later)
    def _():
        pl.semaphore_wait(ready.at[1], 1)
        edge_copy(1).start()

    @pl.when((d == 0) & (c > 0))
    def _():
        edges(0)

    take_first([d], sent_0)
    arrive(4)
    arrive(3)
    arrive(5)
    arrive(2, 6, 1, 7)
    pairs_of(0)

    def d_copy(k, size=1):
        return stage(
            totals.at[pl.ds(d if size == 1 else 0, size)], totals.at[pl.ds(d if size == 1 else 0, size)],
            d_send.at[0], d_recv.at[0], date_peer(k),
        )

    def add_up():
        @pl.when(c == 0)
        def _():
            up_copy(1, count - 1).wait_recv()
            total = power_row[...] + jnp.sum(power_in[1:count, :], axis=0, keepdims=True)
            totals[pl.ds(d, 1), :] = total
            for k in order:
                d_copy(k).start()

    @pl.when((d == GROUP - 1) & (c < count - 1))
    def _():
        edges(1)

    second_copy(1, GROUP - 1).wait_recv()
    take_second()
    pairs_of(1, add_up)

    wide = []
    for q in range(6):
        piece = looked[q // 3, PAIRS * (q % 3) : PAIRS * (q % 3 + 1)]
        wide.append(piece if q % 3 < 2 else piece * (1.0 / 64.0))
    stacked = jnp.concatenate(split3(jnp.concatenate(wide, axis=1)), axis=0)
    placed = dot(select[...], stacked)
    lane = iota((32, 128), 1)
    for q in range(6):
        part = placed[:, 128 * q : 128 * (q + 1)]
        value = jnp.where(
            lane < 64,
            jnp.where(lane < 32, part[0:32], part[32:64]),
            jnp.where(lane < 96, part[64:96], part[96:128]),
        )
        for e in range(GROUP):
            results[e, 4 * q : 4 * q + 4, :] = value[4 * e : 4 * e + 4]

    def out_copy(k, size=1):
        return stage(
            results.at[pl.ds((d + k) % GROUP if size == 1 else 0, size)],
            landed.at[pl.ds(d if size == 1 else 0, size)],
            out_send.at[0], out_recv.at[0], date_peer(k),
        )

    for k in order:
        out_copy(k).start()
    landed[d] = results[d]

    @pl.when(c == 0)
    def _():
        d_copy(1, GROUP - 1).wait_recv()
        parts = jnp.concatenate(split3(totals[...]), axis=1)
        total = jnp.sum(dot(parts, hot[...]) * source_of[...], axis=0, keepdims=True)
        scale = jnp.sqrt(total / (ROWS * WIDTH * count) + 1e-06)
        factor = (1.0 / 64.0) / (scale * pltpu.roll(scale, PAIRS, 1))
        rows = dot(jnp.concatenate(split3(factor), axis=0), own[...])
        scaling[...] = jnp.sum(rows, axis=0, keepdims=True)
        for i in range(near):
            for j in range(count // nz):
                if i + j > 0:
                    down_copy(j * nz + i).start()

    @pl.when(c > 0)
    def _():
        down_copy(0).wait_recv()

    @pl.when(hands_on)
    def _():
        if nz > near:
            pl.semaphore_wait(here, nz - near)
        for i in range(near, nz):
            down_copy(hand - (near - 1) + i).start()

    out_copy(1, GROUP - 1).wait_recv()
    first_copy(1, GROUP - 1).wait_send()
    second_copy(1, GROUP - 1).wait_send()
    out_copy(1, GROUP - 1).wait_send()

    @pl.when(right_later | right_earlier)
    def _():
        edge_copy(0).wait_send()

    @pl.when(left_later | left_earlier)
    def _():
        edge_copy(1).wait_send()

    def sent_down(number):
        stage(
            power_in.at[pl.ds(0, 3 * number)], power_in.at[pl.ds(0, 3 * number)], down_send.at[0],
            down_recv.at[0], {"dates": d, "cols": c},
        ).wait_send()

    @pl.when(c > 0)
    def _():
        up_copy(c).wait_send()

    @pl.when(c == 0)
    def _():
        d_copy(1, GROUP - 1).wait_send()
        sent_down(near * (count // nz) - 1)

    if nz > near:

        @pl.when(hands_on)
        def _():
            sent_down(nz - near)


def place_kernel(landed, scaling, interferogram, coherence):
    for f in range(3):
        for g in range(3):
            block = landed[pl.ds(f * 4 + g, 16, stride=12), :]
            if f < 2:
                block = block * scaling[:, 128 * g : 128 * (g + 1)]
            for j in range(4):
                piece = block[:, 32 * j : 32 * j + 32]
                if f < 2:
                    interferogram[f, 4 * g + j] = piece
                else:
                    coherence[4 * g + j] = piece


def solution(mesh):
    columns = mesh.shape["cols"]
    nz = 8 if columns % 8 == 0 else 2
    sem = pltpu.SemaphoreType.DMA
    vmem = pl.BlockSpec(memory_space=pltpu.VMEM)

    def local(slc, pairs, owner):
        pairs = pairs.T
        owner = owner.reshape(1, PAIRS)
        landed, scaling = pl.pallas_call(
            lambda *refs: kernel(nz, columns, *refs),
            out_shape=(jax.ShapeDtypeStruct((GROUP, 24, 128), F32), jax.ShapeDtypeStruct((1, 384), F32)),
            in_specs=[pl.BlockSpec(memory_space=pl.ANY)] * 3,
            out_specs=(vmem, vmem),
            scratch_shapes=[
                pltpu.VMEM((2, EACH, ROWS, WIDTH), BF16),
                pltpu.SMEM((2, PAIRS), jnp.int32),
                pltpu.VMEM((2, PAIRS), jnp.int32),
                pltpu.VMEM((1, PAIRS), jnp.int32),
                pltpu.VMEM((128, 3 * PAIRS), BF16),
                pltpu.VMEM((128, 3 * 128), BF16),
                pltpu.VMEM((3 * ROWS, 128), BF16),
                pltpu.VMEM((3 * ROWS, 2 * PAIRS), BF16),
                pltpu.VMEM((GROUP, 2 * PAIRS), F32),
                pltpu.VMEM((2 * ROWS, 2 * ROWS), BF16),
                pltpu.VMEM((GROUP, EACH * 2 * PIECES[0], ROWS), BF16),
                pltpu.VMEM((GROUP, EACH * 2 * PIECES[1], ROWS), BF16),
                pltpu.VMEM((GROUP, EACH * 2 * PIECES[0], ROWS), BF16),
                pltpu.VMEM((GROUP, EACH * 2 * PIECES[1], ROWS), BF16),
                pltpu.VMEM((2, EDGE, ROWS), BF16),
                pltpu.VMEM((GROUP, EDGE, ROWS), BF16),
                pltpu.VMEM((GROUP, EDGE, ROWS), BF16),
                pltpu.VMEM((DATES, 2, TILE, ROWS), F32),
                pltpu.VMEM((DATES, PART, ROWS), F32),
                pltpu.VMEM((2 * CHUNK, WINDOW, ROWS), F32),
                pltpu.VMEM((2 * CHUNK * HALF, 2 * ROWS), BF16),
                pltpu.VMEM((6 * PAIRS * 8, ROWS), F32),
                pltpu.VMEM((2, 3 * PAIRS, ROWS), F32),
                pltpu.VMEM((1, ROWS), F32),
                pltpu.VMEM((2 * columns, ROWS), F32),
                pltpu.VMEM((GROUP, ROWS), F32),
                pltpu.VMEM((GROUP, 24, 128), F32),
                sem((1,)), sem((4,)), sem((1,)), sem((1,)),
                sem((2,)), sem((1,)), pltpu.SemaphoreType.REGULAR((2,)), pltpu.SemaphoreType.REGULAR,
                sem((1,)), sem((1,)), sem((1,)), sem((1,)),
                sem((1,)), sem((1,)), sem((1,)), sem((1,)),
                sem((1,)), sem((3,)),
            ],
            compiler_params=pltpu.CompilerParams(
                collective_id=0, has_side_effects=True, vmem_limit_bytes=54682 * 1024
            ),
        )(slc, pairs, owner)
        interferogram, coherence = pl.pallas_call(
            place_kernel,
            out_shape=(
                jax.ShapeDtypeStruct((2, CAP, 16, 32), F32),
                jax.ShapeDtypeStruct((CAP, 16, 32), F32),
            ),
            in_specs=[vmem, vmem],
            out_specs=(vmem, vmem),
            compiler_params=pltpu.CompilerParams(vmem_limit_bytes=2 * 1024 * 1024),
        )(landed.reshape(GROUP * 24, 128), scaling)
        return jnp.swapaxes(interferogram, 2, 3), jnp.swapaxes(coherence, 1, 2)

    return jax.shard_map(
        local,
        mesh=mesh,
        in_specs=(P(None, "dates", None, "cols"), P(), P()),
        out_specs=(P(None, "dates", None, "cols"), P("dates", None, "cols")),
        check_vma=False,
    )
```

```python
import math

import jax
import jax.numpy as jnp
import ml_dtypes
import numpy as np
from jax import lax
from jax.experimental import pallas as pl
from jax.experimental.pallas import tpu as pltpu
from jax.sharding import PartitionSpec as P

MESH = pl.DeviceIdType.MESH
F32 = jnp.float32
BF16 = jnp.bfloat16

TAPS = [math.exp(-k * k / 8.0) for k in range(-4, 5)]
WEIGHTS = [float(np.float32(t / sum(TAPS))) for t in TAPS]
HIGH = [float(np.float32(w).astype(ml_dtypes.bfloat16)) for w in WEIGHTS]
LOW = [float(np.float32(w - h).astype(ml_dtypes.bfloat16)) for w, h in zip(WEIGHTS, HIGH)]

GROUP = 8
EACH = 4
DATES = GROUP * EACH
PAIRS = 64
CAP = 12
ROWS = 128
PART = 32
TILE = PART + 8
WIDTH = GROUP * PART
PIECES = (24, 16)
HALF = PART // 2
WINDOW = HALF + 8
EDGE = EACH * 2 * 8
CHUNK = 32


def split(x):
    high = x.astype(BF16)
    return high, (x - high.astype(F32)).astype(BF16)


def split3(x):
    high = x.astype(BF16)
    rest = x - high.astype(F32)
    mid = rest.astype(BF16)
    return high, mid, (rest - mid.astype(F32)).astype(BF16)


def dot(a, b):
    return jnp.dot(a, b, preferred_element_type=F32)


def iota(shape, axis):
    return lax.broadcasted_iota(jnp.int32, shape, axis)


def cutter(half):
    start, size = (-4, PIECES[0]) if half == 0 else (PIECES[0] - 4, PIECES[1])
    lane = iota((size, WIDTH), 1)
    row = iota((size, WIDTH), 0)
    pieces = [jnp.where(lane == row + (PART * e + start), 1.0, 0.0) for e in range(GROUP)]
    lane = iota((8, WIDTH), 1)
    row = iota((8, WIDTH), 0)
    pieces.append(jnp.where(lane == row + (WIDTH - 4 if half == 0 else -4), 1.0, 0.0))
    return jnp.concatenate(pieces, axis=0).astype(BF16)


def band(weights):
    gap = jnp.abs(iota((ROWS, ROWS), 0) - iota((ROWS, ROWS), 1))
    result = jnp.zeros((ROWS, ROWS), F32)
    for k in range(5):
        result = jnp.where(gap == k, weights[4 + k], result)
    return result.astype(BF16)


def along_columns(ref, index):
    result = WEIGHTS[4] * ref[index, 4 : 4 + HALF, :]
    for k in range(4):
        both = ref[index, k : k + HALF, :] + ref[index, 8 - k : 8 - k + HALF, :]
        result = result + WEIGHTS[k] * both
    return result


def kernel(
    nz, count, slc_hbm, pairs_hbm, owner_hbm, landed, scaling,
    slc, pairs_s, pairs_v, owner_v, select, own, look, hot, source_of, smoother, sent_0, sent_1, got_0, got_1,
    edge_out, edge_left, edge_right, images, roots, fields, lhs, sums, looked,
    power_row, power_in, totals, factor_in, results,
    main_send_0, main_recv_0, main_send_1, main_recv_1, edge_send, edge_recv, ready,
    here, up_send, up_recv, down_send, down_recv, d_send, d_recv, out_send, out_recv, in_sem, table_sem,
):
    load = pltpu.make_async_copy(slc_hbm, slc, in_sem.at[0])
    load.start()

    d = lax.axis_index("dates")
    c = lax.axis_index("cols")
    z = c % nz

    def date_peer(k):
        return {"dates": (d + k) % GROUP, "cols": c}

    right = (c + 1) % count
    left = (c + count - 1) % count
    near = min(3, nz)
    right_later = (z < nz - 1) & (c < count - 1)
    right_earlier = (z == nz - 1) & (c < count - 1)
    left_later = (z == 0) & (c > 0)
    left_earlier = (z > 0) & (c > 0)

    barrier = pltpu.get_barrier_semaphore()

    def greet(device):
        pl.semaphore_signal(barrier, inc=1, device_id=device, device_id_type=MESH)

    for k in range(1, GROUP):
        greet(date_peer(k))

    @pl.when(right_later & (d == GROUP - 1))
    def _():
        for e in range(GROUP):
            greet({"dates": e, "cols": right})

    @pl.when(left_later)
    def _():
        greet({"dates": GROUP - 1, "cols": left})

    @pl.when(left_later & (d == 0))
    def _():
        for e in range(GROUP):
            greet({"dates": e, "cols": left})

    @pl.when(c == 0)
    def _():
        def one(i, carry):
            greet({"dates": d, "cols": i})
            return carry

        lax.fori_loop(1, count, one, 0)

    hands_on = z == near - 1
    handed = z >= near
    hand = c - z + near - 1

    @pl.when(hands_on)
    def _():
        for i in range(near, nz):
            greet({"dates": d, "cols": hand - (near - 1) + i})

    tables = [
        pltpu.make_async_copy(pairs_hbm, pairs_s, table_sem.at[0]),
        pltpu.make_async_copy(pairs_hbm, pairs_v, table_sem.at[1]),
        pltpu.make_async_copy(owner_hbm, owner_v, table_sem.at[2]),
    ]
    for table in tables:
        table.start()

    sent = (sent_0, sent_1)
    edge_in = (edge_left, edge_right)
    got = (got_0, got_1)

    def cut(half, matrix):
        size = PIECES[half]
        for t in range(EACH):
            both = jnp.concatenate([slc[0, t], slc[1, t]], axis=0)
            turned = lax.dot_general(
                matrix, both, (((1,), (1,)), ((), ())), preferred_element_type=F32
            )
            for e in range(GROUP + 1):
                rows = turned[size * e : size * (e + 1)] if e < GROUP else turned[size * GROUP :]
                value = jnp.concatenate([rows[:, :ROWS], rows[:, ROWS:]], axis=0).astype(BF16)
                if e < GROUP:
                    sent[half][e, 2 * size * t : 2 * size * (t + 1), :] = value
                else:
                    edge_out[half, 16 * t : 16 * (t + 1), :] = value

    matrix = cutter(0)
    high = band(HIGH)
    low = band(LOW)
    smoother[:, :ROWS] = jnp.concatenate([high, high], axis=0)
    smoother[:, ROWS:] = jnp.concatenate([low, low], axis=0)
    load.wait()

    def powers():
        power_rows = []
        for t in range(EACH):
            wide = jnp.concatenate([slc[0, t], slc[1, t]], axis=0).astype(F32)
            square = jnp.sum(wide * wide, axis=0, keepdims=True)
            power_rows.append(square[:, :ROWS] + square[:, ROWS:])
        folded = jnp.concatenate(power_rows + [jnp.zeros((8 - EACH, ROWS), F32)], axis=0)
        folded = folded + pltpu.roll(folded, 64, 1)
        folded = folded + pltpu.roll(folded, 32, 1)
        own_lane = (iota((8, ROWS), 1) >> 5) == iota((8, ROWS), 0)
        power_row[...] = jnp.sum(jnp.where(own_lane, folded, 0.0), axis=0, keepdims=True)

    def stage(src, dst, send, recv, peer):
        return pltpu.make_async_remote_copy(
            src_ref=src, dst_ref=dst, send_sem=send, recv_sem=recv, device_id=peer, device_id_type=MESH
        )

    def up_copy(i, size=1):
        return stage(
            power_in.at[pl.ds(0, size)] if size > 1 else power_row, power_in.at[pl.ds(i, size)],
            up_send.at[0], up_recv.at[0], {"dates": d, "cols": 0},
        )

    def down_copy(i):
        return stage(factor_in, factor_in, down_send.at[0], down_recv.at[0], {"dates": d, "cols": i})

    last = (d == GROUP - 1).astype(jnp.int32)

    def tell_ready(side, e, other):
        pl.semaphore_signal(
            ready.at[side], inc=1, device_id={"dates": e, "cols": other}, device_id_type=MESH
        )

    def enter():
        pl.semaphore_wait(
            barrier,
            (GROUP - 1)
            + (c > 0).astype(jnp.int32)
            + handed.astype(jnp.int32)
            + right_earlier.astype(jnp.int32) * (1 + GROUP * last)
            + left_earlier.astype(jnp.int32),
        )

        @pl.when(handed)
        def _():
            pl.semaphore_signal(
                here, inc=1, device_id={"dates": d, "cols": hand}, device_id_type=MESH
            )

        @pl.when(left_earlier & (d == 0))
        def _():
            tell_ready(0, GROUP - 1, left)

        @pl.when(right_earlier & (d == GROUP - 1))
        def _():
            for e in range(GROUP):
                tell_ready(1, e, right)

    def send_up():
        @pl.when(c > 0)
        def _():
            up_copy(c).start()

    late = z >= nz // 2

    @pl.when(late)
    def _():
        powers()
        enter()
        send_up()

    cut(0, matrix)
    pl.when(z < nz // 2)(enter)

    targets = ({"dates": 0, "cols": right}, {"dates": GROUP - 1, "cols": left})

    def edge_copy(side):
        return pltpu.make_async_remote_copy(
            src_ref=edge_out.at[side], dst_ref=edge_in[side].at[d], send_sem=edge_send.at[side],
            recv_sem=edge_recv.at[0], device_id=targets[side], device_id_type=MESH,
        )

    order = (4, 3, 5, 2, 6, 1, 7)
    slots = {4: 0, 3: 1, 5: 2}

    def first_copy(k, size=1):
        return stage(
            sent_0.at[pl.ds((d + k) % GROUP if size == 1 else 0, size)],
            got_0.at[pl.ds(d if size == 1 else 0, size)],
            main_send_0.at[0], main_recv_0.at[slots.get(k, 3)], date_peer(k),
        )

    def second_copy(k, size=1):
        return stage(
            sent_1.at[pl.ds((d + k) % GROUP if size == 1 else 0, size)],
            got_1.at[pl.ds(d if size == 1 else 0, size)],
            main_send_1.at[0], main_recv_1.at[0], date_peer(k),
        )

    for k in order:
        first_copy(k).start()

    @pl.when(z < nz // 2)
    def _():
        powers()
        send_up()

    @pl.when(right_earlier)
    def _():
        edge_copy(0).start()

    cut(1, cutter(1))
    for k in order:
        second_copy(k).start()

    @pl.when(left_earlier)
    def _():
        edge_copy(1).start()

    got_1[d] = sent_1[d]

    @pl.when((d != 0) | (c == 0))
    def _():
        edge_left[...] = jnp.zeros_like(edge_left)

    @pl.when((d != GROUP - 1) | (c == count - 1))
    def _():
        edge_right[...] = jnp.zeros_like(edge_right)


    for table in tables:
        table.wait()
    owner_row = owner_v[...]
    owner_down = jnp.transpose(jnp.broadcast_to(owner_row.astype(F32), (ROWS, PAIRS)))[:, :PAIRS]
    earlier = iota((PAIRS, PAIRS), 0) < iota((PAIRS, PAIRS), 1)
    same = owner_down == owner_row.astype(F32)
    rank = jnp.sum(jnp.where(same & earlier, 1.0, 0.0), axis=0, keepdims=True).astype(jnp.int32)
    place = (rank & 3) * 32 + owner_row * 4 + (rank >> 2)
    one = jnp.where(iota((128, PAIRS), 0) == place, 1.0, 0.0)
    select[...] = jnp.concatenate([one, one, one], axis=1).astype(BF16)
    later = iota((PAIRS, PAIRS), 0) > iota((PAIRS, PAIRS), 1)
    rank_down = jnp.sum(jnp.where(same & later, 1.0, 0.0), axis=1, keepdims=True)
    quarter = (iota((PAIRS, 128), 1) >> 5).astype(F32)
    mine = jnp.where(owner_down[:, :1] == d.astype(F32), rank_down, -1.0)
    masks = [jnp.where(mine == quarter + 4.0 * g, 1.0, 0.0) for g in range(3)]
    masks = jnp.concatenate(masks, axis=1)
    own[...] = jnp.concatenate([masks, jnp.zeros_like(masks)], axis=0).astype(BF16)

    date = jnp.concatenate([pairs_v[0:1, :], pairs_v[1:2, :]], axis=1)
    one = jnp.where((iota((ROWS, 2 * PAIRS), 0) >> 5) == (date & (EACH - 1)), 1.0, 0.0)
    hot[...] = jnp.concatenate([one, one, one], axis=0).astype(BF16)
    source_of[...] = jnp.where(iota((GROUP, 2 * PAIRS), 0) == (date >> 2), 1.0, 0.0)
    one = jnp.where((iota((ROWS, 128), 0) >> 2) == (iota((ROWS, 128), 1) & 31), 1.0, 0.0)
    look[...] = jnp.concatenate([one, one, one], axis=0).astype(BF16)

    def edges(side):
        stage(
            edge_in[side], edge_in[side], edge_send.at[side], edge_recv.at[0], targets[side]
        ).wait_recv()

    def smooth_powers(number):
        for t in range(number):
            big, small = split(along_columns(fields, t))
            lhs[HALF * t : HALF * (t + 1), :ROWS] = big
            lhs[HALF * t : HALF * (t + 1), ROWS:] = small
        smooth = dot(lhs[: number * HALF, :], smoother[...])
        return jnp.sqrt(smooth[:, :ROWS] + smooth[:, ROWS:])

    def take_first(sources, ref):
        size = PIECES[0]
        for i, source in enumerate(sources):
            for t in range(EACH):
                piece = ref[source, 2 * size * t : 2 * size * (t + 1), :].astype(F32)
                edge = edge_left[source, 16 * t : 16 * (t + 1), :].astype(F32)
                real = jnp.concatenate([piece[:8] + edge[:8], piece[8:size]], axis=0)
                imag = jnp.concatenate([piece[size : size + 8] + edge[8:], piece[size + 8 :]], axis=0)
                images[source * EACH + t, 0, :size] = real
                images[source * EACH + t, 1, :size] = imag
                fields[EACH * i + t] = real * real + imag * imag
        smooth = smooth_powers(EACH * len(sources))
        for i, source in enumerate(sources):
            for t in range(EACH):
                at = HALF * (EACH * i + t)
                roots[source * EACH + t, :HALF] = smooth[at : at + HALF]

    def arrive(*ks):
        first_copy(ks[0], len(ks)).wait_recv()
        take_first([(d + GROUP - k) % GROUP for k in ks], got_0)

    def take_second():
        size = PIECES[1]
        for date in range(DATES):
            source, t = date // EACH, date % EACH
            piece = got_1[source, 2 * size * t : 2 * size * (t + 1), :].astype(F32)
            edge = edge_right[source, 16 * t : 16 * (t + 1), :].astype(F32)
            real = jnp.concatenate([piece[:8], piece[8:size] + edge[:8]], axis=0)
            imag = jnp.concatenate([piece[size : size + 8], piece[size + 8 :] + edge[8:]], axis=0)
            images[date, 0, PIECES[0] :] = real
            images[date, 1, PIECES[0] :] = imag
            real = jnp.concatenate([images[date, 0, HALF : PIECES[0]], real], axis=0)
            imag = jnp.concatenate([images[date, 1, HALF : PIECES[0]], imag], axis=0)
            fields[date] = real * real + imag * imag
        smooth = smooth_powers(DATES)
        for date in range(DATES):
            roots[date, HALF:] = smooth[HALF * date : HALF * (date + 1)]

    def pairs_of(half, then=None):
        window = slice(HALF * half, HALF * half + WINDOW)

        def place(field, p):
            return pl.ds(((3 * half + field) * PAIRS + p) * 8, 8)

        def chunk(index, carry):
            dates = []
            for i in range(CHUNK):
                p = index * CHUNK + i
                first = pairs_s[0, p]
                second = pairs_s[1, p]
                dates.append((first, second))
                real_a = images[first, 0, window]
                imag_a = images[first, 1, window]
                real_b = images[second, 0, window]
                imag_b = images[second, 1, window]
                fields[2 * i] = real_a * real_b + imag_a * imag_b
                fields[2 * i + 1] = imag_a * real_b - real_a * imag_b
            for i in range(CHUNK):
                p = index * CHUNK + i
                for f in range(2):
                    n = 2 * i + f
                    big, small = split(along_columns(fields, n))
                    lhs[HALF * n : HALF * (n + 1), :ROWS] = big
                    lhs[HALF * n : HALF * (n + 1), ROWS:] = small
                    sums[place(f, p), :] = fields[n, 4:12, :] + fields[n, 12:20, :]
            smooth = dot(lhs[...], smoother[...])
            smooth = smooth[:, :ROWS] + smooth[:, ROWS:]
            for i in range(CHUNK):
                p = index * CHUNK + i
                first, second = dates[i]
                real = smooth[2 * HALF * i : 2 * HALF * i + HALF]
                imag = smooth[2 * HALF * i + HALF : 2 * HALF * (i + 1)]
                below = (
                    roots[first, HALF * half : HALF * (half + 1)]
                    * roots[second, HALF * half : HALF * (half + 1)]
                )
                value = jnp.sqrt(real * real + imag * imag) / (below + 1e-06)
                sums[place(2, p), :] = value[0:8] + value[8:16]
            return carry

        lax.fori_loop(0, PAIRS // CHUNK, chunk, 0)
        if then is not None:
            then()
        rows = sums[pl.ds(3 * half * PAIRS * 8, 3 * PAIRS, stride=8), :]
        for i in range(1, 8):
            rows = rows + sums[pl.ds(3 * half * PAIRS * 8 + i, 3 * PAIRS, stride=8), :]
        looked[half] = dot(jnp.concatenate(split3(rows), axis=1), look[...])

    @pl.when(right_later)
    def _():
        pl.semaphore_wait(ready.at[0], 1)

        @pl.when(d == GROUP - 1)
        def _():
            for e in range(GROUP - 1):
                tell_ready(0, e, c)

        edge_copy(0).start()

    @pl.when(left_later)
    def _():
        pl.semaphore_wait(ready.at[1], 1)
        edge_copy(1).start()

    @pl.when((d == 0) & (c > 0))
    def _():
        edges(0)

    take_first([d], sent_0)
    arrive(4)
    arrive(3)
    arrive(5)
    arrive(2, 6, 1, 7)
    pairs_of(0)

    def d_copy(k, size=1):
        return stage(
            totals.at[pl.ds(d if size == 1 else 0, size)], totals.at[pl.ds(d if size == 1 else 0, size)],
            d_send.at[0], d_recv.at[0], date_peer(k),
        )

    def add_up():
        @pl.when(c == 0)
        def _():
            up_copy(1, count - 1).wait_recv()
            total = power_row[...] + jnp.sum(power_in[1:count, :], axis=0, keepdims=True)
            totals[pl.ds(d, 1), :] = total
            for k in order:
                d_copy(k).start()

    @pl.when((d == GROUP - 1) & (c < count - 1))
    def _():
        edges(1)

    second_copy(1, GROUP - 1).wait_recv()
    take_second()
    pairs_of(1, add_up)

    wide = []
    for q in range(6):
        piece = looked[q // 3, PAIRS * (q % 3) : PAIRS * (q % 3 + 1)]
        wide.append(piece if q % 3 < 2 else piece * (1.0 / 64.0))
    stacked = jnp.concatenate(split3(jnp.concatenate(wide, axis=1)), axis=0)
    placed = dot(select[...], stacked)
    lane = iota((32, 128), 1)
    for q in range(6):
        part = placed[:, 128 * q : 128 * (q + 1)]
        value = jnp.where(
            lane < 64,
            jnp.where(lane < 32, part[0:32], part[32:64]),
            jnp.where(lane < 96, part[64:96], part[96:128]),
        )
        for e in range(GROUP):
            results[e, 4 * q : 4 * q + 4, :] = value[4 * e : 4 * e + 4]

    def out_copy(k, size=1):
        return stage(
            results.at[pl.ds((d + k) % GROUP if size == 1 else 0, size)],
            landed.at[pl.ds(d if size == 1 else 0, size)],
            out_send.at[0], out_recv.at[0], date_peer(k),
        )

    for k in order:
        out_copy(k).start()
    landed[d] = results[d]

    @pl.when(c == 0)
    def _():
        d_copy(1, GROUP - 1).wait_recv()
        parts = jnp.concatenate(split3(totals[...]), axis=1)
        total = jnp.sum(dot(parts, hot[...]) * source_of[...], axis=0, keepdims=True)
        scale = jnp.sqrt(total / (ROWS * WIDTH * count) + 1e-06)
        factor = (1.0 / 64.0) / (scale * pltpu.roll(scale, PAIRS, 1))
        factor_in[...] = factor
        for i in range(near):
            for j in range(count // nz):
                if i + j > 0:
                    down_copy(j * nz + i).start()

    @pl.when(c > 0)
    def _():
        down_copy(0).wait_recv()

    @pl.when(hands_on)
    def _():
        if nz > near:
            pl.semaphore_wait(here, nz - near)
        for i in range(near, nz):
            down_copy(hand - (near - 1) + i).start()

    factors = dot(jnp.concatenate(split3(factor_in[...]), axis=0), own[...])
    factors = jnp.sum(factors, axis=0, keepdims=True)
    for g in range(3):
        scaling[g : g + 1, :] = factors[:, 128 * g : 128 * (g + 1)]
    out_copy(1, GROUP - 1).wait_recv()
    first_copy(1, GROUP - 1).wait_send()
    second_copy(1, GROUP - 1).wait_send()
    out_copy(1, GROUP - 1).wait_send()

    @pl.when(right_later | right_earlier)
    def _():
        edge_copy(0).wait_send()

    @pl.when(left_later | left_earlier)
    def _():
        edge_copy(1).wait_send()

    def sent_down(number):
        stage(
            power_in.at[pl.ds(0, number)], power_in.at[pl.ds(0, number)], down_send.at[0],
            down_recv.at[0], {"dates": d, "cols": c},
        ).wait_send()

    @pl.when(c > 0)
    def _():
        up_copy(c).wait_send()

    @pl.when(c == 0)
    def _():
        d_copy(1, GROUP - 1).wait_send()
        sent_down(near * (count // nz) - 1)

    if nz > near:

        @pl.when(hands_on)
        def _():
            sent_down(nz - near)


def place_kernel(landed, scaling, interferogram, coherence):
    for f in range(3):
        for g in range(3):
            block = landed[pl.ds(f * 4 + g, 16, stride=12), :]
            if f < 2:
                block = block * scaling[g : g + 1, :]
            for j in range(4):
                piece = block[:, 32 * j : 32 * j + 32]
                if f < 2:
                    interferogram[f, 4 * g + j] = piece
                else:
                    coherence[4 * g + j] = piece


def solution(mesh):
    columns = mesh.shape["cols"]
    nz = 8 if columns % 8 == 0 else 2
    sem = pltpu.SemaphoreType.DMA
    vmem = pl.BlockSpec(memory_space=pltpu.VMEM)

    def local(slc, pairs, owner):
        pairs = pairs.T
        owner = owner.reshape(1, PAIRS)
        landed, scaling = pl.pallas_call(
            lambda *refs: kernel(nz, columns, *refs),
            out_shape=(jax.ShapeDtypeStruct((GROUP, 24, 128), F32), jax.ShapeDtypeStruct((8, 128), F32)),
            in_specs=[pl.BlockSpec(memory_space=pl.ANY)] * 3,
            out_specs=(vmem, vmem),
            scratch_shapes=[
                pltpu.VMEM((2, EACH, ROWS, WIDTH), BF16),
                pltpu.SMEM((2, PAIRS), jnp.int32),
                pltpu.VMEM((2, PAIRS), jnp.int32),
                pltpu.VMEM((1, PAIRS), jnp.int32),
                pltpu.VMEM((128, 3 * PAIRS), BF16),
                pltpu.VMEM((128, 3 * 128), BF16),
                pltpu.VMEM((3 * ROWS, 128), BF16),
                pltpu.VMEM((3 * ROWS, 2 * PAIRS), BF16),
                pltpu.VMEM((GROUP, 2 * PAIRS), F32),
                pltpu.VMEM((2 * ROWS, 2 * ROWS), BF16),
                pltpu.VMEM((GROUP, EACH * 2 * PIECES[0], ROWS), BF16),
                pltpu.VMEM((GROUP, EACH * 2 * PIECES[1], ROWS), BF16),
                pltpu.VMEM((GROUP, EACH * 2 * PIECES[0], ROWS), BF16),
                pltpu.VMEM((GROUP, EACH * 2 * PIECES[1], ROWS), BF16),
                pltpu.VMEM((2, EDGE, ROWS), BF16),
                pltpu.VMEM((GROUP, EDGE, ROWS), BF16),
                pltpu.VMEM((GROUP, EDGE, ROWS), BF16),
                pltpu.VMEM((DATES, 2, TILE, ROWS), F32),
                pltpu.VMEM((DATES, PART, ROWS), F32),
                pltpu.VMEM((2 * CHUNK, WINDOW, ROWS), F32),
                pltpu.VMEM((2 * CHUNK * HALF, 2 * ROWS), BF16),
                pltpu.VMEM((6 * PAIRS * 8, ROWS), F32),
                pltpu.VMEM((2, 3 * PAIRS, ROWS), F32),
                pltpu.VMEM((1, ROWS), F32),
                pltpu.VMEM((columns, ROWS), F32),
                pltpu.VMEM((GROUP, ROWS), F32),
                pltpu.VMEM((1, ROWS), F32),
                pltpu.VMEM((GROUP, 24, 128), F32),
                sem((1,)), sem((4,)), sem((1,)), sem((1,)),
                sem((2,)), sem((1,)), pltpu.SemaphoreType.REGULAR((2,)), pltpu.SemaphoreType.REGULAR,
                sem((1,)), sem((1,)), sem((1,)), sem((1,)),
                sem((1,)), sem((1,)), sem((1,)), sem((1,)),
                sem((1,)), sem((3,)),
            ],
            compiler_params=pltpu.CompilerParams(
                collective_id=0, has_side_effects=True, vmem_limit_bytes=54682 * 1024
            ),
        )(slc, pairs, owner)
        interferogram, coherence = pl.pallas_call(
            place_kernel,
            out_shape=(
                jax.ShapeDtypeStruct((2, CAP, 16, 32), F32),
                jax.ShapeDtypeStruct((CAP, 16, 32), F32),
            ),
            in_specs=[vmem, vmem],
            out_specs=(vmem, vmem),
            compiler_params=pltpu.CompilerParams(vmem_limit_bytes=2 * 1024 * 1024),
        )(landed.reshape(GROUP * 24, 128), scaling)
        return jnp.swapaxes(interferogram, 2, 3), jnp.swapaxes(coherence, 1, 2)

    return jax.shard_map(
        local,
        mesh=mesh,
        in_specs=(P(None, "dates", None, "cols"), P(), P()),
        out_specs=(P(None, "dates", None, "cols"), P("dates", None, "cols")),
        check_vma=False,
    )
```

```python
import math

import jax
import jax.numpy as jnp
import ml_dtypes
import numpy as np
from jax import lax
from jax.experimental import pallas as pl
from jax.experimental.pallas import tpu as pltpu
from jax.sharding import PartitionSpec as P

MESH = pl.DeviceIdType.MESH
F32 = jnp.float32
BF16 = jnp.bfloat16

TAPS = [math.exp(-k * k / 8.0) for k in range(-4, 5)]
WEIGHTS = [float(np.float32(t / sum(TAPS))) for t in TAPS]
HIGH = [float(np.float32(w).astype(ml_dtypes.bfloat16)) for w in WEIGHTS]
LOW = [float(np.float32(w - h).astype(ml_dtypes.bfloat16)) for w, h in zip(WEIGHTS, HIGH)]

GROUP = 8
EACH = 4
DATES = GROUP * EACH
PAIRS = 64
CAP = 12
ROWS = 128
PART = 32
TILE = PART + 8
WIDTH = GROUP * PART
PIECES = (24, 16)
HALF = PART // 2
WINDOW = HALF + 8
EDGE = EACH * 2 * 8
CHUNK = 32


def split(x):
    high = x.astype(BF16)
    return high, (x - high.astype(F32)).astype(BF16)


def split3(x):
    high = x.astype(BF16)
    rest = x - high.astype(F32)
    mid = rest.astype(BF16)
    return high, mid, (rest - mid.astype(F32)).astype(BF16)


def dot(a, b):
    return jnp.dot(a, b, preferred_element_type=F32)


def iota(shape, axis):
    return lax.broadcasted_iota(jnp.int32, shape, axis)


def cutter(half):
    start, size = (-4, PIECES[0]) if half == 0 else (PIECES[0] - 4, PIECES[1])
    lane = iota((size, WIDTH), 1)
    row = iota((size, WIDTH), 0)
    pieces = [jnp.where(lane == row + (PART * e + start), 1.0, 0.0) for e in range(GROUP)]
    lane = iota((8, WIDTH), 1)
    row = iota((8, WIDTH), 0)
    pieces.append(jnp.where(lane == row + (WIDTH - 4 if half == 0 else -4), 1.0, 0.0))
    return jnp.concatenate(pieces, axis=0).astype(BF16)


def band(weights):
    gap = jnp.abs(iota((ROWS, ROWS), 0) - iota((ROWS, ROWS), 1))
    result = jnp.zeros((ROWS, ROWS), F32)
    for k in range(5):
        result = jnp.where(gap == k, weights[4 + k], result)
    return result.astype(BF16)


def along_columns(ref, index):
    result = WEIGHTS[4] * ref[index, 4 : 4 + HALF, :]
    for k in range(4):
        both = ref[index, k : k + HALF, :] + ref[index, 8 - k : 8 - k + HALF, :]
        result = result + WEIGHTS[k] * both
    return result


def kernel(
    nz, count, slc_hbm, pairs_hbm, owner_hbm, landed, scaling,
    slc, pairs_s, pairs_v, owner_v, select, own, look, hot, source_of, smoother, sent_0, sent_1, got_0, got_1,
    edge_out, edge_left, edge_right, images, roots, fields, lhs, sums, looked,
    power_row, power_in, totals, factor_in, results,
    main_send_0, main_recv_0, main_send_1, main_recv_1, edge_send, edge_recv, ready, joined,
    here, up_send, up_recv, down_send, down_recv, d_send, d_recv, out_send, out_recv, in_sem, table_sem,
):
    load = pltpu.make_async_copy(slc_hbm, slc, in_sem.at[0])
    load.start()

    d = lax.axis_index("dates")
    c = lax.axis_index("cols")
    z = c % nz

    def date_peer(k):
        return {"dates": (d + k) % GROUP, "cols": c}

    right = (c + 1) % count
    left = (c + count - 1) % count
    near = min(3, nz)
    right_later = (z < nz - 1) & (c < count - 1)
    right_earlier = (z == nz - 1) & (c < count - 1)
    left_later = (z == 0) & (c > 0)
    left_earlier = (z > 0) & (c > 0)

    barrier = pltpu.get_barrier_semaphore()

    def greet(device):
        pl.semaphore_signal(barrier, inc=1, device_id=device, device_id_type=MESH)

    def turn(e):
        return jnp.where(c == 0, (e + GROUP - 1) % GROUP, e)

    mine_turn = turn(d)
    for k in range(1, GROUP):

        @pl.when(turn((d + k) % GROUP) > mine_turn)
        def _():
            greet(date_peer(k))

    @pl.when(right_later & (d == GROUP - 1))
    def _():
        for e in range(GROUP):
            greet({"dates": e, "cols": right})

    @pl.when(left_later)
    def _():
        greet({"dates": GROUP - 1, "cols": left})

    @pl.when(left_later & (d == 0))
    def _():
        for e in range(GROUP):
            greet({"dates": e, "cols": left})

    @pl.when(c == 0)
    def _():
        def one(i, carry):
            greet({"dates": d, "cols": i})
            return carry

        lax.fori_loop(1, count, one, 0)

    hands_on = z == near - 1
    handed = z >= near
    hand = c - z + near - 1

    @pl.when(hands_on)
    def _():
        for i in range(near, nz):
            greet({"dates": d, "cols": hand - (near - 1) + i})

    tables = [
        pltpu.make_async_copy(pairs_hbm, pairs_s, table_sem.at[0]),
        pltpu.make_async_copy(pairs_hbm, pairs_v, table_sem.at[1]),
        pltpu.make_async_copy(owner_hbm, owner_v, table_sem.at[2]),
    ]
    for table in tables:
        table.start()

    sent = (sent_0, sent_1)
    edge_in = (edge_left, edge_right)
    got = (got_0, got_1)

    def cut(half, matrix):
        size = PIECES[half]
        for t in range(EACH):
            both = jnp.concatenate([slc[0, t], slc[1, t]], axis=0)
            turned = lax.dot_general(
                matrix, both, (((1,), (1,)), ((), ())), preferred_element_type=F32
            )
            for e in range(GROUP + 1):
                rows = turned[size * e : size * (e + 1)] if e < GROUP else turned[size * GROUP :]
                value = jnp.concatenate([rows[:, :ROWS], rows[:, ROWS:]], axis=0).astype(BF16)
                if e < GROUP:
                    sent[half][e, 2 * size * t : 2 * size * (t + 1), :] = value
                else:
                    edge_out[half, 16 * t : 16 * (t + 1), :] = value

    matrix = cutter(0)
    high = band(HIGH)
    low = band(LOW)
    smoother[:, :ROWS] = jnp.concatenate([high, high], axis=0)
    smoother[:, ROWS:] = jnp.concatenate([low, low], axis=0)

    def powers():
        power_rows = []
        for t in range(EACH):
            wide = jnp.concatenate([slc[0, t], slc[1, t]], axis=0).astype(F32)
            square = jnp.sum(wide * wide, axis=0, keepdims=True)
            power_rows.append(square[:, :ROWS] + square[:, ROWS:])
        folded = jnp.concatenate(power_rows + [jnp.zeros((8 - EACH, ROWS), F32)], axis=0)
        folded = folded + pltpu.roll(folded, 64, 1)
        folded = folded + pltpu.roll(folded, 32, 1)
        own_lane = (iota((8, ROWS), 1) >> 5) == iota((8, ROWS), 0)
        power_row[...] = jnp.sum(jnp.where(own_lane, folded, 0.0), axis=0, keepdims=True)

    def stage(src, dst, send, recv, peer):
        return pltpu.make_async_remote_copy(
            src_ref=src, dst_ref=dst, send_sem=send, recv_sem=recv, device_id=peer, device_id_type=MESH
        )

    def up_copy(i, size=1):
        return stage(
            power_in.at[pl.ds(0, size)] if size > 1 else power_row, power_in.at[pl.ds(i, size)],
            up_send.at[0], up_recv.at[0], {"dates": d, "cols": 0},
        )

    def down_copy(i):
        return stage(factor_in, factor_in, down_send.at[0], down_recv.at[0], {"dates": d, "cols": i})

    last = (d == GROUP - 1).astype(jnp.int32)

    def tell_ready(side, e, other):
        pl.semaphore_signal(
            ready.at[side], inc=1, device_id={"dates": e, "cols": other}, device_id_type=MESH
        )

    def enter():
        awaited = (
            mine_turn
            + (c > 0).astype(jnp.int32)
            + handed.astype(jnp.int32)
            + right_earlier.astype(jnp.int32) * (1 + GROUP * last)
            + left_earlier.astype(jnp.int32)
        )

        @pl.when(awaited > 0)
        def _():
            pl.semaphore_wait(barrier, awaited)

        for k in range(1, GROUP):

            @pl.when(turn((d + k) % GROUP) < mine_turn)
            def _():
                pl.semaphore_signal(joined, inc=1, device_id=date_peer(k), device_id_type=MESH)

        @pl.when(handed)
        def _():
            pl.semaphore_signal(
                here, inc=1, device_id={"dates": d, "cols": hand}, device_id_type=MESH
            )

        @pl.when(left_earlier & (d == 0))
        def _():
            tell_ready(0, GROUP - 1, left)

        @pl.when(right_earlier & (d == GROUP - 1))
        def _():
            for e in range(GROUP):
                tell_ready(1, e, right)

    def send_up():
        @pl.when(c > 0)
        def _():
            up_copy(c).start()

    late = z >= nz // 2

    enter()
    load.wait()

    @pl.when(late)
    def _():
        powers()
        send_up()

    cut(0, matrix)

    @pl.when(mine_turn < GROUP - 1)
    def _():
        pl.semaphore_wait(joined, GROUP - 1 - mine_turn)

    targets = ({"dates": 0, "cols": right}, {"dates": GROUP - 1, "cols": left})

    def edge_copy(side):
        return pltpu.make_async_remote_copy(
            src_ref=edge_out.at[side], dst_ref=edge_in[side].at[d], send_sem=edge_send.at[side],
            recv_sem=edge_recv.at[0], device_id=targets[side], device_id_type=MESH,
        )

    order = (4, 3, 5, 2, 6, 1, 7)
    slots = {4: 0, 3: 1, 5: 2}

    def first_copy(k, size=1):
        return stage(
            sent_0.at[pl.ds((d + k) % GROUP if size == 1 else 0, size)],
            got_0.at[pl.ds(d if size == 1 else 0, size)],
            main_send_0.at[0], main_recv_0.at[slots.get(k, 3)], date_peer(k),
        )

    def second_copy(k, size=1):
        return stage(
            sent_1.at[pl.ds((d + k) % GROUP if size == 1 else 0, size)],
            got_1.at[pl.ds(d if size == 1 else 0, size)],
            main_send_1.at[0], main_recv_1.at[0], date_peer(k),
        )

    for k in order:
        first_copy(k).start()

    @pl.when(z < nz // 2)
    def _():
        powers()
        send_up()

    @pl.when(right_earlier)
    def _():
        edge_copy(0).start()

    cut(1, cutter(1))
    for k in order:
        second_copy(k).start()

    @pl.when(left_earlier)
    def _():
        edge_copy(1).start()

    got_1[d] = sent_1[d]

    @pl.when((d != 0) | (c == 0))
    def _():
        edge_left[...] = jnp.zeros_like(edge_left)

    @pl.when((d != GROUP - 1) | (c == count - 1))
    def _():
        edge_right[...] = jnp.zeros_like(edge_right)


    for table in tables:
        table.wait()
    owner_row = owner_v[...]
    owner_down = jnp.transpose(jnp.broadcast_to(owner_row.astype(F32), (ROWS, PAIRS)))[:, :PAIRS]
    earlier = iota((PAIRS, PAIRS), 0) < iota((PAIRS, PAIRS), 1)
    same = owner_down == owner_row.astype(F32)
    rank = jnp.sum(jnp.where(same & earlier, 1.0, 0.0), axis=0, keepdims=True).astype(jnp.int32)
    place = (rank & 3) * 32 + owner_row * 4 + (rank >> 2)
    one = jnp.where(iota((128, PAIRS), 0) == place, 1.0, 0.0)
    select[...] = jnp.concatenate([one, one, one], axis=1).astype(BF16)
    later = iota((PAIRS, PAIRS), 0) > iota((PAIRS, PAIRS), 1)
    rank_down = jnp.sum(jnp.where(same & later, 1.0, 0.0), axis=1, keepdims=True)
    quarter = (iota((PAIRS, 128), 1) >> 5).astype(F32)
    mine = jnp.where(owner_down[:, :1] == d.astype(F32), rank_down, -1.0)
    masks = [jnp.where(mine == quarter + 4.0 * g, 1.0, 0.0) for g in range(3)]
    masks = jnp.concatenate(masks, axis=1)
    own[...] = jnp.concatenate([masks, jnp.zeros_like(masks)], axis=0).astype(BF16)

    date = jnp.concatenate([pairs_v[0:1, :], pairs_v[1:2, :]], axis=1)
    one = jnp.where((iota((ROWS, 2 * PAIRS), 0) >> 5) == (date & (EACH - 1)), 1.0, 0.0)
    hot[...] = jnp.concatenate([one, one, one], axis=0).astype(BF16)
    source_of[...] = jnp.where(iota((GROUP, 2 * PAIRS), 0) == (date >> 2), 1.0, 0.0)
    one = jnp.where((iota((ROWS, 128), 0) >> 2) == (iota((ROWS, 128), 1) & 31), 1.0, 0.0)
    look[...] = jnp.concatenate([one, one, one], axis=0).astype(BF16)

    def edges(side):
        stage(
            edge_in[side], edge_in[side], edge_send.at[side], edge_recv.at[0], targets[side]
        ).wait_recv()

    def smooth_powers(number):
        for t in range(number):
            big, small = split(along_columns(fields, t))
            lhs[HALF * t : HALF * (t + 1), :ROWS] = big
            lhs[HALF * t : HALF * (t + 1), ROWS:] = small
        smooth = dot(lhs[: number * HALF, :], smoother[...])
        return jnp.sqrt(smooth[:, :ROWS] + smooth[:, ROWS:])

    def take_first(sources, ref):
        size = PIECES[0]
        for i, source in enumerate(sources):
            for t in range(EACH):
                piece = ref[source, 2 * size * t : 2 * size * (t + 1), :].astype(F32)
                edge = edge_left[source, 16 * t : 16 * (t + 1), :].astype(F32)
                real = jnp.concatenate([piece[:8] + edge[:8], piece[8:size]], axis=0)
                imag = jnp.concatenate([piece[size : size + 8] + edge[8:], piece[size + 8 :]], axis=0)
                images[source * EACH + t, 0, :size] = real
                images[source * EACH + t, 1, :size] = imag
                fields[EACH * i + t] = real * real + imag * imag
        smooth = smooth_powers(EACH * len(sources))
        for i, source in enumerate(sources):
            for t in range(EACH):
                at = HALF * (EACH * i + t)
                roots[source * EACH + t, :HALF] = smooth[at : at + HALF]

    def arrive(*ks):
        first_copy(ks[0], len(ks)).wait_recv()
        take_first([(d + GROUP - k) % GROUP for k in ks], got_0)

    def take_second():
        size = PIECES[1]
        for date in range(DATES):
            source, t = date // EACH, date % EACH
            piece = got_1[source, 2 * size * t : 2 * size * (t + 1), :].astype(F32)
            edge = edge_right[source, 16 * t : 16 * (t + 1), :].astype(F32)
            real = jnp.concatenate([piece[:8], piece[8:size] + edge[:8]], axis=0)
            imag = jnp.concatenate([piece[size : size + 8], piece[size + 8 :] + edge[8:]], axis=0)
            images[date, 0, PIECES[0] :] = real
            images[date, 1, PIECES[0] :] = imag
            real = jnp.concatenate([images[date, 0, HALF : PIECES[0]], real], axis=0)
            imag = jnp.concatenate([images[date, 1, HALF : PIECES[0]], imag], axis=0)
            fields[date] = real * real + imag * imag
        smooth = smooth_powers(DATES)
        for date in range(DATES):
            roots[date, HALF:] = smooth[HALF * date : HALF * (date + 1)]

    def pairs_of(half, then=None):
        window = slice(HALF * half, HALF * half + WINDOW)

        def place(field, p):
            return pl.ds(((3 * half + field) * PAIRS + p) * 8, 8)

        def chunk(index, carry):
            dates = []
            for i in range(CHUNK):
                p = index * CHUNK + i
                first = pairs_s[0, p]
                second = pairs_s[1, p]
                dates.append((first, second))
                real_a = images[first, 0, window]
                imag_a = images[first, 1, window]
                real_b = images[second, 0, window]
                imag_b = images[second, 1, window]
                fields[2 * i] = real_a * real_b + imag_a * imag_b
                fields[2 * i + 1] = imag_a * real_b - real_a * imag_b
            for i in range(CHUNK):
                p = index * CHUNK + i
                for f in range(2):
                    n = 2 * i + f
                    big, small = split(along_columns(fields, n))
                    lhs[HALF * n : HALF * (n + 1), :ROWS] = big
                    lhs[HALF * n : HALF * (n + 1), ROWS:] = small
                    sums[place(f, p), :] = fields[n, 4:12, :] + fields[n, 12:20, :]
            smooth = dot(lhs[...], smoother[...])
            smooth = smooth[:, :ROWS] + smooth[:, ROWS:]
            for i in range(CHUNK):
                p = index * CHUNK + i
                first, second = dates[i]
                real = smooth[2 * HALF * i : 2 * HALF * i + HALF]
                imag = smooth[2 * HALF * i + HALF : 2 * HALF * (i + 1)]
                below = (
                    roots[first, HALF * half : HALF * (half + 1)]
                    * roots[second, HALF * half : HALF * (half + 1)]
                )
                value = jnp.sqrt(real * real + imag * imag) / (below + 1e-06)
                sums[place(2, p), :] = value[0:8] + value[8:16]
            return carry

        lax.fori_loop(0, PAIRS // CHUNK, chunk, 0)
        if then is not None:
            then()
        rows = sums[pl.ds(3 * half * PAIRS * 8, 3 * PAIRS, stride=8), :]
        for i in range(1, 8):
            rows = rows + sums[pl.ds(3 * half * PAIRS * 8 + i, 3 * PAIRS, stride=8), :]
        looked[half] = dot(jnp.concatenate(split3(rows), axis=1), look[...])

    @pl.when(right_later)
    def _():
        pl.semaphore_wait(ready.at[0], 1)

        @pl.when(d == GROUP - 1)
        def _():
            for e in range(GROUP - 1):
                tell_ready(0, e, c)

        edge_copy(0).start()

    @pl.when(left_later)
    def _():
        pl.semaphore_wait(ready.at[1], 1)
        edge_copy(1).start()

    @pl.when((d == 0) & (c > 0))
    def _():
        edges(0)

    take_first([d], sent_0)
    arrive(4)
    arrive(3)
    arrive(5)
    arrive(2, 6, 1, 7)
    pairs_of(0)

    def d_copy(k, size=1):
        return stage(
            totals.at[pl.ds(d if size == 1 else 0, size)], totals.at[pl.ds(d if size == 1 else 0, size)],
            d_send.at[0], d_recv.at[0], date_peer(k),
        )

    def add_up():
        @pl.when(c == 0)
        def _():
            up_copy(1, count - 1).wait_recv()
            total = power_row[...] + jnp.sum(power_in[1:count, :], axis=0, keepdims=True)
            totals[pl.ds(d, 1), :] = total
            for k in order:
                d_copy(k).start()

    @pl.when((d == GROUP - 1) & (c < count - 1))
    def _():
        edges(1)

    second_copy(1, GROUP - 1).wait_recv()
    take_second()
    pairs_of(1, add_up)

    wide = []
    for q in range(6):
        piece = looked[q // 3, PAIRS * (q % 3) : PAIRS * (q % 3 + 1)]
        wide.append(piece if q % 3 < 2 else piece * (1.0 / 64.0))
    stacked = jnp.concatenate(split3(jnp.concatenate(wide, axis=1)), axis=0)
    placed = dot(select[...], stacked)
    lane = iota((32, 128), 1)
    for q in range(6):
        part = placed[:, 128 * q : 128 * (q + 1)]
        value = jnp.where(
            lane < 64,
            jnp.where(lane < 32, part[0:32], part[32:64]),
            jnp.where(lane < 96, part[64:96], part[96:128]),
        )
        for e in range(GROUP):
            results[e, 4 * q : 4 * q + 4, :] = value[4 * e : 4 * e + 4]

    def out_copy(k, size=1):
        return stage(
            results.at[pl.ds((d + k) % GROUP if size == 1 else 0, size)],
            landed.at[pl.ds(d if size == 1 else 0, size)],
            out_send.at[0], out_recv.at[0], date_peer(k),
        )

    for k in order:
        out_copy(k).start()
    landed[d] = results[d]

    @pl.when(c == 0)
    def _():
        d_copy(1, GROUP - 1).wait_recv()
        parts = jnp.concatenate(split3(totals[...]), axis=1)
        total = jnp.sum(dot(parts, hot[...]) * source_of[...], axis=0, keepdims=True)
        scale = jnp.sqrt(total / (ROWS * WIDTH * count) + 1e-06)
        factor = (1.0 / 64.0) / (scale * pltpu.roll(scale, PAIRS, 1))
        factor_in[...] = factor
        for i in range(near):
            for j in range(count // nz):
                if i + j > 0:
                    down_copy(j * nz + i).start()

    @pl.when(c > 0)
    def _():
        down_copy(0).wait_recv()

    @pl.when(hands_on)
    def _():
        if nz > near:
            pl.semaphore_wait(here, nz - near)
        for i in range(near, nz):
            down_copy(hand - (near - 1) + i).start()

    factors = dot(jnp.concatenate(split3(factor_in[...]), axis=0), own[...])
    factors = jnp.sum(factors, axis=0, keepdims=True)
    for g in range(3):
        scaling[g : g + 1, :] = factors[:, 128 * g : 128 * (g + 1)]
    out_copy(1, GROUP - 1).wait_recv()
    first_copy(1, GROUP - 1).wait_send()
    second_copy(1, GROUP - 1).wait_send()
    out_copy(1, GROUP - 1).wait_send()

    @pl.when(right_later | right_earlier)
    def _():
        edge_copy(0).wait_send()

    @pl.when(left_later | left_earlier)
    def _():
        edge_copy(1).wait_send()

    def sent_down(number):
        stage(
            power_in.at[pl.ds(0, number)], power_in.at[pl.ds(0, number)], down_send.at[0],
            down_recv.at[0], {"dates": d, "cols": c},
        ).wait_send()

    @pl.when(c > 0)
    def _():
        up_copy(c).wait_send()

    @pl.when(c == 0)
    def _():
        d_copy(1, GROUP - 1).wait_send()
        sent_down(near * (count // nz) - 1)

    if nz > near:

        @pl.when(hands_on)
        def _():
            sent_down(nz - near)


def place_kernel(landed, scaling, interferogram, coherence):
    for f in range(3):
        for g in range(3):
            block = landed[pl.ds(f * 4 + g, 16, stride=12), :]
            if f < 2:
                block = block * scaling[g : g + 1, :]
            for j in range(4):
                piece = block[:, 32 * j : 32 * j + 32]
                if f < 2:
                    interferogram[f, 4 * g + j] = piece
                else:
                    coherence[4 * g + j] = piece


def solution(mesh):
    columns = mesh.shape["cols"]
    nz = 8 if columns % 8 == 0 else 2
    sem = pltpu.SemaphoreType.DMA
    vmem = pl.BlockSpec(memory_space=pltpu.VMEM)

    def local(slc, pairs, owner):
        pairs = pairs.T
        owner = owner.reshape(1, PAIRS)
        landed, scaling = pl.pallas_call(
            lambda *refs: kernel(nz, columns, *refs),
            out_shape=(jax.ShapeDtypeStruct((GROUP, 24, 128), F32), jax.ShapeDtypeStruct((8, 128), F32)),
            in_specs=[pl.BlockSpec(memory_space=pl.ANY)] * 3,
            out_specs=(vmem, vmem),
            scratch_shapes=[
                pltpu.VMEM((2, EACH, ROWS, WIDTH), BF16),
                pltpu.SMEM((2, PAIRS), jnp.int32),
                pltpu.VMEM((2, PAIRS), jnp.int32),
                pltpu.VMEM((1, PAIRS), jnp.int32),
                pltpu.VMEM((128, 3 * PAIRS), BF16),
                pltpu.VMEM((128, 3 * 128), BF16),
                pltpu.VMEM((3 * ROWS, 128), BF16),
                pltpu.VMEM((3 * ROWS, 2 * PAIRS), BF16),
                pltpu.VMEM((GROUP, 2 * PAIRS), F32),
                pltpu.VMEM((2 * ROWS, 2 * ROWS), BF16),
                pltpu.VMEM((GROUP, EACH * 2 * PIECES[0], ROWS), BF16),
                pltpu.VMEM((GROUP, EACH * 2 * PIECES[1], ROWS), BF16),
                pltpu.VMEM((GROUP, EACH * 2 * PIECES[0], ROWS), BF16),
                pltpu.VMEM((GROUP, EACH * 2 * PIECES[1], ROWS), BF16),
                pltpu.VMEM((2, EDGE, ROWS), BF16),
                pltpu.VMEM((GROUP, EDGE, ROWS), BF16),
                pltpu.VMEM((GROUP, EDGE, ROWS), BF16),
                pltpu.VMEM((DATES, 2, TILE, ROWS), F32),
                pltpu.VMEM((DATES, PART, ROWS), F32),
                pltpu.VMEM((2 * CHUNK, WINDOW, ROWS), F32),
                pltpu.VMEM((2 * CHUNK * HALF, 2 * ROWS), BF16),
                pltpu.VMEM((6 * PAIRS * 8, ROWS), F32),
                pltpu.VMEM((2, 3 * PAIRS, ROWS), F32),
                pltpu.VMEM((1, ROWS), F32),
                pltpu.VMEM((columns, ROWS), F32),
                pltpu.VMEM((GROUP, ROWS), F32),
                pltpu.VMEM((1, ROWS), F32),
                pltpu.VMEM((GROUP, 24, 128), F32),
                sem((1,)), sem((4,)), sem((1,)), sem((1,)),
                sem((2,)), sem((1,)), pltpu.SemaphoreType.REGULAR((2,)), pltpu.SemaphoreType.REGULAR, pltpu.SemaphoreType.REGULAR,
                sem((1,)), sem((1,)), sem((1,)), sem((1,)),
                sem((1,)), sem((1,)), sem((1,)), sem((1,)),
                sem((1,)), sem((3,)),
            ],
            compiler_params=pltpu.CompilerParams(
                collective_id=0, has_side_effects=True, vmem_limit_bytes=54682 * 1024
            ),
        )(slc, pairs, owner)
        interferogram, coherence = pl.pallas_call(
            place_kernel,
            out_shape=(
                jax.ShapeDtypeStruct((2, CAP, 16, 32), F32),
                jax.ShapeDtypeStruct((CAP, 16, 32), F32),
            ),
            in_specs=[vmem, vmem],
            out_specs=(vmem, vmem),
            compiler_params=pltpu.CompilerParams(vmem_limit_bytes=2 * 1024 * 1024),
        )(landed.reshape(GROUP * 24, 128), scaling)
        return jnp.swapaxes(interferogram, 2, 3), jnp.swapaxes(coherence, 1, 2)

    return jax.shard_map(
        local,
        mesh=mesh,
        in_specs=(P(None, "dates", None, "cols"), P(), P()),
        out_specs=(P(None, "dates", None, "cols"), P("dates", None, "cols")),
        check_vma=False,
    )
```

```python
import math

import jax
import jax.numpy as jnp
import ml_dtypes
import numpy as np
from jax import lax
from jax.experimental import pallas as pl
from jax.experimental.pallas import tpu as pltpu
from jax.sharding import PartitionSpec as P

MESH = pl.DeviceIdType.MESH
F32 = jnp.float32
BF16 = jnp.bfloat16

TAPS = [math.exp(-k * k / 8.0) for k in range(-4, 5)]
WEIGHTS = [float(np.float32(t / sum(TAPS))) for t in TAPS]
HIGH = [float(np.float32(w).astype(ml_dtypes.bfloat16)) for w in WEIGHTS]
LOW = [float(np.float32(w - h).astype(ml_dtypes.bfloat16)) for w, h in zip(WEIGHTS, HIGH)]

GROUP = 8
EACH = 4
DATES = GROUP * EACH
PAIRS = 64
CAP = 12
ROWS = 128
PART = 32
TILE = PART + 8
WIDTH = GROUP * PART
PIECES = (24, 16)
HALF = PART // 2
WINDOW = HALF + 8
EDGE = EACH * 2 * 8
CHUNK = 32


def split(x):
    high = x.astype(BF16)
    return high, (x - high.astype(F32)).astype(BF16)


def split3(x):
    high = x.astype(BF16)
    rest = x - high.astype(F32)
    mid = rest.astype(BF16)
    return high, mid, (rest - mid.astype(F32)).astype(BF16)


def dot(a, b):
    return jnp.dot(a, b, preferred_element_type=F32)


def iota(shape, axis):
    return lax.broadcasted_iota(jnp.int32, shape, axis)


def cutter(half):
    start, size = (-4, PIECES[0]) if half == 0 else (PIECES[0] - 4, PIECES[1])
    lane = iota((size, WIDTH), 1)
    row = iota((size, WIDTH), 0)
    pieces = [jnp.where(lane == row + (PART * e + start), 1.0, 0.0) for e in range(GROUP)]
    lane = iota((8, WIDTH), 1)
    row = iota((8, WIDTH), 0)
    pieces.append(jnp.where(lane == row + (WIDTH - 4 if half == 0 else -4), 1.0, 0.0))
    return jnp.concatenate(pieces, axis=0).astype(BF16)


def band(weights):
    gap = jnp.abs(iota((ROWS, ROWS), 0) - iota((ROWS, ROWS), 1))
    result = jnp.zeros((ROWS, ROWS), F32)
    for k in range(5):
        result = jnp.where(gap == k, weights[4 + k], result)
    return result.astype(BF16)


def along_columns(ref, index):
    result = WEIGHTS[4] * ref[index, 4 : 4 + HALF, :]
    for k in range(4):
        both = ref[index, k : k + HALF, :] + ref[index, 8 - k : 8 - k + HALF, :]
        result = result + WEIGHTS[k] * both
    return result


def kernel(
    nz, count, slc_hbm, pairs_hbm, owner_hbm, landed, scaling,
    slc, pairs_s, pairs_v, owner_v, select, own, look, hot, source_of, smoother, sent_0, sent_1, got_0, got_1,
    edge_out, edge_left, edge_right, images, roots, fields, lhs, sums, looked,
    power_row, power_in, totals, factor_in, results,
    main_send_0, main_recv_0, main_send_1, main_recv_1, edge_send, edge_recv, ready, joined,
    here, up_send, up_recv, down_send, down_recv, d_send, d_recv, out_send, out_recv, in_sem, table_sem,
):
    load = pltpu.make_async_copy(slc_hbm, slc, in_sem.at[0])
    load.start()

    d = lax.axis_index("dates")
    c = lax.axis_index("cols")
    z = c % nz

    def date_peer(k):
        return {"dates": (d + k) % GROUP, "cols": c}

    right = (c + 1) % count
    left = (c + count - 1) % count
    near = min(3, nz)
    right_later = (z < nz - 1) & (c < count - 1)
    right_earlier = (z == nz - 1) & (c < count - 1)
    left_later = (z == 0) & (c > 0)
    left_earlier = (z > 0) & (c > 0)

    barrier = pltpu.get_barrier_semaphore()

    def greet(device):
        pl.semaphore_signal(barrier, inc=1, device_id=device, device_id_type=MESH)

    def turn(e):
        return jnp.where(c == 0, (e + GROUP - 1) % GROUP, e)

    mine_turn = turn(d)
    for k in range(1, GROUP):

        @pl.when(turn((d + k) % GROUP) > mine_turn)
        def _():
            greet(date_peer(k))

    @pl.when(right_later & (d == GROUP - 1))
    def _():
        for e in range(GROUP):
            greet({"dates": e, "cols": right})

    @pl.when(left_later)
    def _():
        greet({"dates": GROUP - 1, "cols": left})

    @pl.when(left_later & (d == 0))
    def _():
        for e in range(GROUP):
            greet({"dates": e, "cols": left})

    hands_on = z == near - 1
    handed = z >= near
    hand = c - z + near - 1

    @pl.when(hands_on)
    def _():
        for i in range(near, nz):
            greet({"dates": d, "cols": hand - (near - 1) + i})

    last = (d == GROUP - 1).astype(jnp.int32)

    def tell_ready(side, e, other):
        pl.semaphore_signal(
            ready.at[side], inc=1, device_id={"dates": e, "cols": other}, device_id_type=MESH
        )

    def enter():
        awaited = (
            mine_turn
            + (c > 0).astype(jnp.int32)
            + handed.astype(jnp.int32)
            + right_earlier.astype(jnp.int32) * (1 + GROUP * last)
            + left_earlier.astype(jnp.int32)
        )

        @pl.when(awaited > 0)
        def _():
            pl.semaphore_wait(barrier, awaited)

        for k in range(1, GROUP):

            @pl.when(turn((d + k) % GROUP) < mine_turn)
            def _():
                pl.semaphore_signal(joined, inc=1, device_id=date_peer(k), device_id_type=MESH)

        @pl.when(handed)
        def _():
            pl.semaphore_signal(
                here, inc=1, device_id={"dates": d, "cols": hand}, device_id_type=MESH
            )

        @pl.when(left_earlier & (d == 0))
        def _():
            tell_ready(0, GROUP - 1, left)

        @pl.when(right_earlier & (d == GROUP - 1))
        def _():
            for e in range(GROUP):
                tell_ready(1, e, right)

    enter()

    @pl.when(c == 0)
    def _():
        def one(i, carry):
            greet({"dates": d, "cols": i})
            return carry

        lax.fori_loop(1, count, one, 0)

    tables = [
        pltpu.make_async_copy(pairs_hbm, pairs_s, table_sem.at[0]),
        pltpu.make_async_copy(pairs_hbm, pairs_v, table_sem.at[1]),
        pltpu.make_async_copy(owner_hbm, owner_v, table_sem.at[2]),
    ]
    for table in tables:
        table.start()

    sent = (sent_0, sent_1)
    edge_in = (edge_left, edge_right)
    got = (got_0, got_1)

    def cut(half, matrix):
        size = PIECES[half]
        for t in range(EACH):
            both = jnp.concatenate([slc[0, t], slc[1, t]], axis=0)
            turned = lax.dot_general(
                matrix, both, (((1,), (1,)), ((), ())), preferred_element_type=F32
            )
            for e in range(GROUP + 1):
                rows = turned[size * e : size * (e + 1)] if e < GROUP else turned[size * GROUP :]
                value = jnp.concatenate([rows[:, :ROWS], rows[:, ROWS:]], axis=0).astype(BF16)
                if e < GROUP:
                    sent[half][e, 2 * size * t : 2 * size * (t + 1), :] = value
                else:
                    edge_out[half, 16 * t : 16 * (t + 1), :] = value

    matrix = cutter(0)
    high = band(HIGH)
    low = band(LOW)
    smoother[:, :ROWS] = jnp.concatenate([high, high], axis=0)
    smoother[:, ROWS:] = jnp.concatenate([low, low], axis=0)

    def powers():
        power_rows = []
        for t in range(EACH):
            wide = jnp.concatenate([slc[0, t], slc[1, t]], axis=0).astype(F32)
            square = jnp.sum(wide * wide, axis=0, keepdims=True)
            power_rows.append(square[:, :ROWS] + square[:, ROWS:])
        folded = jnp.concatenate(power_rows + [jnp.zeros((8 - EACH, ROWS), F32)], axis=0)
        folded = folded + pltpu.roll(folded, 64, 1)
        folded = folded + pltpu.roll(folded, 32, 1)
        own_lane = (iota((8, ROWS), 1) >> 5) == iota((8, ROWS), 0)
        power_row[...] = jnp.sum(jnp.where(own_lane, folded, 0.0), axis=0, keepdims=True)

    def stage(src, dst, send, recv, peer):
        return pltpu.make_async_remote_copy(
            src_ref=src, dst_ref=dst, send_sem=send, recv_sem=recv, device_id=peer, device_id_type=MESH
        )

    def up_copy(i, size=1):
        return stage(
            power_in.at[pl.ds(0, size)] if size > 1 else power_row, power_in.at[pl.ds(i, size)],
            up_send.at[0], up_recv.at[0], {"dates": d, "cols": 0},
        )

    def down_copy(i):
        return stage(factor_in, factor_in, down_send.at[0], down_recv.at[0], {"dates": d, "cols": i})

    def send_up():
        @pl.when(c > 0)
        def _():
            up_copy(c).start()

    late = z >= nz // 2

    load.wait()

    @pl.when(late)
    def _():
        powers()
        send_up()

    cut(0, matrix)

    @pl.when(mine_turn < GROUP - 1)
    def _():
        pl.semaphore_wait(joined, GROUP - 1 - mine_turn)

    targets = ({"dates": 0, "cols": right}, {"dates": GROUP - 1, "cols": left})

    def edge_copy(side):
        return pltpu.make_async_remote_copy(
            src_ref=edge_out.at[side], dst_ref=edge_in[side].at[d], send_sem=edge_send.at[side],
            recv_sem=edge_recv.at[0], device_id=targets[side], device_id_type=MESH,
        )

    order = (4, 3, 5, 2, 6, 1, 7)
    slots = {4: 0, 3: 1, 5: 2}

    def first_copy(k, size=1):
        return stage(
            sent_0.at[pl.ds((d + k) % GROUP if size == 1 else 0, size)],
            got_0.at[pl.ds(d if size == 1 else 0, size)],
            main_send_0.at[0], main_recv_0.at[slots.get(k, 3)], date_peer(k),
        )

    def second_copy(k, size=1):
        return stage(
            sent_1.at[pl.ds((d + k) % GROUP if size == 1 else 0, size)],
            got_1.at[pl.ds(d if size == 1 else 0, size)],
            main_send_1.at[0], main_recv_1.at[0], date_peer(k),
        )

    for k in order:
        first_copy(k).start()

    @pl.when(z < nz // 2)
    def _():
        powers()
        send_up()

    @pl.when(right_earlier)
    def _():
        edge_copy(0).start()

    cut(1, cutter(1))
    for k in order:
        second_copy(k).start()

    @pl.when(left_earlier)
    def _():
        edge_copy(1).start()

    got_1[d] = sent_1[d]

    @pl.when((d != 0) | (c == 0))
    def _():
        edge_left[...] = jnp.zeros_like(edge_left)

    @pl.when((d != GROUP - 1) | (c == count - 1))
    def _():
        edge_right[...] = jnp.zeros_like(edge_right)


    for table in tables:
        table.wait()
    owner_row = owner_v[...]
    owner_down = jnp.transpose(jnp.broadcast_to(owner_row.astype(F32), (ROWS, PAIRS)))[:, :PAIRS]
    earlier = iota((PAIRS, PAIRS), 0) < iota((PAIRS, PAIRS), 1)
    same = owner_down == owner_row.astype(F32)
    rank = jnp.sum(jnp.where(same & earlier, 1.0, 0.0), axis=0, keepdims=True).astype(jnp.int32)
    place = (rank & 3) * 32 + owner_row * 4 + (rank >> 2)
    one = jnp.where(iota((128, PAIRS), 0) == place, 1.0, 0.0)
    select[...] = jnp.concatenate([one, one, one], axis=1).astype(BF16)
    later = iota((PAIRS, PAIRS), 0) > iota((PAIRS, PAIRS), 1)
    rank_down = jnp.sum(jnp.where(same & later, 1.0, 0.0), axis=1, keepdims=True)
    quarter = (iota((PAIRS, 128), 1) >> 5).astype(F32)
    mine = jnp.where(owner_down[:, :1] == d.astype(F32), rank_down, -1.0)
    masks = [jnp.where(mine == quarter + 4.0 * g, 1.0, 0.0) for g in range(3)]
    masks = jnp.concatenate(masks, axis=1)
    own[...] = jnp.concatenate([masks, jnp.zeros_like(masks)], axis=0).astype(BF16)

    date = jnp.concatenate([pairs_v[0:1, :], pairs_v[1:2, :]], axis=1)
    one = jnp.where((iota((ROWS, 2 * PAIRS), 0) >> 5) == (date & (EACH - 1)), 1.0, 0.0)
    hot[...] = jnp.concatenate([one, one, one], axis=0).astype(BF16)
    source_of[...] = jnp.where(iota((GROUP, 2 * PAIRS), 0) == (date >> 2), 1.0, 0.0)
    one = jnp.where((iota((ROWS, 128), 0) >> 2) == (iota((ROWS, 128), 1) & 31), 1.0, 0.0)
    look[...] = jnp.concatenate([one, one, one], axis=0).astype(BF16)

    def edges(side):
        stage(
            edge_in[side], edge_in[side], edge_send.at[side], edge_recv.at[0], targets[side]
        ).wait_recv()

    def smooth_powers(number):
        for t in range(number):
            big, small = split(along_columns(fields, t))
            lhs[HALF * t : HALF * (t + 1), :ROWS] = big
            lhs[HALF * t : HALF * (t + 1), ROWS:] = small
        smooth = dot(lhs[: number * HALF, :], smoother[...])
        return jnp.sqrt(smooth[:, :ROWS] + smooth[:, ROWS:])

    def take_first(sources, ref):
        size = PIECES[0]
        for i, source in enumerate(sources):
            for t in range(EACH):
                piece = ref[source, 2 * size * t : 2 * size * (t + 1), :].astype(F32)
                edge = edge_left[source, 16 * t : 16 * (t + 1), :].astype(F32)
                real = jnp.concatenate([piece[:8] + edge[:8], piece[8:size]], axis=0)
                imag = jnp.concatenate([piece[size : size + 8] + edge[8:], piece[size + 8 :]], axis=0)
                images[source * EACH + t, 0, :size] = real
                images[source * EACH + t, 1, :size] = imag
                fields[EACH * i + t] = real * real + imag * imag
        smooth = smooth_powers(EACH * len(sources))
        for i, source in enumerate(sources):
            for t in range(EACH):
                at = HALF * (EACH * i + t)
                roots[source * EACH + t, :HALF] = smooth[at : at + HALF]

    def arrive(*ks):
        first_copy(ks[0], len(ks)).wait_recv()
        take_first([(d + GROUP - k) % GROUP for k in ks], got_0)

    def take_second():
        size = PIECES[1]
        for date in range(DATES):
            source, t = date // EACH, date % EACH
            piece = got_1[source, 2 * size * t : 2 * size * (t + 1), :].astype(F32)
            edge = edge_right[source, 16 * t : 16 * (t + 1), :].astype(F32)
            real = jnp.concatenate([piece[:8], piece[8:size] + edge[:8]], axis=0)
            imag = jnp.concatenate([piece[size : size + 8], piece[size + 8 :] + edge[8:]], axis=0)
            images[date, 0, PIECES[0] :] = real
            images[date, 1, PIECES[0] :] = imag
            real = jnp.concatenate([images[date, 0, HALF : PIECES[0]], real], axis=0)
            imag = jnp.concatenate([images[date, 1, HALF : PIECES[0]], imag], axis=0)
            fields[date] = real * real + imag * imag
        smooth = smooth_powers(DATES)
        for date in range(DATES):
            roots[date, HALF:] = smooth[HALF * date : HALF * (date + 1)]

    def pairs_of(half, then=None):
        window = slice(HALF * half, HALF * half + WINDOW)

        def place(field, p):
            return pl.ds(((3 * half + field) * PAIRS + p) * 8, 8)

        def chunk(index, carry):
            dates = []
            for i in range(CHUNK):
                p = index * CHUNK + i
                first = pairs_s[0, p]
                second = pairs_s[1, p]
                dates.append((first, second))
                real_a = images[first, 0, window]
                imag_a = images[first, 1, window]
                real_b = images[second, 0, window]
                imag_b = images[second, 1, window]
                fields[2 * i] = real_a * real_b + imag_a * imag_b
                fields[2 * i + 1] = imag_a * real_b - real_a * imag_b
            for i in range(CHUNK):
                p = index * CHUNK + i
                for f in range(2):
                    n = 2 * i + f
                    big, small = split(along_columns(fields, n))
                    lhs[HALF * n : HALF * (n + 1), :ROWS] = big
                    lhs[HALF * n : HALF * (n + 1), ROWS:] = small
                    sums[place(f, p), :] = fields[n, 4:12, :] + fields[n, 12:20, :]
            smooth = dot(lhs[...], smoother[...])
            smooth = smooth[:, :ROWS] + smooth[:, ROWS:]
            for i in range(CHUNK):
                p = index * CHUNK + i
                first, second = dates[i]
                real = smooth[2 * HALF * i : 2 * HALF * i + HALF]
                imag = smooth[2 * HALF * i + HALF : 2 * HALF * (i + 1)]
                below = (
                    roots[first, HALF * half : HALF * (half + 1)]
                    * roots[second, HALF * half : HALF * (half + 1)]
                )
                value = jnp.sqrt(real * real + imag * imag) / (below + 1e-06)
                sums[place(2, p), :] = value[0:8] + value[8:16]
            return carry

        lax.fori_loop(0, PAIRS // CHUNK, chunk, 0)
        if then is not None:
            then()
        rows = sums[pl.ds(3 * half * PAIRS * 8, 3 * PAIRS, stride=8), :]
        for i in range(1, 8):
            rows = rows + sums[pl.ds(3 * half * PAIRS * 8 + i, 3 * PAIRS, stride=8), :]
        looked[half] = dot(jnp.concatenate(split3(rows), axis=1), look[...])

    @pl.when(right_later)
    def _():
        pl.semaphore_wait(ready.at[0], 1)

        @pl.when(d == GROUP - 1)
        def _():
            for e in range(GROUP - 1):
                tell_ready(0, e, c)

        edge_copy(0).start()

    @pl.when(left_later)
    def _():
        pl.semaphore_wait(ready.at[1], 1)
        edge_copy(1).start()

    @pl.when((d == 0) & (c > 0))
    def _():
        edges(0)

    take_first([d], sent_0)
    arrive(4)
    arrive(3)
    arrive(5)
    arrive(2, 6, 1, 7)
    pairs_of(0)

    def d_copy(k, size=1):
        return stage(
            totals.at[pl.ds(d if size == 1 else 0, size)], totals.at[pl.ds(d if size == 1 else 0, size)],
            d_send.at[0], d_recv.at[0], date_peer(k),
        )

    def add_up():
        @pl.when(c == 0)
        def _():
            up_copy(1, count - 1).wait_recv()
            total = power_row[...] + jnp.sum(power_in[1:count, :], axis=0, keepdims=True)
            totals[pl.ds(d, 1), :] = total
            for k in order:
                d_copy(k).start()

    @pl.when((d == GROUP - 1) & (c < count - 1))
    def _():
        edges(1)

    second_copy(1, GROUP - 1).wait_recv()
    take_second()
    pairs_of(1, add_up)

    wide = []
    for q in range(6):
        piece = looked[q // 3, PAIRS * (q % 3) : PAIRS * (q % 3 + 1)]
        wide.append(piece if q % 3 < 2 else piece * (1.0 / 64.0))
    stacked = jnp.concatenate(split3(jnp.concatenate(wide, axis=1)), axis=0)
    placed = dot(select[...], stacked)
    lane = iota((32, 128), 1)
    for q in range(6):
        part = placed[:, 128 * q : 128 * (q + 1)]
        value = jnp.where(
            lane < 64,
            jnp.where(lane < 32, part[0:32], part[32:64]),
            jnp.where(lane < 96, part[64:96], part[96:128]),
        )
        for e in range(GROUP):
            results[e, 4 * q : 4 * q + 4, :] = value[4 * e : 4 * e + 4]

    def out_copy(k, size=1):
        return stage(
            results.at[pl.ds((d + k) % GROUP if size == 1 else 0, size)],
            landed.at[pl.ds(d if size == 1 else 0, size)],
            out_send.at[0], out_recv.at[0], date_peer(k),
        )

    for k in order:
        out_copy(k).start()
    landed[d] = results[d]

    @pl.when(c == 0)
    def _():
        d_copy(1, GROUP - 1).wait_recv()
        parts = jnp.concatenate(split3(totals[...]), axis=1)
        total = jnp.sum(dot(parts, hot[...]) * source_of[...], axis=0, keepdims=True)
        scale = jnp.sqrt(total / (ROWS * WIDTH * count) + 1e-06)
        factor = (1.0 / 64.0) / (scale * pltpu.roll(scale, PAIRS, 1))
        factor_in[...] = factor
        for i in range(near):
            for j in range(count // nz):
                if i + j > 0:
                    down_copy(j * nz + i).start()

    @pl.when(c > 0)
    def _():
        down_copy(0).wait_recv()

    @pl.when(hands_on)
    def _():
        if nz > near:
            pl.semaphore_wait(here, nz - near)
        for i in range(near, nz):
            down_copy(hand - (near - 1) + i).start()

    factors = dot(jnp.concatenate(split3(factor_in[...]), axis=0), own[...])
    factors = jnp.sum(factors, axis=0, keepdims=True)
    for g in range(3):
        scaling[g : g + 1, :] = factors[:, 128 * g : 128 * (g + 1)]
    out_copy(1, GROUP - 1).wait_recv()
    first_copy(1, GROUP - 1).wait_send()
    second_copy(1, GROUP - 1).wait_send()
    out_copy(1, GROUP - 1).wait_send()

    @pl.when(right_later | right_earlier)
    def _():
        edge_copy(0).wait_send()

    @pl.when(left_later | left_earlier)
    def _():
        edge_copy(1).wait_send()

    def sent_down(number):
        stage(
            power_in.at[pl.ds(0, number)], power_in.at[pl.ds(0, number)], down_send.at[0],
            down_recv.at[0], {"dates": d, "cols": c},
        ).wait_send()

    @pl.when(c > 0)
    def _():
        up_copy(c).wait_send()

    @pl.when(c == 0)
    def _():
        d_copy(1, GROUP - 1).wait_send()
        sent_down(near * (count // nz) - 1)

    if nz > near:

        @pl.when(hands_on)
        def _():
            sent_down(nz - near)


def place_kernel(landed, scaling, interferogram, coherence):
    for f in range(3):
        for g in range(3):
            block = landed[pl.ds(f * 4 + g, 16, stride=12), :]
            if f < 2:
                block = block * scaling[g : g + 1, :]
            for j in range(4):
                piece = block[:, 32 * j : 32 * j + 32]
                if f < 2:
                    interferogram[f, 4 * g + j] = piece
                else:
                    coherence[4 * g + j] = piece


def solution(mesh):
    columns = mesh.shape["cols"]
    nz = 8 if columns % 8 == 0 else 2
    sem = pltpu.SemaphoreType.DMA
    vmem = pl.BlockSpec(memory_space=pltpu.VMEM)

    def local(slc, pairs, owner):
        pairs = pairs.T
        owner = owner.reshape(1, PAIRS)
        landed, scaling = pl.pallas_call(
            lambda *refs: kernel(nz, columns, *refs),
            out_shape=(jax.ShapeDtypeStruct((GROUP, 24, 128), F32), jax.ShapeDtypeStruct((8, 128), F32)),
            in_specs=[pl.BlockSpec(memory_space=pl.ANY)] * 3,
            out_specs=(vmem, vmem),
            scratch_shapes=[
                pltpu.VMEM((2, EACH, ROWS, WIDTH), BF16),
                pltpu.SMEM((2, PAIRS), jnp.int32),
                pltpu.VMEM((2, PAIRS), jnp.int32),
                pltpu.VMEM((1, PAIRS), jnp.int32),
                pltpu.VMEM((128, 3 * PAIRS), BF16),
                pltpu.VMEM((128, 3 * 128), BF16),
                pltpu.VMEM((3 * ROWS, 128), BF16),
                pltpu.VMEM((3 * ROWS, 2 * PAIRS), BF16),
                pltpu.VMEM((GROUP, 2 * PAIRS), F32),
                pltpu.VMEM((2 * ROWS, 2 * ROWS), BF16),
                pltpu.VMEM((GROUP, EACH * 2 * PIECES[0], ROWS), BF16),
                pltpu.VMEM((GROUP, EACH * 2 * PIECES[1], ROWS), BF16),
                pltpu.VMEM((GROUP, EACH * 2 * PIECES[0], ROWS), BF16),
                pltpu.VMEM((GROUP, EACH * 2 * PIECES[1], ROWS), BF16),
                pltpu.VMEM((2, EDGE, ROWS), BF16),
                pltpu.VMEM((GROUP, EDGE, ROWS), BF16),
                pltpu.VMEM((GROUP, EDGE, ROWS), BF16),
                pltpu.VMEM((DATES, 2, TILE, ROWS), F32),
                pltpu.VMEM((DATES, PART, ROWS), F32),
                pltpu.VMEM((2 * CHUNK, WINDOW, ROWS), F32),
                pltpu.VMEM((2 * CHUNK * HALF, 2 * ROWS), BF16),
                pltpu.VMEM((6 * PAIRS * 8, ROWS), F32),
                pltpu.VMEM((2, 3 * PAIRS, ROWS), F32),
                pltpu.VMEM((1, ROWS), F32),
                pltpu.VMEM((columns, ROWS), F32),
                pltpu.VMEM((GROUP, ROWS), F32),
                pltpu.VMEM((1, ROWS), F32),
                pltpu.VMEM((GROUP, 24, 128), F32),
                sem((1,)), sem((4,)), sem((1,)), sem((1,)),
                sem((2,)), sem((1,)), pltpu.SemaphoreType.REGULAR((2,)), pltpu.SemaphoreType.REGULAR, pltpu.SemaphoreType.REGULAR,
                sem((1,)), sem((1,)), sem((1,)), sem((1,)),
                sem((1,)), sem((1,)), sem((1,)), sem((1,)),
                sem((1,)), sem((3,)),
            ],
            compiler_params=pltpu.CompilerParams(
                collective_id=0, has_side_effects=True, vmem_limit_bytes=54682 * 1024
            ),
        )(slc, pairs, owner)
        interferogram, coherence = pl.pallas_call(
            place_kernel,
            out_shape=(
                jax.ShapeDtypeStruct((2, CAP, 16, 32), F32),
                jax.ShapeDtypeStruct((CAP, 16, 32), F32),
            ),
            in_specs=[vmem, vmem],
            out_specs=(vmem, vmem),
            compiler_params=pltpu.CompilerParams(vmem_limit_bytes=2 * 1024 * 1024),
        )(landed.reshape(GROUP * 24, 128), scaling)
        return jnp.swapaxes(interferogram, 2, 3), jnp.swapaxes(coherence, 1, 2)

    return jax.shard_map(
        local,
        mesh=mesh,
        in_specs=(P(None, "dates", None, "cols"), P(), P()),
        out_specs=(P(None, "dates", None, "cols"), P("dates", None, "cols")),
        check_vma=False,
    )
```

```python
import math

import jax
import jax.numpy as jnp
import ml_dtypes
import numpy as np
from jax import lax
from jax.experimental import pallas as pl
from jax.experimental.pallas import tpu as pltpu
from jax.sharding import PartitionSpec as P

MESH = pl.DeviceIdType.MESH
F32 = jnp.float32
BF16 = jnp.bfloat16

TAPS = [math.exp(-k * k / 8.0) for k in range(-4, 5)]
WEIGHTS = [float(np.float32(t / sum(TAPS))) for t in TAPS]
HIGH = [float(np.float32(w).astype(ml_dtypes.bfloat16)) for w in WEIGHTS]
LOW = [float(np.float32(w - h).astype(ml_dtypes.bfloat16)) for w, h in zip(WEIGHTS, HIGH)]

GROUP = 8
EACH = 4
DATES = GROUP * EACH
PAIRS = 64
CAP = 12
ROWS = 128
PART = 32
TILE = PART + 8
WIDTH = GROUP * PART
PIECES = (24, 16)
HALF = PART // 2
WINDOW = HALF + 8
EDGE = EACH * 2 * 8
CHUNK = 32


def split(x):
    high = x.astype(BF16)
    return high, (x - high.astype(F32)).astype(BF16)


def split3(x):
    high = x.astype(BF16)
    rest = x - high.astype(F32)
    mid = rest.astype(BF16)
    return high, mid, (rest - mid.astype(F32)).astype(BF16)


def dot(a, b):
    return jnp.dot(a, b, preferred_element_type=F32)


def iota(shape, axis):
    return lax.broadcasted_iota(jnp.int32, shape, axis)


def cutter(half):
    start, size = (-4, PIECES[0]) if half == 0 else (PIECES[0] - 4, PIECES[1])
    lane = iota((size, WIDTH), 1)
    row = iota((size, WIDTH), 0)
    pieces = [jnp.where(lane == row + (PART * e + start), 1.0, 0.0) for e in range(GROUP)]
    lane = iota((8, WIDTH), 1)
    row = iota((8, WIDTH), 0)
    pieces.append(jnp.where(lane == row + (WIDTH - 4 if half == 0 else -4), 1.0, 0.0))
    return jnp.concatenate(pieces, axis=0).astype(BF16)


def band(weights):
    gap = jnp.abs(iota((ROWS, ROWS), 0) - iota((ROWS, ROWS), 1))
    result = jnp.zeros((ROWS, ROWS), F32)
    for k in range(5):
        result = jnp.where(gap == k, weights[4 + k], result)
    return result.astype(BF16)


def along_columns(ref, index):
    result = WEIGHTS[4] * ref[index, 4 : 4 + HALF, :]
    for k in range(4):
        both = ref[index, k : k + HALF, :] + ref[index, 8 - k : 8 - k + HALF, :]
        result = result + WEIGHTS[k] * both
    return result


def kernel(
    nz, count, slc_hbm, pairs_hbm, owner_hbm, landed, scaling,
    slc, pairs_s, pairs_v, owner_v, select, own, look, hot, source_of, smoother, sent_0, sent_1, got_0, got_1,
    edge_out, edge_left, edge_right, images, roots, fields, lhs, sums, looked,
    power_row, power_in, totals, factor_in, results,
    main_send_0, main_recv_0, main_send_1, main_recv_1, edge_send, edge_recv, ready,
    here, up_send, up_recv, down_send, down_recv, d_send, d_recv, out_send, out_recv, in_sem, table_sem,
):
    load = pltpu.make_async_copy(slc_hbm, slc, in_sem.at[0])
    load.start()

    d = lax.axis_index("dates")
    c = lax.axis_index("cols")
    z = c % nz

    def date_peer(k):
        return {"dates": (d + k) % GROUP, "cols": c}

    right = (c + 1) % count
    left = (c + count - 1) % count
    near = min(3, nz)
    right_later = (z < nz - 1) & (c < count - 1)
    right_earlier = (z == nz - 1) & (c < count - 1)
    left_later = (z == 0) & (c > 0)
    left_earlier = (z > 0) & (c > 0)

    barrier = pltpu.get_barrier_semaphore()

    def greet(device):
        pl.semaphore_signal(barrier, inc=1, device_id=device, device_id_type=MESH)

    for k in range(1, GROUP):
        greet(date_peer(k))

    @pl.when(right_later & (d == GROUP - 1))
    def _():
        for e in range(GROUP):
            greet({"dates": e, "cols": right})

    @pl.when(left_later)
    def _():
        greet({"dates": GROUP - 1, "cols": left})

    @pl.when(left_later & (d == 0))
    def _():
        for e in range(GROUP):
            greet({"dates": e, "cols": left})

    @pl.when(c == 0)
    def _():
        def one(i, carry):
            greet({"dates": d, "cols": i})
            return carry

        lax.fori_loop(1, count, one, 0)

    hands_on = z == near - 1
    handed = z >= near
    hand = c - z + near - 1

    @pl.when(hands_on)
    def _():
        for i in range(near, nz):
            greet({"dates": d, "cols": hand - (near - 1) + i})

    tables = [
        pltpu.make_async_copy(pairs_hbm, pairs_s, table_sem.at[0]),
        pltpu.make_async_copy(pairs_hbm, pairs_v, table_sem.at[1]),
        pltpu.make_async_copy(owner_hbm, owner_v, table_sem.at[2]),
    ]
    for table in tables:
        table.start()

    sent = (sent_0, sent_1)
    edge_in = (edge_left, edge_right)
    got = (got_0, got_1)

    def cut(half, matrix):
        size = PIECES[half]
        for t in range(EACH):
            both = jnp.concatenate([slc[0, t], slc[1, t]], axis=0)
            turned = lax.dot_general(
                matrix, both, (((1,), (1,)), ((), ())), preferred_element_type=F32
            )
            for e in range(GROUP + 1):
                rows = turned[size * e : size * (e + 1)] if e < GROUP else turned[size * GROUP :]
                value = jnp.concatenate([rows[:, :ROWS], rows[:, ROWS:]], axis=0).astype(BF16)
                if e < GROUP:
                    sent[half][e, 2 * size * t : 2 * size * (t + 1), :] = value
                else:
                    edge_out[half, 16 * t : 16 * (t + 1), :] = value

    matrix = cutter(0)
    high = band(HIGH)
    low = band(LOW)
    smoother[:, :ROWS] = jnp.concatenate([high, high], axis=0)
    smoother[:, ROWS:] = jnp.concatenate([low, low], axis=0)
    load.wait()

    def powers():
        power_rows = []
        for t in range(EACH):
            wide = jnp.concatenate([slc[0, t], slc[1, t]], axis=0).astype(F32)
            square = jnp.sum(wide * wide, axis=0, keepdims=True)
            power_rows.append(square[:, :ROWS] + square[:, ROWS:])
        folded = jnp.concatenate(power_rows + [jnp.zeros((8 - EACH, ROWS), F32)], axis=0)
        folded = folded + pltpu.roll(folded, 64, 1)
        folded = folded + pltpu.roll(folded, 32, 1)
        own_lane = (iota((8, ROWS), 1) >> 5) == iota((8, ROWS), 0)
        power_row[...] = jnp.sum(jnp.where(own_lane, folded, 0.0), axis=0, keepdims=True)

    def stage(src, dst, send, recv, peer):
        return pltpu.make_async_remote_copy(
            src_ref=src, dst_ref=dst, send_sem=send, recv_sem=recv, device_id=peer, device_id_type=MESH
        )

    def up_copy(i, size=1):
        return stage(
            power_in.at[pl.ds(0, size)] if size > 1 else power_row, power_in.at[pl.ds(i, size)],
            up_send.at[0], up_recv.at[0], {"dates": d, "cols": 0},
        )

    def down_copy(i):
        return stage(factor_in, factor_in, down_send.at[0], down_recv.at[0], {"dates": d, "cols": i})

    last = (d == GROUP - 1).astype(jnp.int32)

    def tell_ready(side, e, other):
        pl.semaphore_signal(
            ready.at[side], inc=1, device_id={"dates": e, "cols": other}, device_id_type=MESH
        )

    def enter():
        pl.semaphore_wait(
            barrier,
            (GROUP - 1)
            + (c > 0).astype(jnp.int32)
            + handed.astype(jnp.int32)
            + right_earlier.astype(jnp.int32) * (1 + GROUP * last)
            + left_earlier.astype(jnp.int32),
        )

        @pl.when(handed)
        def _():
            pl.semaphore_signal(
                here, inc=1, device_id={"dates": d, "cols": hand}, device_id_type=MESH
            )

        @pl.when(left_earlier & (d == 0))
        def _():
            tell_ready(0, GROUP - 1, left)

        @pl.when(right_earlier & (d == GROUP - 1))
        def _():
            for e in range(GROUP):
                tell_ready(1, e, right)

    def send_up():
        @pl.when(c > 0)
        def _():
            up_copy(c).start()

    late = z >= nz // 2

    @pl.when(late)
    def _():
        powers()
        enter()
        send_up()

    cut(0, matrix)
    pl.when(z < nz // 2)(enter)

    targets = ({"dates": 0, "cols": right}, {"dates": GROUP - 1, "cols": left})

    def edge_copy(side):
        return pltpu.make_async_remote_copy(
            src_ref=edge_out.at[side], dst_ref=edge_in[side].at[d], send_sem=edge_send.at[side],
            recv_sem=edge_recv.at[0], device_id=targets[side], device_id_type=MESH,
        )

    order = (4, 3, 5, 2, 6, 1, 7)
    slots = {4: 0, 3: 1, 5: 2}

    def first_copy(k, size=1):
        return stage(
            sent_0.at[pl.ds((d + k) % GROUP if size == 1 else 0, size)],
            got_0.at[pl.ds(d if size == 1 else 0, size)],
            main_send_0.at[0], main_recv_0.at[slots.get(k, 3)], date_peer(k),
        )

    def second_copy(k, size=1):
        return stage(
            sent_1.at[pl.ds((d + k) % GROUP if size == 1 else 0, size)],
            got_1.at[pl.ds(d if size == 1 else 0, size)],
            main_send_1.at[0], main_recv_1.at[0], date_peer(k),
        )

    for k in order:
        first_copy(k).start()

    @pl.when(z < nz // 2)
    def _():
        powers()
        send_up()

    @pl.when(right_earlier)
    def _():
        edge_copy(0).start()

    cut(1, cutter(1))
    for k in order:
        second_copy(k).start()

    @pl.when(left_earlier)
    def _():
        edge_copy(1).start()

    got_1[d] = sent_1[d]

    @pl.when((d != 0) | (c == 0))
    def _():
        edge_left[...] = jnp.zeros_like(edge_left)

    @pl.when((d != GROUP - 1) | (c == count - 1))
    def _():
        edge_right[...] = jnp.zeros_like(edge_right)


    for table in tables:
        table.wait()
    owner_row = owner_v[...]
    owner_down = jnp.transpose(jnp.broadcast_to(owner_row.astype(F32), (ROWS, PAIRS)))[:, :PAIRS]
    earlier = iota((PAIRS, PAIRS), 0) < iota((PAIRS, PAIRS), 1)
    same = owner_down == owner_row.astype(F32)
    rank = jnp.sum(jnp.where(same & earlier, 1.0, 0.0), axis=0, keepdims=True).astype(jnp.int32)
    place = (rank & 3) * 32 + owner_row * 4 + (rank >> 2)
    one = jnp.where(iota((128, PAIRS), 0) == place, 1.0, 0.0)
    select[...] = jnp.concatenate([one, one, one], axis=1).astype(BF16)
    later = iota((PAIRS, PAIRS), 0) > iota((PAIRS, PAIRS), 1)
    rank_down = jnp.sum(jnp.where(same & later, 1.0, 0.0), axis=1, keepdims=True)
    quarter = (iota((PAIRS, 128), 1) >> 5).astype(F32)
    mine = jnp.where(owner_down[:, :1] == d.astype(F32), rank_down, -1.0)
    masks = [jnp.where(mine == quarter + 4.0 * g, 1.0, 0.0) for g in range(3)]
    masks = jnp.concatenate(masks, axis=1)
    own[...] = jnp.concatenate([masks, jnp.zeros_like(masks)], axis=0).astype(BF16)

    date = jnp.concatenate([pairs_v[0:1, :], pairs_v[1:2, :]], axis=1)
    one = jnp.where((iota((ROWS, 2 * PAIRS), 0) >> 5) == (date & (EACH - 1)), 1.0, 0.0)
    hot[...] = jnp.concatenate([one, one, one], axis=0).astype(BF16)
    source_of[...] = jnp.where(iota((GROUP, 2 * PAIRS), 0) == (date >> 2), 1.0, 0.0)
    one = jnp.where((iota((ROWS, 128), 0) >> 2) == (iota((ROWS, 128), 1) & 31), 1.0, 0.0)
    look[...] = jnp.concatenate([one, one, one], axis=0).astype(BF16)

    def edges(side):
        stage(
            edge_in[side], edge_in[side], edge_send.at[side], edge_recv.at[0], targets[side]
        ).wait_recv()

    def smooth_powers(number):
        for t in range(number):
            big, small = split(along_columns(fields, t))
            lhs[HALF * t : HALF * (t + 1), :ROWS] = big
            lhs[HALF * t : HALF * (t + 1), ROWS:] = small
        smooth = dot(lhs[: number * HALF, :], smoother[...])
        return jnp.sqrt(smooth[:, :ROWS] + smooth[:, ROWS:])

    def take_first(sources, ref):
        size = PIECES[0]
        for i, source in enumerate(sources):
            for t in range(EACH):
                piece = ref[source, 2 * size * t : 2 * size * (t + 1), :].astype(F32)
                edge = edge_left[source, 16 * t : 16 * (t + 1), :].astype(F32)
                real = jnp.concatenate([piece[:8] + edge[:8], piece[8:size]], axis=0)
                imag = jnp.concatenate([piece[size : size + 8] + edge[8:], piece[size + 8 :]], axis=0)
                images[source * EACH + t, 0, :size] = real
                images[source * EACH + t, 1, :size] = imag
                fields[EACH * i + t] = real * real + imag * imag
        smooth = smooth_powers(EACH * len(sources))
        for i, source in enumerate(sources):
            for t in range(EACH):
                at = HALF * (EACH * i + t)
                roots[source * EACH + t, :HALF] = smooth[at : at + HALF]

    def arrive(*ks):
        first_copy(ks[0], len(ks)).wait_recv()
        take_first([(d + GROUP - k) % GROUP for k in ks], got_0)

    def take_second():
        size = PIECES[1]
        for date in range(DATES):
            source, t = date // EACH, date % EACH
            piece = got_1[source, 2 * size * t : 2 * size * (t + 1), :].astype(F32)
            edge = edge_right[source, 16 * t : 16 * (t + 1), :].astype(F32)
            real = jnp.concatenate([piece[:8], piece[8:size] + edge[:8]], axis=0)
            imag = jnp.concatenate([piece[size : size + 8], piece[size + 8 :] + edge[8:]], axis=0)
            images[date, 0, PIECES[0] :] = real
            images[date, 1, PIECES[0] :] = imag
            real = jnp.concatenate([images[date, 0, HALF : PIECES[0]], real], axis=0)
            imag = jnp.concatenate([images[date, 1, HALF : PIECES[0]], imag], axis=0)
            fields[date] = real * real + imag * imag
        smooth = smooth_powers(DATES)
        for date in range(DATES):
            roots[date, HALF:] = smooth[HALF * date : HALF * (date + 1)]

    def pairs_of(half, then=None):
        window = slice(HALF * half, HALF * half + WINDOW)

        def place(field, p):
            return pl.ds(((3 * half + field) * PAIRS + p) * 8, 8)

        def chunk(index, carry):
            dates = []
            for i in range(CHUNK):
                p = index * CHUNK + i
                first = pairs_s[0, p]
                second = pairs_s[1, p]
                dates.append((first, second))
                real_a = images[first, 0, window]
                imag_a = images[first, 1, window]
                real_b = images[second, 0, window]
                imag_b = images[second, 1, window]
                fields[2 * i] = real_a * real_b + imag_a * imag_b
                fields[2 * i + 1] = imag_a * real_b - real_a * imag_b
            for i in range(CHUNK):
                p = index * CHUNK + i
                for f in range(2):
                    n = 2 * i + f
                    big, small = split(along_columns(fields, n))
                    lhs[HALF * n : HALF * (n + 1), :ROWS] = big
                    lhs[HALF * n : HALF * (n + 1), ROWS:] = small
                    sums[place(f, p), :] = fields[n, 4:12, :] + fields[n, 12:20, :]
            smooth = dot(lhs[...], smoother[...])
            smooth = smooth[:, :ROWS] + smooth[:, ROWS:]
            for i in range(CHUNK):
                p = index * CHUNK + i
                first, second = dates[i]
                real = smooth[2 * HALF * i : 2 * HALF * i + HALF]
                imag = smooth[2 * HALF * i + HALF : 2 * HALF * (i + 1)]
                below = (
                    roots[first, HALF * half : HALF * (half + 1)]
                    * roots[second, HALF * half : HALF * (half + 1)]
                )
                value = jnp.sqrt(real * real + imag * imag) / (below + 1e-06)
                sums[place(2, p), :] = value[0:8] + value[8:16]
            return carry

        lax.fori_loop(0, PAIRS // CHUNK, chunk, 0)
        if then is not None:
            then()
        rows = sums[pl.ds(3 * half * PAIRS * 8, 3 * PAIRS, stride=8), :]
        for i in range(1, 8):
            rows = rows + sums[pl.ds(3 * half * PAIRS * 8 + i, 3 * PAIRS, stride=8), :]
        looked[half] = dot(jnp.concatenate(split3(rows), axis=1), look[...])

    @pl.when(right_later)
    def _():
        pl.semaphore_wait(ready.at[0], 1)

        @pl.when(d == GROUP - 1)
        def _():
            for e in range(GROUP - 1):
                tell_ready(0, e, c)

        edge_copy(0).start()

    @pl.when(left_later)
    def _():
        pl.semaphore_wait(ready.at[1], 1)
        edge_copy(1).start()

    @pl.when((d == 0) & (c > 0))
    def _():
        edges(0)

    take_first([d], sent_0)
    arrive(4)
    arrive(3)
    arrive(5)
    arrive(2, 6, 1, 7)
    pairs_of(0)

    def d_copy(k, size=1):
        return stage(
            totals.at[pl.ds(d if size == 1 else 0, size)], totals.at[pl.ds(d if size == 1 else 0, size)],
            d_send.at[0], d_recv.at[0], date_peer(k),
        )

    def add_up():
        @pl.when(c == 0)
        def _():
            up_copy(1, count - 1).wait_recv()
            total = power_row[...] + jnp.sum(power_in[1:count, :], axis=0, keepdims=True)
            totals[pl.ds(d, 1), :] = total
            for k in order:
                d_copy(k).start()

    @pl.when((d == GROUP - 1) & (c < count - 1))
    def _():
        edges(1)

    second_copy(1, GROUP - 1).wait_recv()
    take_second()
    pairs_of(1, add_up)

    wide = []
    for q in range(6):
        piece = looked[q // 3, PAIRS * (q % 3) : PAIRS * (q % 3 + 1)]
        wide.append(piece if q % 3 < 2 else piece * (1.0 / 64.0))
    stacked = jnp.concatenate(split3(jnp.concatenate(wide, axis=1)), axis=0)
    placed = dot(select[...], stacked)
    lane = iota((32, 128), 1)
    for q in range(6):
        part = placed[:, 128 * q : 128 * (q + 1)]
        value = jnp.where(
            lane < 64,
            jnp.where(lane < 32, part[0:32], part[32:64]),
            jnp.where(lane < 96, part[64:96], part[96:128]),
        )
        for e in range(GROUP):
            results[e, 4 * q : 4 * q + 4, :] = value[4 * e : 4 * e + 4]

    def out_copy(k, size=1):
        return stage(
            results.at[pl.ds((d + k) % GROUP if size == 1 else 0, size)],
            landed.at[pl.ds(d if size == 1 else 0, size)],
            out_send.at[0], out_recv.at[0], date_peer(k),
        )

    for k in order:
        out_copy(k).start()
    landed[d] = results[d]

    @pl.when(c == 0)
    def _():
        d_copy(1, GROUP - 1).wait_recv()
        parts = jnp.concatenate(split3(totals[...]), axis=1)
        total = jnp.sum(dot(parts, hot[...]) * source_of[...], axis=0, keepdims=True)
        scale = jnp.sqrt(total / (ROWS * WIDTH * count) + 1e-06)
        factor = (1.0 / 64.0) / (scale * pltpu.roll(scale, PAIRS, 1))
        factor_in[...] = factor
        for j in range(1, count // nz):
            down_copy(j * nz).start()

    @pl.when(c > 0)
    def _():
        down_copy(0).wait_recv()

    @pl.when(hands_on)
    def _():
        if nz > near:
            pl.semaphore_wait(here, nz - near)
        for i in range(near, nz):
            down_copy(hand - (near - 1) + i).start()

    factors = dot(jnp.concatenate(split3(factor_in[...]), axis=0), own[...])
    factors = jnp.sum(factors, axis=0, keepdims=True)
    for g in range(3):
        scaling[g : g + 1, :] = factors[:, 128 * g : 128 * (g + 1)]

    @pl.when(c == 0)
    def _():
        for i in range(1, near):
            for j in range(count // nz):
                down_copy(j * nz + i).start()

    out_copy(1, GROUP - 1).wait_recv()
    first_copy(1, GROUP - 1).wait_send()
    second_copy(1, GROUP - 1).wait_send()
    out_copy(1, GROUP - 1).wait_send()

    @pl.when(right_later | right_earlier)
    def _():
        edge_copy(0).wait_send()

    @pl.when(left_later | left_earlier)
    def _():
        edge_copy(1).wait_send()

    def sent_down(number):
        stage(
            power_in.at[pl.ds(0, number)], power_in.at[pl.ds(0, number)], down_send.at[0],
            down_recv.at[0], {"dates": d, "cols": c},
        ).wait_send()

    @pl.when(c > 0)
    def _():
        up_copy(c).wait_send()

    @pl.when(c == 0)
    def _():
        d_copy(1, GROUP - 1).wait_send()
        sent_down(near * (count // nz) - 1)

    if nz > near:

        @pl.when(hands_on)
        def _():
            sent_down(nz - near)


def place_kernel(landed, scaling, interferogram, coherence):
    for f in range(3):
        for g in range(3):
            block = landed[pl.ds(f * 4 + g, 16, stride=12), :]
            if f < 2:
                block = block * scaling[g : g + 1, :]
            for j in range(4):
                piece = block[:, 32 * j : 32 * j + 32]
                if f < 2:
                    interferogram[f, 4 * g + j] = piece
                else:
                    coherence[4 * g + j] = piece


def solution(mesh):
    columns = mesh.shape["cols"]
    nz = 8 if columns % 8 == 0 else 2
    sem = pltpu.SemaphoreType.DMA
    vmem = pl.BlockSpec(memory_space=pltpu.VMEM)

    def local(slc, pairs, owner):
        pairs = pairs.T
        owner = owner.reshape(1, PAIRS)
        landed, scaling = pl.pallas_call(
            lambda *refs: kernel(nz, columns, *refs),
            out_shape=(jax.ShapeDtypeStruct((GROUP, 24, 128), F32), jax.ShapeDtypeStruct((8, 128), F32)),
            in_specs=[pl.BlockSpec(memory_space=pl.ANY)] * 3,
            out_specs=(vmem, vmem),
            scratch_shapes=[
                pltpu.VMEM((2, EACH, ROWS, WIDTH), BF16),
                pltpu.SMEM((2, PAIRS), jnp.int32),
                pltpu.VMEM((2, PAIRS), jnp.int32),
                pltpu.VMEM((1, PAIRS), jnp.int32),
                pltpu.VMEM((128, 3 * PAIRS), BF16),
                pltpu.VMEM((128, 3 * 128), BF16),
                pltpu.VMEM((3 * ROWS, 128), BF16),
                pltpu.VMEM((3 * ROWS, 2 * PAIRS), BF16),
                pltpu.VMEM((GROUP, 2 * PAIRS), F32),
                pltpu.VMEM((2 * ROWS, 2 * ROWS), BF16),
                pltpu.VMEM((GROUP, EACH * 2 * PIECES[0], ROWS), BF16),
                pltpu.VMEM((GROUP, EACH * 2 * PIECES[1], ROWS), BF16),
                pltpu.VMEM((GROUP, EACH * 2 * PIECES[0], ROWS), BF16),
                pltpu.VMEM((GROUP, EACH * 2 * PIECES[1], ROWS), BF16),
                pltpu.VMEM((2, EDGE, ROWS), BF16),
                pltpu.VMEM((GROUP, EDGE, ROWS), BF16),
                pltpu.VMEM((GROUP, EDGE, ROWS), BF16),
                pltpu.VMEM((DATES, 2, TILE, ROWS), F32),
                pltpu.VMEM((DATES, PART, ROWS), F32),
                pltpu.VMEM((2 * CHUNK, WINDOW, ROWS), F32),
                pltpu.VMEM((2 * CHUNK * HALF, 2 * ROWS), BF16),
                pltpu.VMEM((6 * PAIRS * 8, ROWS), F32),
                pltpu.VMEM((2, 3 * PAIRS, ROWS), F32),
                pltpu.VMEM((1, ROWS), F32),
                pltpu.VMEM((columns, ROWS), F32),
                pltpu.VMEM((GROUP, ROWS), F32),
                pltpu.VMEM((1, ROWS), F32),
                pltpu.VMEM((GROUP, 24, 128), F32),
                sem((1,)), sem((4,)), sem((1,)), sem((1,)),
                sem((2,)), sem((1,)), pltpu.SemaphoreType.REGULAR((2,)), pltpu.SemaphoreType.REGULAR,
                sem((1,)), sem((1,)), sem((1,)), sem((1,)),
                sem((1,)), sem((1,)), sem((1,)), sem((1,)),
                sem((1,)), sem((3,)),
            ],
            compiler_params=pltpu.CompilerParams(
                collective_id=0, has_side_effects=True, vmem_limit_bytes=54682 * 1024
            ),
        )(slc, pairs, owner)
        interferogram, coherence = pl.pallas_call(
            place_kernel,
            out_shape=(
                jax.ShapeDtypeStruct((2, CAP, 16, 32), F32),
                jax.ShapeDtypeStruct((CAP, 16, 32), F32),
            ),
            in_specs=[vmem, vmem],
            out_specs=(vmem, vmem),
            compiler_params=pltpu.CompilerParams(vmem_limit_bytes=2 * 1024 * 1024),
        )(landed.reshape(GROUP * 24, 128), scaling)
        return jnp.swapaxes(interferogram, 2, 3), jnp.swapaxes(coherence, 1, 2)

    return jax.shard_map(
        local,
        mesh=mesh,
        in_specs=(P(None, "dates", None, "cols"), P(), P()),
        out_specs=(P(None, "dates", None, "cols"), P("dates", None, "cols")),
        check_vma=False,
    )
```
